32 devices in a mesh: grp: 2 (over y), seq: 4 (over z), mem: 2 (over x), rep: 2 (over core).
Axes of the slice: x: 2, y: 2, z: 4, core: 2. Of those that a mesh axis runs over, the one named last changes fastest.
Arguments:
- video_cache: bfloat16 [3, 1536, 4096], P(None, ('grp', 'seq'), 'mem'), parts along dimension 1, may hold values from -2.390625 to 2.390625
- plan: int32 [16], P('grp'), parts along dimension 0, may hold values from 0 to 1
- alignment: int32 [2048], P(('grp', 'seq')), parts along dimension 0, may hold values from 0 to 23, as said below
- audio_tokens: bfloat16 [2048, 2048], P(('grp', 'seq')), parts along dimension 0, may hold values from -64 to 64
- kv_weight: bfloat16 [4096, 4096], P('seq', ('mem', 'rep')), may hold values from -0.09375 to 0.09375
- query_weight: bfloat16 [2048, 2048], P('seq', ('mem', 'rep')), may hold values from -0.125 to 0.125
- out_weight: bfloat16 [2048, 2048], P(('mem', 'rep'), 'seq'), may hold values from -0.125 to 0.125
Outputs:
- video_features: bfloat16 [1536, 4096], P(('grp', 'seq'), 'mem'), parts along dimension 0
- audio_output: bfloat16 [2048, 2048], P(('grp', 'seq'), ('mem', 'rep')), parts along dimension 0
The draws below stay inside these ranges and needn't reach their ends.
There are 2 independent parts, one for each index of `grp`. The reference program is written for one: setup_inputs(seed, part) draws one part's arguments, and reference() takes and returns one part's arrays. A program takes and returns all parts, laid end to end along the dimension named above; an argument that names none is the same for every part. Nothing has to cross between parts.
Inputs may be any that keep to these rules, and one draw needn't show every extreme that they name: `alignment`: frames rise with the token index up to a jitter of one frame; the first token is aligned with frame 0 and the last with frame 24 - 1.
All inputs are finite; a program needn't handle non-finite values.
Results may differ from the reference program's by a relative error of at most 0.0035.
Values may be sent and summed in bfloat16 or wider, within the bound.
No kernel may reach another device: no remote copies, remote signals or barrier semaphores. Data moves between devices by JAX's collectives and lax.ppermute only.
A program may use at most 64 MiB of HBM per device.

```python
import jax
import jax.numpy as jnp
from jax import lax

DV = 4096
DA = 2048
HEADS_A = 16
HEAD_DIM = 128
FRAMES = 24
HISTORY = 8
TV = 768
TA = 1024


def draw_plan(key, part):
    key = jax.random.fold_in(key, 1)
    first, second, third = jax.random.split(key, 3)
    last_fresh = HISTORY - jax.random.randint(first, (), 1, 4)
    prior_fresh = last_fresh - jax.random.randint(second, (), 1, 4)
    flags = jax.random.randint(third, (HISTORY,), 0, 2)
    step_ids = jnp.arange(HISTORY, dtype=jnp.int32)
    flags = jnp.where(step_ids > prior_fresh, 0, flags)
    flags = jnp.where(step_ids == prior_fresh, 1, flags)
    flags = jnp.where(step_ids == last_fresh, 1, flags)
    return flags.astype(jnp.int32)


def draw_alignment(key, part):
    key = jax.random.fold_in(key, 2)
    positions = jnp.arange(TA, dtype=jnp.int32)
    jitter = jax.random.randint(key, (TA,), -1, 2)
    frames = jnp.clip(positions * FRAMES // TA + jitter, 0, FRAMES - 1)
    frames = jnp.where(positions == 0, 0, frames)
    frames = jnp.where(positions == TA - 1, FRAMES - 1, frames)
    return frames.astype(jnp.int32)


def draw_audio_tokens(key, part):
    key = jax.random.fold_in(key, 3)
    return jnp.clip(jax.random.normal(key, (TA, DA), jnp.float32), -6.0, 6.0).astype(jnp.bfloat16)


def level_of(key, extent, shards, least, top_value):
    factor_of, own = 1.0, jax.random.fold_in(key, 6)
    for position, blocks in shards:
        steps = jnp.exp(jax.random.uniform(jax.random.fold_in(own, position), (blocks,), jnp.float32, least / len(shards), top_value / len(shards)))
        factor_of = factor_of * jnp.repeat(steps, extent[position] // blocks).reshape([-1 if axis == position else 1 for axis in range(len(extent))])
    return factor_of


def bell_draw(key, extent, width, reach, pieces=(), kind=jnp.bfloat16):
    level = level_of(key, extent, pieces, -0.22, 0.18) if pieces else 1.0
    entries = jax.random.normal(key, extent, jnp.float32) * width * level
    return jnp.minimum(jnp.maximum(entries, -reach), reach).astype(kind)


def setup_inputs(seed: int = 0, part: int = 0) -> dict:
    arg_keys = jax.random.split(jax.random.key(seed), 8)
    part_splits = jax.random.split(jax.random.fold_in(arg_keys[7], part), 8)
    return {
        "video_cache": bell_draw(part_splits[0], (3, TV, DV), 0.4, 2.390625, ((1, 4), (2, 2))),
        "plan": draw_plan(jax.random.fold_in(jax.random.fold_in(arg_keys[7], part), 71), part),
        "alignment": draw_alignment(jax.random.fold_in(jax.random.fold_in(arg_keys[7], part), 71), part),
        "audio_tokens": draw_audio_tokens(jax.random.fold_in(jax.random.fold_in(arg_keys[7], part), 71), part),
        "kv_weight": bell_draw(arg_keys[4], (DV, 2 * DA), DV ** -0.5, 0.09375, ((0, 4), (1, 4))),
        "query_weight": bell_draw(arg_keys[5], (DA, DA), DA ** -0.5, 0.125, ((0, 4), (1, 4))),
        "out_weight": bell_draw(arg_keys[6], (DA, DA), DA ** -0.5, 0.125, ((0, 4), (1, 4))),
    }


SLOPE = 4.0


def taylor_ratio(plan):
    history = plan.shape[0]
    step_ids = jnp.arange(history, dtype=jnp.int32)
    marked = step_ids * plan
    last_fresh = jnp.max(marked)
    prior_fresh = jnp.max(jnp.where(step_ids < last_fresh, marked, 0))
    return (history - last_fresh).astype(jnp.float32) / (last_fresh - prior_fresh).astype(jnp.float32)


def combine(orders, step_ratio):
    values = orders.astype(jnp.float32)
    return (values[0] + step_ratio * values[1] + 0.5 * step_ratio * step_ratio * values[2]).astype(jnp.bfloat16)


def reference(video_cache, plan, alignment, audio_tokens, kv_weight, query_weight, out_weight):
    step_ratio = taylor_ratio(plan)
    video_features = combine(video_cache, step_ratio)
    kv_all = jnp.dot(video_features, kv_weight, preferred_element_type=jnp.float32).astype(jnp.bfloat16)
    kv_all = kv_all.reshape(TV, HEADS_A, 2, HEAD_DIM)
    key_heads = jnp.transpose(kv_all[:, :, 0, :], (1, 0, 2))
    value_heads = jnp.transpose(kv_all[:, :, 1, :], (1, 0, 2))
    queries = jnp.dot(audio_tokens, query_weight, preferred_element_type=jnp.float32).astype(jnp.bfloat16)
    query_heads = jnp.transpose(queries.reshape(TA, HEADS_A, HEAD_DIM), (1, 0, 2))
    frames_video = (jnp.arange(TV, dtype=jnp.int32) * FRAMES) // TV
    distance_bias = -SLOPE * jnp.abs(frames_video[None, :] - alignment[:, None]).astype(jnp.float32) / FRAMES
    scale = 1.0 / (HEAD_DIM ** 0.5)

    def one_head(operands):
        query_rows, key_rows, value_rows = operands
        scores = jnp.dot(query_rows, key_rows.T, preferred_element_type=jnp.float32) * scale + distance_bias
        row_max = jnp.max(scores, axis=1, keepdims=True)
        exp_terms = jnp.exp(scores - row_max)
        weighted = jnp.dot(exp_terms.astype(jnp.bfloat16), value_rows, preferred_element_type=jnp.float32)
        row_sum = jnp.sum(exp_terms, axis=1, keepdims=True)
        return (weighted / row_sum).astype(jnp.bfloat16)

    attended = lax.map(one_head, (query_heads, key_heads, value_heads))
    attended = jnp.transpose(attended, (1, 0, 2)).reshape(TA, DA)
    update = jnp.dot(attended, out_weight, preferred_element_type=jnp.float32)
    audio_output = (audio_tokens.astype(jnp.float32) + update).astype(jnp.bfloat16)
    return video_features, audio_output
```

```python
import math

import jax
import jax.numpy as jnp
from jax import lax
from jax.sharding import PartitionSpec as P

HEAD_DIM = 128
FRAMES = 24


SLOPE = 4.0


def taylor_ratio(plan):
    history = plan.shape[0]
    step_ids = jnp.arange(history, dtype=jnp.int32)
    marked = step_ids * plan
    last_fresh = jnp.max(marked)
    prior_fresh = jnp.max(jnp.where(step_ids < last_fresh, marked, 0))
    return (history - last_fresh).astype(jnp.float32) / (last_fresh - prior_fresh).astype(
        jnp.float32
    )


def combine(orders, step_ratio):
    values = orders.astype(jnp.float32)
    return (values[0] + step_ratio * values[1] + 0.5 * step_ratio * step_ratio * values[2]).astype(
        jnp.bfloat16
    )


def general(video_cache, plan, alignment, audio_tokens, kv_weight, query_weight, out_weight):
    step_ratio = taylor_ratio(plan)
    own_part = combine(video_cache, step_ratio)
    features_all = lax.all_gather(own_part, "mem", axis=1, tiled=True)
    video_rows = features_all.shape[0]
    kv_local = jnp.dot(
        features_all,
        lax.all_gather(kv_weight, "seq", axis=0, tiled=True),
        preferred_element_type=jnp.float32,
    )
    head_size = HEAD_DIM
    local_heads = query_weight.shape[1] // head_size
    kv_local = kv_local.astype(jnp.bfloat16).reshape(video_rows, local_heads, 2, head_size)
    key_rows = kv_local[:, :, 0, :]
    value_rows = kv_local[:, :, 1, :]
    query_full, out_full = (
        lax.all_gather(query_weight, "seq", axis=0, tiled=True),
        lax.all_gather(out_weight, "seq", axis=1, tiled=True),
    )
    audio_rows = audio_tokens.shape[0]
    queries = jnp.dot(audio_tokens, query_full, preferred_element_type=jnp.float32).astype(
        jnp.bfloat16
    )
    queries = queries.reshape(audio_rows, local_heads, head_size)
    scale = 1.0 / head_size**0.5
    span = video_rows * lax.axis_size("seq")
    initial = (
        jnp.full((local_heads, audio_rows), -1e30, jnp.float32),
        jnp.zeros((local_heads, audio_rows), jnp.float32),
        jnp.zeros((local_heads, audio_rows, head_size), jnp.float32),
    )
    key_piece = lax.all_gather(key_rows, "seq", axis=0, tiled=True)
    value_piece = lax.all_gather(value_rows, "seq", axis=0, tiled=True)
    row_count = key_piece.shape[0]
    block_len = math.gcd(row_count, 1024)

    def advance(block_index, carried):
        row_max, row_sum, weighted = carried
        key_block = lax.dynamic_slice_in_dim(key_piece, block_index * block_len, block_len, 0)
        value_block = lax.dynamic_slice_in_dim(value_piece, block_index * block_len, block_len, 0)
        positions = block_index * block_len + jnp.arange(block_len, dtype=jnp.int32)
        frames_video = positions * FRAMES // span
        distance_bias = (
            -SLOPE
            * jnp.abs(frames_video[None, :] - alignment[:, None]).astype(jnp.float32)
            / FRAMES
        )
        scores = (
            jnp.einsum("qhd,khd->hqk", queries, key_block, preferred_element_type=jnp.float32)
            * scale
        )
        scores = scores + distance_bias[None]
        new_max = jnp.maximum(row_max, jnp.max(scores, axis=2))
        rescale = jnp.exp(row_max - new_max)
        exp_terms = jnp.exp(scores - new_max[:, :, None])
        row_sum = row_sum * rescale + jnp.sum(exp_terms, axis=2)
        weighted = weighted * rescale[:, :, None] + jnp.einsum(
            "hqk,khd->hqd",
            exp_terms.astype(jnp.bfloat16),
            value_block,
            preferred_element_type=jnp.float32,
        )
        return (new_max, row_sum, weighted)

    row_max, row_sum, weighted = lax.fori_loop(0, row_count // block_len, advance, initial)
    attended = (weighted / row_sum[:, :, None]).astype(jnp.bfloat16)
    attended = jnp.transpose(attended, (1, 0, 2)).reshape(audio_rows, local_heads * head_size)
    partial_update = jnp.dot(attended, out_full, preferred_element_type=jnp.float32)
    update = lax.psum_scatter(
        partial_update.astype(jnp.bfloat16), ("mem", "rep"), scatter_dimension=1, tiled=True
    ).astype(jnp.float32)
    own_columns = update.shape[1]
    residual = lax.dynamic_slice_in_dim(
        audio_tokens, lax.axis_index(("mem", "rep")) * own_columns, own_columns, 1
    )
    audio_output = (residual.astype(jnp.float32) + update).astype(jnp.bfloat16)
    return (own_part, audio_output)


def fresh_ratio(plan):
    history = plan.shape[0]
    mask = jnp.sum(plan << jnp.arange(history, dtype=jnp.int32))
    last_fresh = 31 - lax.clz(mask)
    prior_fresh = 31 - lax.clz(mask - (1 << last_fresh))
    return (history - last_fresh).astype(jnp.float32) / (last_fresh - prior_fresh).astype(
        jnp.float32
    )


def swap(value, axis, bit):
    size = lax.axis_size(axis)
    return lax.ppermute(value, axis, [(i, i ^ bit) for i in range(size)])


def whole_weight(shard):
    seq_at, grp_at = lax.axis_index("seq"), lax.axis_index("grp")
    rows, columns = shard.shape
    half = lax.dynamic_slice_in_dim(shard, grp_at * (rows // 2), rows // 2, 0)
    partner = swap(half, "seq", 1)
    even = seq_at % 2 == 0
    pair = jnp.stack([jnp.where(even, half, partner), jnp.where(even, partner, half)])
    middle = lax.ppermute(pair, "seq", [(1, 2), (2, 1)])
    edge = lax.ppermute(middle, "seq", [(1, 0), (2, 3)])
    far = jnp.where((seq_at == 1) | (seq_at == 2), middle, edge)
    partner_rest = swap(partner, "grp", 1)
    far_rest = swap(far, "grp", 1)
    whole = jnp.zeros((4, 2, rows // 2, columns), shard.dtype)
    whole = lax.dynamic_update_slice(whole, shard.reshape(1, 2, rows // 2, columns), (seq_at, 0, 0, 0))
    far_at = 2 - seq_at // 2 * 2
    for value, group in ((partner, grp_at), (partner_rest, 1 - grp_at)):
        whole = lax.dynamic_update_slice(whole, value[None, None], (seq_at ^ 1, group, 0, 0))
    for value, group in ((far, grp_at), (far_rest, 1 - grp_at)):
        whole = lax.dynamic_update_slice(whole, value[:, None], (far_at, group, 0, 0))
    return whole.reshape(4, rows, columns)


def by_head(video_cache, plan, alignment, audio_tokens, kv_weight, query_weight, out_weight):
    seq_size = lax.axis_size("seq")
    seq_at, mem_at, rep_at = (lax.axis_index(name) for name in ("seq", "mem", "rep"))
    place = mem_at * 2 + rep_at
    step_ratio = fresh_ratio(plan)
    video_rows, mem_columns = video_cache.shape[1:]
    depth = kv_weight.shape[0]

    align_all = lax.all_to_all(
        jnp.broadcast_to(alignment[None], (seq_size, alignment.shape[0])), "seq", 0, 0, tiled=True
    ).reshape(-1)
    query_full = whole_weight(query_weight).reshape(-1, query_weight.shape[1])

    own_half = combine(lax.dynamic_slice_in_dim(video_cache, rep_at * depth, depth, 2), step_ratio)
    moves = []
    for source in range(seq_size * seq_size):
        tokens, columns = divmod(source, seq_size)
        moves.append((source, columns * seq_size + tokens % 2 * 2 + tokens // 2))
    turned = lax.ppermute(own_half, ("seq", "mem", "rep"), moves)
    beside = swap(turned, "rep", 1)
    across = swap(turned, "mem", 1)
    across_beside = swap(across, "rep", 1)
    features = (
        jnp.concatenate([turned, beside], axis=0),
        jnp.concatenate([across, across_beside], axis=0),
    )

    head_columns = 2 * HEAD_DIM
    kv_parts = []
    for rows in features:

        def partial_kv(head):
            columns = lax.dynamic_slice_in_dim(kv_weight, head * head_columns, head_columns, 1)
            return jnp.dot(rows, columns, preferred_element_type=jnp.float32)

        arrived = [
            swap(partial_kv(seq_at ^ bit).astype(jnp.bfloat16), "seq", bit) for bit in (3, 2, 1)
        ]
        kv_rows = partial_kv(seq_at)
        for term in arrived:
            kv_rows = kv_rows + term.astype(jnp.float32)
        kv_parts.append(kv_rows.astype(jnp.bfloat16))
    kv_rows = jnp.concatenate(kv_parts, axis=0)
    key_rows, value_rows = kv_rows[:, :HEAD_DIM], kv_rows[:, HEAD_DIM:]

    queries = jnp.dot(audio_tokens, query_full, preferred_element_type=jnp.float32).astype(
        jnp.bfloat16
    )
    queries = lax.all_to_all(queries, "seq", split_axis=1, concat_axis=0, tiled=True)
    out_full = whole_weight(out_weight)
    own_part = combine(video_cache, step_ratio)

    span = video_rows * seq_size
    places = jnp.stack([place, place ^ 1, place ^ 2, place ^ 3])
    tokens = places % 2 * 2 + places // 2
    positions = (
        tokens[:, None] * video_rows + jnp.arange(video_rows, dtype=jnp.int32)[None, :]
    ).reshape(span)
    frames_video = positions * FRAMES // span
    distance_bias = (
        -SLOPE * jnp.abs(frames_video[None, :] - align_all[:, None]).astype(jnp.float32) / FRAMES
    )
    scores = (
        jnp.dot(queries, key_rows.T, preferred_element_type=jnp.float32) * (1.0 / HEAD_DIM**0.5)
        + distance_bias
    )
    exp_terms = jnp.exp(scores - jnp.max(scores, axis=1, keepdims=True))
    weighted = jnp.dot(
        exp_terms.astype(jnp.bfloat16), value_rows, preferred_element_type=jnp.float32
    )
    attended = (weighted / jnp.sum(exp_terms, axis=1, keepdims=True)).astype(jnp.bfloat16)
    attended = lax.all_to_all(attended, "seq", split_axis=0, concat_axis=1, tiled=True)

    def partial_update(block):
        columns = lax.dynamic_index_in_dim(out_full, block, 0, keepdims=False)
        return jnp.dot(attended, columns, preferred_element_type=jnp.float32)

    sent = jnp.stack([partial_update(place ^ 3), partial_update(place ^ 1)]).astype(jnp.bfloat16)
    came = swap(sent, "rep", 1).astype(jnp.float32)
    far = (partial_update(place ^ 2) + came[0]).astype(jnp.bfloat16)
    update = partial_update(place) + came[1] + swap(far, "mem", 1).astype(jnp.float32)
    own_columns = update.shape[1]
    residual = lax.dynamic_slice_in_dim(audio_tokens, place * own_columns, own_columns, 1)
    audio_output = (residual.astype(jnp.float32) + update).astype(jnp.bfloat16)
    return (own_part, audio_output)


def solution(mesh):
    sizes = dict(mesh.shape)
    square = (sizes["grp"], sizes["seq"], sizes["mem"], sizes["rep"]) == (2, 4, 2, 2)

    def on_device(*arrays):
        heads = arrays[5].shape[1] // HEAD_DIM
        return (by_head if square and heads == sizes["seq"] else general)(*arrays)

    return jax.shard_map(
        on_device,
        mesh=mesh,
        in_specs=(
            P(None, ("grp", "seq"), "mem"),
            P("grp"),
            P(("grp", "seq")),
            P(("grp", "seq"), None),
            P("seq", ("mem", "rep")),
            P("seq", ("mem", "rep")),
            P(("mem", "rep"), "seq"),
        ),
        out_specs=(P(("grp", "seq"), "mem"), P(("grp", "seq"), ("mem", "rep"))),
        check_vma=False,
    )
```

```python
import math

import jax
import jax.numpy as jnp
from jax import lax
from jax.experimental import pallas as pl
from jax.experimental.pallas import tpu as pltpu
from jax.sharding import PartitionSpec as P

HEAD_DIM = 128
FRAMES = 24


SLOPE = 4.0


def taylor_ratio(plan):
    history = plan.shape[0]
    step_ids = jnp.arange(history, dtype=jnp.int32)
    marked = step_ids * plan
    last_fresh = jnp.max(marked)
    prior_fresh = jnp.max(jnp.where(step_ids < last_fresh, marked, 0))
    return (history - last_fresh).astype(jnp.float32) / (last_fresh - prior_fresh).astype(
        jnp.float32
    )


def combine(orders, step_ratio):
    values = orders.astype(jnp.float32)
    return (values[0] + step_ratio * values[1] + 0.5 * step_ratio * step_ratio * values[2]).astype(
        jnp.bfloat16
    )


def general(video_cache, plan, alignment, audio_tokens, kv_weight, query_weight, out_weight):
    step_ratio = taylor_ratio(plan)
    own_part = combine(video_cache, step_ratio)
    features_all = lax.all_gather(own_part, "mem", axis=1, tiled=True)
    video_rows = features_all.shape[0]
    kv_local = jnp.dot(
        features_all,
        lax.all_gather(kv_weight, "seq", axis=0, tiled=True),
        preferred_element_type=jnp.float32,
    )
    head_size = HEAD_DIM
    local_heads = query_weight.shape[1] // head_size
    kv_local = kv_local.astype(jnp.bfloat16).reshape(video_rows, local_heads, 2, head_size)
    key_rows = kv_local[:, :, 0, :]
    value_rows = kv_local[:, :, 1, :]
    query_full, out_full = (
        lax.all_gather(query_weight, "seq", axis=0, tiled=True),
        lax.all_gather(out_weight, "seq", axis=1, tiled=True),
    )
    audio_rows = audio_tokens.shape[0]
    queries = jnp.dot(audio_tokens, query_full, preferred_element_type=jnp.float32).astype(
        jnp.bfloat16
    )
    queries = queries.reshape(audio_rows, local_heads, head_size)
    scale = 1.0 / head_size**0.5
    span = video_rows * lax.axis_size("seq")
    initial = (
        jnp.full((local_heads, audio_rows), -1e30, jnp.float32),
        jnp.zeros((local_heads, audio_rows), jnp.float32),
        jnp.zeros((local_heads, audio_rows, head_size), jnp.float32),
    )
    key_piece = lax.all_gather(key_rows, "seq", axis=0, tiled=True)
    value_piece = lax.all_gather(value_rows, "seq", axis=0, tiled=True)
    row_count = key_piece.shape[0]
    block_len = math.gcd(row_count, 1024)

    def advance(block_index, carried):
        row_max, row_sum, weighted = carried
        key_block = lax.dynamic_slice_in_dim(key_piece, block_index * block_len, block_len, 0)
        value_block = lax.dynamic_slice_in_dim(value_piece, block_index * block_len, block_len, 0)
        positions = block_index * block_len + jnp.arange(block_len, dtype=jnp.int32)
        frames_video = positions * FRAMES // span
        distance_bias = (
            -SLOPE
            * jnp.abs(frames_video[None, :] - alignment[:, None]).astype(jnp.float32)
            / FRAMES
        )
        scores = (
            jnp.einsum("qhd,khd->hqk", queries, key_block, preferred_element_type=jnp.float32)
            * scale
        )
        scores = scores + distance_bias[None]
        new_max = jnp.maximum(row_max, jnp.max(scores, axis=2))
        rescale = jnp.exp(row_max - new_max)
        exp_terms = jnp.exp(scores - new_max[:, :, None])
        row_sum = row_sum * rescale + jnp.sum(exp_terms, axis=2)
        weighted = weighted * rescale[:, :, None] + jnp.einsum(
            "hqk,khd->hqd",
            exp_terms.astype(jnp.bfloat16),
            value_block,
            preferred_element_type=jnp.float32,
        )
        return (new_max, row_sum, weighted)

    row_max, row_sum, weighted = lax.fori_loop(0, row_count // block_len, advance, initial)
    attended = (weighted / row_sum[:, :, None]).astype(jnp.bfloat16)
    attended = jnp.transpose(attended, (1, 0, 2)).reshape(audio_rows, local_heads * head_size)
    partial_update = jnp.dot(attended, out_full, preferred_element_type=jnp.float32)
    update = lax.psum_scatter(
        partial_update.astype(jnp.bfloat16), ("mem", "rep"), scatter_dimension=1, tiled=True
    ).astype(jnp.float32)
    own_columns = update.shape[1]
    residual = lax.dynamic_slice_in_dim(
        audio_tokens, lax.axis_index(("mem", "rep")) * own_columns, own_columns, 1
    )
    audio_output = (residual.astype(jnp.float32) + update).astype(jnp.bfloat16)
    return (own_part, audio_output)


def swap(value, axis, bit):
    size = lax.axis_size(axis)
    return lax.ppermute(value, axis, [(i, i ^ bit) for i in range(size)])


VMEM = pl.BlockSpec(memory_space=pltpu.VMEM)
SMEM = pl.BlockSpec(memory_space=pltpu.SMEM)
ANY = pl.BlockSpec(memory_space=pl.ANY)


def kernel_call(body, outs, ins, after=(), scratch=(), smem=(), loose_in=(), loose_out=(), limit=14):
    def whole(*refs):
        body(*refs[: len(ins)], *refs[len(ins) + len(after) :])

    spots = [
        SMEM if i in smem else ANY if i in loose_in else VMEM for i in range(1, len(ins))
    ]
    return pl.pallas_call(
        whole,
        out_shape=outs,
        in_specs=[SMEM, *spots] + [ANY] * len(after),
        out_specs=[ANY if i in loose_out else VMEM for i in range(len(outs))],
        scratch_shapes=scratch,
        compiler_params=pltpu.CompilerParams(vmem_limit_bytes=limit * 2**20),
    )(*ins, *after)


def plan_ratio(plan_ref, columns):
    history = plan_ref.shape[0]
    last_fresh, prior_fresh = jnp.int32(0), jnp.int32(0)
    for step in range(history):
        fresh = plan_ref[step] == 1
        prior_fresh = jnp.where(fresh, last_fresh, prior_fresh)
        last_fresh = jnp.where(fresh, step, last_fresh)
    ahead = jnp.full((1, columns), history - last_fresh, jnp.int32).astype(jnp.float32)
    apart = jnp.full((1, columns), last_fresh - prior_fresh, jnp.int32).astype(jnp.float32)
    return ahead / apart


def taylor_rows(cache_ref, out_ref, step_ratio, first, last):
    half_square = 0.5 * step_ratio * step_ratio
    for at in range(first, last, 16):
        terms = [cache_ref[order, at : at + 16, :].astype(jnp.float32) for order in range(3)]
        out_ref[at : at + 16, :] = (
            terms[0] + step_ratio * terms[1] + half_square * terms[2]
        ).astype(jnp.bfloat16)


def taylor_body(plan_ref, cache_ref, out_ref):
    rows, columns = out_ref.shape
    taylor_rows(cache_ref, out_ref, plan_ratio(plan_ref, columns), 0, rows)


def taylor(video_cache, plan, width):
    orders, rows, columns = video_cache.shape
    return pl.pallas_call(
        taylor_body,
        out_shape=jax.ShapeDtypeStruct((rows, columns), jnp.bfloat16),
        grid=(columns // width,),
        in_specs=[SMEM, pl.BlockSpec((orders, rows, width), lambda i: (0, 0, i))],
        out_specs=pl.BlockSpec((rows, width), lambda i: (0, i)),
        compiler_params=pltpu.CompilerParams(vmem_limit_bytes=8 * 2**20),
    )(plan, video_cache)


def first_body(
    scalars,
    plan_ref,
    cache_ref,
    audio_ref,
    kv_ref,
    query_ref,
    out_w,
    packed_ref,
    other_ref,
    half_ref,
    held_ref,
    sems,
):
    rep_at, mem_at, grp_at = scalars[0], scalars[1], scalars[2]
    rows, width = held_ref.shape[1:]
    width = width // 2
    copies = []

    def copy(source, target):
        copies.append(pltpu.make_async_copy(source, target, sems.at[len(copies)]))

    def part(index, size):
        return pl.ds(pl.multiple_of(index * size, size), size)

    blocks = 4
    step = rows // blocks
    for block in range(blocks):
        at = pl.ds(block * step, step)
        for shard in range(2):
            copy(
                cache_ref.at[:, at, part(2 * shard + rep_at, width)],
                held_ref.at[:, at, pl.ds(shard * width, width)],
            )
    lane = width // 2
    for shard in range(2):
        copy(
            audio_ref.at[:, part(2 * (2 * mem_at + shard) + rep_at, lane)],
            packed_ref.at[pl.ds(2 * rows, audio_ref.shape[0]), pl.ds(shard * lane, lane)],
        )
    depth, columns = kv_ref.shape[0] // 2, query_ref.shape[1]
    copy(kv_ref.at[part(1 - rep_at, depth)], other_ref.at[pl.ds(0, depth)])
    quarter = query_ref.shape[0] // 4
    for side in range(2):
        copy(
            query_ref.at[part(2 * (1 - rep_at) + side, quarter)],
            other_ref.at[pl.ds(depth, quarter), pl.ds(side * columns, columns)],
        )
    copy(out_w.at[part(grp_at, half_ref.shape[0])], half_ref)
    for started in copies:
        started.start()
    step_ratio = plan_ratio(plan_ref, width)
    for block in range(blocks):
        for shard in range(2):
            copies[2 * block + shard].wait()
            taylor_rows(
                held_ref.at[:, :, pl.ds(shard * width, width)],
                packed_ref.at[pl.ds(shard * rows, rows)],
                step_ratio,
                block * step,
                (block + 1) * step,
            )
    for started in copies[2 * blocks :]:
        started.wait()


def weight_body(scalars, kv_ref, query_ref, other_ref, own_ref, *piece_refs):
    seq_at, rep_at, grp_at = scalars[0], scalars[1], scalars[2]
    kv_half, query_half = kv_ref.shape[0] // 2, query_ref.shape[0] // 2
    kv_rows, query_rows = kv_half // 2, query_half // 2
    fold = query_rows // 2

    def fill(out_ref, bit, group, kv_at, query_at):
        head = seq_at ^ bit
        width = 2 * HEAD_DIM
        lanes = pl.ds(pl.multiple_of(head * width, width), width)
        at = pl.ds(pl.multiple_of(rep_at * kv_half + group * kv_rows, kv_rows), kv_rows)
        out_ref[kv_at : kv_at + kv_rows, :width] = kv_ref[at, lanes]
        at = pl.ds(pl.multiple_of(group * kv_rows, kv_rows), kv_rows)
        out_ref[kv_at : kv_at + kv_rows, width:] = other_ref[at, lanes]
        lanes = pl.ds(pl.multiple_of(head * HEAD_DIM, HEAD_DIM), HEAD_DIM)
        other_lanes = pl.ds(
            pl.multiple_of(group * query_ref.shape[1] + head * HEAD_DIM, HEAD_DIM), HEAD_DIM
        )
        for side in range(2):
            first = rep_at * query_half + group * query_rows + side * fold
            at = pl.ds(pl.multiple_of(first, fold), fold)
            to = slice(query_at, query_at + fold)
            out_ref[to, side * width : side * width + HEAD_DIM] = query_ref[at, lanes]
            out_ref[to, side * width + HEAD_DIM : (side + 1) * width] = other_ref[
                kv_half + side * fold : kv_half + (side + 1) * fold, other_lanes
            ]

    for group in range(2):
        fill(own_ref, 0, group, group * kv_rows, kv_half + group * fold)
    for bit, piece_ref in enumerate(piece_refs, 1):
        fill(piece_ref, bit, grp_at, 0, kv_rows)


def products_body(scalars, *refs):
    packed_refs, weight_refs = refs[:8], refs[8:15]
    send_ref, keep_ref, rows_ref, audio_ref, kv_ref, query_ref = refs[15:]
    seq_at, mem_at, grp_at = scalars[0], scalars[1], scalars[2]
    rows = rows_ref.shape[1] // 4
    audio_rows = audio_ref.shape[1] // 4
    lane = audio_ref.shape[2]
    for at, packed_ref in enumerate(packed_refs):
        slot, mem = divmod(at, 2)
        for part in range(2):
            shard = 2 * (mem_at ^ mem) + part
            rows_ref[shard, slot * rows : (slot + 1) * rows, :] = packed_ref[
                part * rows : (part + 1) * rows, :
            ]
            audio_ref[shard, slot * audio_rows : (slot + 1) * audio_rows, :] = packed_ref[
                2 * rows :, part * lane : (part + 1) * lane
            ]
    kv_half = kv_ref.shape[1] // 2
    fold = query_ref.shape[1] // 4
    width = query_ref.shape[2]

    def place(piece_ref, shard, group, kv_at, query_at):
        to = pl.ds(pl.multiple_of(group * kv_half, kv_half), kv_half)
        kv_ref[shard, to, :] = piece_ref[kv_at : kv_at + kv_half, :]
        for side in range(2):
            to = pl.ds(pl.multiple_of((2 * group + side) * fold, fold), fold)
            query_ref[shard, to, :] = piece_ref[
                query_at : query_at + fold, side * width : (side + 1) * width
            ]

    for group in range(2):
        place(weight_refs[0], seq_at, group, group * kv_half, 2 * kv_half + group * fold)
    for bit in range(1, 4):
        place(weight_refs[2 * bit - 1], seq_at ^ bit, grp_at, 0, kv_half)
        place(weight_refs[2 * bit], seq_at ^ bit, 1 - grp_at, 0, kv_half)

    def summed(left_ref, right_ref):
        total = jnp.dot(left_ref[0], right_ref[0], preferred_element_type=jnp.float32)
        for shard in range(1, 4):
            total += jnp.dot(
                left_ref[shard], right_ref[shard], preferred_element_type=jnp.float32
            )
        return total

    count = 4 * rows
    columns = keep_ref.shape[1]
    total = summed(rows_ref, kv_ref)
    keep_ref[:count, :] = total[:, :columns]
    send_ref[:count, :] = total[:, columns:]
    total = summed(audio_ref, query_ref)
    folded = 2 * audio_rows
    for side in range(2):
        at = slice(side * folded, (side + 1) * folded)
        to = slice(side * HEAD_DIM, (side + 1) * HEAD_DIM)
        keep_ref[count:, to] = total[at, :HEAD_DIM]
        send_ref[count:, to] = total[at, HEAD_DIM:]


def attend(queries, kv_ref, frames_ref, align):
    scores = lax.dot_general(
        queries,
        kv_ref[:, :HEAD_DIM],
        (((1,), (1,)), ((), ())),
        preferred_element_type=jnp.float32,
    ) * (1.0 / HEAD_DIM**0.5)
    scores = scores - SLOPE * jnp.abs(frames_ref[...] - align) / FRAMES
    exp_terms = jnp.exp(scores - jnp.max(scores, axis=1, keepdims=True))
    weighted = jnp.dot(
        exp_terms.astype(jnp.bfloat16), kv_ref[:, HEAD_DIM:], preferred_element_type=jnp.float32
    )
    return (weighted / jnp.sum(exp_terms, axis=1, keepdims=True)).astype(jnp.bfloat16)


def attention_body(scalars, frames_ref, align_ref, keep_ref, came_ref, *refs):
    *out_refs, kv_ref, query_ref = refs
    count, audio_rows = kv_ref.shape[0], query_ref.shape[1]

    def summed(rows, columns=slice(None)):
        return (keep_ref[rows, columns] + came_ref[rows, columns]).astype(jnp.bfloat16)

    kv_ref[...] = summed(slice(0, count))
    for slot in range(4):
        side, half = divmod(slot, 2)
        query_ref[scalars[slot]] = summed(
            slice(count + half * audio_rows, count + (half + 1) * audio_rows),
            slice(side * HEAD_DIM, (side + 1) * HEAD_DIM),
        )
    for bit, out_ref in enumerate(out_refs):
        block = scalars[0] ^ bit
        out_ref[...] = attend(query_ref[block], kv_ref, frames_ref, align_ref[block])


def out_body(
    scalars,
    own_ref,
    near_ref,
    far_ref,
    farther_ref,
    own_w,
    partner_w,
    partner_rest_w,
    far_w,
    far_rest_w,
    send_ref,
    keep_ref,
    heads_ref,
    weight_ref,
    sem,
):
    seq_at, grp_at, place = scalars[0], scalars[1], scalars[2]
    copy = pltpu.make_async_copy(own_w, weight_ref.at[0], sem)
    copy.start()
    for bit, head_ref in enumerate((own_ref, near_ref, far_ref, farther_ref)):
        heads_ref[seq_at ^ bit] = head_ref[...]
    heads = jnp.concatenate([heads_ref[head] for head in range(heads_ref.shape[0])], axis=1)
    depth = partner_w.shape[0]
    mine = pl.ds(pl.multiple_of(grp_at * depth, depth), depth)
    rest = pl.ds(pl.multiple_of((1 - grp_at) * depth, depth), depth)
    weight_ref[1, mine] = partner_w[...]
    weight_ref[1, rest] = partner_rest_w[...]
    for far in range(2):
        weight_ref[2 + far, mine] = far_w[far]
        weight_ref[2 + far, rest] = far_rest_w[far]
    middle = 2 - seq_at // 2
    for at, block in ((1, seq_at ^ 1), (2, middle), (3, middle ^ 1), (0, seq_at)):
        if at == 0:
            copy.wait()
        slot = block ^ place
        value = jnp.dot(heads, weight_ref[at], preferred_element_type=jnp.float32)

        @pl.when(slot % 2 == 1)
        def _():
            send_ref[slot // 2] = value.astype(send_ref.dtype)

        @pl.when(slot % 2 == 0)
        def _():
            keep_ref[slot // 2] = value


def by_head(video_cache, plan, alignment, audio_tokens, kv_weight, query_weight, out_weight):
    seq_size = lax.axis_size("seq")
    seq_at, mem_at, rep_at = (lax.axis_index(name) for name in ("seq", "mem", "rep"))
    grp_at = lax.axis_index("grp")
    place = mem_at * 2 + rep_at
    video_rows = video_cache.shape[1]
    audio_rows = audio_tokens.shape[0]
    half_depth, width = kv_weight.shape[0] // 2, 2 * HEAD_DIM
    query_quarter = query_weight.shape[0] // 4

    def bfloat(*shape):
        return jax.ShapeDtypeStruct(shape, jnp.bfloat16)

    packed, other, half = kernel_call(
        first_body,
        [
            bfloat(2 * video_rows + audio_rows, half_depth),
            bfloat(half_depth + query_quarter, kv_weight.shape[1]),
            bfloat(out_weight.shape[0] // 2, out_weight.shape[1]),
        ],
        [
            jnp.stack([rep_at, mem_at, grp_at]),
            plan,
            video_cache,
            audio_tokens,
            kv_weight,
            query_weight,
            out_weight,
        ],
        scratch=[
            pltpu.VMEM((3, video_rows, 2 * half_depth), jnp.bfloat16),
            pltpu.SemaphoreType.DMA((14,)),
        ],
        smem=(1,),
        loose_in=(2, 3, 4, 5, 6),
    )

    other = swap(other, "rep", 1)
    rows = half_depth // 2 + query_quarter // 2
    weight_own, *pieces = kernel_call(
        weight_body,
        [bfloat(2 * rows, 2 * width)] + [bfloat(rows, 2 * width)] * 3,
        [jnp.stack([seq_at, rep_at, grp_at]), kv_weight, query_weight, other],
    )
    weights = [weight_own]
    for bit, piece in enumerate(pieces, 1):
        piece = swap(piece, "seq", bit)
        weights += [piece, swap(piece, "grp", 1)]

    inner, outward = [(1, 2), (2, 1)], [(1, 0), (2, 3)]
    is_inner = (seq_at == 1) | (seq_at == 2)
    partner = swap(packed, "seq", 1)
    align_all = lax.all_to_all(
        jnp.broadcast_to(alignment[None], (seq_size, audio_rows)), "seq", 0, 0, tiled=True
    ).astype(jnp.float32)
    inner_own = lax.ppermute(packed, "seq", inner)
    inner_partner = lax.ppermute(partner, "seq", inner)
    third = jnp.where(is_inner, inner_own, lax.ppermute(inner_own, "seq", outward))
    fourth = jnp.where(is_inner, inner_partner, lax.ppermute(inner_partner, "seq", outward))
    tokens = []
    for value in (packed, partner, third, fourth):
        tokens += [value, swap(value, "mem", 1)]
    middle = 2 - seq_at // 2
    blocks = jnp.stack([seq_at, seq_at ^ 1, middle, middle ^ 1])

    rows = seq_size * (video_rows + audio_rows // 2)
    sums = jax.ShapeDtypeStruct((rows, width), jnp.float32)
    send, keep = kernel_call(
        products_body,
        [sums, sums],
        [jnp.stack([seq_at, mem_at, grp_at]), *tokens, *weights],
        scratch=[
            pltpu.VMEM((4, seq_size * video_rows, half_depth), jnp.bfloat16),
            pltpu.VMEM((4, seq_size * audio_rows, 2 * query_quarter), jnp.bfloat16),
            pltpu.VMEM((4, half_depth, 2 * width), jnp.bfloat16),
            pltpu.VMEM((4, 2 * query_quarter, width), jnp.bfloat16),
        ],
        limit=26,
    )
    came = swap(send, "rep", 1)

    half, _ = lax.optimization_barrier((half, third))
    out_partner = swap(half, "seq", 1)
    out_pair = lax.ppermute(jnp.stack([half, out_partner]), "seq", inner)
    far = jnp.where(is_inner, out_pair, lax.ppermute(out_pair, "seq", outward))
    partner_rest, far_rest = swap(out_partner, "grp", 1), swap(far, "grp", 1)

    span = video_rows * seq_size
    positions = blocks[:, None] * video_rows + jnp.arange(video_rows, dtype=jnp.int32)[None, :]
    frames_video = (positions.reshape(1, span) * FRAMES // span).astype(jnp.float32)
    own_piece, near_piece, far_piece, farther_piece = kernel_call(
        attention_body,
        [bfloat(audio_rows, HEAD_DIM)] * 4,
        [blocks, frames_video, align_all[:, :, None], keep, came],
        scratch=[
            pltpu.VMEM((span, width), jnp.bfloat16),
            pltpu.VMEM((seq_size, audio_rows, HEAD_DIM), jnp.bfloat16),
        ],
    )
    far_piece = swap(far_piece, "seq", 2)
    farther_piece = swap(farther_piece, "seq", 3)
    near_piece = swap(near_piece, "seq", 1)

    columns = out_weight.shape[1]
    send, keep = kernel_call(
        out_body,
        [
            jax.ShapeDtypeStruct((2, audio_rows, columns), jnp.bfloat16),
            jax.ShapeDtypeStruct((2, audio_rows, columns), jnp.float32),
        ],
        [
            jnp.stack([seq_at, grp_at, place]),
            own_piece,
            near_piece,
            far_piece,
            farther_piece,
            out_weight,
            out_partner,
            partner_rest,
            far,
            far_rest,
        ],
        scratch=[
            pltpu.VMEM((seq_size, audio_rows, HEAD_DIM), jnp.bfloat16),
            pltpu.VMEM((seq_size, *out_weight.shape), jnp.bfloat16),
            pltpu.SemaphoreType.DMA,
        ],
        loose_in=(5,),
    )
    came = swap(send, "rep", 1)
    across = swap((keep[1] + came[1].astype(jnp.float32)).astype(jnp.bfloat16), "mem", 1)
    residual = lax.dynamic_slice_in_dim(audio_tokens, place * columns, columns, 1)
    own_part = taylor(video_cache, plan, 2 * half_depth)
    base = residual.astype(jnp.float32) + (keep[0] + came[0].astype(jnp.float32))
    base, across = lax.optimization_barrier((base, across))
    audio_output = (base + across.astype(jnp.float32)).astype(jnp.bfloat16)
    return (own_part, audio_output)


def solution(mesh):
    sizes = dict(mesh.shape)
    square = (sizes["grp"], sizes["seq"], sizes["mem"], sizes["rep"]) == (2, 4, 2, 2)

    def on_device(*arrays):
        heads = arrays[5].shape[1] // HEAD_DIM
        return (by_head if square and heads == sizes["seq"] else general)(*arrays)

    return jax.shard_map(
        on_device,
        mesh=mesh,
        in_specs=(
            P(None, ("grp", "seq"), "mem"),
            P("grp"),
            P(("grp", "seq")),
            P(("grp", "seq"), None),
            P("seq", ("mem", "rep")),
            P("seq", ("mem", "rep")),
            P(("mem", "rep"), "seq"),
        ),
        out_specs=(P(("grp", "seq"), "mem"), P(("grp", "seq"), ("mem", "rep"))),
        check_vma=False,
    )
```

```python
import math

import jax
import jax.numpy as jnp
from jax import lax
from jax.experimental import pallas as pl
from jax.experimental.pallas import tpu as pltpu
from jax.sharding import PartitionSpec as P

HEAD_DIM = 128
FRAMES = 24


SLOPE = 4.0


def taylor_ratio(plan):
    history = plan.shape[0]
    step_ids = jnp.arange(history, dtype=jnp.int32)
    marked = step_ids * plan
    last_fresh = jnp.max(marked)
    prior_fresh = jnp.max(jnp.where(step_ids < last_fresh, marked, 0))
    return (history - last_fresh).astype(jnp.float32) / (last_fresh - prior_fresh).astype(
        jnp.float32
    )


def combine(orders, step_ratio):
    values = orders.astype(jnp.float32)
    return (values[0] + step_ratio * values[1] + 0.5 * step_ratio * step_ratio * values[2]).astype(
        jnp.bfloat16
    )


def general(video_cache, plan, alignment, audio_tokens, kv_weight, query_weight, out_weight):
    step_ratio = taylor_ratio(plan)
    own_part = combine(video_cache, step_ratio)
    features_all = lax.all_gather(own_part, "mem", axis=1, tiled=True)
    video_rows = features_all.shape[0]
    kv_local = jnp.dot(
        features_all,
        lax.all_gather(kv_weight, "seq", axis=0, tiled=True),
        preferred_element_type=jnp.float32,
    )
    head_size = HEAD_DIM
    local_heads = query_weight.shape[1] // head_size
    kv_local = kv_local.astype(jnp.bfloat16).reshape(video_rows, local_heads, 2, head_size)
    key_rows = kv_local[:, :, 0, :]
    value_rows = kv_local[:, :, 1, :]
    query_full, out_full = (
        lax.all_gather(query_weight, "seq", axis=0, tiled=True),
        lax.all_gather(out_weight, "seq", axis=1, tiled=True),
    )
    audio_rows = audio_tokens.shape[0]
    queries = jnp.dot(audio_tokens, query_full, preferred_element_type=jnp.float32).astype(
        jnp.bfloat16
    )
    queries = queries.reshape(audio_rows, local_heads, head_size)
    scale = 1.0 / head_size**0.5
    span = video_rows * lax.axis_size("seq")
    initial = (
        jnp.full((local_heads, audio_rows), -1e30, jnp.float32),
        jnp.zeros((local_heads, audio_rows), jnp.float32),
        jnp.zeros((local_heads, audio_rows, head_size), jnp.float32),
    )
    key_piece = lax.all_gather(key_rows, "seq", axis=0, tiled=True)
    value_piece = lax.all_gather(value_rows, "seq", axis=0, tiled=True)
    row_count = key_piece.shape[0]
    block_len = math.gcd(row_count, 1024)

    def advance(block_index, carried):
        row_max, row_sum, weighted = carried
        key_block = lax.dynamic_slice_in_dim(key_piece, block_index * block_len, block_len, 0)
        value_block = lax.dynamic_slice_in_dim(value_piece, block_index * block_len, block_len, 0)
        positions = block_index * block_len + jnp.arange(block_len, dtype=jnp.int32)
        frames_video = positions * FRAMES // span
        distance_bias = (
            -SLOPE
            * jnp.abs(frames_video[None, :] - alignment[:, None]).astype(jnp.float32)
            / FRAMES
        )
        scores = (
            jnp.einsum("qhd,khd->hqk", queries, key_block, preferred_element_type=jnp.float32)
            * scale
        )
        scores = scores + distance_bias[None]
        new_max = jnp.maximum(row_max, jnp.max(scores, axis=2))
        rescale = jnp.exp(row_max - new_max)
        exp_terms = jnp.exp(scores - new_max[:, :, None])
        row_sum = row_sum * rescale + jnp.sum(exp_terms, axis=2)
        weighted = weighted * rescale[:, :, None] + jnp.einsum(
            "hqk,khd->hqd",
            exp_terms.astype(jnp.bfloat16),
            value_block,
            preferred_element_type=jnp.float32,
        )
        return (new_max, row_sum, weighted)

    row_max, row_sum, weighted = lax.fori_loop(0, row_count // block_len, advance, initial)
    attended = (weighted / row_sum[:, :, None]).astype(jnp.bfloat16)
    attended = jnp.transpose(attended, (1, 0, 2)).reshape(audio_rows, local_heads * head_size)
    partial_update = jnp.dot(attended, out_full, preferred_element_type=jnp.float32)
    update = lax.psum_scatter(
        partial_update.astype(jnp.bfloat16), ("mem", "rep"), scatter_dimension=1, tiled=True
    ).astype(jnp.float32)
    own_columns = update.shape[1]
    residual = lax.dynamic_slice_in_dim(
        audio_tokens, lax.axis_index(("mem", "rep")) * own_columns, own_columns, 1
    )
    audio_output = (residual.astype(jnp.float32) + update).astype(jnp.bfloat16)
    return (own_part, audio_output)


def swap(value, axis, bit):
    size = lax.axis_size(axis)
    return lax.ppermute(value, axis, [(i, i ^ bit) for i in range(size)])


VMEM = pl.BlockSpec(memory_space=pltpu.VMEM)
SMEM = pl.BlockSpec(memory_space=pltpu.SMEM)
ANY = pl.BlockSpec(memory_space=pl.ANY)
HBM = pl.BlockSpec(memory_space=pltpu.HBM)


def kernel_call(body, outs, ins, after=(), scratch=(), smem=(), loose_in=(), loose_out=(), limit=14):
    def whole(*refs):
        body(*refs[: len(ins)], *refs[len(ins) + len(after) :])

    spots = [
        SMEM if i in smem else HBM if i in loose_in else VMEM for i in range(1, len(ins))
    ]
    return pl.pallas_call(
        whole,
        out_shape=outs,
        in_specs=[SMEM, *spots] + [ANY] * len(after),
        out_specs=[HBM if i in loose_out else VMEM for i in range(len(outs))],
        scratch_shapes=scratch,
        compiler_params=pltpu.CompilerParams(vmem_limit_bytes=limit * 2**20),
    )(*ins, *after)


def plan_ratio(plan_ref, columns):
    history = plan_ref.shape[0]
    last_fresh, prior_fresh = jnp.int32(0), jnp.int32(0)
    for step in range(history):
        fresh = plan_ref[step] == 1
        prior_fresh = jnp.where(fresh, last_fresh, prior_fresh)
        last_fresh = jnp.where(fresh, step, last_fresh)
    ahead = jnp.full((1, columns), history - last_fresh, jnp.int32).astype(jnp.float32)
    apart = jnp.full((1, columns), last_fresh - prior_fresh, jnp.int32).astype(jnp.float32)
    return ahead / apart


def taylor_rows(cache_ref, out_ref, step_ratio, first, last):
    half_square = 0.5 * step_ratio * step_ratio
    for at in range(first, last, 16):
        terms = [cache_ref[order, at : at + 16, :].astype(jnp.float32) for order in range(3)]
        out_ref[at : at + 16, :] = (
            terms[0] + step_ratio * terms[1] + half_square * terms[2]
        ).astype(jnp.bfloat16)


def taylor_body(plan_ref, cache_ref, out_ref):
    rows, columns = out_ref.shape
    taylor_rows(cache_ref, out_ref, plan_ratio(plan_ref, columns), 0, rows)


def taylor(video_cache, plan, width):
    orders, rows, columns = video_cache.shape
    return pl.pallas_call(
        taylor_body,
        out_shape=jax.ShapeDtypeStruct((rows, columns), jnp.bfloat16),
        grid=(columns // width,),
        in_specs=[SMEM, pl.BlockSpec((orders, rows, width), lambda i: (0, 0, i))],
        out_specs=pl.BlockSpec((rows, width), lambda i: (0, i)),
        compiler_params=pltpu.CompilerParams(vmem_limit_bytes=8 * 2**20),
    )(plan, video_cache)


def first_body(
    scalars,
    plan_ref,
    cache_ref,
    audio_ref,
    kv_ref,
    query_ref,
    out_w,
    packed_ref,
    other_ref,
    half_ref,
    held_ref,
    sems,
):
    rep_at, mem_at, grp_at = scalars[0], scalars[1], scalars[2]
    rows, width = held_ref.shape[1:]
    width = width // 2
    copies = []

    def copy(source, target):
        copies.append(pltpu.make_async_copy(source, target, sems.at[len(copies)]))

    def part(index, size):
        return pl.ds(pl.multiple_of(index * size, size), size)

    blocks = 4
    step = rows // blocks
    for block in range(blocks):
        at = pl.ds(block * step, step)
        for shard in range(2):
            copy(
                cache_ref.at[:, at, part(2 * shard + rep_at, width)],
                held_ref.at[:, at, pl.ds(shard * width, width)],
            )
    lane = width // 2
    for shard in range(2):
        copy(
            audio_ref.at[:, part(2 * (2 * mem_at + shard) + rep_at, lane)],
            packed_ref.at[pl.ds(2 * rows, audio_ref.shape[0]), pl.ds(shard * lane, lane)],
        )
    depth, columns = kv_ref.shape[0] // 2, query_ref.shape[1]
    copy(kv_ref.at[part(1 - rep_at, depth)], other_ref.at[pl.ds(0, depth)])
    quarter = query_ref.shape[0] // 4
    for side in range(2):
        copy(
            query_ref.at[part(2 * (1 - rep_at) + side, quarter)],
            other_ref.at[pl.ds(depth, quarter), pl.ds(side * columns, columns)],
        )
    copy(out_w.at[part(grp_at, half_ref.shape[0])], half_ref)
    for started in copies:
        started.start()
    step_ratio = plan_ratio(plan_ref, width)
    for block in range(blocks):
        for shard in range(2):
            copies[2 * block + shard].wait()
            taylor_rows(
                held_ref.at[:, :, pl.ds(shard * width, width)],
                packed_ref.at[pl.ds(shard * rows, rows)],
                step_ratio,
                block * step,
                (block + 1) * step,
            )
    for started in copies[2 * blocks :]:
        started.wait()


def weight_body(scalars, kv_ref, query_ref, other_ref, own_ref, *piece_refs):
    seq_at, rep_at, grp_at = scalars[0], scalars[1], scalars[2]
    kv_half, query_half = kv_ref.shape[0] // 2, query_ref.shape[0] // 2
    kv_rows, query_rows = kv_half // 2, query_half // 2
    fold = query_rows // 2

    def fill(out_ref, bit, group, kv_at, query_at):
        head = seq_at ^ bit
        width = 2 * HEAD_DIM
        lanes = pl.ds(pl.multiple_of(head * width, width), width)
        at = pl.ds(pl.multiple_of(rep_at * kv_half + group * kv_rows, kv_rows), kv_rows)
        out_ref[kv_at : kv_at + kv_rows, :width] = kv_ref[at, lanes]
        at = pl.ds(pl.multiple_of(group * kv_rows, kv_rows), kv_rows)
        out_ref[kv_at : kv_at + kv_rows, width:] = other_ref[at, lanes]
        lanes = pl.ds(pl.multiple_of(head * HEAD_DIM, HEAD_DIM), HEAD_DIM)
        other_lanes = pl.ds(
            pl.multiple_of(group * query_ref.shape[1] + head * HEAD_DIM, HEAD_DIM), HEAD_DIM
        )
        for side in range(2):
            first = rep_at * query_half + group * query_rows + side * fold
            at = pl.ds(pl.multiple_of(first, fold), fold)
            to = slice(query_at, query_at + fold)
            out_ref[to, side * width : side * width + HEAD_DIM] = query_ref[at, lanes]
            out_ref[to, side * width + HEAD_DIM : (side + 1) * width] = other_ref[
                kv_half + side * fold : kv_half + (side + 1) * fold, other_lanes
            ]

    for group in range(2):
        fill(own_ref, 0, group, group * kv_rows, kv_half + group * fold)
    for bit, piece_ref in enumerate(piece_refs, 1):
        fill(piece_ref, bit, grp_at, 0, kv_rows)


def products_body(scalars, *refs):
    packed_refs, weight_refs = refs[:8], refs[8:15]
    send_ref, keep_ref, rows_ref, audio_ref, kv_ref, query_ref = refs[15:]
    seq_at, mem_at, grp_at = scalars[0], scalars[1], scalars[2]
    rows, audio_rows = rows_ref.shape[0] // 4, audio_ref.shape[0] // 4
    depth, lane = rows_ref.shape[1] // 4, audio_ref.shape[1] // 4
    for at, packed_ref in enumerate(packed_refs):
        slot, mem = divmod(at, 2)
        for part in range(2):
            shard = 2 * (mem_at ^ mem) + part
            lanes = pl.ds(pl.multiple_of(shard * depth, depth), depth)
            rows_ref[slot * rows : (slot + 1) * rows, lanes] = packed_ref[
                part * rows : (part + 1) * rows, :
            ]
            lanes = pl.ds(pl.multiple_of(shard * lane, lane), lane)
            audio_ref[slot * audio_rows : (slot + 1) * audio_rows, lanes] = packed_ref[
                2 * rows :, part * lane : (part + 1) * lane
            ]
    kv_half, fold = depth // 2, lane // 4
    width = query_ref.shape[1]

    def place(piece_ref, shard, group, kv_at, query_at):
        to = pl.ds(pl.multiple_of((2 * shard + group) * kv_half, kv_half), kv_half)
        kv_ref[to, :] = piece_ref[kv_at : kv_at + kv_half, :]
        for side in range(2):
            to = pl.ds(pl.multiple_of((4 * shard + 2 * group + side) * fold, fold), fold)
            query_ref[to, :] = piece_ref[
                query_at : query_at + fold, side * width : (side + 1) * width
            ]

    for group in range(2):
        place(weight_refs[0], seq_at, group, group * kv_half, 2 * kv_half + group * fold)
    for bit in range(1, 4):
        place(weight_refs[2 * bit - 1], seq_at ^ bit, grp_at, 0, kv_half)
        place(weight_refs[2 * bit], seq_at ^ bit, 1 - grp_at, 0, kv_half)

    count = 4 * rows
    columns = keep_ref.shape[1]
    total = jnp.dot(rows_ref[...], kv_ref[...], preferred_element_type=jnp.float32)
    keep_ref[:count, :] = total[:, :columns]
    send_ref[:count, :] = total[:, columns:]
    total = jnp.dot(audio_ref[...], query_ref[...], preferred_element_type=jnp.float32)
    folded = 2 * audio_rows
    for side in range(2):
        at = slice(side * folded, (side + 1) * folded)
        to = slice(side * HEAD_DIM, (side + 1) * HEAD_DIM)
        keep_ref[count:, to] = total[at, :HEAD_DIM]
        send_ref[count:, to] = total[at, HEAD_DIM:]


def attend(queries, kv_ref, frames_ref, align):
    scores = lax.dot_general(
        queries,
        kv_ref[:, :HEAD_DIM],
        (((1,), (1,)), ((), ())),
        preferred_element_type=jnp.float32,
    ) * (1.0 / HEAD_DIM**0.5)
    scores = scores - SLOPE * jnp.abs(frames_ref[...] - align) / FRAMES
    exp_terms = jnp.exp(scores - jnp.max(scores, axis=1, keepdims=True))
    weighted = jnp.dot(
        exp_terms.astype(jnp.bfloat16), kv_ref[:, HEAD_DIM:], preferred_element_type=jnp.float32
    )
    return (weighted / jnp.sum(exp_terms, axis=1, keepdims=True)).astype(jnp.bfloat16)


def attention_body(scalars, frames_ref, align_ref, keep_ref, came_ref, *refs):
    *out_refs, kv_ref, query_ref = refs
    count, audio_rows = kv_ref.shape[0], query_ref.shape[1]

    def summed(rows, columns=slice(None)):
        return (keep_ref[rows, columns] + came_ref[rows, columns]).astype(jnp.bfloat16)

    kv_ref[...] = summed(slice(0, count))
    for slot in range(4):
        side, half = divmod(slot, 2)
        query_ref[scalars[slot]] = summed(
            slice(count + half * audio_rows, count + (half + 1) * audio_rows),
            slice(side * HEAD_DIM, (side + 1) * HEAD_DIM),
        )
    for bit, out_ref in enumerate(out_refs):
        block = scalars[0] ^ bit
        out_ref[...] = attend(query_ref[block], kv_ref, frames_ref, align_ref[block])


def out_body(
    scalars,
    own_ref,
    near_ref,
    far_ref,
    farther_ref,
    own_w,
    partner_w,
    partner_rest_w,
    far_w,
    far_rest_w,
    send_ref,
    keep_ref,
    heads_ref,
    weight_ref,
    sem,
):
    seq_at, grp_at, place = scalars[0], scalars[1], scalars[2]
    copy = pltpu.make_async_copy(own_w, weight_ref.at[0], sem)
    copy.start()
    for bit, head_ref in enumerate((own_ref, near_ref, far_ref, farther_ref)):
        heads_ref[seq_at ^ bit] = head_ref[...]
    heads = jnp.concatenate([heads_ref[head] for head in range(heads_ref.shape[0])], axis=1)
    depth = partner_w.shape[0]
    mine = pl.ds(pl.multiple_of(grp_at * depth, depth), depth)
    rest = pl.ds(pl.multiple_of((1 - grp_at) * depth, depth), depth)
    weight_ref[1, mine] = partner_w[...]
    weight_ref[1, rest] = partner_rest_w[...]
    for far in range(2):
        weight_ref[2 + far, mine] = far_w[far]
        weight_ref[2 + far, rest] = far_rest_w[far]
    middle = 2 - seq_at // 2
    for at, block in ((1, seq_at ^ 1), (2, middle), (3, middle ^ 1), (0, seq_at)):
        if at == 0:
            copy.wait()
        slot = block ^ place
        value = jnp.dot(heads, weight_ref[at], preferred_element_type=jnp.float32)

        @pl.when(slot % 2 == 1)
        def _():
            send_ref[slot // 2] = value.astype(send_ref.dtype)

        @pl.when(slot % 2 == 0)
        def _():
            keep_ref[slot // 2] = value


def by_head(video_cache, plan, alignment, audio_tokens, kv_weight, query_weight, out_weight):
    seq_size = lax.axis_size("seq")
    seq_at, mem_at, rep_at = (lax.axis_index(name) for name in ("seq", "mem", "rep"))
    grp_at = lax.axis_index("grp")
    place = mem_at * 2 + rep_at
    video_rows = video_cache.shape[1]
    audio_rows = audio_tokens.shape[0]
    half_depth, width = kv_weight.shape[0] // 2, 2 * HEAD_DIM
    query_quarter = query_weight.shape[0] // 4

    def bfloat(*shape):
        return jax.ShapeDtypeStruct(shape, jnp.bfloat16)

    packed, other, half = kernel_call(
        first_body,
        [
            bfloat(2 * video_rows + audio_rows, half_depth),
            bfloat(half_depth + query_quarter, kv_weight.shape[1]),
            bfloat(out_weight.shape[0] // 2, out_weight.shape[1]),
        ],
        [
            jnp.stack([rep_at, mem_at, grp_at]),
            plan,
            video_cache,
            audio_tokens,
            kv_weight,
            query_weight,
            out_weight,
        ],
        scratch=[
            pltpu.VMEM((3, video_rows, 2 * half_depth), jnp.bfloat16),
            pltpu.SemaphoreType.DMA((14,)),
        ],
        smem=(1,),
        loose_in=(2, 3, 4, 5, 6),
        limit=61,
    )

    other = swap(other, "rep", 1)
    rows = half_depth // 2 + query_quarter // 2
    weight_own, *pieces = kernel_call(
        weight_body,
        [bfloat(2 * rows, 2 * width)] + [bfloat(rows, 2 * width)] * 3,
        [jnp.stack([seq_at, rep_at, grp_at]), kv_weight, query_weight, other],
    )
    pieces = [swap(piece, "seq", bit) for bit, piece in enumerate(pieces, 1)]

    inner, outward = [(1, 2), (2, 1)], [(1, 0), (2, 3)]
    is_inner = (seq_at == 1) | (seq_at == 2)
    partner = swap(packed, "seq", 1)
    align_all = lax.all_to_all(
        jnp.broadcast_to(alignment[None], (seq_size, audio_rows)), "seq", 0, 0, tiled=True
    ).astype(jnp.float32)
    inner_own = lax.ppermute(packed, "seq", inner)
    partner, inner_own, align_all, weight_own = lax.optimization_barrier(
        (partner, inner_own, align_all, weight_own)
    )
    out_partner = swap(half, "seq", 1)
    inner_partner = lax.ppermute(partner, "seq", inner)
    third = jnp.where(is_inner, inner_own, lax.ppermute(inner_own, "seq", outward))
    third, pieces[0], out_partner = lax.optimization_barrier((third, pieces[0], out_partner))
    fourth = jnp.where(is_inner, inner_partner, lax.ppermute(inner_partner, "seq", outward))
    out_pair = lax.ppermute(jnp.stack([half, out_partner]), "seq", inner)
    fourth, pieces[1], pieces[2], out_pair = lax.optimization_barrier(
        (fourth, pieces[1], pieces[2], out_pair)
    )
    weights = [weight_own]
    for piece in pieces:
        weights += [piece, swap(piece, "grp", 1)]
    tokens = []
    for value in (packed, partner, third, fourth):
        tokens += [value, swap(value, "mem", 1)]
    middle = 2 - seq_at // 2
    blocks = jnp.stack([seq_at, seq_at ^ 1, middle, middle ^ 1])

    partner_rest = swap(out_partner, "grp", 1)
    far = jnp.where(is_inner, out_pair, lax.ppermute(out_pair, "seq", outward))
    far_rest = swap(far, "grp", 1)

    rows = seq_size * (video_rows + audio_rows // 2)
    sums = jax.ShapeDtypeStruct((rows, width), jnp.float32)
    send, keep = kernel_call(
        products_body,
        [sums, sums],
        [jnp.stack([seq_at, mem_at, grp_at]), *tokens, *weights],
        scratch=[
            pltpu.VMEM((seq_size * video_rows, 4 * half_depth), jnp.bfloat16),
            pltpu.VMEM((seq_size * audio_rows, 8 * query_quarter), jnp.bfloat16),
            pltpu.VMEM((4 * half_depth, 2 * width), jnp.bfloat16),
            pltpu.VMEM((8 * query_quarter, width), jnp.bfloat16),
        ],
        after=(far, partner_rest),
        limit=26,
    )
    came = swap(send, "rep", 1)

    span = video_rows * seq_size
    positions = blocks[:, None] * video_rows + jnp.arange(video_rows, dtype=jnp.int32)[None, :]
    frames_video = (positions.reshape(1, span) * FRAMES // span).astype(jnp.float32)
    own_piece, near_piece, far_piece, farther_piece = kernel_call(
        attention_body,
        [bfloat(audio_rows, HEAD_DIM)] * 4,
        [blocks, frames_video, align_all[:, :, None], keep, came],
        scratch=[
            pltpu.VMEM((span, width), jnp.bfloat16),
            pltpu.VMEM((seq_size, audio_rows, HEAD_DIM), jnp.bfloat16),
        ],
    )
    far_piece = swap(far_piece, "seq", 2)
    farther_piece = swap(farther_piece, "seq", 3)
    near_piece = swap(near_piece, "seq", 1)

    columns = out_weight.shape[1]
    send, keep = kernel_call(
        out_body,
        [
            jax.ShapeDtypeStruct((2, audio_rows, columns), jnp.bfloat16),
            jax.ShapeDtypeStruct((2, audio_rows, columns), jnp.float32),
        ],
        [
            jnp.stack([seq_at, grp_at, place]),
            own_piece,
            near_piece,
            far_piece,
            farther_piece,
            out_weight,
            out_partner,
            partner_rest,
            far,
            far_rest,
        ],
        scratch=[
            pltpu.VMEM((seq_size, audio_rows, HEAD_DIM), jnp.bfloat16),
            pltpu.VMEM((seq_size, *out_weight.shape), jnp.bfloat16),
            pltpu.SemaphoreType.DMA,
        ],
        loose_in=(5,),
    )
    came = swap(send, "rep", 1)
    across = swap((keep[1] + came[1].astype(jnp.float32)).astype(jnp.bfloat16), "mem", 1)
    residual = lax.dynamic_slice_in_dim(audio_tokens, place * columns, columns, 1)
    own_part = taylor(video_cache, plan, 2 * half_depth)
    base = residual.astype(jnp.float32) + (keep[0] + came[0].astype(jnp.float32))
    base, across = lax.optimization_barrier((base, across))
    audio_output = (base + across.astype(jnp.float32)).astype(jnp.bfloat16)
    return (own_part, audio_output)


def solution(mesh):
    sizes = dict(mesh.shape)
    square = (sizes["grp"], sizes["seq"], sizes["mem"], sizes["rep"]) == (2, 4, 2, 2)

    def on_device(*arrays):
        heads = arrays[5].shape[1] // HEAD_DIM
        return (by_head if square and heads == sizes["seq"] else general)(*arrays)

    return jax.shard_map(
        on_device,
        mesh=mesh,
        in_specs=(
            P(None, ("grp", "seq"), "mem"),
            P("grp"),
            P(("grp", "seq")),
            P(("grp", "seq"), None),
            P("seq", ("mem", "rep")),
            P("seq", ("mem", "rep")),
            P(("mem", "rep"), "seq"),
        ),
        out_specs=(P(("grp", "seq"), "mem"), P(("grp", "seq"), ("mem", "rep"))),
        check_vma=False,
    )
```

```python
import math

import jax
import jax.numpy as jnp
from jax import lax
from jax.experimental import pallas as pl
from jax.experimental.pallas import tpu as pltpu
from jax.sharding import PartitionSpec as P

HEAD_DIM = 128
FRAMES = 24


SLOPE = 4.0


def taylor_ratio(plan):
    history = plan.shape[0]
    step_ids = jnp.arange(history, dtype=jnp.int32)
    marked = step_ids * plan
    last_fresh = jnp.max(marked)
    prior_fresh = jnp.max(jnp.where(step_ids < last_fresh, marked, 0))
    return (history - last_fresh).astype(jnp.float32) / (last_fresh - prior_fresh).astype(
        jnp.float32
    )


def combine(orders, step_ratio):
    values = orders.astype(jnp.float32)
    return (values[0] + step_ratio * values[1] + 0.5 * step_ratio * step_ratio * values[2]).astype(
        jnp.bfloat16
    )


def general(video_cache, plan, alignment, audio_tokens, kv_weight, query_weight, out_weight):
    step_ratio = taylor_ratio(plan)
    own_part = combine(video_cache, step_ratio)
    features_all = lax.all_gather(own_part, "mem", axis=1, tiled=True)
    video_rows = features_all.shape[0]
    kv_local = jnp.dot(
        features_all,
        lax.all_gather(kv_weight, "seq", axis=0, tiled=True),
        preferred_element_type=jnp.float32,
    )
    head_size = HEAD_DIM
    local_heads = query_weight.shape[1] // head_size
    kv_local = kv_local.astype(jnp.bfloat16).reshape(video_rows, local_heads, 2, head_size)
    key_rows = kv_local[:, :, 0, :]
    value_rows = kv_local[:, :, 1, :]
    query_full, out_full = (
        lax.all_gather(query_weight, "seq", axis=0, tiled=True),
        lax.all_gather(out_weight, "seq", axis=1, tiled=True),
    )
    audio_rows = audio_tokens.shape[0]
    queries = jnp.dot(audio_tokens, query_full, preferred_element_type=jnp.float32).astype(
        jnp.bfloat16
    )
    queries = queries.reshape(audio_rows, local_heads, head_size)
    scale = 1.0 / head_size**0.5
    span = video_rows * lax.axis_size("seq")
    initial = (
        jnp.full((local_heads, audio_rows), -1e30, jnp.float32),
        jnp.zeros((local_heads, audio_rows), jnp.float32),
        jnp.zeros((local_heads, audio_rows, head_size), jnp.float32),
    )
    key_piece = lax.all_gather(key_rows, "seq", axis=0, tiled=True)
    value_piece = lax.all_gather(value_rows, "seq", axis=0, tiled=True)
    row_count = key_piece.shape[0]
    block_len = math.gcd(row_count, 1024)

    def advance(block_index, carried):
        row_max, row_sum, weighted = carried
        key_block = lax.dynamic_slice_in_dim(key_piece, block_index * block_len, block_len, 0)
        value_block = lax.dynamic_slice_in_dim(value_piece, block_index * block_len, block_len, 0)
        positions = block_index * block_len + jnp.arange(block_len, dtype=jnp.int32)
        frames_video = positions * FRAMES // span
        distance_bias = (
            -SLOPE
            * jnp.abs(frames_video[None, :] - alignment[:, None]).astype(jnp.float32)
            / FRAMES
        )
        scores = (
            jnp.einsum("qhd,khd->hqk", queries, key_block, preferred_element_type=jnp.float32)
            * scale
        )
        scores = scores + distance_bias[None]
        new_max = jnp.maximum(row_max, jnp.max(scores, axis=2))
        rescale = jnp.exp(row_max - new_max)
        exp_terms = jnp.exp(scores - new_max[:, :, None])
        row_sum = row_sum * rescale + jnp.sum(exp_terms, axis=2)
        weighted = weighted * rescale[:, :, None] + jnp.einsum(
            "hqk,khd->hqd",
            exp_terms.astype(jnp.bfloat16),
            value_block,
            preferred_element_type=jnp.float32,
        )
        return (new_max, row_sum, weighted)

    row_max, row_sum, weighted = lax.fori_loop(0, row_count // block_len, advance, initial)
    attended = (weighted / row_sum[:, :, None]).astype(jnp.bfloat16)
    attended = jnp.transpose(attended, (1, 0, 2)).reshape(audio_rows, local_heads * head_size)
    partial_update = jnp.dot(attended, out_full, preferred_element_type=jnp.float32)
    update = lax.psum_scatter(
        partial_update.astype(jnp.bfloat16), ("mem", "rep"), scatter_dimension=1, tiled=True
    ).astype(jnp.float32)
    own_columns = update.shape[1]
    residual = lax.dynamic_slice_in_dim(
        audio_tokens, lax.axis_index(("mem", "rep")) * own_columns, own_columns, 1
    )
    audio_output = (residual.astype(jnp.float32) + update).astype(jnp.bfloat16)
    return (own_part, audio_output)


def swap(value, axis, bit):
    size = lax.axis_size(axis)
    return lax.ppermute(value, axis, [(i, i ^ bit) for i in range(size)])


VMEM = pl.BlockSpec(memory_space=pltpu.VMEM)
SMEM = pl.BlockSpec(memory_space=pltpu.SMEM)
ANY = pl.BlockSpec(memory_space=pl.ANY)
HBM = pl.BlockSpec(memory_space=pltpu.HBM)


def kernel_call(body, outs, ins, after=(), scratch=(), smem=(), loose_in=(), limit=14):
    def whole(*refs):
        body(*refs[: len(ins)], *refs[len(ins) + len(after) :])

    spots = [SMEM if i in smem else HBM if i in loose_in else VMEM for i in range(len(ins))]
    return pl.pallas_call(
        whole,
        out_shape=outs,
        in_specs=spots + [ANY] * len(after),
        out_specs=[VMEM] * len(outs),
        scratch_shapes=scratch,
        compiler_params=pltpu.CompilerParams(vmem_limit_bytes=limit * 2**20),
    )(*ins, *after)


def plan_ratio(plan_ref, columns):
    history = plan_ref.shape[0]
    last_fresh, prior_fresh = jnp.int32(0), jnp.int32(0)
    for step in range(history):
        fresh = plan_ref[step] == 1
        prior_fresh = jnp.where(fresh, last_fresh, prior_fresh)
        last_fresh = jnp.where(fresh, step, last_fresh)
    ahead = jnp.full((1, columns), history - last_fresh, jnp.int32).astype(jnp.float32)
    apart = jnp.full((1, columns), last_fresh - prior_fresh, jnp.int32).astype(jnp.float32)
    return ahead / apart


def taylor_rows(cache_ref, out_ref, step_ratio, first, last):
    half_square = 0.5 * step_ratio * step_ratio
    for at in range(first, last, 16):
        terms = [cache_ref[order, at : at + 16, :].astype(jnp.float32) for order in range(3)]
        out_ref[at : at + 16, :] = (
            terms[0] + step_ratio * terms[1] + half_square * terms[2]
        ).astype(jnp.bfloat16)


def taylor_body(plan_ref, cache_ref, out_ref):
    rows, columns = out_ref.shape
    taylor_rows(cache_ref, out_ref, plan_ratio(plan_ref, columns), 0, rows)


def taylor(video_cache, plan, width):
    orders, rows, columns = video_cache.shape
    return pl.pallas_call(
        taylor_body,
        out_shape=jax.ShapeDtypeStruct((rows, columns), jnp.bfloat16),
        grid=(columns // width,),
        in_specs=[SMEM, pl.BlockSpec((orders, rows, width), lambda i: (0, 0, i))],
        out_specs=pl.BlockSpec((rows, width), lambda i: (0, i)),
        compiler_params=pltpu.CompilerParams(vmem_limit_bytes=8 * 2**20),
    )(plan, video_cache)


def first_body(
    plan_ref,
    cache_ref,
    audio_ref,
    kv_ref,
    query_ref,
    out_w,
    packed_ref,
    other_ref,
    half_ref,
    held_ref,
    sems,
):
    rep_at, mem_at, grp_at = (lax.axis_index(name) for name in ("rep", "mem", "grp"))
    rows, width = held_ref.shape[1:]
    width = width // 2
    copies = []

    def copy(source, target):
        copies.append(pltpu.make_async_copy(source, target, sems.at[len(copies)]))

    def part(index, size):
        return pl.ds(pl.multiple_of(index * size, size), size)

    blocks = 4
    step = rows // blocks
    for block in range(blocks):
        at = pl.ds(block * step, step)
        for shard in range(2):
            copy(
                cache_ref.at[:, at, part(2 * shard + rep_at, width)],
                held_ref.at[:, at, pl.ds(shard * width, width)],
            )
    lane = width // 2
    for shard in range(2):
        copy(
            audio_ref.at[:, part(2 * (2 * mem_at + shard) + rep_at, lane)],
            packed_ref.at[pl.ds(2 * rows, audio_ref.shape[0]), pl.ds(shard * lane, lane)],
        )
    depth, columns = kv_ref.shape[0] // 2, query_ref.shape[1]
    copy(kv_ref.at[part(1 - rep_at, depth)], other_ref.at[pl.ds(0, depth)])
    quarter = query_ref.shape[0] // 4
    for side in range(2):
        copy(
            query_ref.at[part(2 * (1 - rep_at) + side, quarter)],
            other_ref.at[pl.ds(depth, quarter), pl.ds(side * columns, columns)],
        )
    copy(out_w.at[part(grp_at, half_ref.shape[0])], half_ref)
    for started in copies:
        started.start()
    step_ratio = plan_ratio(plan_ref, width)
    for block in range(blocks):
        for shard in range(2):
            copies[2 * block + shard].wait()
            taylor_rows(
                held_ref.at[:, :, pl.ds(shard * width, width)],
                packed_ref.at[pl.ds(shard * rows, rows)],
                step_ratio,
                block * step,
                (block + 1) * step,
            )
    for started in copies[2 * blocks :]:
        started.wait()


def weight_body(kv_ref, query_ref, other_ref, own_ref, *piece_refs):
    seq_at, rep_at, grp_at = (lax.axis_index(name) for name in ("seq", "rep", "grp"))
    kv_half, query_half = kv_ref.shape[0] // 2, query_ref.shape[0] // 2
    kv_rows, query_rows = kv_half // 2, query_half // 2
    fold = query_rows // 2

    def fill(out_ref, bit, group, kv_at, query_at):
        head = seq_at ^ bit
        width = 2 * HEAD_DIM
        lanes = pl.ds(pl.multiple_of(head * width, width), width)
        at = pl.ds(pl.multiple_of(rep_at * kv_half + group * kv_rows, kv_rows), kv_rows)
        out_ref[kv_at : kv_at + kv_rows, :width] = kv_ref[at, lanes]
        at = pl.ds(pl.multiple_of(group * kv_rows, kv_rows), kv_rows)
        out_ref[kv_at : kv_at + kv_rows, width:] = other_ref[at, lanes]
        lanes = pl.ds(pl.multiple_of(head * HEAD_DIM, HEAD_DIM), HEAD_DIM)
        other_lanes = pl.ds(
            pl.multiple_of(group * query_ref.shape[1] + head * HEAD_DIM, HEAD_DIM), HEAD_DIM
        )
        for side in range(2):
            first = rep_at * query_half + group * query_rows + side * fold
            at = pl.ds(pl.multiple_of(first, fold), fold)
            to = slice(query_at, query_at + fold)
            out_ref[to, side * width : side * width + HEAD_DIM] = query_ref[at, lanes]
            out_ref[to, side * width + HEAD_DIM : (side + 1) * width] = other_ref[
                kv_half + side * fold : kv_half + (side + 1) * fold, other_lanes
            ]

    for group in range(2):
        fill(own_ref, 0, group, group * kv_rows, kv_half + group * fold)
    for bit, piece_ref in enumerate(piece_refs, 1):
        fill(piece_ref, bit, grp_at, 0, kv_rows)


def products_body(*refs):
    packed_refs, weight_refs = refs[:8], refs[8:15]
    send_ref, keep_ref, rows_ref, audio_ref, kv_ref, query_ref = refs[15:]
    seq_at, mem_at, grp_at = (lax.axis_index(name) for name in ("seq", "mem", "grp"))
    rows, audio_rows = rows_ref.shape[0] // 4, audio_ref.shape[0] // 4
    depth, lane = rows_ref.shape[1] // 4, audio_ref.shape[1] // 4
    for at, packed_ref in enumerate(packed_refs):
        slot, mem = divmod(at, 2)
        for part in range(2):
            shard = 2 * (mem_at ^ mem) + part
            lanes = pl.ds(pl.multiple_of(shard * depth, depth), depth)
            rows_ref[slot * rows : (slot + 1) * rows, lanes] = packed_ref[
                part * rows : (part + 1) * rows, :
            ]
            lanes = pl.ds(pl.multiple_of(shard * lane, lane), lane)
            audio_ref[slot * audio_rows : (slot + 1) * audio_rows, lanes] = packed_ref[
                2 * rows :, part * lane : (part + 1) * lane
            ]
    kv_half, fold = depth // 2, lane // 4
    width = query_ref.shape[1]

    def place(piece_ref, shard, group, kv_at, query_at):
        to = pl.ds(pl.multiple_of((2 * shard + group) * kv_half, kv_half), kv_half)
        kv_ref[to, :] = piece_ref[kv_at : kv_at + kv_half, :]
        for side in range(2):
            to = pl.ds(pl.multiple_of((4 * shard + 2 * group + side) * fold, fold), fold)
            query_ref[to, :] = piece_ref[
                query_at : query_at + fold, side * width : (side + 1) * width
            ]

    for group in range(2):
        place(weight_refs[0], seq_at, group, group * kv_half, 2 * kv_half + group * fold)
    for bit in range(1, 4):
        place(weight_refs[2 * bit - 1], seq_at ^ bit, grp_at, 0, kv_half)
        place(weight_refs[2 * bit], seq_at ^ bit, 1 - grp_at, 0, kv_half)

    count = 4 * rows
    columns = keep_ref.shape[1]
    total = jnp.dot(rows_ref[...], kv_ref[...], preferred_element_type=jnp.float32)
    keep_ref[:count, :] = total[:, :columns]
    send_ref[:count, :] = total[:, columns:]
    total = jnp.dot(audio_ref[...], query_ref[...], preferred_element_type=jnp.float32)
    folded = 2 * audio_rows
    for side in range(2):
        at = slice(side * folded, (side + 1) * folded)
        to = slice(side * HEAD_DIM, (side + 1) * HEAD_DIM)
        keep_ref[count:, to] = total[at, :HEAD_DIM]
        send_ref[count:, to] = total[at, HEAD_DIM:]


def attend(queries, kv_ref, frames_ref, align):
    scores = lax.dot_general(
        queries,
        kv_ref[:, :HEAD_DIM],
        (((1,), (1,)), ((), ())),
        preferred_element_type=jnp.float32,
    ) * (1.0 / HEAD_DIM**0.5)
    scores = scores - SLOPE * jnp.abs(frames_ref[...] - align) / FRAMES
    exp_terms = jnp.exp(scores - jnp.max(scores, axis=1, keepdims=True))
    weighted = jnp.dot(
        exp_terms.astype(jnp.bfloat16), kv_ref[:, HEAD_DIM:], preferred_element_type=jnp.float32
    )
    return (weighted / jnp.sum(exp_terms, axis=1, keepdims=True)).astype(jnp.bfloat16)


def attention_body(frames_ref, align_ref, keep_ref, came_ref, *refs):
    *out_refs, kv_ref, query_ref = refs
    count, audio_rows = kv_ref.shape[0], query_ref.shape[1]

    def summed(rows, columns=slice(None)):
        return (keep_ref[rows, columns] + came_ref[rows, columns]).astype(jnp.bfloat16)

    kv_ref[...] = summed(slice(0, count))
    for slot in range(4):
        side, half = divmod(slot, 2)
        query_ref[slot] = summed(
            slice(count + half * audio_rows, count + (half + 1) * audio_rows),
            slice(side * HEAD_DIM, (side + 1) * HEAD_DIM),
        )
    for bit, out_ref in enumerate(out_refs):
        align = align_ref[lax.axis_index("seq") ^ bit]
        out_ref[...] = attend(query_ref[bit], kv_ref, frames_ref, align)


def out_body(*refs):
    piece_refs, (own_w, *part_refs), (send_ref, keep_ref, heads_ref, weight_ref, sem) = (
        refs[:4],
        refs[4:11],
        refs[11:],
    )
    seq_at, grp_at = lax.axis_index("seq"), lax.axis_index("grp")
    place = lax.axis_index("mem") * 2 + lax.axis_index("rep")
    copy = pltpu.make_async_copy(own_w, weight_ref.at[0], sem)
    copy.start()
    for bit, piece_ref in enumerate(piece_refs):
        heads_ref[seq_at ^ bit] = piece_ref[...]
    heads = jnp.concatenate([heads_ref[head] for head in range(heads_ref.shape[0])], axis=1)
    depth = part_refs[0].shape[0]
    mine = pl.ds(pl.multiple_of(grp_at * depth, depth), depth)
    rest = pl.ds(pl.multiple_of((1 - grp_at) * depth, depth), depth)
    for bit in range(1, 4):
        weight_ref[bit, mine] = part_refs[2 * bit - 2][...]
        weight_ref[bit, rest] = part_refs[2 * bit - 1][...]
    for bit in (1, 2, 3, 0):
        if bit == 0:
            copy.wait()
        slot = seq_at ^ bit ^ place
        value = jnp.dot(heads, weight_ref[bit], preferred_element_type=jnp.float32)

        @pl.when(slot % 2 == 1)
        def _():
            send_ref[slot // 2] = value.astype(send_ref.dtype)

        @pl.when(slot % 2 == 0)
        def _():
            keep_ref[slot // 2] = value


def by_head(video_cache, plan, alignment, audio_tokens, kv_weight, query_weight, out_weight):
    seq_size = lax.axis_size("seq")
    seq_at = lax.axis_index("seq")
    place = lax.axis_index("mem") * 2 + lax.axis_index("rep")
    video_rows = video_cache.shape[1]
    audio_rows = audio_tokens.shape[0]
    half_depth, width = kv_weight.shape[0] // 2, 2 * HEAD_DIM
    query_quarter = query_weight.shape[0] // 4

    def bfloat(*shape):
        return jax.ShapeDtypeStruct(shape, jnp.bfloat16)

    packed, other, out_half = kernel_call(
        first_body,
        [
            bfloat(2 * video_rows + audio_rows, half_depth),
            bfloat(half_depth + query_quarter, kv_weight.shape[1]),
            bfloat(out_weight.shape[0] // 2, out_weight.shape[1]),
        ],
        [plan, video_cache, audio_tokens, kv_weight, query_weight, out_weight],
        scratch=[
            pltpu.VMEM((3, video_rows, 2 * half_depth), jnp.bfloat16),
            pltpu.SemaphoreType.DMA((14,)),
        ],
        smem=(0,),
        loose_in=(1, 2, 3, 4, 5),
        limit=61,
    )

    tokens = [packed, swap(packed, "seq", 1), swap(packed, "seq", 2)]
    across = [swap(packed, "mem", 1)]
    other = swap(other, "rep", 1)
    rows = half_depth // 2 + query_quarter // 2
    weight_own, *pieces = kernel_call(
        weight_body,
        [bfloat(2 * rows, 2 * width)] + [bfloat(rows, 2 * width)] * 3,
        [kv_weight, query_weight, other],
    )
    pieces[0] = swap(pieces[0], "seq", 1)
    align_all = lax.all_to_all(
        jnp.broadcast_to(alignment[None], (seq_size, audio_rows)), "seq", 0, 0, tiled=True
    ).astype(jnp.float32)
    tokens[1], tokens[2], across[0], pieces[0], align_all = lax.optimization_barrier(
        (tokens[1], tokens[2], across[0], pieces[0], align_all)
    )

    tokens.append(swap(tokens[2], "seq", 1))
    across += [swap(tokens[1], "mem", 1), swap(tokens[2], "mem", 1)]
    pieces[1:] = [swap(piece, "seq", bit) for bit, piece in enumerate(pieces[1:], 2)]
    rest = [swap(pieces[0], "grp", 1)]
    tokens[3], across[1], across[2], pieces[1], pieces[2], rest[0], out_half = (
        lax.optimization_barrier(
            (tokens[3], across[1], across[2], pieces[1], pieces[2], rest[0], out_half)
        )
    )

    across.append(swap(tokens[3], "mem", 1))
    rest += [swap(piece, "grp", 1) for piece in pieces[1:]]
    out_parts = [swap(out_half, "seq", 1), swap(out_half, "seq", 2)]
    weights = [weight_own]
    for piece, other in zip(pieces, rest):
        weights += [piece, other]
    rows = seq_size * (video_rows + audio_rows // 2)
    sums = jax.ShapeDtypeStruct((rows, width), jnp.float32)
    send, keep = kernel_call(
        products_body,
        [sums, sums],
        [value for pair in zip(tokens, across) for value in pair] + weights,
        after=out_parts,
        scratch=[
            pltpu.VMEM((seq_size * video_rows, 4 * half_depth), jnp.bfloat16),
            pltpu.VMEM((seq_size * audio_rows, 8 * query_quarter), jnp.bfloat16),
            pltpu.VMEM((4 * half_depth, 2 * width), jnp.bfloat16),
            pltpu.VMEM((8 * query_quarter, width), jnp.bfloat16),
        ],
        limit=26,
    )
    came = swap(send, "rep", 1)
    out_parts.append(swap(out_parts[1], "seq", 1))

    span = video_rows * seq_size
    blocks = jnp.stack([seq_at, seq_at ^ 1, seq_at ^ 2, seq_at ^ 3])
    positions = blocks[:, None] * video_rows + jnp.arange(video_rows, dtype=jnp.int32)[None, :]
    frames_video = (positions.reshape(1, span) * FRAMES // span).astype(jnp.float32)
    own_piece, near_piece, far_piece, farther_piece = kernel_call(
        attention_body,
        [bfloat(audio_rows, HEAD_DIM)] * 4,
        [frames_video, align_all[:, :, None], keep, came],
        after=(out_parts[2],),
        scratch=[
            pltpu.VMEM((span, width), jnp.bfloat16),
            pltpu.VMEM((seq_size, audio_rows, HEAD_DIM), jnp.bfloat16),
        ],
    )
    far_piece = swap(far_piece, "seq", 2)
    farther_piece = swap(farther_piece, "seq", 3)
    near_piece = swap(near_piece, "seq", 1)

    columns = out_weight.shape[1]
    weights = [out_weight]
    for part in out_parts:
        weights += [part, swap(part, "grp", 1)]
    send, keep = kernel_call(
        out_body,
        [
            jax.ShapeDtypeStruct((2, audio_rows, columns), jnp.bfloat16),
            jax.ShapeDtypeStruct((2, audio_rows, columns), jnp.float32),
        ],
        [own_piece, near_piece, far_piece, farther_piece, *weights],
        scratch=[
            pltpu.VMEM((seq_size, audio_rows, HEAD_DIM), jnp.bfloat16),
            pltpu.VMEM((seq_size, *out_weight.shape), jnp.bfloat16),
            pltpu.SemaphoreType.DMA,
        ],
        loose_in=(4,),
    )
    came = swap(send, "rep", 1)
    across = swap((keep[1] + came[1].astype(jnp.float32)).astype(jnp.bfloat16), "mem", 1)
    residual = lax.dynamic_slice_in_dim(audio_tokens, place * columns, columns, 1)
    own_part = taylor(video_cache, plan, 2 * half_depth)
    base = residual.astype(jnp.float32) + (keep[0] + came[0].astype(jnp.float32))
    base, across = lax.optimization_barrier((base, across))
    audio_output = (base + across.astype(jnp.float32)).astype(jnp.bfloat16)
    return (own_part, audio_output)


def solution(mesh):
    sizes = dict(mesh.shape)
    square = (sizes["grp"], sizes["seq"], sizes["mem"], sizes["rep"]) == (2, 4, 2, 2)

    def on_device(*arrays):
        heads = arrays[5].shape[1] // HEAD_DIM
        return (by_head if square and heads == sizes["seq"] else general)(*arrays)

    return jax.shard_map(
        on_device,
        mesh=mesh,
        in_specs=(
            P(None, ("grp", "seq"), "mem"),
            P("grp"),
            P(("grp", "seq")),
            P(("grp", "seq"), None),
            P("seq", ("mem", "rep")),
            P("seq", ("mem", "rep")),
            P(("mem", "rep"), "seq"),
        ),
        out_specs=(P(("grp", "seq"), "mem"), P(("grp", "seq"), ("mem", "rep"))),
        check_vma=False,
    )
```

```python
import math

import jax
import jax.numpy as jnp
from jax import lax
from jax.experimental import pallas as pl
from jax.experimental.pallas import tpu as pltpu
from jax.sharding import PartitionSpec as P

HEAD_DIM = 128
FRAMES = 24


SLOPE = 4.0


def taylor_ratio(plan):
    history = plan.shape[0]
    step_ids = jnp.arange(history, dtype=jnp.int32)
    marked = step_ids * plan
    last_fresh = jnp.max(marked)
    prior_fresh = jnp.max(jnp.where(step_ids < last_fresh, marked, 0))
    return (history - last_fresh).astype(jnp.float32) / (last_fresh - prior_fresh).astype(
        jnp.float32
    )


def combine(orders, step_ratio):
    values = orders.astype(jnp.float32)
    return (values[0] + step_ratio * values[1] + 0.5 * step_ratio * step_ratio * values[2]).astype(
        jnp.bfloat16
    )


def general(video_cache, plan, alignment, audio_tokens, kv_weight, query_weight, out_weight):
    step_ratio = taylor_ratio(plan)
    own_part = combine(video_cache, step_ratio)
    features_all = lax.all_gather(own_part, "mem", axis=1, tiled=True)
    video_rows = features_all.shape[0]
    kv_local = jnp.dot(
        features_all,
        lax.all_gather(kv_weight, "seq", axis=0, tiled=True),
        preferred_element_type=jnp.float32,
    )
    head_size = HEAD_DIM
    local_heads = query_weight.shape[1] // head_size
    kv_local = kv_local.astype(jnp.bfloat16).reshape(video_rows, local_heads, 2, head_size)
    key_rows = kv_local[:, :, 0, :]
    value_rows = kv_local[:, :, 1, :]
    query_full, out_full = (
        lax.all_gather(query_weight, "seq", axis=0, tiled=True),
        lax.all_gather(out_weight, "seq", axis=1, tiled=True),
    )
    audio_rows = audio_tokens.shape[0]
    queries = jnp.dot(audio_tokens, query_full, preferred_element_type=jnp.float32).astype(
        jnp.bfloat16
    )
    queries = queries.reshape(audio_rows, local_heads, head_size)
    scale = 1.0 / head_size**0.5
    span = video_rows * lax.axis_size("seq")
    initial = (
        jnp.full((local_heads, audio_rows), -1e30, jnp.float32),
        jnp.zeros((local_heads, audio_rows), jnp.float32),
        jnp.zeros((local_heads, audio_rows, head_size), jnp.float32),
    )
    key_piece = lax.all_gather(key_rows, "seq", axis=0, tiled=True)
    value_piece = lax.all_gather(value_rows, "seq", axis=0, tiled=True)
    row_count = key_piece.shape[0]
    block_len = math.gcd(row_count, 1024)

    def advance(block_index, carried):
        row_max, row_sum, weighted = carried
        key_block = lax.dynamic_slice_in_dim(key_piece, block_index * block_len, block_len, 0)
        value_block = lax.dynamic_slice_in_dim(value_piece, block_index * block_len, block_len, 0)
        positions = block_index * block_len + jnp.arange(block_len, dtype=jnp.int32)
        frames_video = positions * FRAMES // span
        distance_bias = (
            -SLOPE
            * jnp.abs(frames_video[None, :] - alignment[:, None]).astype(jnp.float32)
            / FRAMES
        )
        scores = (
            jnp.einsum("qhd,khd->hqk", queries, key_block, preferred_element_type=jnp.float32)
            * scale
        )
        scores = scores + distance_bias[None]
        new_max = jnp.maximum(row_max, jnp.max(scores, axis=2))
        rescale = jnp.exp(row_max - new_max)
        exp_terms = jnp.exp(scores - new_max[:, :, None])
        row_sum = row_sum * rescale + jnp.sum(exp_terms, axis=2)
        weighted = weighted * rescale[:, :, None] + jnp.einsum(
            "hqk,khd->hqd",
            exp_terms.astype(jnp.bfloat16),
            value_block,
            preferred_element_type=jnp.float32,
        )
        return (new_max, row_sum, weighted)

    row_max, row_sum, weighted = lax.fori_loop(0, row_count // block_len, advance, initial)
    attended = (weighted / row_sum[:, :, None]).astype(jnp.bfloat16)
    attended = jnp.transpose(attended, (1, 0, 2)).reshape(audio_rows, local_heads * head_size)
    partial_update = jnp.dot(attended, out_full, preferred_element_type=jnp.float32)
    update = lax.psum_scatter(
        partial_update.astype(jnp.bfloat16), ("mem", "rep"), scatter_dimension=1, tiled=True
    ).astype(jnp.float32)
    own_columns = update.shape[1]
    residual = lax.dynamic_slice_in_dim(
        audio_tokens, lax.axis_index(("mem", "rep")) * own_columns, own_columns, 1
    )
    audio_output = (residual.astype(jnp.float32) + update).astype(jnp.bfloat16)
    return (own_part, audio_output)


def swap(value, axis, bit):
    size = lax.axis_size(axis)
    return lax.ppermute(value, axis, [(i, i ^ bit) for i in range(size)])


VMEM = pl.BlockSpec(memory_space=pltpu.VMEM)
SMEM = pl.BlockSpec(memory_space=pltpu.SMEM)
ANY = pl.BlockSpec(memory_space=pl.ANY)
HBM = pl.BlockSpec(memory_space=pltpu.HBM)


def kernel_call(body, outs, ins, after=(), scratch=(), smem=(), loose_in=(), loose_out=(), limit=14):
    def whole(*refs):
        body(*refs[: len(ins)], *refs[len(ins) + len(after) :])

    spots = [SMEM if i in smem else HBM if i in loose_in else VMEM for i in range(len(ins))]
    return pl.pallas_call(
        whole,
        out_shape=outs,
        in_specs=spots + [ANY] * len(after),
        out_specs=[HBM if i in loose_out else VMEM for i in range(len(outs))],
        scratch_shapes=scratch,
        compiler_params=pltpu.CompilerParams(vmem_limit_bytes=limit * 2**20),
    )(*ins, *after)


def plan_ratio(plan_ref, columns):
    history = plan_ref.shape[0]
    last_fresh, prior_fresh = jnp.int32(0), jnp.int32(0)
    for step in range(history):
        fresh = plan_ref[step] == 1
        prior_fresh = jnp.where(fresh, last_fresh, prior_fresh)
        last_fresh = jnp.where(fresh, step, last_fresh)
    ahead = jnp.full((1, columns), history - last_fresh, jnp.int32).astype(jnp.float32)
    apart = jnp.full((1, columns), last_fresh - prior_fresh, jnp.int32).astype(jnp.float32)
    return ahead / apart


def taylor_rows(cache_ref, out_ref, step_ratio, first, last):
    half_square = 0.5 * step_ratio * step_ratio
    for at in range(first, last, 16):
        terms = [cache_ref[order, at : at + 16, :].astype(jnp.float32) for order in range(3)]
        out_ref[at : at + 16, :] = (
            terms[0] + step_ratio * terms[1] + half_square * terms[2]
        ).astype(jnp.bfloat16)


def taylor_body(plan_ref, cache_ref, out_ref):
    rows, columns = out_ref.shape
    taylor_rows(cache_ref, out_ref, plan_ratio(plan_ref, columns), 0, rows)


def taylor(video_cache, plan, width):
    orders, rows, columns = video_cache.shape
    return pl.pallas_call(
        taylor_body,
        out_shape=jax.ShapeDtypeStruct((rows, columns), jnp.bfloat16),
        grid=(columns // width,),
        in_specs=[SMEM, pl.BlockSpec((orders, rows, width), lambda i: (0, 0, i))],
        out_specs=pl.BlockSpec((rows, width), lambda i: (0, i)),
        compiler_params=pltpu.CompilerParams(vmem_limit_bytes=8 * 2**20),
    )(plan, video_cache)


def first_body(
    plan_ref,
    cache_ref,
    audio_ref,
    kv_ref,
    query_ref,
    out_w,
    packed_ref,
    other_ref,
    half_ref,
    held_ref,
    made_ref,
    sems,
):
    rep_at, mem_at, grp_at = (lax.axis_index(name) for name in ("rep", "mem", "grp"))
    rows, width = held_ref.shape[1:]
    width = width // 2
    copies = []

    def copy(source, target):
        copies.append(pltpu.make_async_copy(source, target, sems.at[len(copies)]))

    def part(index, size):
        return pl.ds(pl.multiple_of(index * size, size), size)

    blocks = 4
    step = rows // blocks
    for block in range(blocks):
        at = pl.ds(block * step, step)
        for shard in range(2):
            copy(
                cache_ref.at[:, at, part(2 * shard + rep_at, width)],
                held_ref.at[:, at, pl.ds(shard * width, width)],
            )
    lane = width // 2
    for shard in range(2):
        copy(
            audio_ref.at[:, part(2 * (2 * mem_at + shard) + rep_at, lane)],
            packed_ref.at[pl.ds(2 * rows, audio_ref.shape[0]), pl.ds(shard * lane, lane)],
        )
    depth, columns = kv_ref.shape[0] // 2, query_ref.shape[1]
    copy(kv_ref.at[part(1 - rep_at, depth)], other_ref.at[pl.ds(0, depth)])
    quarter = query_ref.shape[0] // 4
    for side in range(2):
        copy(
            query_ref.at[part(2 * (1 - rep_at) + side, quarter)],
            other_ref.at[pl.ds(depth, quarter), pl.ds(side * columns, columns)],
        )
    copy(out_w.at[part(grp_at, half_ref.shape[0])], half_ref)
    for started in copies:
        started.start()
    step_ratio = plan_ratio(plan_ref, width)
    for block in range(blocks):
        for shard in range(2):
            copies[2 * block + shard].wait()
            taylor_rows(
                held_ref.at[:, :, pl.ds(shard * width, width)],
                made_ref.at[pl.ds(shard * rows, rows)],
                step_ratio,
                block * step,
                (block + 1) * step,
            )
            at = pl.ds(shard * rows + block * step, step)
            copy(made_ref.at[at], packed_ref.at[at])
            copies[-1].start()
    for started in copies[2 * blocks :]:
        started.wait()


def weight_body(kv_ref, query_ref, other_ref, own_ref, *piece_refs):
    seq_at, rep_at, grp_at = (lax.axis_index(name) for name in ("seq", "rep", "grp"))
    kv_half, query_half = kv_ref.shape[0] // 2, query_ref.shape[0] // 2
    kv_rows, query_rows = kv_half // 2, query_half // 2
    fold = query_rows // 2

    def fill(out_ref, bit, group, kv_at, query_at):
        head = seq_at ^ bit
        width = 2 * HEAD_DIM
        lanes = pl.ds(pl.multiple_of(head * width, width), width)
        at = pl.ds(pl.multiple_of(rep_at * kv_half + group * kv_rows, kv_rows), kv_rows)
        out_ref[kv_at : kv_at + kv_rows, :width] = kv_ref[at, lanes]
        at = pl.ds(pl.multiple_of(group * kv_rows, kv_rows), kv_rows)
        out_ref[kv_at : kv_at + kv_rows, width:] = other_ref[at, lanes]
        lanes = pl.ds(pl.multiple_of(head * HEAD_DIM, HEAD_DIM), HEAD_DIM)
        other_lanes = pl.ds(
            pl.multiple_of(group * query_ref.shape[1] + head * HEAD_DIM, HEAD_DIM), HEAD_DIM
        )
        for side in range(2):
            first = rep_at * query_half + group * query_rows + side * fold
            at = pl.ds(pl.multiple_of(first, fold), fold)
            to = slice(query_at, query_at + fold)
            out_ref[to, side * width : side * width + HEAD_DIM] = query_ref[at, lanes]
            out_ref[to, side * width + HEAD_DIM : (side + 1) * width] = other_ref[
                kv_half + side * fold : kv_half + (side + 1) * fold, other_lanes
            ]

    for group in range(2):
        fill(own_ref, 0, group, group * kv_rows, kv_half + group * fold)
    for bit, piece_ref in enumerate(piece_refs, 1):
        fill(piece_ref, bit, grp_at, 0, kv_rows)


def products_body(*refs):
    packed_refs, weight_refs = refs[:8], refs[8:15]
    send_ref, keep_ref, rows_ref, audio_ref, kv_ref, query_ref = refs[15:]
    seq_at, mem_at, grp_at = (lax.axis_index(name) for name in ("seq", "mem", "grp"))
    rows, audio_rows = rows_ref.shape[0] // 4, audio_ref.shape[0] // 4
    depth, lane = rows_ref.shape[1] // 4, audio_ref.shape[1] // 4
    for at, packed_ref in enumerate(packed_refs):
        slot, mem = divmod(at, 2)
        for part in range(2):
            shard = 2 * (mem_at ^ mem) + part
            lanes = pl.ds(pl.multiple_of(shard * depth, depth), depth)
            rows_ref[slot * rows : (slot + 1) * rows, lanes] = packed_ref[
                part * rows : (part + 1) * rows, :
            ]
            lanes = pl.ds(pl.multiple_of(shard * lane, lane), lane)
            audio_ref[slot * audio_rows : (slot + 1) * audio_rows, lanes] = packed_ref[
                2 * rows :, part * lane : (part + 1) * lane
            ]
    kv_half, fold = depth // 2, lane // 4
    width = query_ref.shape[1]

    def place(piece_ref, shard, group, kv_at, query_at):
        to = pl.ds(pl.multiple_of((2 * shard + group) * kv_half, kv_half), kv_half)
        kv_ref[to, :] = piece_ref[kv_at : kv_at + kv_half, :]
        for side in range(2):
            to = pl.ds(pl.multiple_of((4 * shard + 2 * group + side) * fold, fold), fold)
            query_ref[to, :] = piece_ref[
                query_at : query_at + fold, side * width : (side + 1) * width
            ]

    for group in range(2):
        place(weight_refs[0], seq_at, group, group * kv_half, 2 * kv_half + group * fold)
    for bit in range(1, 4):
        place(weight_refs[2 * bit - 1], seq_at ^ bit, grp_at, 0, kv_half)
        place(weight_refs[2 * bit], seq_at ^ bit, 1 - grp_at, 0, kv_half)

    count = 4 * rows
    columns = keep_ref.shape[1]
    total = jnp.dot(rows_ref[...], kv_ref[...], preferred_element_type=jnp.float32)
    keep_ref[:count, :] = total[:, :columns]
    send_ref[:count, :] = total[:, columns:]
    total = jnp.dot(audio_ref[...], query_ref[...], preferred_element_type=jnp.float32)
    folded = 2 * audio_rows
    for side in range(2):
        at = slice(side * folded, (side + 1) * folded)
        to = slice(side * HEAD_DIM, (side + 1) * HEAD_DIM)
        keep_ref[count:, to] = total[at, :HEAD_DIM]
        send_ref[count:, to] = total[at, HEAD_DIM:]


def attend(queries, kv_ref, frames_ref, align):
    scores = lax.dot_general(
        queries,
        kv_ref[:, :HEAD_DIM],
        (((1,), (1,)), ((), ())),
        preferred_element_type=jnp.float32,
    ) * (1.0 / HEAD_DIM**0.5)
    scores = scores - SLOPE * jnp.abs(frames_ref[...] - align) / FRAMES
    exp_terms = jnp.exp(scores - jnp.max(scores, axis=1, keepdims=True))
    weighted = jnp.dot(
        exp_terms.astype(jnp.bfloat16), kv_ref[:, HEAD_DIM:], preferred_element_type=jnp.float32
    )
    return (weighted / jnp.sum(exp_terms, axis=1, keepdims=True)).astype(jnp.bfloat16)


def attention_body(frames_ref, align_ref, keep_ref, came_ref, *refs):
    *out_refs, kv_ref, query_ref = refs
    count, audio_rows = kv_ref.shape[0], query_ref.shape[1]

    def summed(rows, columns=slice(None)):
        return (keep_ref[rows, columns] + came_ref[rows, columns]).astype(jnp.bfloat16)

    kv_ref[...] = summed(slice(0, count))
    for slot in range(4):
        side, half = divmod(slot, 2)
        query_ref[slot] = summed(
            slice(count + half * audio_rows, count + (half + 1) * audio_rows),
            slice(side * HEAD_DIM, (side + 1) * HEAD_DIM),
        )
    for bit, out_ref in enumerate(out_refs):
        align = align_ref[lax.axis_index("seq") ^ bit]
        out_ref[...] = attend(query_ref[bit], kv_ref, frames_ref, align)


def out_body(*refs):
    piece_refs, (own_w, *part_refs), (send_ref, keep_ref, heads_ref, weight_ref, sem) = (
        refs[:4],
        refs[4:11],
        refs[11:],
    )
    seq_at, grp_at = lax.axis_index("seq"), lax.axis_index("grp")
    place = lax.axis_index("mem") * 2 + lax.axis_index("rep")
    copy = pltpu.make_async_copy(own_w, weight_ref.at[0], sem)
    copy.start()
    for bit, piece_ref in enumerate(piece_refs):
        heads_ref[seq_at ^ bit] = piece_ref[...]
    heads = jnp.concatenate([heads_ref[head] for head in range(heads_ref.shape[0])], axis=1)
    depth = part_refs[0].shape[0]
    mine = pl.ds(pl.multiple_of(grp_at * depth, depth), depth)
    rest = pl.ds(pl.multiple_of((1 - grp_at) * depth, depth), depth)
    for bit in range(1, 4):
        weight_ref[bit, mine] = part_refs[2 * bit - 2][...]
        weight_ref[bit, rest] = part_refs[2 * bit - 1][...]
    for bit in (1, 2, 3, 0):
        if bit == 0:
            copy.wait()
        slot = seq_at ^ bit ^ place
        value = jnp.dot(heads, weight_ref[bit], preferred_element_type=jnp.float32)

        @pl.when(slot % 2 == 1)
        def _():
            send_ref[slot // 2] = value.astype(send_ref.dtype)

        @pl.when(slot % 2 == 0)
        def _():
            keep_ref[slot // 2] = value


def by_head(video_cache, plan, alignment, audio_tokens, kv_weight, query_weight, out_weight):
    seq_size = lax.axis_size("seq")
    seq_at = lax.axis_index("seq")
    place = lax.axis_index("mem") * 2 + lax.axis_index("rep")
    video_rows = video_cache.shape[1]
    audio_rows = audio_tokens.shape[0]
    half_depth, width = kv_weight.shape[0] // 2, 2 * HEAD_DIM
    query_quarter = query_weight.shape[0] // 4

    def bfloat(*shape):
        return jax.ShapeDtypeStruct(shape, jnp.bfloat16)

    packed, other, out_half = kernel_call(
        first_body,
        [
            bfloat(2 * video_rows + audio_rows, half_depth),
            bfloat(half_depth + query_quarter, kv_weight.shape[1]),
            bfloat(out_weight.shape[0] // 2, out_weight.shape[1]),
        ],
        [plan, video_cache, audio_tokens, kv_weight, query_weight, out_weight],
        scratch=[
            pltpu.VMEM((3, video_rows, 2 * half_depth), jnp.bfloat16),
            pltpu.VMEM((2 * video_rows, half_depth), jnp.bfloat16),
            pltpu.SemaphoreType.DMA((22,)),
        ],
        smem=(0,),
        loose_in=(1, 2, 3, 4, 5),
        loose_out=(0, 1, 2),
        limit=61,
    )

    tokens = [packed, swap(packed, "seq", 1), swap(packed, "seq", 2)]
    across = [swap(packed, "mem", 1)]
    other = swap(other, "rep", 1)
    rows = half_depth // 2 + query_quarter // 2
    weight_own, *pieces = kernel_call(
        weight_body,
        [bfloat(2 * rows, 2 * width)] + [bfloat(rows, 2 * width)] * 3,
        [kv_weight, query_weight, other],
    )
    pieces[0] = swap(pieces[0], "seq", 1)
    align_all = lax.all_to_all(
        jnp.broadcast_to(alignment[None], (seq_size, audio_rows)), "seq", 0, 0, tiled=True
    ).astype(jnp.float32)
    tokens[1], tokens[2], across[0], pieces[0], align_all = lax.optimization_barrier(
        (tokens[1], tokens[2], across[0], pieces[0], align_all)
    )

    tokens.append(swap(tokens[2], "seq", 1))
    across += [swap(tokens[1], "mem", 1), swap(tokens[2], "mem", 1)]
    pieces[1:] = [swap(piece, "seq", bit) for bit, piece in enumerate(pieces[1:], 2)]
    rest = [swap(pieces[0], "grp", 1)]
    tokens[3], across[1], across[2], pieces[1], pieces[2], rest[0], out_half = (
        lax.optimization_barrier(
            (tokens[3], across[1], across[2], pieces[1], pieces[2], rest[0], out_half)
        )
    )

    across.append(swap(tokens[3], "mem", 1))
    rest += [swap(piece, "grp", 1) for piece in pieces[1:]]
    out_parts = [swap(out_half, "seq", 1), swap(out_half, "seq", 2)]
    weights = [weight_own]
    for piece, other in zip(pieces, rest):
        weights += [piece, other]
    rows = seq_size * (video_rows + audio_rows // 2)
    sums = jax.ShapeDtypeStruct((rows, width), jnp.float32)
    send, keep = kernel_call(
        products_body,
        [sums, sums],
        [value for pair in zip(tokens, across) for value in pair] + weights,
        after=out_parts,
        scratch=[
            pltpu.VMEM((seq_size * video_rows, 4 * half_depth), jnp.bfloat16),
            pltpu.VMEM((seq_size * audio_rows, 8 * query_quarter), jnp.bfloat16),
            pltpu.VMEM((4 * half_depth, 2 * width), jnp.bfloat16),
            pltpu.VMEM((8 * query_quarter, width), jnp.bfloat16),
        ],
        limit=26,
    )
    came = swap(send, "rep", 1)
    out_parts.append(swap(out_parts[1], "seq", 1))

    span = video_rows * seq_size
    blocks = jnp.stack([seq_at, seq_at ^ 1, seq_at ^ 2, seq_at ^ 3])
    positions = blocks[:, None] * video_rows + jnp.arange(video_rows, dtype=jnp.int32)[None, :]
    frames_video = (positions.reshape(1, span) * FRAMES // span).astype(jnp.float32)
    own_piece, near_piece, far_piece, farther_piece = kernel_call(
        attention_body,
        [bfloat(audio_rows, HEAD_DIM)] * 4,
        [frames_video, align_all[:, :, None], keep, came],
        scratch=[
            pltpu.VMEM((span, width), jnp.bfloat16),
            pltpu.VMEM((seq_size, audio_rows, HEAD_DIM), jnp.bfloat16),
        ],
    )
    far_piece = swap(far_piece, "seq", 2)
    farther_piece = swap(farther_piece, "seq", 3)
    near_piece = swap(near_piece, "seq", 1)

    columns = out_weight.shape[1]
    weights = [out_weight]
    for part in out_parts:
        weights += [part, swap(part, "grp", 1)]
    send, keep = kernel_call(
        out_body,
        [
            jax.ShapeDtypeStruct((2, audio_rows, columns), jnp.bfloat16),
            jax.ShapeDtypeStruct((2, audio_rows, columns), jnp.float32),
        ],
        [own_piece, near_piece, far_piece, farther_piece, *weights],
        scratch=[
            pltpu.VMEM((seq_size, audio_rows, HEAD_DIM), jnp.bfloat16),
            pltpu.VMEM((seq_size, *out_weight.shape), jnp.bfloat16),
            pltpu.SemaphoreType.DMA,
        ],
        loose_in=(4,),
    )
    came = swap(send, "rep", 1)
    across = swap((keep[1] + came[1].astype(jnp.float32)).astype(jnp.bfloat16), "mem", 1)
    residual = lax.dynamic_slice_in_dim(audio_tokens, place * columns, columns, 1)
    own_part = taylor(video_cache, plan, 2 * half_depth)
    base = residual.astype(jnp.float32) + (keep[0] + came[0].astype(jnp.float32))
    base, across = lax.optimization_barrier((base, across))
    audio_output = (base + across.astype(jnp.float32)).astype(jnp.bfloat16)
    return (own_part, audio_output)


def solution(mesh):
    sizes = dict(mesh.shape)
    square = (sizes["grp"], sizes["seq"], sizes["mem"], sizes["rep"]) == (2, 4, 2, 2)

    def on_device(*arrays):
        heads = arrays[5].shape[1] // HEAD_DIM
        return (by_head if square and heads == sizes["seq"] else general)(*arrays)

    return jax.shard_map(
        on_device,
        mesh=mesh,
        in_specs=(
            P(None, ("grp", "seq"), "mem"),
            P("grp"),
            P(("grp", "seq")),
            P(("grp", "seq"), None),
            P("seq", ("mem", "rep")),
            P("seq", ("mem", "rep")),
            P(("mem", "rep"), "seq"),
        ),
        out_specs=(P(("grp", "seq"), "mem"), P(("grp", "seq"), ("mem", "rep"))),
        check_vma=False,
    )
```

```python
import math

import jax
import jax.numpy as jnp
from jax import lax
from jax.experimental import pallas as pl
from jax.experimental.pallas import tpu as pltpu
from jax.sharding import PartitionSpec as P

HEAD_DIM = 128
FRAMES = 24


SLOPE = 4.0


def taylor_ratio(plan):
    history = plan.shape[0]
    step_ids = jnp.arange(history, dtype=jnp.int32)
    marked = step_ids * plan
    last_fresh = jnp.max(marked)
    prior_fresh = jnp.max(jnp.where(step_ids < last_fresh, marked, 0))
    return (history - last_fresh).astype(jnp.float32) / (last_fresh - prior_fresh).astype(
        jnp.float32
    )


def combine(orders, step_ratio):
    values = orders.astype(jnp.float32)
    return (values[0] + step_ratio * values[1] + 0.5 * step_ratio * step_ratio * values[2]).astype(
        jnp.bfloat16
    )


def general(video_cache, plan, alignment, audio_tokens, kv_weight, query_weight, out_weight):
    step_ratio = taylor_ratio(plan)
    own_part = combine(video_cache, step_ratio)
    features_all = lax.all_gather(own_part, "mem", axis=1, tiled=True)
    video_rows = features_all.shape[0]
    kv_local = jnp.dot(
        features_all,
        lax.all_gather(kv_weight, "seq", axis=0, tiled=True),
        preferred_element_type=jnp.float32,
    )
    head_size = HEAD_DIM
    local_heads = query_weight.shape[1] // head_size
    kv_local = kv_local.astype(jnp.bfloat16).reshape(video_rows, local_heads, 2, head_size)
    key_rows = kv_local[:, :, 0, :]
    value_rows = kv_local[:, :, 1, :]
    query_full, out_full = (
        lax.all_gather(query_weight, "seq", axis=0, tiled=True),
        lax.all_gather(out_weight, "seq", axis=1, tiled=True),
    )
    audio_rows = audio_tokens.shape[0]
    queries = jnp.dot(audio_tokens, query_full, preferred_element_type=jnp.float32).astype(
        jnp.bfloat16
    )
    queries = queries.reshape(audio_rows, local_heads, head_size)
    scale = 1.0 / head_size**0.5
    span = video_rows * lax.axis_size("seq")
    initial = (
        jnp.full((local_heads, audio_rows), -1e30, jnp.float32),
        jnp.zeros((local_heads, audio_rows), jnp.float32),
        jnp.zeros((local_heads, audio_rows, head_size), jnp.float32),
    )
    key_piece = lax.all_gather(key_rows, "seq", axis=0, tiled=True)
    value_piece = lax.all_gather(value_rows, "seq", axis=0, tiled=True)
    row_count = key_piece.shape[0]
    block_len = math.gcd(row_count, 1024)

    def advance(block_index, carried):
        row_max, row_sum, weighted = carried
        key_block = lax.dynamic_slice_in_dim(key_piece, block_index * block_len, block_len, 0)
        value_block = lax.dynamic_slice_in_dim(value_piece, block_index * block_len, block_len, 0)
        positions = block_index * block_len + jnp.arange(block_len, dtype=jnp.int32)
        frames_video = positions * FRAMES // span
        distance_bias = (
            -SLOPE
            * jnp.abs(frames_video[None, :] - alignment[:, None]).astype(jnp.float32)
            / FRAMES
        )
        scores = (
            jnp.einsum("qhd,khd->hqk", queries, key_block, preferred_element_type=jnp.float32)
            * scale
        )
        scores = scores + distance_bias[None]
        new_max = jnp.maximum(row_max, jnp.max(scores, axis=2))
        rescale = jnp.exp(row_max - new_max)
        exp_terms = jnp.exp(scores - new_max[:, :, None])
        row_sum = row_sum * rescale + jnp.sum(exp_terms, axis=2)
        weighted = weighted * rescale[:, :, None] + jnp.einsum(
            "hqk,khd->hqd",
            exp_terms.astype(jnp.bfloat16),
            value_block,
            preferred_element_type=jnp.float32,
        )
        return (new_max, row_sum, weighted)

    row_max, row_sum, weighted = lax.fori_loop(0, row_count // block_len, advance, initial)
    attended = (weighted / row_sum[:, :, None]).astype(jnp.bfloat16)
    attended = jnp.transpose(attended, (1, 0, 2)).reshape(audio_rows, local_heads * head_size)
    partial_update = jnp.dot(attended, out_full, preferred_element_type=jnp.float32)
    update = lax.psum_scatter(
        partial_update.astype(jnp.bfloat16), ("mem", "rep"), scatter_dimension=1, tiled=True
    ).astype(jnp.float32)
    own_columns = update.shape[1]
    residual = lax.dynamic_slice_in_dim(
        audio_tokens, lax.axis_index(("mem", "rep")) * own_columns, own_columns, 1
    )
    audio_output = (residual.astype(jnp.float32) + update).astype(jnp.bfloat16)
    return (own_part, audio_output)


def swap(value, axis, bit):
    size = lax.axis_size(axis)
    return lax.ppermute(value, axis, [(i, i ^ bit) for i in range(size)])


VMEM = pl.BlockSpec(memory_space=pltpu.VMEM)
SMEM = pl.BlockSpec(memory_space=pltpu.SMEM)
ANY = pl.BlockSpec(memory_space=pl.ANY)
HBM = pl.BlockSpec(memory_space=pltpu.HBM)


def kernel_call(body, outs, ins, after=(), scratch=(), smem=(), loose_in=(), loose_out=(), limit=14):
    def whole(*refs):
        body(*refs[: len(ins)], *refs[len(ins) + len(after) :])

    spots = [SMEM if i in smem else HBM if i in loose_in else VMEM for i in range(len(ins))]
    return pl.pallas_call(
        whole,
        out_shape=outs,
        in_specs=spots + [ANY] * len(after),
        out_specs=[HBM if i in loose_out else VMEM for i in range(len(outs))],
        scratch_shapes=scratch,
        compiler_params=pltpu.CompilerParams(vmem_limit_bytes=limit * 2**20),
    )(*ins, *after)


def plan_ratio(plan_ref, columns):
    history = plan_ref.shape[0]
    last_fresh, prior_fresh = jnp.int32(0), jnp.int32(0)
    for step in range(history):
        fresh = plan_ref[step] == 1
        prior_fresh = jnp.where(fresh, last_fresh, prior_fresh)
        last_fresh = jnp.where(fresh, step, last_fresh)
    ahead = jnp.full((1, columns), history - last_fresh, jnp.int32).astype(jnp.float32)
    apart = jnp.full((1, columns), last_fresh - prior_fresh, jnp.int32).astype(jnp.float32)
    return ahead / apart


def taylor_rows(cache_ref, out_ref, step_ratio, first, last):
    half_square = 0.5 * step_ratio * step_ratio
    for at in range(first, last, 16):
        terms = [cache_ref[order, at : at + 16, :].astype(jnp.float32) for order in range(3)]
        out_ref[at : at + 16, :] = (
            terms[0] + step_ratio * terms[1] + half_square * terms[2]
        ).astype(jnp.bfloat16)


def taylor_body(plan_ref, cache_ref, out_ref):
    rows, columns = out_ref.shape
    taylor_rows(cache_ref, out_ref, plan_ratio(plan_ref, columns), 0, rows)


def taylor(video_cache, plan, width):
    orders, rows, columns = video_cache.shape
    return pl.pallas_call(
        taylor_body,
        out_shape=jax.ShapeDtypeStruct((rows, columns), jnp.bfloat16),
        grid=(columns // width,),
        in_specs=[SMEM, pl.BlockSpec((orders, rows, width), lambda i: (0, 0, i))],
        out_specs=pl.BlockSpec((rows, width), lambda i: (0, i)),
        compiler_params=pltpu.CompilerParams(vmem_limit_bytes=8 * 2**20),
    )(plan, video_cache)


def first_body(
    plan_ref,
    cache_ref,
    audio_ref,
    kv_ref,
    query_ref,
    out_w,
    packed_ref,
    other_ref,
    half_ref,
    held_ref,
    made_ref,
    other_vmem,
    half_vmem,
    sems,
):
    rep_at, mem_at, grp_at = (lax.axis_index(name) for name in ("rep", "mem", "grp"))
    rows, width = held_ref.shape[1:]
    width = width // 2
    copies = []

    def copy(source, target):
        copies.append(pltpu.make_async_copy(source, target, sems.at[len(copies)]))

    def part(index, size):
        return pl.ds(pl.multiple_of(index * size, size), size)

    blocks = 4
    step = rows // blocks
    for block in range(blocks):
        at = pl.ds(block * step, step)
        for shard in range(2):
            copy(
                cache_ref.at[:, at, part(2 * shard + rep_at, width)],
                held_ref.at[:, at, pl.ds(shard * width, width)],
            )
    lane = width // 2
    for shard in range(2):
        copy(
            audio_ref.at[:, part(2 * (2 * mem_at + shard) + rep_at, lane)],
            made_ref.at[pl.ds(2 * rows, audio_ref.shape[0]), pl.ds(shard * lane, lane)],
        )
    depth, columns = kv_ref.shape[0] // 2, query_ref.shape[1]
    copy(kv_ref.at[part(1 - rep_at, depth)], other_vmem.at[pl.ds(0, depth)])
    quarter = query_ref.shape[0] // 4
    for side in range(2):
        copy(
            query_ref.at[part(2 * (1 - rep_at) + side, quarter)],
            other_vmem.at[pl.ds(depth, quarter), pl.ds(side * columns, columns)],
        )
    copy(out_w.at[part(grp_at, half_ref.shape[0])], half_vmem)
    for started in copies:
        started.start()
    step_ratio = plan_ratio(plan_ref, width)
    for block in range(blocks):
        for shard in range(2):
            copies[2 * block + shard].wait()
            taylor_rows(
                held_ref.at[:, :, pl.ds(shard * width, width)],
                made_ref.at[pl.ds(shard * rows, rows)],
                step_ratio,
                block * step,
                (block + 1) * step,
            )
            at = pl.ds(shard * rows + block * step, step)
            copy(made_ref.at[at], packed_ref.at[at])
            copies[-1].start()
    audio_at = pl.ds(2 * rows, audio_ref.shape[0])
    stages = (
        (2, made_ref.at[audio_at], packed_ref.at[audio_at]),
        (3, other_vmem, other_ref),
        (1, half_vmem, half_ref),
    )
    at = 2 * blocks
    for count, source, target in stages:
        for arriving in copies[at : at + count]:
            arriving.wait()
        at += count
        copy(source, target)
        copies[-1].start()
    for leaving in copies[at:]:
        leaving.wait()


def weight_body(kv_ref, query_ref, other_ref, own_ref, *piece_refs):
    seq_at, rep_at, grp_at = (lax.axis_index(name) for name in ("seq", "rep", "grp"))
    kv_half, query_half = kv_ref.shape[0] // 2, query_ref.shape[0] // 2
    kv_rows, query_rows = kv_half // 2, query_half // 2
    fold = query_rows // 2

    def fill(out_ref, bit, group, kv_at, query_at):
        head = seq_at ^ bit
        width = 2 * HEAD_DIM
        lanes = pl.ds(pl.multiple_of(head * width, width), width)
        at = pl.ds(pl.multiple_of(rep_at * kv_half + group * kv_rows, kv_rows), kv_rows)
        out_ref[kv_at : kv_at + kv_rows, :width] = kv_ref[at, lanes]
        at = pl.ds(pl.multiple_of(group * kv_rows, kv_rows), kv_rows)
        out_ref[kv_at : kv_at + kv_rows, width:] = other_ref[at, lanes]
        lanes = pl.ds(pl.multiple_of(head * HEAD_DIM, HEAD_DIM), HEAD_DIM)
        other_lanes = pl.ds(
            pl.multiple_of(group * query_ref.shape[1] + head * HEAD_DIM, HEAD_DIM), HEAD_DIM
        )
        for side in range(2):
            first = rep_at * query_half + group * query_rows + side * fold
            at = pl.ds(pl.multiple_of(first, fold), fold)
            to = slice(query_at, query_at + fold)
            out_ref[to, side * width : side * width + HEAD_DIM] = query_ref[at, lanes]
            out_ref[to, side * width + HEAD_DIM : (side + 1) * width] = other_ref[
                kv_half + side * fold : kv_half + (side + 1) * fold, other_lanes
            ]

    for group in range(2):
        fill(own_ref, 0, group, group * kv_rows, kv_half + group * fold)
    for bit, piece_ref in enumerate(piece_refs, 1):
        fill(piece_ref, bit, grp_at, 0, kv_rows)


def products_body(*refs):
    packed_refs, weight_refs = refs[:8], refs[8:15]
    send_ref, keep_ref, rows_ref, audio_ref, kv_ref, query_ref = refs[15:]
    seq_at, mem_at, grp_at = (lax.axis_index(name) for name in ("seq", "mem", "grp"))
    rows, audio_rows = rows_ref.shape[0] // 4, audio_ref.shape[0] // 4
    depth, lane = rows_ref.shape[1] // 4, audio_ref.shape[1] // 4
    for at, packed_ref in enumerate(packed_refs):
        slot, mem = divmod(at, 2)
        for part in range(2):
            shard = 2 * (mem_at ^ mem) + part
            lanes = pl.ds(pl.multiple_of(shard * depth, depth), depth)
            rows_ref[slot * rows : (slot + 1) * rows, lanes] = packed_ref[
                part * rows : (part + 1) * rows, :
            ]
            lanes = pl.ds(pl.multiple_of(shard * lane, lane), lane)
            audio_ref[slot * audio_rows : (slot + 1) * audio_rows, lanes] = packed_ref[
                2 * rows :, part * lane : (part + 1) * lane
            ]
    kv_half, fold = depth // 2, lane // 4
    width = query_ref.shape[1]

    def place(piece_ref, shard, group, kv_at, query_at):
        to = pl.ds(pl.multiple_of((2 * shard + group) * kv_half, kv_half), kv_half)
        kv_ref[to, :] = piece_ref[kv_at : kv_at + kv_half, :]
        for side in range(2):
            to = pl.ds(pl.multiple_of((4 * shard + 2 * group + side) * fold, fold), fold)
            query_ref[to, :] = piece_ref[
                query_at : query_at + fold, side * width : (side + 1) * width
            ]

    for group in range(2):
        place(weight_refs[0], seq_at, group, group * kv_half, 2 * kv_half + group * fold)
    for bit in range(1, 4):
        place(weight_refs[2 * bit - 1], seq_at ^ bit, grp_at, 0, kv_half)
        place(weight_refs[2 * bit], seq_at ^ bit, 1 - grp_at, 0, kv_half)

    count = 4 * rows
    columns = keep_ref.shape[1]
    total = jnp.dot(rows_ref[...], kv_ref[...], preferred_element_type=jnp.float32)
    keep_ref[:count, :] = total[:, :columns]
    send_ref[:count, :] = total[:, columns:]
    total = jnp.dot(audio_ref[...], query_ref[...], preferred_element_type=jnp.float32)
    folded = 2 * audio_rows
    for side in range(2):
        at = slice(side * folded, (side + 1) * folded)
        to = slice(side * HEAD_DIM, (side + 1) * HEAD_DIM)
        keep_ref[count:, to] = total[at, :HEAD_DIM]
        send_ref[count:, to] = total[at, HEAD_DIM:]


def attend(queries, kv_ref, frames_ref, align):
    scores = lax.dot_general(
        queries,
        kv_ref[:, :HEAD_DIM],
        (((1,), (1,)), ((), ())),
        preferred_element_type=jnp.float32,
    ) * (1.0 / HEAD_DIM**0.5)
    scores = scores - SLOPE * jnp.abs(frames_ref[...] - align) / FRAMES
    exp_terms = jnp.exp(scores - jnp.max(scores, axis=1, keepdims=True))
    weighted = jnp.dot(
        exp_terms.astype(jnp.bfloat16), kv_ref[:, HEAD_DIM:], preferred_element_type=jnp.float32
    )
    return (weighted / jnp.sum(exp_terms, axis=1, keepdims=True)).astype(jnp.bfloat16)


def attention_body(frames_ref, align_ref, keep_ref, came_ref, *refs):
    *out_refs, kv_ref, query_ref = refs
    count, audio_rows = kv_ref.shape[0], query_ref.shape[1]

    def summed(rows, columns=slice(None)):
        return (keep_ref[rows, columns] + came_ref[rows, columns]).astype(jnp.bfloat16)

    kv_ref[...] = summed(slice(0, count))
    for slot in range(4):
        side, half = divmod(slot, 2)
        query_ref[slot] = summed(
            slice(count + half * audio_rows, count + (half + 1) * audio_rows),
            slice(side * HEAD_DIM, (side + 1) * HEAD_DIM),
        )
    for bit, out_ref in enumerate(out_refs):
        align = align_ref[lax.axis_index("seq") ^ bit]
        out_ref[...] = attend(query_ref[bit], kv_ref, frames_ref, align)


def out_body(*refs):
    piece_refs, (own_w, *part_refs), (send_ref, keep_ref, heads_ref, weight_ref, sem) = (
        refs[:4],
        refs[4:11],
        refs[11:],
    )
    seq_at, grp_at = lax.axis_index("seq"), lax.axis_index("grp")
    place = lax.axis_index("mem") * 2 + lax.axis_index("rep")
    copy = pltpu.make_async_copy(own_w, weight_ref.at[0], sem)
    copy.start()
    for bit, piece_ref in enumerate(piece_refs):
        heads_ref[seq_at ^ bit] = piece_ref[...]
    heads = jnp.concatenate([heads_ref[head] for head in range(heads_ref.shape[0])], axis=1)
    depth = part_refs[0].shape[0]
    mine = pl.ds(pl.multiple_of(grp_at * depth, depth), depth)
    rest = pl.ds(pl.multiple_of((1 - grp_at) * depth, depth), depth)
    for bit in range(1, 4):
        weight_ref[bit, mine] = part_refs[2 * bit - 2][...]
        weight_ref[bit, rest] = part_refs[2 * bit - 1][...]
    for bit in (1, 2, 3, 0):
        if bit == 0:
            copy.wait()
        slot = seq_at ^ bit ^ place
        value = jnp.dot(heads, weight_ref[bit], preferred_element_type=jnp.float32)

        @pl.when(slot % 2 == 1)
        def _():
            send_ref[slot // 2] = value.astype(send_ref.dtype)

        @pl.when(slot % 2 == 0)
        def _():
            keep_ref[slot // 2] = value


def by_head(video_cache, plan, alignment, audio_tokens, kv_weight, query_weight, out_weight):
    seq_size = lax.axis_size("seq")
    seq_at = lax.axis_index("seq")
    place = lax.axis_index("mem") * 2 + lax.axis_index("rep")
    video_rows = video_cache.shape[1]
    audio_rows = audio_tokens.shape[0]
    half_depth, width = kv_weight.shape[0] // 2, 2 * HEAD_DIM
    query_quarter = query_weight.shape[0] // 4

    def bfloat(*shape):
        return jax.ShapeDtypeStruct(shape, jnp.bfloat16)

    packed, other, out_half = kernel_call(
        first_body,
        [
            bfloat(2 * video_rows + audio_rows, half_depth),
            bfloat(half_depth + query_quarter, kv_weight.shape[1]),
            bfloat(out_weight.shape[0] // 2, out_weight.shape[1]),
        ],
        [plan, video_cache, audio_tokens, kv_weight, query_weight, out_weight],
        scratch=[
            pltpu.VMEM((3, video_rows, 2 * half_depth), jnp.bfloat16),
            pltpu.VMEM((2 * video_rows + audio_rows, half_depth), jnp.bfloat16),
            pltpu.VMEM((half_depth + query_quarter, kv_weight.shape[1]), jnp.bfloat16),
            pltpu.VMEM((out_weight.shape[0] // 2, out_weight.shape[1]), jnp.bfloat16),
            pltpu.SemaphoreType.DMA((25,)),
        ],
        smem=(0,),
        loose_in=(1, 2, 3, 4, 5),
        loose_out=(0, 1, 2),
        limit=61,
    )

    tokens = [packed, swap(packed, "seq", 1), swap(packed, "seq", 2)]
    across = [swap(packed, "mem", 1)]
    other = swap(other, "rep", 1)
    rows = half_depth // 2 + query_quarter // 2
    weight_own, *pieces = kernel_call(
        weight_body,
        [bfloat(2 * rows, 2 * width)] + [bfloat(rows, 2 * width)] * 3,
        [kv_weight, query_weight, other],
    )
    pieces[0] = swap(pieces[0], "seq", 1)
    align_all = lax.all_to_all(
        jnp.broadcast_to(alignment[None], (seq_size, audio_rows)), "seq", 0, 0, tiled=True
    ).astype(jnp.float32)
    tokens[1], tokens[2], across[0], pieces[0], align_all = lax.optimization_barrier(
        (tokens[1], tokens[2], across[0], pieces[0], align_all)
    )

    tokens.append(swap(tokens[2], "seq", 1))
    across += [swap(tokens[1], "mem", 1), swap(tokens[2], "mem", 1)]
    pieces[1:] = [swap(piece, "seq", bit) for bit, piece in enumerate(pieces[1:], 2)]
    rest = [swap(pieces[0], "grp", 1)]
    tokens[3], across[1], across[2], pieces[1], pieces[2], rest[0], out_half = (
        lax.optimization_barrier(
            (tokens[3], across[1], across[2], pieces[1], pieces[2], rest[0], out_half)
        )
    )

    across.append(swap(tokens[3], "mem", 1))
    rest += [swap(piece, "grp", 1) for piece in pieces[1:]]
    out_parts = [swap(out_half, "seq", 1), swap(out_half, "seq", 2)]
    weights = [weight_own]
    for piece, other in zip(pieces, rest):
        weights += [piece, other]
    rows = seq_size * (video_rows + audio_rows // 2)
    sums = jax.ShapeDtypeStruct((rows, width), jnp.float32)
    send, keep = kernel_call(
        products_body,
        [sums, sums],
        [value for pair in zip(tokens, across) for value in pair] + weights,
        after=out_parts[:1],
        scratch=[
            pltpu.VMEM((seq_size * video_rows, 4 * half_depth), jnp.bfloat16),
            pltpu.VMEM((seq_size * audio_rows, 8 * query_quarter), jnp.bfloat16),
            pltpu.VMEM((4 * half_depth, 2 * width), jnp.bfloat16),
            pltpu.VMEM((8 * query_quarter, width), jnp.bfloat16),
        ],
        limit=26,
    )
    out_parts.append(swap(out_parts[1], "seq", 1))
    send, out_parts[2] = lax.optimization_barrier((send, out_parts[2]))
    came = swap(send, "rep", 1)

    span = video_rows * seq_size
    blocks = jnp.stack([seq_at, seq_at ^ 1, seq_at ^ 2, seq_at ^ 3])
    positions = blocks[:, None] * video_rows + jnp.arange(video_rows, dtype=jnp.int32)[None, :]
    frames_video = (positions.reshape(1, span) * FRAMES // span).astype(jnp.float32)
    own_piece, near_piece, far_piece, farther_piece = kernel_call(
        attention_body,
        [bfloat(audio_rows, HEAD_DIM)] * 4,
        [frames_video, align_all[:, :, None], keep, came],
        scratch=[
            pltpu.VMEM((span, width), jnp.bfloat16),
            pltpu.VMEM((seq_size, audio_rows, HEAD_DIM), jnp.bfloat16),
        ],
    )
    far_piece = swap(far_piece, "seq", 2)
    farther_piece = swap(farther_piece, "seq", 3)
    near_piece = swap(near_piece, "seq", 1)

    columns = out_weight.shape[1]
    weights = [out_weight]
    for part in out_parts:
        weights += [part, swap(part, "grp", 1)]
    send, keep = kernel_call(
        out_body,
        [
            jax.ShapeDtypeStruct((2, audio_rows, columns), jnp.bfloat16),
            jax.ShapeDtypeStruct((2, audio_rows, columns), jnp.float32),
        ],
        [own_piece, near_piece, far_piece, farther_piece, *weights],
        scratch=[
            pltpu.VMEM((seq_size, audio_rows, HEAD_DIM), jnp.bfloat16),
            pltpu.VMEM((seq_size, *out_weight.shape), jnp.bfloat16),
            pltpu.SemaphoreType.DMA,
        ],
        loose_in=(4,),
    )
    came = swap(send, "rep", 1)
    across = swap((keep[1] + came[1].astype(jnp.float32)).astype(jnp.bfloat16), "mem", 1)
    residual = lax.dynamic_slice_in_dim(audio_tokens, place * columns, columns, 1)
    own_part = taylor(video_cache, plan, 2 * half_depth)
    base = residual.astype(jnp.float32) + (keep[0] + came[0].astype(jnp.float32))
    base, across = lax.optimization_barrier((base, across))
    audio_output = (base + across.astype(jnp.float32)).astype(jnp.bfloat16)
    return (own_part, audio_output)


def solution(mesh):
    sizes = dict(mesh.shape)
    square = (sizes["grp"], sizes["seq"], sizes["mem"], sizes["rep"]) == (2, 4, 2, 2)

    def on_device(*arrays):
        heads = arrays[5].shape[1] // HEAD_DIM
        return (by_head if square and heads == sizes["seq"] else general)(*arrays)

    return jax.shard_map(
        on_device,
        mesh=mesh,
        in_specs=(
            P(None, ("grp", "seq"), "mem"),
            P("grp"),
            P(("grp", "seq")),
            P(("grp", "seq"), None),
            P("seq", ("mem", "rep")),
            P("seq", ("mem", "rep")),
            P(("mem", "rep"), "seq"),
        ),
        out_specs=(P(("grp", "seq"), "mem"), P(("grp", "seq"), ("mem", "rep"))),
        check_vma=False,
    )
```

```python
import math

import jax
import jax.numpy as jnp
from jax import lax
from jax.experimental import pallas as pl
from jax.experimental.pallas import tpu as pltpu
from jax.sharding import PartitionSpec as P

HEAD_DIM = 128
FRAMES = 24


SLOPE = 4.0


def taylor_ratio(plan):
    history = plan.shape[0]
    step_ids = jnp.arange(history, dtype=jnp.int32)
    marked = step_ids * plan
    last_fresh = jnp.max(marked)
    prior_fresh = jnp.max(jnp.where(step_ids < last_fresh, marked, 0))
    return (history - last_fresh).astype(jnp.float32) / (last_fresh - prior_fresh).astype(
        jnp.float32
    )


def combine(orders, step_ratio):
    values = orders.astype(jnp.float32)
    return (values[0] + step_ratio * values[1] + 0.5 * step_ratio * step_ratio * values[2]).astype(
        jnp.bfloat16
    )


def general(video_cache, plan, alignment, audio_tokens, kv_weight, query_weight, out_weight):
    step_ratio = taylor_ratio(plan)
    own_part = combine(video_cache, step_ratio)
    features_all = lax.all_gather(own_part, "mem", axis=1, tiled=True)
    video_rows = features_all.shape[0]
    kv_local = jnp.dot(
        features_all,
        lax.all_gather(kv_weight, "seq", axis=0, tiled=True),
        preferred_element_type=jnp.float32,
    )
    head_size = HEAD_DIM
    local_heads = query_weight.shape[1] // head_size
    kv_local = kv_local.astype(jnp.bfloat16).reshape(video_rows, local_heads, 2, head_size)
    key_rows = kv_local[:, :, 0, :]
    value_rows = kv_local[:, :, 1, :]
    query_full, out_full = (
        lax.all_gather(query_weight, "seq", axis=0, tiled=True),
        lax.all_gather(out_weight, "seq", axis=1, tiled=True),
    )
    audio_rows = audio_tokens.shape[0]
    queries = jnp.dot(audio_tokens, query_full, preferred_element_type=jnp.float32).astype(
        jnp.bfloat16
    )
    queries = queries.reshape(audio_rows, local_heads, head_size)
    scale = 1.0 / head_size**0.5
    span = video_rows * lax.axis_size("seq")
    initial = (
        jnp.full((local_heads, audio_rows), -1e30, jnp.float32),
        jnp.zeros((local_heads, audio_rows), jnp.float32),
        jnp.zeros((local_heads, audio_rows, head_size), jnp.float32),
    )
    key_piece = lax.all_gather(key_rows, "seq", axis=0, tiled=True)
    value_piece = lax.all_gather(value_rows, "seq", axis=0, tiled=True)
    row_count = key_piece.shape[0]
    block_len = math.gcd(row_count, 1024)

    def advance(block_index, carried):
        row_max, row_sum, weighted = carried
        key_block = lax.dynamic_slice_in_dim(key_piece, block_index * block_len, block_len, 0)
        value_block = lax.dynamic_slice_in_dim(value_piece, block_index * block_len, block_len, 0)
        positions = block_index * block_len + jnp.arange(block_len, dtype=jnp.int32)
        frames_video = positions * FRAMES // span
        distance_bias = (
            -SLOPE
            * jnp.abs(frames_video[None, :] - alignment[:, None]).astype(jnp.float32)
            / FRAMES
        )
        scores = (
            jnp.einsum("qhd,khd->hqk", queries, key_block, preferred_element_type=jnp.float32)
            * scale
        )
        scores = scores + distance_bias[None]
        new_max = jnp.maximum(row_max, jnp.max(scores, axis=2))
        rescale = jnp.exp(row_max - new_max)
        exp_terms = jnp.exp(scores - new_max[:, :, None])
        row_sum = row_sum * rescale + jnp.sum(exp_terms, axis=2)
        weighted = weighted * rescale[:, :, None] + jnp.einsum(
            "hqk,khd->hqd",
            exp_terms.astype(jnp.bfloat16),
            value_block,
            preferred_element_type=jnp.float32,
        )
        return (new_max, row_sum, weighted)

    row_max, row_sum, weighted = lax.fori_loop(0, row_count // block_len, advance, initial)
    attended = (weighted / row_sum[:, :, None]).astype(jnp.bfloat16)
    attended = jnp.transpose(attended, (1, 0, 2)).reshape(audio_rows, local_heads * head_size)
    partial_update = jnp.dot(attended, out_full, preferred_element_type=jnp.float32)
    update = lax.psum_scatter(
        partial_update.astype(jnp.bfloat16), ("mem", "rep"), scatter_dimension=1, tiled=True
    ).astype(jnp.float32)
    own_columns = update.shape[1]
    residual = lax.dynamic_slice_in_dim(
        audio_tokens, lax.axis_index(("mem", "rep")) * own_columns, own_columns, 1
    )
    audio_output = (residual.astype(jnp.float32) + update).astype(jnp.bfloat16)
    return (own_part, audio_output)


def swap(value, axis, bit):
    size = lax.axis_size(axis)
    return lax.ppermute(value, axis, [(i, i ^ bit) for i in range(size)])


VMEM = pl.BlockSpec(memory_space=pltpu.VMEM)
SMEM = pl.BlockSpec(memory_space=pltpu.SMEM)
ANY = pl.BlockSpec(memory_space=pl.ANY)
HBM = pl.BlockSpec(memory_space=pltpu.HBM)


def kernel_call(body, outs, ins, after=(), scratch=(), smem=(), loose_in=(), loose_out=(), limit=14):
    def whole(*refs):
        body(*refs[: len(ins)], *refs[len(ins) + len(after) :])

    spots = [SMEM if i in smem else HBM if i in loose_in else VMEM for i in range(len(ins))]
    return pl.pallas_call(
        whole,
        out_shape=outs,
        in_specs=spots + [ANY] * len(after),
        out_specs=[HBM if i in loose_out else VMEM for i in range(len(outs))],
        scratch_shapes=scratch,
        compiler_params=pltpu.CompilerParams(vmem_limit_bytes=limit * 2**20),
    )(*ins, *after)


def plan_ratio(plan_ref, columns):
    history = plan_ref.shape[0]
    last_fresh, prior_fresh = jnp.int32(0), jnp.int32(0)
    for step in range(history):
        fresh = plan_ref[step] == 1
        prior_fresh = jnp.where(fresh, last_fresh, prior_fresh)
        last_fresh = jnp.where(fresh, step, last_fresh)
    ahead = jnp.full((1, columns), history - last_fresh, jnp.int32).astype(jnp.float32)
    apart = jnp.full((1, columns), last_fresh - prior_fresh, jnp.int32).astype(jnp.float32)
    return ahead / apart


def taylor_rows(cache_ref, out_ref, step_ratio, first, last):
    half_square = 0.5 * step_ratio * step_ratio
    for at in range(first, last, 16):
        terms = [cache_ref[order, at : at + 16, :].astype(jnp.float32) for order in range(3)]
        out_ref[at : at + 16, :] = (
            terms[0] + step_ratio * terms[1] + half_square * terms[2]
        ).astype(jnp.bfloat16)


def taylor_body(plan_ref, cache_ref, out_ref):
    rows, columns = out_ref.shape
    taylor_rows(cache_ref, out_ref, plan_ratio(plan_ref, columns), 0, rows)


def taylor(video_cache, plan, width):
    orders, rows, columns = video_cache.shape
    return pl.pallas_call(
        taylor_body,
        out_shape=jax.ShapeDtypeStruct((rows, columns), jnp.bfloat16),
        grid=(columns // width,),
        in_specs=[SMEM, pl.BlockSpec((orders, rows, width), lambda i: (0, 0, i))],
        out_specs=pl.BlockSpec((rows, width), lambda i: (0, i)),
        compiler_params=pltpu.CompilerParams(vmem_limit_bytes=8 * 2**20),
    )(plan, video_cache)


def first_body(
    plan_ref,
    cache_ref,
    audio_ref,
    kv_ref,
    query_ref,
    out_w,
    packed_ref,
    other_ref,
    half_ref,
    held_ref,
    made_ref,
    other_vmem,
    half_vmem,
    plan_smem,
    sems,
):
    rep_at, mem_at, grp_at = (lax.axis_index(name) for name in ("rep", "mem", "grp"))
    rows, width = held_ref.shape[1:]
    width = width // 2
    copies = []

    def copy(source, target):
        copies.append(pltpu.make_async_copy(source, target, sems.at[len(copies)]))

    def part(index, size):
        return pl.ds(pl.multiple_of(index * size, size), size)

    plan_copy = pltpu.make_async_copy(plan_ref, plan_smem, sems.at[25])
    plan_copy.start()
    blocks = 4
    step = rows // blocks
    for block in range(blocks):
        at = pl.ds(block * step, step)
        for shard in range(2):
            copy(
                cache_ref.at[:, at, part(2 * shard + rep_at, width)],
                held_ref.at[:, at, pl.ds(shard * width, width)],
            )
    lane = width // 2
    for shard in range(2):
        copy(
            audio_ref.at[:, part(2 * (2 * mem_at + shard) + rep_at, lane)],
            made_ref.at[pl.ds(2 * rows, audio_ref.shape[0]), pl.ds(shard * lane, lane)],
        )
    depth, columns = kv_ref.shape[0] // 2, query_ref.shape[1]
    copy(kv_ref.at[part(1 - rep_at, depth)], other_vmem.at[pl.ds(0, depth)])
    quarter = query_ref.shape[0] // 4
    for side in range(2):
        copy(
            query_ref.at[part(2 * (1 - rep_at) + side, quarter)],
            other_vmem.at[pl.ds(depth, quarter), pl.ds(side * columns, columns)],
        )
    copy(out_w.at[part(grp_at, half_ref.shape[0])], half_vmem)
    for started in copies:
        started.start()
    plan_copy.wait()
    step_ratio = plan_ratio(plan_smem, width)
    for block in range(blocks):
        for shard in range(2):
            copies[2 * block + shard].wait()
            taylor_rows(
                held_ref.at[:, :, pl.ds(shard * width, width)],
                made_ref.at[pl.ds(shard * rows, rows)],
                step_ratio,
                block * step,
                (block + 1) * step,
            )
            at = pl.ds(shard * rows + block * step, step)
            copy(made_ref.at[at], packed_ref.at[at])
            copies[-1].start()
    audio_at = pl.ds(2 * rows, audio_ref.shape[0])
    stages = (
        (2, made_ref.at[audio_at], packed_ref.at[audio_at]),
        (3, other_vmem, other_ref),
        (1, half_vmem, half_ref),
    )
    at = 2 * blocks
    for count, source, target in stages:
        for arriving in copies[at : at + count]:
            arriving.wait()
        at += count
        copy(source, target)
        copies[-1].start()
    for leaving in copies[at:]:
        leaving.wait()


def weight_body(kv_ref, query_ref, other_ref, own_ref, *piece_refs):
    seq_at, rep_at, grp_at = (lax.axis_index(name) for name in ("seq", "rep", "grp"))
    kv_half, query_half = kv_ref.shape[0] // 2, query_ref.shape[0] // 2
    kv_rows, query_rows = kv_half // 2, query_half // 2
    fold = query_rows // 2

    def fill(out_ref, bit, group, kv_at, query_at):
        head = seq_at ^ bit
        width = 2 * HEAD_DIM
        lanes = pl.ds(pl.multiple_of(head * width, width), width)
        at = pl.ds(pl.multiple_of(rep_at * kv_half + group * kv_rows, kv_rows), kv_rows)
        out_ref[kv_at : kv_at + kv_rows, :width] = kv_ref[at, lanes]
        at = pl.ds(pl.multiple_of(group * kv_rows, kv_rows), kv_rows)
        out_ref[kv_at : kv_at + kv_rows, width:] = other_ref[at, lanes]
        lanes = pl.ds(pl.multiple_of(head * HEAD_DIM, HEAD_DIM), HEAD_DIM)
        other_lanes = pl.ds(
            pl.multiple_of(group * query_ref.shape[1] + head * HEAD_DIM, HEAD_DIM), HEAD_DIM
        )
        for side in range(2):
            first = rep_at * query_half + group * query_rows + side * fold
            at = pl.ds(pl.multiple_of(first, fold), fold)
            to = slice(query_at, query_at + fold)
            out_ref[to, side * width : side * width + HEAD_DIM] = query_ref[at, lanes]
            out_ref[to, side * width + HEAD_DIM : (side + 1) * width] = other_ref[
                kv_half + side * fold : kv_half + (side + 1) * fold, other_lanes
            ]

    for group in range(2):
        fill(own_ref, 0, group, group * kv_rows, kv_half + group * fold)
    for bit, piece_ref in enumerate(piece_refs, 1):
        fill(piece_ref, bit, grp_at, 0, kv_rows)


def products_body(*refs):
    packed_refs, weight_refs = refs[:8], refs[8:15]
    send_ref, keep_ref, rows_ref, audio_ref, kv_ref, query_ref = refs[15:]
    seq_at, mem_at, grp_at = (lax.axis_index(name) for name in ("seq", "mem", "grp"))
    rows, audio_rows = rows_ref.shape[0] // 4, audio_ref.shape[0] // 4
    depth, lane = rows_ref.shape[1] // 4, audio_ref.shape[1] // 4
    for at, packed_ref in enumerate(packed_refs):
        slot, mem = divmod(at, 2)
        for part in range(2):
            shard = 2 * (mem_at ^ mem) + part
            lanes = pl.ds(pl.multiple_of(shard * depth, depth), depth)
            rows_ref[slot * rows : (slot + 1) * rows, lanes] = packed_ref[
                part * rows : (part + 1) * rows, :
            ]
            lanes = pl.ds(pl.multiple_of(shard * lane, lane), lane)
            audio_ref[slot * audio_rows : (slot + 1) * audio_rows, lanes] = packed_ref[
                2 * rows :, part * lane : (part + 1) * lane
            ]
    kv_half, fold = depth // 2, lane // 4
    width = query_ref.shape[1]

    def place(piece_ref, shard, group, kv_at, query_at):
        to = pl.ds(pl.multiple_of((2 * shard + group) * kv_half, kv_half), kv_half)
        kv_ref[to, :] = piece_ref[kv_at : kv_at + kv_half, :]
        for side in range(2):
            to = pl.ds(pl.multiple_of((4 * shard + 2 * group + side) * fold, fold), fold)
            query_ref[to, :] = piece_ref[
                query_at : query_at + fold, side * width : (side + 1) * width
            ]

    for group in range(2):
        place(weight_refs[0], seq_at, group, group * kv_half, 2 * kv_half + group * fold)
    for bit in range(1, 4):
        place(weight_refs[2 * bit - 1], seq_at ^ bit, grp_at, 0, kv_half)
        place(weight_refs[2 * bit], seq_at ^ bit, 1 - grp_at, 0, kv_half)

    count = 4 * rows
    columns = keep_ref.shape[1]
    total = jnp.dot(rows_ref[...], kv_ref[...], preferred_element_type=jnp.float32)
    keep_ref[:count, :] = total[:, :columns]
    send_ref[:count, :] = total[:, columns:]
    total = jnp.dot(audio_ref[...], query_ref[...], preferred_element_type=jnp.float32)
    folded = 2 * audio_rows
    for side in range(2):
        at = slice(side * folded, (side + 1) * folded)
        to = slice(side * HEAD_DIM, (side + 1) * HEAD_DIM)
        keep_ref[count:, to] = total[at, :HEAD_DIM]
        send_ref[count:, to] = total[at, HEAD_DIM:]


def attend(queries, kv_ref, frames_ref, align):
    scores = lax.dot_general(
        queries,
        kv_ref[:, :HEAD_DIM],
        (((1,), (1,)), ((), ())),
        preferred_element_type=jnp.float32,
    ) * (1.0 / HEAD_DIM**0.5)
    scores = scores - SLOPE * jnp.abs(frames_ref[...] - align) / FRAMES
    exp_terms = jnp.exp(scores - jnp.max(scores, axis=1, keepdims=True))
    weighted = jnp.dot(
        exp_terms.astype(jnp.bfloat16), kv_ref[:, HEAD_DIM:], preferred_element_type=jnp.float32
    )
    return (weighted / jnp.sum(exp_terms, axis=1, keepdims=True)).astype(jnp.bfloat16)


def attention_body(frames_ref, align_ref, keep_ref, came_ref, *refs):
    *out_refs, kv_ref, query_ref = refs
    count, audio_rows = kv_ref.shape[0], query_ref.shape[1]

    def summed(rows, columns=slice(None)):
        return (keep_ref[rows, columns] + came_ref[rows, columns]).astype(jnp.bfloat16)

    kv_ref[...] = summed(slice(0, count))
    for slot in range(4):
        side, half = divmod(slot, 2)
        query_ref[slot] = summed(
            slice(count + half * audio_rows, count + (half + 1) * audio_rows),
            slice(side * HEAD_DIM, (side + 1) * HEAD_DIM),
        )
    for bit, out_ref in enumerate(out_refs):
        align = align_ref[lax.axis_index("seq") ^ bit]
        out_ref[...] = attend(query_ref[bit], kv_ref, frames_ref, align)


def out_body(*refs):
    piece_refs, (own_w, partner_w, *part_refs), (send_ref, keep_ref, heads_ref, weight_ref, sem) = (
        refs[:4],
        refs[4:10],
        refs[10:],
    )
    seq_at, grp_at = lax.axis_index("seq"), lax.axis_index("grp")
    place = lax.axis_index("mem") * 2 + lax.axis_index("rep")
    copy = pltpu.make_async_copy(own_w, weight_ref.at[0], sem)
    copy.start()
    for bit, piece_ref in enumerate(piece_refs):
        heads_ref[seq_at ^ bit] = piece_ref[...]
    heads = jnp.concatenate([heads_ref[head] for head in range(heads_ref.shape[0])], axis=1)
    depth = part_refs[0].shape[0]
    mine = pl.ds(pl.multiple_of(grp_at * depth, depth), depth)
    rest = pl.ds(pl.multiple_of((1 - grp_at) * depth, depth), depth)
    for bit in range(2):
        weight_ref[1 + bit, mine] = part_refs[2 * bit][...]
        weight_ref[1 + bit, rest] = part_refs[2 * bit + 1][...]
    for bit in (1, 2, 3, 0):
        if bit == 0:
            copy.wait()
        slot = seq_at ^ bit ^ place
        weight = partner_w[...] if bit == 1 else weight_ref[max(bit - 1, 0)]
        value = jnp.dot(heads, weight, preferred_element_type=jnp.float32)

        @pl.when(slot % 2 == 1)
        def _():
            send_ref[slot // 2] = value.astype(send_ref.dtype)

        @pl.when(slot % 2 == 0)
        def _():
            keep_ref[slot // 2] = value


def by_head(video_cache, plan, alignment, audio_tokens, kv_weight, query_weight, out_weight):
    seq_size = lax.axis_size("seq")
    seq_at = lax.axis_index("seq")
    place = lax.axis_index("mem") * 2 + lax.axis_index("rep")
    video_rows = video_cache.shape[1]
    audio_rows = audio_tokens.shape[0]
    half_depth, width = kv_weight.shape[0] // 2, 2 * HEAD_DIM
    query_quarter = query_weight.shape[0] // 4

    def bfloat(*shape):
        return jax.ShapeDtypeStruct(shape, jnp.bfloat16)

    packed, other, out_half = kernel_call(
        first_body,
        [
            bfloat(2 * video_rows + audio_rows, half_depth),
            bfloat(half_depth + query_quarter, kv_weight.shape[1]),
            bfloat(out_weight.shape[0] // 2, out_weight.shape[1]),
        ],
        [plan, video_cache, audio_tokens, kv_weight, query_weight, out_weight],
        scratch=[
            pltpu.VMEM((3, video_rows, 2 * half_depth), jnp.bfloat16),
            pltpu.VMEM((2 * video_rows + audio_rows, half_depth), jnp.bfloat16),
            pltpu.VMEM((half_depth + query_quarter, kv_weight.shape[1]), jnp.bfloat16),
            pltpu.VMEM((out_weight.shape[0] // 2, out_weight.shape[1]), jnp.bfloat16),
            pltpu.SMEM(plan.shape, jnp.int32),
            pltpu.SemaphoreType.DMA((26,)),
        ],
        loose_in=(0, 1, 2, 3, 4, 5),
        loose_out=(0, 1, 2),
        limit=61,
    )

    tokens = [packed, swap(packed, "seq", 1), swap(packed, "seq", 2)]
    across = [swap(packed, "mem", 1)]
    other = swap(other, "rep", 1)
    rows = half_depth // 2 + query_quarter // 2
    weight_own, *pieces = kernel_call(
        weight_body,
        [bfloat(2 * rows, 2 * width)] + [bfloat(rows, 2 * width)] * 3,
        [kv_weight, query_weight, other],
    )
    pieces[0] = swap(pieces[0], "seq", 1)
    align_all = lax.all_to_all(
        jnp.broadcast_to(alignment[None], (seq_size, audio_rows)), "seq", 0, 0, tiled=True
    ).astype(jnp.float32)
    tokens[1], tokens[2], across[0], pieces[0], align_all = lax.optimization_barrier(
        (tokens[1], tokens[2], across[0], pieces[0], align_all)
    )

    tokens.append(swap(tokens[2], "seq", 1))
    across += [swap(tokens[1], "mem", 1), swap(tokens[2], "mem", 1)]
    pieces[1:] = [swap(piece, "seq", bit) for bit, piece in enumerate(pieces[1:], 2)]
    rest = [swap(pieces[0], "grp", 1)]
    tokens[3], across[1], across[2], pieces[1], pieces[2], rest[0], out_half = (
        lax.optimization_barrier(
            (tokens[3], across[1], across[2], pieces[1], pieces[2], rest[0], out_half)
        )
    )

    across.append(swap(tokens[3], "mem", 1))
    rest += [swap(piece, "grp", 1) for piece in pieces[1:]]
    out_partner, out_third = swap(out_weight, "seq", 1), swap(out_half, "seq", 2)
    weights = [weight_own]
    for piece, other in zip(pieces, rest):
        weights += [piece, other]
    rows = seq_size * (video_rows + audio_rows // 2)
    sums = jax.ShapeDtypeStruct((rows, width), jnp.float32)
    send, keep = kernel_call(
        products_body,
        [sums, sums],
        [value for pair in zip(tokens, across) for value in pair] + weights,
        after=(out_partner,),
        scratch=[
            pltpu.VMEM((seq_size * video_rows, 4 * half_depth), jnp.bfloat16),
            pltpu.VMEM((seq_size * audio_rows, 8 * query_quarter), jnp.bfloat16),
            pltpu.VMEM((4 * half_depth, 2 * width), jnp.bfloat16),
            pltpu.VMEM((8 * query_quarter, width), jnp.bfloat16),
        ],
        limit=26,
    )
    out_fourth, third_rest = swap(out_third, "seq", 1), swap(out_third, "grp", 1)
    send, out_fourth, third_rest = lax.optimization_barrier((send, out_fourth, third_rest))
    came = swap(send, "rep", 1)
    fourth_rest = swap(out_fourth, "grp", 1)

    span = video_rows * seq_size
    blocks = jnp.stack([seq_at, seq_at ^ 1, seq_at ^ 2, seq_at ^ 3])
    positions = blocks[:, None] * video_rows + jnp.arange(video_rows, dtype=jnp.int32)[None, :]
    frames_video = (positions.reshape(1, span) * FRAMES // span).astype(jnp.float32)
    own_piece, near_piece, far_piece, farther_piece = kernel_call(
        attention_body,
        [bfloat(audio_rows, HEAD_DIM)] * 4,
        [frames_video, align_all[:, :, None], keep, came],
        scratch=[
            pltpu.VMEM((span, width), jnp.bfloat16),
            pltpu.VMEM((seq_size, audio_rows, HEAD_DIM), jnp.bfloat16),
        ],
    )
    far_piece = swap(far_piece, "seq", 2)
    farther_piece = swap(farther_piece, "seq", 3)
    near_piece = swap(near_piece, "seq", 1)

    columns = out_weight.shape[1]
    weights = [out_weight, out_partner, out_third, third_rest, out_fourth, fourth_rest]
    send, keep = kernel_call(
        out_body,
        [
            jax.ShapeDtypeStruct((2, audio_rows, columns), jnp.bfloat16),
            jax.ShapeDtypeStruct((2, audio_rows, columns), jnp.float32),
        ],
        [own_piece, near_piece, far_piece, farther_piece, *weights],
        scratch=[
            pltpu.VMEM((seq_size, audio_rows, HEAD_DIM), jnp.bfloat16),
            pltpu.VMEM((3, *out_weight.shape), jnp.bfloat16),
            pltpu.SemaphoreType.DMA,
        ],
        loose_in=(4,),
    )
    came = swap(send, "rep", 1)
    across = swap((keep[1] + came[1].astype(jnp.float32)).astype(jnp.bfloat16), "mem", 1)
    residual = lax.dynamic_slice_in_dim(audio_tokens, place * columns, columns, 1)
    own_part = taylor(video_cache, plan, 2 * half_depth)
    base = residual.astype(jnp.float32) + (keep[0] + came[0].astype(jnp.float32))
    base, across = lax.optimization_barrier((base, across))
    audio_output = (base + across.astype(jnp.float32)).astype(jnp.bfloat16)
    return (own_part, audio_output)


def solution(mesh):
    sizes = dict(mesh.shape)
    square = (sizes["grp"], sizes["seq"], sizes["mem"], sizes["rep"]) == (2, 4, 2, 2)

    def on_device(*arrays):
        heads = arrays[5].shape[1] // HEAD_DIM
        return (by_head if square and heads == sizes["seq"] else general)(*arrays)

    return jax.shard_map(
        on_device,
        mesh=mesh,
        in_specs=(
            P(None, ("grp", "seq"), "mem"),
            P("grp"),
            P(("grp", "seq")),
            P(("grp", "seq"), None),
            P("seq", ("mem", "rep")),
            P("seq", ("mem", "rep")),
            P(("mem", "rep"), "seq"),
        ),
        out_specs=(P(("grp", "seq"), "mem"), P(("grp", "seq"), ("mem", "rep"))),
        check_vma=False,
    )
```

```python
import math

import jax
import jax.numpy as jnp
from jax import lax
from jax.experimental import pallas as pl
from jax.experimental.pallas import tpu as pltpu
from jax.sharding import PartitionSpec as P

HEAD_DIM = 128
FRAMES = 24


SLOPE = 4.0


def taylor_ratio(plan):
    history = plan.shape[0]
    step_ids = jnp.arange(history, dtype=jnp.int32)
    marked = step_ids * plan
    last_fresh = jnp.max(marked)
    prior_fresh = jnp.max(jnp.where(step_ids < last_fresh, marked, 0))
    return (history - last_fresh).astype(jnp.float32) / (last_fresh - prior_fresh).astype(
        jnp.float32
    )


def combine(orders, step_ratio):
    values = orders.astype(jnp.float32)
    return (values[0] + step_ratio * values[1] + 0.5 * step_ratio * step_ratio * values[2]).astype(
        jnp.bfloat16
    )


def general(video_cache, plan, alignment, audio_tokens, kv_weight, query_weight, out_weight):
    step_ratio = taylor_ratio(plan)
    own_part = combine(video_cache, step_ratio)
    features_all = lax.all_gather(own_part, "mem", axis=1, tiled=True)
    video_rows = features_all.shape[0]
    kv_local = jnp.dot(
        features_all,
        lax.all_gather(kv_weight, "seq", axis=0, tiled=True),
        preferred_element_type=jnp.float32,
    )
    head_size = HEAD_DIM
    local_heads = query_weight.shape[1] // head_size
    kv_local = kv_local.astype(jnp.bfloat16).reshape(video_rows, local_heads, 2, head_size)
    key_rows = kv_local[:, :, 0, :]
    value_rows = kv_local[:, :, 1, :]
    query_full, out_full = (
        lax.all_gather(query_weight, "seq", axis=0, tiled=True),
        lax.all_gather(out_weight, "seq", axis=1, tiled=True),
    )
    audio_rows = audio_tokens.shape[0]
    queries = jnp.dot(audio_tokens, query_full, preferred_element_type=jnp.float32).astype(
        jnp.bfloat16
    )
    queries = queries.reshape(audio_rows, local_heads, head_size)
    scale = 1.0 / head_size**0.5
    span = video_rows * lax.axis_size("seq")
    initial = (
        jnp.full((local_heads, audio_rows), -1e30, jnp.float32),
        jnp.zeros((local_heads, audio_rows), jnp.float32),
        jnp.zeros((local_heads, audio_rows, head_size), jnp.float32),
    )
    key_piece = lax.all_gather(key_rows, "seq", axis=0, tiled=True)
    value_piece = lax.all_gather(value_rows, "seq", axis=0, tiled=True)
    row_count = key_piece.shape[0]
    block_len = math.gcd(row_count, 1024)

    def advance(block_index, carried):
        row_max, row_sum, weighted = carried
        key_block = lax.dynamic_slice_in_dim(key_piece, block_index * block_len, block_len, 0)
        value_block = lax.dynamic_slice_in_dim(value_piece, block_index * block_len, block_len, 0)
        positions = block_index * block_len + jnp.arange(block_len, dtype=jnp.int32)
        frames_video = positions * FRAMES // span
        distance_bias = (
            -SLOPE
            * jnp.abs(frames_video[None, :] - alignment[:, None]).astype(jnp.float32)
            / FRAMES
        )
        scores = (
            jnp.einsum("qhd,khd->hqk", queries, key_block, preferred_element_type=jnp.float32)
            * scale
        )
        scores = scores + distance_bias[None]
        new_max = jnp.maximum(row_max, jnp.max(scores, axis=2))
        rescale = jnp.exp(row_max - new_max)
        exp_terms = jnp.exp(scores - new_max[:, :, None])
        row_sum = row_sum * rescale + jnp.sum(exp_terms, axis=2)
        weighted = weighted * rescale[:, :, None] + jnp.einsum(
            "hqk,khd->hqd",
            exp_terms.astype(jnp.bfloat16),
            value_block,
            preferred_element_type=jnp.float32,
        )
        return (new_max, row_sum, weighted)

    row_max, row_sum, weighted = lax.fori_loop(0, row_count // block_len, advance, initial)
    attended = (weighted / row_sum[:, :, None]).astype(jnp.bfloat16)
    attended = jnp.transpose(attended, (1, 0, 2)).reshape(audio_rows, local_heads * head_size)
    partial_update = jnp.dot(attended, out_full, preferred_element_type=jnp.float32)
    update = lax.psum_scatter(
        partial_update.astype(jnp.bfloat16), ("mem", "rep"), scatter_dimension=1, tiled=True
    ).astype(jnp.float32)
    own_columns = update.shape[1]
    residual = lax.dynamic_slice_in_dim(
        audio_tokens, lax.axis_index(("mem", "rep")) * own_columns, own_columns, 1
    )
    audio_output = (residual.astype(jnp.float32) + update).astype(jnp.bfloat16)
    return (own_part, audio_output)


def swap(value, axis, bit):
    size = lax.axis_size(axis)
    return lax.ppermute(value, axis, [(i, i ^ bit) for i in range(size)])


VMEM = pl.BlockSpec(memory_space=pltpu.VMEM)
SMEM = pl.BlockSpec(memory_space=pltpu.SMEM)
ANY = pl.BlockSpec(memory_space=pl.ANY)
HBM = pl.BlockSpec(memory_space=pltpu.HBM)


def kernel_call(body, outs, ins, after=(), scratch=(), smem=(), loose_in=(), loose_out=(), limit=14):
    def whole(*refs):
        body(*refs[: len(ins)], *refs[len(ins) + len(after) :])

    spots = [SMEM if i in smem else HBM if i in loose_in else VMEM for i in range(len(ins))]
    return pl.pallas_call(
        whole,
        out_shape=outs,
        in_specs=spots + [ANY] * len(after),
        out_specs=[HBM if i in loose_out else VMEM for i in range(len(outs))],
        scratch_shapes=scratch,
        compiler_params=pltpu.CompilerParams(vmem_limit_bytes=limit * 2**20),
    )(*ins, *after)


def plan_ratio(plan_ref, columns):
    history = plan_ref.shape[0]
    last_fresh, prior_fresh = jnp.int32(0), jnp.int32(0)
    for step in range(history):
        fresh = plan_ref[step] == 1
        prior_fresh = jnp.where(fresh, last_fresh, prior_fresh)
        last_fresh = jnp.where(fresh, step, last_fresh)
    ahead = jnp.full((1, columns), history - last_fresh, jnp.int32).astype(jnp.float32)
    apart = jnp.full((1, columns), last_fresh - prior_fresh, jnp.int32).astype(jnp.float32)
    return ahead / apart


def taylor_rows(cache_ref, out_ref, step_ratio, first, last):
    half_square = 0.5 * step_ratio * step_ratio
    for at in range(first, last, 16):
        terms = [cache_ref[order, at : at + 16, :].astype(jnp.float32) for order in range(3)]
        out_ref[at : at + 16, :] = (
            terms[0] + step_ratio * terms[1] + half_square * terms[2]
        ).astype(jnp.bfloat16)


def taylor_body(plan_ref, cache_ref, out_ref):
    rows, columns = out_ref.shape
    taylor_rows(cache_ref, out_ref, plan_ratio(plan_ref, columns), 0, rows)


def taylor(video_cache, plan, width):
    orders, rows, columns = video_cache.shape
    return pl.pallas_call(
        taylor_body,
        out_shape=jax.ShapeDtypeStruct((rows, columns), jnp.bfloat16),
        grid=(columns // width,),
        in_specs=[SMEM, pl.BlockSpec((orders, rows, width), lambda i: (0, 0, i))],
        out_specs=pl.BlockSpec((rows, width), lambda i: (0, i)),
        compiler_params=pltpu.CompilerParams(vmem_limit_bytes=6 * 2**20),
    )(plan, video_cache)


def first_body(
    plan_ref,
    cache_ref,
    audio_ref,
    kv_ref,
    query_ref,
    out_w,
    packed_ref,
    other_ref,
    half_ref,
    held_ref,
    made_ref,
    other_vmem,
    half_vmem,
    plan_smem,
    sems,
):
    rep_at, mem_at, grp_at = (lax.axis_index(name) for name in ("rep", "mem", "grp"))
    rows, width = held_ref.shape[1:]
    width = width // 2
    copies = []

    def copy(source, target):
        copies.append(pltpu.make_async_copy(source, target, sems.at[len(copies)]))

    def part(index, size):
        return pl.ds(pl.multiple_of(index * size, size), size)

    plan_copy = pltpu.make_async_copy(plan_ref, plan_smem, sems.at[25])
    plan_copy.start()
    blocks = 4
    step = rows // blocks
    for block in range(blocks):
        at = pl.ds(block * step, step)
        for shard in range(2):
            copy(
                cache_ref.at[:, at, part(2 * shard + rep_at, width)],
                held_ref.at[:, at, pl.ds(shard * width, width)],
            )
    lane = width // 2
    for shard in range(2):
        copy(
            audio_ref.at[:, part(2 * (2 * mem_at + shard) + rep_at, lane)],
            made_ref.at[pl.ds(2 * rows, audio_ref.shape[0]), pl.ds(shard * lane, lane)],
        )
    depth, columns = kv_ref.shape[0] // 2, query_ref.shape[1]
    copy(kv_ref.at[part(1 - rep_at, depth)], other_vmem.at[pl.ds(0, depth)])
    quarter = query_ref.shape[0] // 4
    for side in range(2):
        copy(
            query_ref.at[part(2 * (1 - rep_at) + side, quarter)],
            other_vmem.at[pl.ds(depth, quarter), pl.ds(side * columns, columns)],
        )
    copy(out_w.at[part(grp_at, half_ref.shape[0])], half_vmem)
    for started in copies:
        started.start()
    plan_copy.wait()
    step_ratio = plan_ratio(plan_smem, width)
    for block in range(blocks):
        for shard in range(2):
            copies[2 * block + shard].wait()
            taylor_rows(
                held_ref.at[:, :, pl.ds(shard * width, width)],
                made_ref.at[pl.ds(shard * rows, rows)],
                step_ratio,
                block * step,
                (block + 1) * step,
            )
            at = pl.ds(shard * rows + block * step, step)
            copy(made_ref.at[at], packed_ref.at[at])
            copies[-1].start()
    audio_at = pl.ds(2 * rows, audio_ref.shape[0])
    stages = (
        (2, made_ref.at[audio_at], packed_ref.at[audio_at]),
        (3, other_vmem, other_ref),
        (1, half_vmem, half_ref),
    )
    at = 2 * blocks
    for count, source, target in stages:
        for arriving in copies[at : at + count]:
            arriving.wait()
        at += count
        copy(source, target)
        copies[-1].start()
    for leaving in copies[at:]:
        leaving.wait()


def weight_body(kv_ref, query_ref, other_ref, own_ref, *piece_refs):
    seq_at, rep_at, grp_at = (lax.axis_index(name) for name in ("seq", "rep", "grp"))
    kv_half, query_half = kv_ref.shape[0] // 2, query_ref.shape[0] // 2
    kv_rows, query_rows = kv_half // 2, query_half // 2
    fold = query_rows // 2

    def fill(out_ref, bit, group, kv_at, query_at):
        head = seq_at ^ bit
        width = 2 * HEAD_DIM
        lanes = pl.ds(pl.multiple_of(head * width, width), width)
        at = pl.ds(pl.multiple_of(rep_at * kv_half + group * kv_rows, kv_rows), kv_rows)
        out_ref[kv_at : kv_at + kv_rows, :width] = kv_ref[at, lanes]
        at = pl.ds(pl.multiple_of(group * kv_rows, kv_rows), kv_rows)
        out_ref[kv_at : kv_at + kv_rows, width:] = other_ref[at, lanes]
        lanes = pl.ds(pl.multiple_of(head * HEAD_DIM, HEAD_DIM), HEAD_DIM)
        other_lanes = pl.ds(
            pl.multiple_of(group * query_ref.shape[1] + head * HEAD_DIM, HEAD_DIM), HEAD_DIM
        )
        for side in range(2):
            first = rep_at * query_half + group * query_rows + side * fold
            at = pl.ds(pl.multiple_of(first, fold), fold)
            to = slice(query_at, query_at + fold)
            out_ref[to, side * width : side * width + HEAD_DIM] = query_ref[at, lanes]
            out_ref[to, side * width + HEAD_DIM : (side + 1) * width] = other_ref[
                kv_half + side * fold : kv_half + (side + 1) * fold, other_lanes
            ]

    for group in range(2):
        fill(own_ref, 0, group, group * kv_rows, kv_half + group * fold)
    for bit, piece_ref in enumerate(piece_refs, 1):
        fill(piece_ref, bit, grp_at, 0, kv_rows)


def products_body(*refs):
    packed_refs, weight_refs = refs[:8], refs[8:15]
    send_ref, keep_ref, rows_ref, audio_ref, kv_ref, query_ref = refs[15:]
    seq_at, mem_at, grp_at = (lax.axis_index(name) for name in ("seq", "mem", "grp"))
    rows, audio_rows = rows_ref.shape[0] // 4, audio_ref.shape[0] // 4
    depth, lane = rows_ref.shape[1] // 4, audio_ref.shape[1] // 4
    for at, packed_ref in enumerate(packed_refs):
        slot, mem = divmod(at, 2)
        for part in range(2):
            shard = 2 * (mem_at ^ mem) + part
            lanes = pl.ds(pl.multiple_of(shard * depth, depth), depth)
            rows_ref[slot * rows : (slot + 1) * rows, lanes] = packed_ref[
                part * rows : (part + 1) * rows, :
            ]
            lanes = pl.ds(pl.multiple_of(shard * lane, lane), lane)
            audio_ref[slot * audio_rows : (slot + 1) * audio_rows, lanes] = packed_ref[
                2 * rows :, part * lane : (part + 1) * lane
            ]
    kv_half, fold = depth // 2, lane // 4
    width = query_ref.shape[1]

    def place(piece_ref, shard, group, kv_at, query_at):
        to = pl.ds(pl.multiple_of((2 * shard + group) * kv_half, kv_half), kv_half)
        kv_ref[to, :] = piece_ref[kv_at : kv_at + kv_half, :]
        for side in range(2):
            to = pl.ds(pl.multiple_of((4 * shard + 2 * group + side) * fold, fold), fold)
            query_ref[to, :] = piece_ref[
                query_at : query_at + fold, side * width : (side + 1) * width
            ]

    for group in range(2):
        place(weight_refs[0], seq_at, group, group * kv_half, 2 * kv_half + group * fold)
    for bit in range(1, 4):
        place(weight_refs[2 * bit - 1], seq_at ^ bit, grp_at, 0, kv_half)
        place(weight_refs[2 * bit], seq_at ^ bit, 1 - grp_at, 0, kv_half)

    count = 4 * rows
    columns = keep_ref.shape[1]
    total = jnp.dot(rows_ref[...], kv_ref[...], preferred_element_type=jnp.float32)
    keep_ref[:count, :] = total[:, :columns]
    send_ref[:count, :] = total[:, columns:]
    total = jnp.dot(audio_ref[...], query_ref[...], preferred_element_type=jnp.float32)
    folded = 2 * audio_rows
    for side in range(2):
        at = slice(side * folded, (side + 1) * folded)
        to = slice(side * HEAD_DIM, (side + 1) * HEAD_DIM)
        keep_ref[count:, to] = total[at, :HEAD_DIM]
        send_ref[count:, to] = total[at, HEAD_DIM:]


def attend(queries, kv_ref, frames_ref, align):
    scores = lax.dot_general(
        queries,
        kv_ref[:, :HEAD_DIM],
        (((1,), (1,)), ((), ())),
        preferred_element_type=jnp.float32,
    ) * (1.0 / HEAD_DIM**0.5)
    scores = scores - SLOPE * jnp.abs(frames_ref[...] - align) / FRAMES
    exp_terms = jnp.exp(scores - jnp.max(scores, axis=1, keepdims=True))
    weighted = jnp.dot(
        exp_terms.astype(jnp.bfloat16), kv_ref[:, HEAD_DIM:], preferred_element_type=jnp.float32
    )
    return (weighted / jnp.sum(exp_terms, axis=1, keepdims=True)).astype(jnp.bfloat16)


def attention_body(frames_ref, align_ref, keep_ref, came_ref, *refs):
    *out_refs, kv_ref, query_ref = refs
    count, audio_rows = kv_ref.shape[0], query_ref.shape[1]

    def summed(rows, columns=slice(None)):
        return (keep_ref[rows, columns] + came_ref[rows, columns]).astype(jnp.bfloat16)

    kv_ref[...] = summed(slice(0, count))
    for slot in range(4):
        side, half = divmod(slot, 2)
        query_ref[slot] = summed(
            slice(count + half * audio_rows, count + (half + 1) * audio_rows),
            slice(side * HEAD_DIM, (side + 1) * HEAD_DIM),
        )
    for bit, out_ref in enumerate(out_refs):
        out_ref[...] = attend(query_ref[bit], kv_ref, frames_ref, align_ref[bit])


def out_body(*refs):
    piece_refs, (own_w, partner_w, *part_refs), (send_ref, keep_ref, heads_ref, weight_ref, sem) = (
        refs[:4],
        refs[4:10],
        refs[10:],
    )
    seq_at, grp_at = lax.axis_index("seq"), lax.axis_index("grp")
    place = lax.axis_index("mem") * 2 + lax.axis_index("rep")
    copy = pltpu.make_async_copy(own_w, weight_ref.at[0], sem)
    copy.start()
    for bit, piece_ref in enumerate(piece_refs):
        heads_ref[seq_at ^ bit] = piece_ref[...]
    heads = jnp.concatenate([heads_ref[head] for head in range(heads_ref.shape[0])], axis=1)
    depth = part_refs[0].shape[0]
    mine = pl.ds(pl.multiple_of(grp_at * depth, depth), depth)
    rest = pl.ds(pl.multiple_of((1 - grp_at) * depth, depth), depth)
    for bit in range(2):
        weight_ref[1 + bit, mine] = part_refs[2 * bit][...]
        weight_ref[1 + bit, rest] = part_refs[2 * bit + 1][...]
    for bit in (1, 2, 3, 0):
        if bit == 0:
            copy.wait()
        slot = seq_at ^ bit ^ place
        weight = partner_w[...] if bit == 1 else weight_ref[max(bit - 1, 0)]
        value = jnp.dot(heads, weight, preferred_element_type=jnp.float32)

        @pl.when(slot % 2 == 1)
        def _():
            send_ref[slot // 2] = value.astype(send_ref.dtype)

        @pl.when(slot % 2 == 0)
        def _():
            keep_ref[slot // 2] = value


def by_head(video_cache, plan, alignment, audio_tokens, kv_weight, query_weight, out_weight):
    seq_size = lax.axis_size("seq")
    seq_at = lax.axis_index("seq")
    place = lax.axis_index("mem") * 2 + lax.axis_index("rep")
    video_rows = video_cache.shape[1]
    audio_rows = audio_tokens.shape[0]
    half_depth, width = kv_weight.shape[0] // 2, 2 * HEAD_DIM
    query_quarter = query_weight.shape[0] // 4

    def bfloat(*shape):
        return jax.ShapeDtypeStruct(shape, jnp.bfloat16)

    packed, other, out_half = kernel_call(
        first_body,
        [
            bfloat(2 * video_rows + audio_rows, half_depth),
            bfloat(half_depth + query_quarter, kv_weight.shape[1]),
            bfloat(out_weight.shape[0] // 2, out_weight.shape[1]),
        ],
        [plan, video_cache, audio_tokens, kv_weight, query_weight, out_weight],
        scratch=[
            pltpu.VMEM((3, video_rows, 2 * half_depth), jnp.bfloat16),
            pltpu.VMEM((2 * video_rows + audio_rows, half_depth), jnp.bfloat16),
            pltpu.VMEM((half_depth + query_quarter, kv_weight.shape[1]), jnp.bfloat16),
            pltpu.VMEM((out_weight.shape[0] // 2, out_weight.shape[1]), jnp.bfloat16),
            pltpu.SMEM(plan.shape, jnp.int32),
            pltpu.SemaphoreType.DMA((26,)),
        ],
        loose_in=(0, 1, 2, 3, 4, 5),
        loose_out=(0, 1, 2),
        limit=61,
    )

    tokens = [packed, swap(packed, "seq", 1), swap(packed, "seq", 2)]
    across = [swap(packed, "mem", 1)]
    other = swap(other, "rep", 1)
    rows = half_depth // 2 + query_quarter // 2
    weight_own, *pieces = kernel_call(
        weight_body,
        [bfloat(2 * rows, 2 * width)] + [bfloat(rows, 2 * width)] * 3,
        [kv_weight, query_weight, other],
        limit=4,
    )
    pieces[0] = swap(pieces[0], "seq", 1)
    aligns = [alignment, *(swap(alignment, "seq", bit) for bit in (1, 2, 3))]
    tokens[1], tokens[2], across[0], pieces[0], *aligns = lax.optimization_barrier(
        (tokens[1], tokens[2], across[0], pieces[0], *aligns)
    )

    tokens.append(swap(tokens[2], "seq", 1))
    across += [swap(tokens[1], "mem", 1), swap(tokens[2], "mem", 1)]
    pieces[1:] = [swap(piece, "seq", bit) for bit, piece in enumerate(pieces[1:], 2)]
    rest = [swap(pieces[0], "grp", 1)]
    tokens[3], across[1], across[2], pieces[1], pieces[2], rest[0], out_half = (
        lax.optimization_barrier(
            (tokens[3], across[1], across[2], pieces[1], pieces[2], rest[0], out_half)
        )
    )

    across.append(swap(tokens[3], "mem", 1))
    rest += [swap(piece, "grp", 1) for piece in pieces[1:]]
    out_partner, out_third = swap(out_weight, "seq", 1), swap(out_half, "seq", 2)
    weights = [weight_own]
    for piece, other in zip(pieces, rest):
        weights += [piece, other]
    rows = seq_size * (video_rows + audio_rows // 2)
    sums = jax.ShapeDtypeStruct((rows, width), jnp.float32)
    send, keep = kernel_call(
        products_body,
        [sums, sums],
        [value for pair in zip(tokens, across) for value in pair] + weights,
        after=(out_partner,),
        scratch=[
            pltpu.VMEM((seq_size * video_rows, 4 * half_depth), jnp.bfloat16),
            pltpu.VMEM((seq_size * audio_rows, 8 * query_quarter), jnp.bfloat16),
            pltpu.VMEM((4 * half_depth, 2 * width), jnp.bfloat16),
            pltpu.VMEM((8 * query_quarter, width), jnp.bfloat16),
        ],
        limit=15,
    )
    out_fourth, third_rest = swap(out_third, "seq", 1), swap(out_third, "grp", 1)
    came = swap(send, "rep", 1)

    span = video_rows * seq_size
    blocks = jnp.stack([seq_at, seq_at ^ 1, seq_at ^ 2, seq_at ^ 3])
    positions = blocks[:, None] * video_rows + jnp.arange(video_rows, dtype=jnp.int32)[None, :]
    frames_video = (positions.reshape(1, span) * FRAMES // span).astype(jnp.float32)
    own_piece, near_piece, far_piece, farther_piece = kernel_call(
        attention_body,
        [bfloat(audio_rows, HEAD_DIM)] * 4,
        [frames_video, jnp.stack(aligns).astype(jnp.float32)[:, :, None], keep, came],
        scratch=[
            pltpu.VMEM((span, width), jnp.bfloat16),
            pltpu.VMEM((seq_size, audio_rows, HEAD_DIM), jnp.bfloat16),
        ],
        limit=9,
    )
    out_fourth, own_piece = lax.optimization_barrier((out_fourth, own_piece))
    fourth_rest = swap(out_fourth, "grp", 1)
    far_piece = swap(far_piece, "seq", 2)
    farther_piece = swap(farther_piece, "seq", 3)
    near_piece = swap(near_piece, "seq", 1)

    columns = out_weight.shape[1]
    weights = [out_weight, out_partner, out_third, third_rest, out_fourth, fourth_rest]
    send, keep = kernel_call(
        out_body,
        [
            jax.ShapeDtypeStruct((2, audio_rows, columns), jnp.bfloat16),
            jax.ShapeDtypeStruct((2, audio_rows, columns), jnp.float32),
        ],
        [own_piece, near_piece, far_piece, farther_piece, *weights],
        scratch=[
            pltpu.VMEM((seq_size, audio_rows, HEAD_DIM), jnp.bfloat16),
            pltpu.VMEM((3, *out_weight.shape), jnp.bfloat16),
            pltpu.SemaphoreType.DMA,
        ],
        loose_in=(4,),
        limit=7,
    )
    came = swap(send, "rep", 1)
    across = swap((keep[1] + came[1].astype(jnp.float32)).astype(jnp.bfloat16), "mem", 1)
    residual = lax.dynamic_slice_in_dim(audio_tokens, place * columns, columns, 1)
    own_part = taylor(video_cache, plan, 2 * half_depth)
    base = residual.astype(jnp.float32) + (keep[0] + came[0].astype(jnp.float32))
    base, across = lax.optimization_barrier((base, across))
    audio_output = (base + across.astype(jnp.float32)).astype(jnp.bfloat16)
    return (own_part, audio_output)


def solution(mesh):
    sizes = dict(mesh.shape)
    square = (sizes["grp"], sizes["seq"], sizes["mem"], sizes["rep"]) == (2, 4, 2, 2)

    def on_device(*arrays):
        heads = arrays[5].shape[1] // HEAD_DIM
        return (by_head if square and heads == sizes["seq"] else general)(*arrays)

    return jax.shard_map(
        on_device,
        mesh=mesh,
        in_specs=(
            P(None, ("grp", "seq"), "mem"),
            P("grp"),
            P(("grp", "seq")),
            P(("grp", "seq"), None),
            P("seq", ("mem", "rep")),
            P("seq", ("mem", "rep")),
            P(("mem", "rep"), "seq"),
        ),
        out_specs=(P(("grp", "seq"), "mem"), P(("grp", "seq"), ("mem", "rep"))),
        check_vma=False,
    )
```

```python
import math

import jax
import jax.numpy as jnp
from jax import lax
from jax.experimental import pallas as pl
from jax.experimental.pallas import tpu as pltpu
from jax.sharding import PartitionSpec as P

HEAD_DIM = 128
FRAMES = 24


SLOPE = 4.0


def taylor_ratio(plan):
    history = plan.shape[0]
    step_ids = jnp.arange(history, dtype=jnp.int32)
    marked = step_ids * plan
    last_fresh = jnp.max(marked)
    prior_fresh = jnp.max(jnp.where(step_ids < last_fresh, marked, 0))
    return (history - last_fresh).astype(jnp.float32) / (last_fresh - prior_fresh).astype(
        jnp.float32
    )


def combine(orders, step_ratio):
    values = orders.astype(jnp.float32)
    return (values[0] + step_ratio * values[1] + 0.5 * step_ratio * step_ratio * values[2]).astype(
        jnp.bfloat16
    )


def general(video_cache, plan, alignment, audio_tokens, kv_weight, query_weight, out_weight):
    step_ratio = taylor_ratio(plan)
    own_part = combine(video_cache, step_ratio)
    features_all = lax.all_gather(own_part, "mem", axis=1, tiled=True)
    video_rows = features_all.shape[0]
    kv_local = jnp.dot(
        features_all,
        lax.all_gather(kv_weight, "seq", axis=0, tiled=True),
        preferred_element_type=jnp.float32,
    )
    head_size = HEAD_DIM
    local_heads = query_weight.shape[1] // head_size
    kv_local = kv_local.astype(jnp.bfloat16).reshape(video_rows, local_heads, 2, head_size)
    key_rows = kv_local[:, :, 0, :]
    value_rows = kv_local[:, :, 1, :]
    query_full, out_full = (
        lax.all_gather(query_weight, "seq", axis=0, tiled=True),
        lax.all_gather(out_weight, "seq", axis=1, tiled=True),
    )
    audio_rows = audio_tokens.shape[0]
    queries = jnp.dot(audio_tokens, query_full, preferred_element_type=jnp.float32).astype(
        jnp.bfloat16
    )
    queries = queries.reshape(audio_rows, local_heads, head_size)
    scale = 1.0 / head_size**0.5
    span = video_rows * lax.axis_size("seq")
    initial = (
        jnp.full((local_heads, audio_rows), -1e30, jnp.float32),
        jnp.zeros((local_heads, audio_rows), jnp.float32),
        jnp.zeros((local_heads, audio_rows, head_size), jnp.float32),
    )
    key_piece = lax.all_gather(key_rows, "seq", axis=0, tiled=True)
    value_piece = lax.all_gather(value_rows, "seq", axis=0, tiled=True)
    row_count = key_piece.shape[0]
    block_len = math.gcd(row_count, 1024)

    def advance(block_index, carried):
        row_max, row_sum, weighted = carried
        key_block = lax.dynamic_slice_in_dim(key_piece, block_index * block_len, block_len, 0)
        value_block = lax.dynamic_slice_in_dim(value_piece, block_index * block_len, block_len, 0)
        positions = block_index * block_len + jnp.arange(block_len, dtype=jnp.int32)
        frames_video = positions * FRAMES // span
        distance_bias = (
            -SLOPE
            * jnp.abs(frames_video[None, :] - alignment[:, None]).astype(jnp.float32)
            / FRAMES
        )
        scores = (
            jnp.einsum("qhd,khd->hqk", queries, key_block, preferred_element_type=jnp.float32)
            * scale
        )
        scores = scores + distance_bias[None]
        new_max = jnp.maximum(row_max, jnp.max(scores, axis=2))
        rescale = jnp.exp(row_max - new_max)
        exp_terms = jnp.exp(scores - new_max[:, :, None])
        row_sum = row_sum * rescale + jnp.sum(exp_terms, axis=2)
        weighted = weighted * rescale[:, :, None] + jnp.einsum(
            "hqk,khd->hqd",
            exp_terms.astype(jnp.bfloat16),
            value_block,
            preferred_element_type=jnp.float32,
        )
        return (new_max, row_sum, weighted)

    row_max, row_sum, weighted = lax.fori_loop(0, row_count // block_len, advance, initial)
    attended = (weighted / row_sum[:, :, None]).astype(jnp.bfloat16)
    attended = jnp.transpose(attended, (1, 0, 2)).reshape(audio_rows, local_heads * head_size)
    partial_update = jnp.dot(attended, out_full, preferred_element_type=jnp.float32)
    update = lax.psum_scatter(
        partial_update.astype(jnp.bfloat16), ("mem", "rep"), scatter_dimension=1, tiled=True
    ).astype(jnp.float32)
    own_columns = update.shape[1]
    residual = lax.dynamic_slice_in_dim(
        audio_tokens, lax.axis_index(("mem", "rep")) * own_columns, own_columns, 1
    )
    audio_output = (residual.astype(jnp.float32) + update).astype(jnp.bfloat16)
    return (own_part, audio_output)


def swap(value, axis, bit):
    size = lax.axis_size(axis)
    return lax.ppermute(value, axis, [(i, i ^ bit) for i in range(size)])


VMEM = pl.BlockSpec(memory_space=pltpu.VMEM)
SMEM = pl.BlockSpec(memory_space=pltpu.SMEM)
ANY = pl.BlockSpec(memory_space=pl.ANY)
HBM = pl.BlockSpec(memory_space=pltpu.HBM)


def kernel_call(body, outs, ins, after=(), scratch=(), smem=(), loose_in=(), loose_out=(), limit=14):
    def whole(*refs):
        body(*refs[: len(ins)], *refs[len(ins) + len(after) :])

    spots = [SMEM if i in smem else HBM if i in loose_in else VMEM for i in range(len(ins))]
    return pl.pallas_call(
        whole,
        out_shape=outs,
        in_specs=spots + [ANY] * len(after),
        out_specs=[HBM if i in loose_out else VMEM for i in range(len(outs))],
        scratch_shapes=scratch,
        compiler_params=pltpu.CompilerParams(vmem_limit_bytes=limit * 2**20),
    )(*ins, *after)


def plan_ratio(plan_ref, columns):
    history = plan_ref.shape[0]
    last_fresh, prior_fresh = jnp.int32(0), jnp.int32(0)
    for step in range(history):
        fresh = plan_ref[step] == 1
        prior_fresh = jnp.where(fresh, last_fresh, prior_fresh)
        last_fresh = jnp.where(fresh, step, last_fresh)
    ahead = jnp.full((1, columns), history - last_fresh, jnp.int32).astype(jnp.float32)
    apart = jnp.full((1, columns), last_fresh - prior_fresh, jnp.int32).astype(jnp.float32)
    return ahead / apart


def taylor_rows(cache_ref, out_ref, step_ratio, first, last):
    half_square = 0.5 * step_ratio * step_ratio
    for at in range(first, last, 16):
        terms = [cache_ref[order, at : at + 16, :].astype(jnp.float32) for order in range(3)]
        out_ref[at : at + 16, :] = (
            terms[0] + step_ratio * terms[1] + half_square * terms[2]
        ).astype(jnp.bfloat16)


def taylor_body(plan_ref, cache_ref, out_ref):
    rows, columns = out_ref.shape
    taylor_rows(cache_ref, out_ref, plan_ratio(plan_ref, columns), 0, rows)


def taylor(video_cache, plan, width):
    orders, rows, columns = video_cache.shape
    return pl.pallas_call(
        taylor_body,
        out_shape=jax.ShapeDtypeStruct((rows, columns), jnp.bfloat16),
        grid=(columns // width,),
        in_specs=[SMEM, pl.BlockSpec((orders, rows, width), lambda i: (0, 0, i))],
        out_specs=pl.BlockSpec((rows, width), lambda i: (0, i)),
        compiler_params=pltpu.CompilerParams(vmem_limit_bytes=6 * 2**20),
    )(plan, video_cache)


def first_body(
    plan_ref,
    cache_ref,
    audio_ref,
    kv_ref,
    query_ref,
    out_w,
    packed_ref,
    other_ref,
    half_ref,
    held_ref,
    made_ref,
    other_vmem,
    half_vmem,
    plan_smem,
    sems,
):
    rep_at, mem_at, grp_at = (lax.axis_index(name) for name in ("rep", "mem", "grp"))
    rows, width = held_ref.shape[1:]
    width = width // 2
    copies = []

    def copy(source, target):
        copies.append(pltpu.make_async_copy(source, target, sems.at[len(copies)]))

    def part(index, size):
        return pl.ds(pl.multiple_of(index * size, size), size)

    plan_copy = pltpu.make_async_copy(plan_ref, plan_smem, sems.at[25])
    plan_copy.start()
    blocks = 4
    step = rows // blocks
    for block in range(blocks):
        at = pl.ds(block * step, step)
        for shard in range(2):
            copy(
                cache_ref.at[:, at, part(2 * shard + rep_at, width)],
                held_ref.at[:, at, pl.ds(shard * width, width)],
            )
    lane = width // 2
    for shard in range(2):
        copy(
            audio_ref.at[:, part(2 * (2 * mem_at + shard) + rep_at, lane)],
            made_ref.at[pl.ds(2 * rows, audio_ref.shape[0]), pl.ds(shard * lane, lane)],
        )
    depth, columns = kv_ref.shape[0] // 2, query_ref.shape[1]
    copy(kv_ref.at[part(1 - rep_at, depth)], other_vmem.at[pl.ds(0, depth)])
    quarter = query_ref.shape[0] // 4
    for side in range(2):
        copy(
            query_ref.at[part(2 * (1 - rep_at) + side, quarter)],
            other_vmem.at[pl.ds(depth, quarter), pl.ds(side * columns, columns)],
        )
    copy(out_w.at[part(grp_at, half_ref.shape[0])], half_vmem)
    for started in copies:
        started.start()
    plan_copy.wait()
    step_ratio = plan_ratio(plan_smem, width)
    for block in range(blocks):
        for shard in range(2):
            copies[2 * block + shard].wait()
            taylor_rows(
                held_ref.at[:, :, pl.ds(shard * width, width)],
                made_ref.at[pl.ds(shard * rows, rows)],
                step_ratio,
                block * step,
                (block + 1) * step,
            )
            at = pl.ds(shard * rows + block * step, step)
            copy(made_ref.at[at], packed_ref.at[at])
            copies[-1].start()
    audio_at = pl.ds(2 * rows, audio_ref.shape[0])
    stages = (
        (2, made_ref.at[audio_at], packed_ref.at[audio_at]),
        (3, other_vmem, other_ref),
        (1, half_vmem, half_ref),
    )
    at = 2 * blocks
    for count, source, target in stages:
        for arriving in copies[at : at + count]:
            arriving.wait()
        at += count
        copy(source, target)
        copies[-1].start()
    for leaving in copies[at:]:
        leaving.wait()


def weight_body(align_ref, kv_ref, query_ref, other_ref, own_ref, *piece_refs):
    seq_at, rep_at, grp_at = (lax.axis_index(name) for name in ("seq", "rep", "grp"))
    kv_half, query_half = kv_ref.shape[0] // 2, query_ref.shape[0] // 2
    kv_rows, query_rows = kv_half // 2, query_half // 2
    fold = query_rows // 2

    def fill(out_ref, bit, group, kv_at, query_at):
        head = seq_at ^ bit
        width = 2 * HEAD_DIM
        lanes = pl.ds(pl.multiple_of(head * width, width), width)
        at = pl.ds(pl.multiple_of(rep_at * kv_half + group * kv_rows, kv_rows), kv_rows)
        out_ref[kv_at : kv_at + kv_rows, :width] = kv_ref[at, lanes]
        at = pl.ds(pl.multiple_of(group * kv_rows, kv_rows), kv_rows)
        out_ref[kv_at : kv_at + kv_rows, width:] = other_ref[at, lanes]
        lanes = pl.ds(pl.multiple_of(head * HEAD_DIM, HEAD_DIM), HEAD_DIM)
        other_lanes = pl.ds(
            pl.multiple_of(group * query_ref.shape[1] + head * HEAD_DIM, HEAD_DIM), HEAD_DIM
        )
        for side in range(2):
            first = rep_at * query_half + group * query_rows + side * fold
            at = pl.ds(pl.multiple_of(first, fold), fold)
            to = slice(query_at, query_at + fold)
            out_ref[to, side * width : side * width + HEAD_DIM] = query_ref[at, lanes]
            out_ref[to, side * width + HEAD_DIM : (side + 1) * width] = other_ref[
                kv_half + side * fold : kv_half + (side + 1) * fold, other_lanes
            ]

    for group in range(2):
        fill(own_ref, 0, group, group * kv_rows, kv_half + group * fold)
    for bit, piece_ref in enumerate(piece_refs, 1):
        fill(piece_ref, bit, grp_at, 0, kv_rows)
        spare = (piece_ref.shape[0] - kv_rows - fold, piece_ref.shape[1])
        align = align_ref[...].astype(jnp.float32).astype(piece_ref.dtype)
        row = jnp.concatenate(
            [align, jnp.zeros((1, spare[1] - align.shape[1]), piece_ref.dtype)], axis=1
        )
        piece_ref[kv_rows + fold :, :] = jnp.broadcast_to(row, spare)


def products_body(*refs):
    packed_refs, weight_refs = refs[:8], refs[8:15]
    own_align, align_ref, send_ref, keep_ref, rows_ref, audio_ref, kv_ref, query_ref = refs[15:]
    seq_at, mem_at, grp_at = (lax.axis_index(name) for name in ("seq", "mem", "grp"))
    rows, audio_rows = rows_ref.shape[0] // 4, audio_ref.shape[0] // 4
    depth, lane = rows_ref.shape[1] // 4, audio_ref.shape[1] // 4
    for at, packed_ref in enumerate(packed_refs):
        slot, mem = divmod(at, 2)
        for part in range(2):
            shard = 2 * (mem_at ^ mem) + part
            lanes = pl.ds(pl.multiple_of(shard * depth, depth), depth)
            rows_ref[slot * rows : (slot + 1) * rows, lanes] = packed_ref[
                part * rows : (part + 1) * rows, :
            ]
            lanes = pl.ds(pl.multiple_of(shard * lane, lane), lane)
            audio_ref[slot * audio_rows : (slot + 1) * audio_rows, lanes] = packed_ref[
                2 * rows :, part * lane : (part + 1) * lane
            ]
    kv_half, fold = depth // 2, lane // 4
    width = query_ref.shape[1]

    def place(piece_ref, shard, group, kv_at, query_at):
        to = pl.ds(pl.multiple_of((2 * shard + group) * kv_half, kv_half), kv_half)
        kv_ref[to, :] = piece_ref[kv_at : kv_at + kv_half, :]
        for side in range(2):
            to = pl.ds(pl.multiple_of((4 * shard + 2 * group + side) * fold, fold), fold)
            query_ref[to, :] = piece_ref[
                query_at : query_at + fold, side * width : (side + 1) * width
            ]

    for group in range(2):
        place(weight_refs[0], seq_at, group, group * kv_half, 2 * kv_half + group * fold)
    for bit in range(1, 4):
        place(weight_refs[2 * bit - 1], seq_at ^ bit, grp_at, 0, kv_half)
        place(weight_refs[2 * bit], seq_at ^ bit, 1 - grp_at, 0, kv_half)
        align_ref[bit] = weight_refs[2 * bit - 1][kv_half + fold :, : align_ref.shape[2]]
    align_ref[0] = jnp.broadcast_to(
        own_align[...].astype(jnp.float32).astype(align_ref.dtype), align_ref.shape[1:]
    )

    count = 4 * rows
    columns = keep_ref.shape[1]
    total = jnp.dot(rows_ref[...], kv_ref[...], preferred_element_type=jnp.float32)
    keep_ref[:count, :] = total[:, :columns]
    send_ref[:count, :] = total[:, columns:]
    total = jnp.dot(audio_ref[...], query_ref[...], preferred_element_type=jnp.float32)
    folded = 2 * audio_rows
    for side in range(2):
        at = slice(side * folded, (side + 1) * folded)
        to = slice(side * HEAD_DIM, (side + 1) * HEAD_DIM)
        keep_ref[count:, to] = total[at, :HEAD_DIM]
        send_ref[count:, to] = total[at, HEAD_DIM:]


def attend(queries, kv_ref, frames_ref, align):
    scores = lax.dot_general(
        queries,
        kv_ref[:, :HEAD_DIM],
        (((1,), (1,)), ((), ())),
        preferred_element_type=jnp.float32,
    ) * (1.0 / HEAD_DIM**0.5)
    scores = scores - SLOPE * jnp.abs(frames_ref[...] - align) / FRAMES
    exp_terms = jnp.exp(scores - jnp.max(scores, axis=1, keepdims=True))
    weighted = jnp.dot(
        exp_terms.astype(jnp.bfloat16), kv_ref[:, HEAD_DIM:], preferred_element_type=jnp.float32
    )
    return (weighted / jnp.sum(exp_terms, axis=1, keepdims=True)).astype(jnp.bfloat16)


def attention_body(frames_ref, align_ref, keep_ref, came_ref, *refs):
    *out_refs, kv_ref, query_ref = refs
    count, audio_rows = kv_ref.shape[0], query_ref.shape[1]

    def summed(rows, columns=slice(None)):
        return (keep_ref[rows, columns] + came_ref[rows, columns]).astype(jnp.bfloat16)

    kv_ref[...] = summed(slice(0, count))
    for slot in range(4):
        side, half = divmod(slot, 2)
        query_ref[slot] = summed(
            slice(count + half * audio_rows, count + (half + 1) * audio_rows),
            slice(side * HEAD_DIM, (side + 1) * HEAD_DIM),
        )
    for bit, out_ref in enumerate(out_refs):
        align = align_ref[bit].astype(jnp.float32)[:8].T[:, :1]
        out_ref[...] = attend(query_ref[bit], kv_ref, frames_ref, align)


def out_body(*refs):
    piece_refs, (own_w, *part_refs), (send_ref, keep_ref, heads_ref, weight_ref, sem) = (
        refs[:4],
        refs[4:11],
        refs[11:],
    )
    seq_at, grp_at = lax.axis_index("seq"), lax.axis_index("grp")
    place = lax.axis_index("mem") * 2 + lax.axis_index("rep")
    copy = pltpu.make_async_copy(own_w, weight_ref.at[0], sem)
    copy.start()
    for bit, piece_ref in enumerate(piece_refs):
        heads_ref[seq_at ^ bit] = piece_ref[...]
    heads = jnp.concatenate([heads_ref[head] for head in range(heads_ref.shape[0])], axis=1)
    depth = part_refs[0].shape[0]
    mine = pl.ds(pl.multiple_of(grp_at * depth, depth), depth)
    rest = pl.ds(pl.multiple_of((1 - grp_at) * depth, depth), depth)
    for bit in range(1, 4):
        weight_ref[bit, mine] = part_refs[2 * bit - 2][...]
        weight_ref[bit, rest] = part_refs[2 * bit - 1][...]
    for bit in (1, 2, 3, 0):
        if bit == 0:
            copy.wait()
        slot = seq_at ^ bit ^ place
        value = jnp.dot(heads, weight_ref[bit], preferred_element_type=jnp.float32)

        @pl.when(slot % 2 == 1)
        def _():
            send_ref[slot // 2] = value.astype(send_ref.dtype)

        @pl.when(slot % 2 == 0)
        def _():
            keep_ref[slot // 2] = value


def by_head(video_cache, plan, alignment, audio_tokens, kv_weight, query_weight, out_weight):
    seq_size = lax.axis_size("seq")
    seq_at = lax.axis_index("seq")
    place = lax.axis_index("mem") * 2 + lax.axis_index("rep")
    video_rows = video_cache.shape[1]
    audio_rows = audio_tokens.shape[0]
    half_depth, width = kv_weight.shape[0] // 2, 2 * HEAD_DIM
    query_quarter = query_weight.shape[0] // 4

    def bfloat(*shape):
        return jax.ShapeDtypeStruct(shape, jnp.bfloat16)

    packed, other, out_half = kernel_call(
        first_body,
        [
            bfloat(2 * video_rows + audio_rows, half_depth),
            bfloat(half_depth + query_quarter, kv_weight.shape[1]),
            bfloat(out_weight.shape[0] // 2, out_weight.shape[1]),
        ],
        [plan, video_cache, audio_tokens, kv_weight, query_weight, out_weight],
        scratch=[
            pltpu.VMEM((3, video_rows, 2 * half_depth), jnp.bfloat16),
            pltpu.VMEM((2 * video_rows + audio_rows, half_depth), jnp.bfloat16),
            pltpu.VMEM((half_depth + query_quarter, kv_weight.shape[1]), jnp.bfloat16),
            pltpu.VMEM((out_weight.shape[0] // 2, out_weight.shape[1]), jnp.bfloat16),
            pltpu.SMEM(plan.shape, jnp.int32),
            pltpu.SemaphoreType.DMA((26,)),
        ],
        loose_in=(0, 1, 2, 3, 4, 5),
        loose_out=(0, 1, 2),
        limit=61,
    )

    tokens = [packed, swap(packed, "seq", 1), swap(packed, "seq", 2)]
    across = [swap(packed, "mem", 1)]
    other = swap(other, "rep", 1)
    rows = half_depth // 2 + query_quarter // 2
    weight_own, *pieces = kernel_call(
        weight_body,
        [bfloat(2 * rows, 2 * width)] + [bfloat(rows + 16, 2 * width)] * 3,
        [alignment[None], kv_weight, query_weight, other],
        limit=4,
    )
    pieces = [swap(piece, "seq", bit) for bit, piece in enumerate(pieces, 1)]

    across.append(swap(tokens[1], "mem", 1))
    tokens.append(swap(tokens[2], "seq", 1))
    across.append(swap(tokens[2], "mem", 1))
    pieces[0], across[0], across[1] = lax.optimization_barrier(
        (pieces[0], across[0], across[1])
    )
    rest = [swap(pieces[0], "grp", 1)]
    tokens[3], across[2], rest[0], pieces[1] = lax.optimization_barrier(
        (tokens[3], across[2], rest[0], pieces[1])
    )
    across.append(swap(tokens[3], "mem", 1))
    rest += [swap(piece, "grp", 1) for piece in pieces[1:]]

    out_half, tokens[3] = lax.optimization_barrier((out_half, tokens[3]))
    out_third, out_partner = swap(out_half, "seq", 2), swap(out_half, "seq", 1)
    weights = [weight_own]
    for piece, other in zip(pieces, rest):
        weights += [piece, other]
    rows = seq_size * (video_rows + audio_rows // 2)
    sums = jax.ShapeDtypeStruct((rows, width), jnp.float32)
    aligns, send, keep = kernel_call(
        products_body,
        [bfloat(4, 16, audio_rows), sums, sums],
        [value for pair in zip(tokens, across) for value in pair] + weights + [alignment[None]],
        scratch=[
            pltpu.VMEM((seq_size * video_rows, 4 * half_depth), jnp.bfloat16),
            pltpu.VMEM((seq_size * audio_rows, 8 * query_quarter), jnp.bfloat16),
            pltpu.VMEM((4 * half_depth, 2 * width), jnp.bfloat16),
            pltpu.VMEM((8 * query_quarter, width), jnp.bfloat16),
        ],
        limit=15,
    )
    send, out_third, out_partner = lax.optimization_barrier((send, out_third, out_partner))
    came = swap(send, "rep", 1)
    out_fourth, third_rest = swap(out_third, "seq", 1), swap(out_third, "grp", 1)
    partner_rest = swap(out_partner, "grp", 1)

    span = video_rows * seq_size
    blocks = jnp.stack([seq_at, seq_at ^ 1, seq_at ^ 2, seq_at ^ 3])
    positions = blocks[:, None] * video_rows + jnp.arange(video_rows, dtype=jnp.int32)[None, :]
    frames_video = (positions.reshape(1, span) * FRAMES // span).astype(jnp.float32)
    own_piece, near_piece, far_piece, farther_piece = kernel_call(
        attention_body,
        [bfloat(audio_rows, HEAD_DIM)] * 4,
        [frames_video, aligns, keep, came],
        scratch=[
            pltpu.VMEM((span, width), jnp.bfloat16),
            pltpu.VMEM((seq_size, audio_rows, HEAD_DIM), jnp.bfloat16),
        ],
        limit=9,
    )
    out_fourth, own_piece = lax.optimization_barrier((out_fourth, own_piece))
    fourth_rest = swap(out_fourth, "grp", 1)
    far_piece = swap(far_piece, "seq", 2)
    farther_piece = swap(farther_piece, "seq", 3)
    near_piece = swap(near_piece, "seq", 1)

    columns = out_weight.shape[1]
    weights = [out_weight, out_partner, partner_rest]
    weights += [out_third, third_rest, out_fourth, fourth_rest]
    send, keep = kernel_call(
        out_body,
        [
            jax.ShapeDtypeStruct((2, audio_rows, columns), jnp.bfloat16),
            jax.ShapeDtypeStruct((2, audio_rows, columns), jnp.float32),
        ],
        [own_piece, near_piece, far_piece, farther_piece, *weights],
        scratch=[
            pltpu.VMEM((seq_size, audio_rows, HEAD_DIM), jnp.bfloat16),
            pltpu.VMEM((seq_size, *out_weight.shape), jnp.bfloat16),
            pltpu.SemaphoreType.DMA,
        ],
        loose_in=(4,),
        limit=7,
    )
    came = swap(send, "rep", 1)
    across = swap((keep[1] + came[1].astype(jnp.float32)).astype(jnp.bfloat16), "mem", 1)
    residual = lax.dynamic_slice_in_dim(audio_tokens, place * columns, columns, 1)
    own_part = taylor(video_cache, plan, 2 * half_depth)
    base = residual.astype(jnp.float32) + (keep[0] + came[0].astype(jnp.float32))
    base, across = lax.optimization_barrier((base, across))
    audio_output = (base + across.astype(jnp.float32)).astype(jnp.bfloat16)
    return (own_part, audio_output)


def solution(mesh):
    sizes = dict(mesh.shape)
    square = (sizes["grp"], sizes["seq"], sizes["mem"], sizes["rep"]) == (2, 4, 2, 2)

    def on_device(*arrays):
        heads = arrays[5].shape[1] // HEAD_DIM
        return (by_head if square and heads == sizes["seq"] else general)(*arrays)

    return jax.shard_map(
        on_device,
        mesh=mesh,
        in_specs=(
            P(None, ("grp", "seq"), "mem"),
            P("grp"),
            P(("grp", "seq")),
            P(("grp", "seq"), None),
            P("seq", ("mem", "rep")),
            P("seq", ("mem", "rep")),
            P(("mem", "rep"), "seq"),
        ),
        out_specs=(P(("grp", "seq"), "mem"), P(("grp", "seq"), ("mem", "rep"))),
        check_vma=False,
    )
```

```python
import math

import jax
import jax.numpy as jnp
from jax import lax
from jax.experimental import pallas as pl
from jax.experimental.pallas import tpu as pltpu
from jax.sharding import PartitionSpec as P

HEAD_DIM = 128
FRAMES = 24


SLOPE = 4.0


def taylor_ratio(plan):
    history = plan.shape[0]
    step_ids = jnp.arange(history, dtype=jnp.int32)
    marked = step_ids * plan
    last_fresh = jnp.max(marked)
    prior_fresh = jnp.max(jnp.where(step_ids < last_fresh, marked, 0))
    return (history - last_fresh).astype(jnp.float32) / (last_fresh - prior_fresh).astype(
        jnp.float32
    )


def combine(orders, step_ratio):
    values = orders.astype(jnp.float32)
    return (values[0] + step_ratio * values[1] + 0.5 * step_ratio * step_ratio * values[2]).astype(
        jnp.bfloat16
    )


def general(video_cache, plan, alignment, audio_tokens, kv_weight, query_weight, out_weight):
    step_ratio = taylor_ratio(plan)
    own_part = combine(video_cache, step_ratio)
    features_all = lax.all_gather(own_part, "mem", axis=1, tiled=True)
    video_rows = features_all.shape[0]
    kv_local = jnp.dot(
        features_all,
        lax.all_gather(kv_weight, "seq", axis=0, tiled=True),
        preferred_element_type=jnp.float32,
    )
    head_size = HEAD_DIM
    local_heads = query_weight.shape[1] // head_size
    kv_local = kv_local.astype(jnp.bfloat16).reshape(video_rows, local_heads, 2, head_size)
    key_rows = kv_local[:, :, 0, :]
    value_rows = kv_local[:, :, 1, :]
    query_full, out_full = (
        lax.all_gather(query_weight, "seq", axis=0, tiled=True),
        lax.all_gather(out_weight, "seq", axis=1, tiled=True),
    )
    audio_rows = audio_tokens.shape[0]
    queries = jnp.dot(audio_tokens, query_full, preferred_element_type=jnp.float32).astype(
        jnp.bfloat16
    )
    queries = queries.reshape(audio_rows, local_heads, head_size)
    scale = 1.0 / head_size**0.5
    span = video_rows * lax.axis_size("seq")
    initial = (
        jnp.full((local_heads, audio_rows), -1e30, jnp.float32),
        jnp.zeros((local_heads, audio_rows), jnp.float32),
        jnp.zeros((local_heads, audio_rows, head_size), jnp.float32),
    )
    key_piece = lax.all_gather(key_rows, "seq", axis=0, tiled=True)
    value_piece = lax.all_gather(value_rows, "seq", axis=0, tiled=True)
    row_count = key_piece.shape[0]
    block_len = math.gcd(row_count, 1024)

    def advance(block_index, carried):
        row_max, row_sum, weighted = carried
        key_block = lax.dynamic_slice_in_dim(key_piece, block_index * block_len, block_len, 0)
        value_block = lax.dynamic_slice_in_dim(value_piece, block_index * block_len, block_len, 0)
        positions = block_index * block_len + jnp.arange(block_len, dtype=jnp.int32)
        frames_video = positions * FRAMES // span
        distance_bias = (
            -SLOPE
            * jnp.abs(frames_video[None, :] - alignment[:, None]).astype(jnp.float32)
            / FRAMES
        )
        scores = (
            jnp.einsum("qhd,khd->hqk", queries, key_block, preferred_element_type=jnp.float32)
            * scale
        )
        scores = scores + distance_bias[None]
        new_max = jnp.maximum(row_max, jnp.max(scores, axis=2))
        rescale = jnp.exp(row_max - new_max)
        exp_terms = jnp.exp(scores - new_max[:, :, None])
        row_sum = row_sum * rescale + jnp.sum(exp_terms, axis=2)
        weighted = weighted * rescale[:, :, None] + jnp.einsum(
            "hqk,khd->hqd",
            exp_terms.astype(jnp.bfloat16),
            value_block,
            preferred_element_type=jnp.float32,
        )
        return (new_max, row_sum, weighted)

    row_max, row_sum, weighted = lax.fori_loop(0, row_count // block_len, advance, initial)
    attended = (weighted / row_sum[:, :, None]).astype(jnp.bfloat16)
    attended = jnp.transpose(attended, (1, 0, 2)).reshape(audio_rows, local_heads * head_size)
    partial_update = jnp.dot(attended, out_full, preferred_element_type=jnp.float32)
    update = lax.psum_scatter(
        partial_update.astype(jnp.bfloat16), ("mem", "rep"), scatter_dimension=1, tiled=True
    ).astype(jnp.float32)
    own_columns = update.shape[1]
    residual = lax.dynamic_slice_in_dim(
        audio_tokens, lax.axis_index(("mem", "rep")) * own_columns, own_columns, 1
    )
    audio_output = (residual.astype(jnp.float32) + update).astype(jnp.bfloat16)
    return (own_part, audio_output)


def swap(value, axis, bit):
    size = lax.axis_size(axis)
    return lax.ppermute(value, axis, [(i, i ^ bit) for i in range(size)])


VMEM = pl.BlockSpec(memory_space=pltpu.VMEM)
SMEM = pl.BlockSpec(memory_space=pltpu.SMEM)
ANY = pl.BlockSpec(memory_space=pl.ANY)
HBM = pl.BlockSpec(memory_space=pltpu.HBM)


def kernel_call(body, outs, ins, after=(), scratch=(), smem=(), loose_in=(), loose_out=(), limit=14):
    def whole(*refs):
        body(*refs[: len(ins)], *refs[len(ins) + len(after) :])

    spots = [SMEM if i in smem else HBM if i in loose_in else VMEM for i in range(len(ins))]
    return pl.pallas_call(
        whole,
        out_shape=outs,
        in_specs=spots + [ANY] * len(after),
        out_specs=[HBM if i in loose_out else VMEM for i in range(len(outs))],
        scratch_shapes=scratch,
        compiler_params=pltpu.CompilerParams(vmem_limit_bytes=limit * 2**20),
    )(*ins, *after)


def plan_ratio(plan_ref, columns):
    history = plan_ref.shape[0]
    last_fresh, prior_fresh = jnp.int32(0), jnp.int32(0)
    for step in range(history):
        fresh = plan_ref[step] == 1
        prior_fresh = jnp.where(fresh, last_fresh, prior_fresh)
        last_fresh = jnp.where(fresh, step, last_fresh)
    ahead = jnp.full((1, columns), history - last_fresh, jnp.int32).astype(jnp.float32)
    apart = jnp.full((1, columns), last_fresh - prior_fresh, jnp.int32).astype(jnp.float32)
    return ahead / apart


def taylor_rows(cache_ref, out_ref, step_ratio, first, last):
    half_square = 0.5 * step_ratio * step_ratio
    for at in range(first, last, 16):
        terms = [cache_ref[order, at : at + 16, :].astype(jnp.float32) for order in range(3)]
        out_ref[at : at + 16, :] = (
            terms[0] + step_ratio * terms[1] + half_square * terms[2]
        ).astype(jnp.bfloat16)


def taylor_body(plan_ref, cache_ref, out_ref):
    rows, columns = out_ref.shape
    taylor_rows(cache_ref, out_ref, plan_ratio(plan_ref, columns), 0, rows)


def taylor(video_cache, plan, width):
    orders, rows, columns = video_cache.shape
    return pl.pallas_call(
        taylor_body,
        out_shape=jax.ShapeDtypeStruct((rows, columns), jnp.bfloat16),
        grid=(columns // width,),
        in_specs=[SMEM, pl.BlockSpec((orders, rows, width), lambda i: (0, 0, i))],
        out_specs=pl.BlockSpec((rows, width), lambda i: (0, i)),
        compiler_params=pltpu.CompilerParams(vmem_limit_bytes=6 * 2**20),
    )(plan, video_cache)


def first_body(
    plan_ref,
    cache_ref,
    audio_ref,
    kv_ref,
    query_ref,
    out_w,
    packed_ref,
    other_ref,
    half_ref,
    held_ref,
    made_ref,
    other_vmem,
    half_vmem,
    plan_smem,
    sems,
):
    rep_at, mem_at, grp_at = (lax.axis_index(name) for name in ("rep", "mem", "grp"))
    rows, width = held_ref.shape[1:]
    width = width // 2
    copies = []

    def copy(source, target):
        copies.append(pltpu.make_async_copy(source, target, sems.at[len(copies)]))

    def part(index, size):
        return pl.ds(pl.multiple_of(index * size, size), size)

    plan_copy = pltpu.make_async_copy(plan_ref, plan_smem, sems.at[25])
    plan_copy.start()
    blocks = 4
    step = rows // blocks
    for block in range(blocks):
        at = pl.ds(block * step, step)
        for shard in range(2):
            copy(
                cache_ref.at[:, at, part(2 * shard + rep_at, width)],
                held_ref.at[:, at, pl.ds(shard * width, width)],
            )
    lane = width // 2
    for shard in range(2):
        copy(
            audio_ref.at[:, part(2 * (2 * mem_at + shard) + rep_at, lane)],
            made_ref.at[pl.ds(2 * rows, audio_ref.shape[0]), pl.ds(shard * lane, lane)],
        )
    depth, columns = kv_ref.shape[0] // 2, query_ref.shape[1]
    copy(kv_ref.at[part(1 - rep_at, depth)], other_vmem.at[pl.ds(0, depth)])
    quarter = query_ref.shape[0] // 4
    for side in range(2):
        copy(
            query_ref.at[part(2 * (1 - rep_at) + side, quarter)],
            other_vmem.at[pl.ds(depth, quarter), pl.ds(side * columns, columns)],
        )
    copy(out_w.at[part(grp_at, half_ref.shape[0])], half_vmem)
    for started in copies:
        started.start()
    plan_copy.wait()
    step_ratio = plan_ratio(plan_smem, width)
    for block in range(blocks):
        for shard in range(2):
            copies[2 * block + shard].wait()
            taylor_rows(
                held_ref.at[:, :, pl.ds(shard * width, width)],
                made_ref.at[pl.ds(shard * rows, rows)],
                step_ratio,
                block * step,
                (block + 1) * step,
            )
            at = pl.ds(shard * rows + block * step, step)
            copy(made_ref.at[at], packed_ref.at[at])
            copies[-1].start()
    audio_at = pl.ds(2 * rows, audio_ref.shape[0])
    stages = (
        (2, made_ref.at[audio_at], packed_ref.at[audio_at]),
        (3, other_vmem, other_ref),
        (1, half_vmem, half_ref),
    )
    at = 2 * blocks
    for count, source, target in stages:
        for arriving in copies[at : at + count]:
            arriving.wait()
        at += count
        copy(source, target)
        copies[-1].start()
    for leaving in copies[at:]:
        leaving.wait()


def weight_body(align_ref, kv_ref, query_ref, other_ref, own_ref, *piece_refs):
    seq_at, rep_at, grp_at = (lax.axis_index(name) for name in ("seq", "rep", "grp"))
    kv_half, query_half = kv_ref.shape[0] // 2, query_ref.shape[0] // 2
    kv_rows, query_rows = kv_half // 2, query_half // 2
    fold = query_rows // 2

    def fill(out_ref, bit, group, kv_at, query_at):
        head = seq_at ^ bit
        width = 2 * HEAD_DIM
        lanes = pl.ds(pl.multiple_of(head * width, width), width)
        at = pl.ds(pl.multiple_of(rep_at * kv_half + group * kv_rows, kv_rows), kv_rows)
        out_ref[kv_at : kv_at + kv_rows, :width] = kv_ref[at, lanes]
        at = pl.ds(pl.multiple_of(group * kv_rows, kv_rows), kv_rows)
        out_ref[kv_at : kv_at + kv_rows, width:] = other_ref[at, lanes]
        lanes = pl.ds(pl.multiple_of(head * HEAD_DIM, HEAD_DIM), HEAD_DIM)
        other_lanes = pl.ds(
            pl.multiple_of(group * query_ref.shape[1] + head * HEAD_DIM, HEAD_DIM), HEAD_DIM
        )
        for side in range(2):
            first = rep_at * query_half + group * query_rows + side * fold
            at = pl.ds(pl.multiple_of(first, fold), fold)
            to = slice(query_at, query_at + fold)
            out_ref[to, side * width : side * width + HEAD_DIM] = query_ref[at, lanes]
            out_ref[to, side * width + HEAD_DIM : (side + 1) * width] = other_ref[
                kv_half + side * fold : kv_half + (side + 1) * fold, other_lanes
            ]

    for group in range(2):
        fill(own_ref, 0, group, group * kv_rows, kv_half + group * fold)
    for bit, piece_ref in enumerate(piece_refs, 1):
        fill(piece_ref, bit, grp_at, 0, kv_rows)
        spare = (piece_ref.shape[0] - kv_rows - fold, piece_ref.shape[1])
        align = align_ref[...].astype(jnp.float32).astype(piece_ref.dtype)
        row = jnp.concatenate(
            [align, jnp.zeros((1, spare[1] - align.shape[1]), piece_ref.dtype)], axis=1
        )
        piece_ref[kv_rows + fold :, :] = jnp.broadcast_to(row, spare)


def products_body(*refs):
    packed_refs, weight_refs = refs[:8], refs[8:15]
    own_align, align_ref, send_ref, keep_ref, rows_ref, audio_ref, kv_ref, query_ref = refs[15:]
    seq_at, mem_at, grp_at = (lax.axis_index(name) for name in ("seq", "mem", "grp"))
    rows, audio_rows = rows_ref.shape[0] // 4, audio_ref.shape[0] // 4
    depth, lane = rows_ref.shape[1] // 4, audio_ref.shape[1] // 4
    for at, packed_ref in enumerate(packed_refs):
        slot, mem = divmod(at, 2)
        for part in range(2):
            shard = 2 * (mem_at ^ mem) + part
            lanes = pl.ds(pl.multiple_of(shard * depth, depth), depth)
            rows_ref[slot * rows : (slot + 1) * rows, lanes] = packed_ref[
                part * rows : (part + 1) * rows, :
            ]
            lanes = pl.ds(pl.multiple_of(shard * lane, lane), lane)
            audio_ref[slot * audio_rows : (slot + 1) * audio_rows, lanes] = packed_ref[
                2 * rows :, part * lane : (part + 1) * lane
            ]
    kv_half, fold = depth // 2, lane // 4
    width = query_ref.shape[1]

    def place(piece_ref, shard, group, kv_at, query_at):
        to = pl.ds(pl.multiple_of((2 * shard + group) * kv_half, kv_half), kv_half)
        kv_ref[to, :] = piece_ref[kv_at : kv_at + kv_half, :]
        for side in range(2):
            to = pl.ds(pl.multiple_of((4 * shard + 2 * group + side) * fold, fold), fold)
            query_ref[to, :] = piece_ref[
                query_at : query_at + fold, side * width : (side + 1) * width
            ]

    for group in range(2):
        place(weight_refs[0], seq_at, group, group * kv_half, 2 * kv_half + group * fold)
    for bit in range(1, 4):
        place(weight_refs[2 * bit - 1], seq_at ^ bit, grp_at, 0, kv_half)
        place(weight_refs[2 * bit], seq_at ^ bit, 1 - grp_at, 0, kv_half)
        align_ref[bit] = weight_refs[2 * bit - 1][kv_half + fold :, : align_ref.shape[2]]
    align_ref[0] = jnp.broadcast_to(
        own_align[...].astype(jnp.float32).astype(align_ref.dtype), align_ref.shape[1:]
    )

    count = 4 * rows
    columns = keep_ref.shape[1]
    total = jnp.dot(rows_ref[...], kv_ref[...], preferred_element_type=jnp.float32)
    keep_ref[:count, :] = total[:, :columns]
    send_ref[:count, :] = total[:, columns:]
    total = jnp.dot(audio_ref[...], query_ref[...], preferred_element_type=jnp.float32)
    folded = 2 * audio_rows
    for side in range(2):
        at = slice(side * folded, (side + 1) * folded)
        to = slice(side * HEAD_DIM, (side + 1) * HEAD_DIM)
        keep_ref[count:, to] = total[at, :HEAD_DIM]
        send_ref[count:, to] = total[at, HEAD_DIM:]


def attend(queries, kv_ref, frames_ref, align):
    scores = lax.dot_general(
        queries,
        kv_ref[:, :HEAD_DIM],
        (((1,), (1,)), ((), ())),
        preferred_element_type=jnp.float32,
    ) * (1.0 / HEAD_DIM**0.5)
    scores = scores - SLOPE * jnp.abs(frames_ref[...] - align) / FRAMES
    exp_terms = jnp.exp(scores - jnp.max(scores, axis=1, keepdims=True))
    weighted = jnp.dot(
        exp_terms.astype(jnp.bfloat16), kv_ref[:, HEAD_DIM:], preferred_element_type=jnp.float32
    )
    return (weighted / jnp.sum(exp_terms, axis=1, keepdims=True)).astype(jnp.bfloat16)


def attention_body(frames_ref, align_ref, keep_ref, came_ref, *refs):
    *out_refs, kv_ref, query_ref = refs
    count, audio_rows = kv_ref.shape[0], query_ref.shape[1]

    def summed(rows, columns=slice(None)):
        return (keep_ref[rows, columns] + came_ref[rows, columns]).astype(jnp.bfloat16)

    kv_ref[...] = summed(slice(0, count))
    for slot in range(4):
        side, half = divmod(slot, 2)
        query_ref[slot] = summed(
            slice(count + half * audio_rows, count + (half + 1) * audio_rows),
            slice(side * HEAD_DIM, (side + 1) * HEAD_DIM),
        )
    for bit, out_ref in enumerate(out_refs):
        align = align_ref[bit].astype(jnp.float32)[:8].T[:, :1]
        out_ref[...] = attend(query_ref[bit], kv_ref, frames_ref, align)


def out_body(*refs):
    piece_refs, (own_w, *part_refs), (send_ref, keep_ref, heads_ref, weight_ref, sem) = (
        refs[:4],
        refs[4:11],
        refs[11:],
    )
    seq_at, grp_at = lax.axis_index("seq"), lax.axis_index("grp")
    place = lax.axis_index("mem") * 2 + lax.axis_index("rep")
    copy = pltpu.make_async_copy(own_w, weight_ref.at[0], sem)
    copy.start()
    for bit, piece_ref in enumerate(piece_refs):
        heads_ref[seq_at ^ bit] = piece_ref[...]
    heads = jnp.concatenate([heads_ref[head] for head in range(heads_ref.shape[0])], axis=1)
    depth = part_refs[0].shape[0]
    mine = pl.ds(pl.multiple_of(grp_at * depth, depth), depth)
    rest = pl.ds(pl.multiple_of((1 - grp_at) * depth, depth), depth)
    for bit in range(1, 4):
        weight_ref[bit, mine] = part_refs[2 * bit - 2][...]
        weight_ref[bit, rest] = part_refs[2 * bit - 1][...]
    for bit in (1, 2, 3, 0):
        if bit == 0:
            copy.wait()
        slot = seq_at ^ bit ^ place
        value = jnp.dot(heads, weight_ref[bit], preferred_element_type=jnp.float32)

        @pl.when(slot % 2 == 1)
        def _():
            send_ref[slot // 2] = value.astype(send_ref.dtype)

        @pl.when(slot % 2 == 0)
        def _():
            keep_ref[slot // 2] = value


def by_head(video_cache, plan, alignment, audio_tokens, kv_weight, query_weight, out_weight):
    seq_size = lax.axis_size("seq")
    seq_at = lax.axis_index("seq")
    place = lax.axis_index("mem") * 2 + lax.axis_index("rep")
    video_rows = video_cache.shape[1]
    audio_rows = audio_tokens.shape[0]
    half_depth, width = kv_weight.shape[0] // 2, 2 * HEAD_DIM
    query_quarter = query_weight.shape[0] // 4

    def bfloat(*shape):
        return jax.ShapeDtypeStruct(shape, jnp.bfloat16)

    packed, other, out_half = kernel_call(
        first_body,
        [
            bfloat(2 * video_rows + audio_rows, half_depth),
            bfloat(half_depth + query_quarter, kv_weight.shape[1]),
            bfloat(out_weight.shape[0] // 2, out_weight.shape[1]),
        ],
        [plan, video_cache, audio_tokens, kv_weight, query_weight, out_weight],
        scratch=[
            pltpu.VMEM((3, video_rows, 2 * half_depth), jnp.bfloat16),
            pltpu.VMEM((2 * video_rows + audio_rows, half_depth), jnp.bfloat16),
            pltpu.VMEM((half_depth + query_quarter, kv_weight.shape[1]), jnp.bfloat16),
            pltpu.VMEM((out_weight.shape[0] // 2, out_weight.shape[1]), jnp.bfloat16),
            pltpu.SMEM(plan.shape, jnp.int32),
            pltpu.SemaphoreType.DMA((26,)),
        ],
        loose_in=(0, 1, 2, 3, 4, 5),
        loose_out=(0, 1, 2),
        limit=61,
    )

    tokens = [packed, swap(packed, "seq", 1)]
    across = [swap(packed, "mem", 1)]
    other = swap(other, "rep", 1)
    rows = half_depth // 2 + query_quarter // 2
    weight_own, *pieces = kernel_call(
        weight_body,
        [bfloat(2 * rows, 2 * width)] + [bfloat(rows + 16, 2 * width)] * 3,
        [alignment[None], kv_weight, query_weight, other],
        limit=4,
    )
    packed, weight_own = lax.optimization_barrier((packed, weight_own))
    tokens.append(swap(packed, "seq", 2))
    pieces = [swap(piece, "seq", bit) for bit, piece in enumerate(pieces, 1)]

    across.append(swap(tokens[1], "mem", 1))
    tokens.append(swap(tokens[2], "seq", 1))
    across.append(swap(tokens[2], "mem", 1))
    pieces[0], across[0], across[1] = lax.optimization_barrier(
        (pieces[0], across[0], across[1])
    )
    rest = [swap(pieces[0], "grp", 1)]
    tokens[3], across[2], rest[0], pieces[1] = lax.optimization_barrier(
        (tokens[3], across[2], rest[0], pieces[1])
    )
    across.append(swap(tokens[3], "mem", 1))
    rest.append(swap(pieces[1], "grp", 1))
    pieces[2], rest[1] = lax.optimization_barrier((pieces[2], rest[1]))
    rest.append(swap(pieces[2], "grp", 1))

    out_half, tokens[3] = lax.optimization_barrier((out_half, tokens[3]))
    out_third, out_partner = swap(out_half, "seq", 2), swap(out_half, "seq", 1)
    weights = [weight_own]
    for piece, other in zip(pieces, rest):
        weights += [piece, other]
    rows = seq_size * (video_rows + audio_rows // 2)
    sums = jax.ShapeDtypeStruct((rows, width), jnp.float32)
    aligns, send, keep = kernel_call(
        products_body,
        [bfloat(4, 16, audio_rows), sums, sums],
        [value for pair in zip(tokens, across) for value in pair] + weights + [alignment[None]],
        after=(out_third, out_partner),
        scratch=[
            pltpu.VMEM((seq_size * video_rows, 4 * half_depth), jnp.bfloat16),
            pltpu.VMEM((seq_size * audio_rows, 8 * query_quarter), jnp.bfloat16),
            pltpu.VMEM((4 * half_depth, 2 * width), jnp.bfloat16),
            pltpu.VMEM((8 * query_quarter, width), jnp.bfloat16),
        ],
        limit=15,
    )
    came = swap(send, "rep", 1)
    out_fourth, third_rest = swap(out_third, "seq", 1), swap(out_third, "grp", 1)
    partner_rest = swap(out_partner, "grp", 1)

    span = video_rows * seq_size
    blocks = jnp.stack([seq_at, seq_at ^ 1, seq_at ^ 2, seq_at ^ 3])
    positions = blocks[:, None] * video_rows + jnp.arange(video_rows, dtype=jnp.int32)[None, :]
    frames_video = (positions.reshape(1, span) * FRAMES // span).astype(jnp.float32)
    own_piece, near_piece, far_piece, farther_piece = kernel_call(
        attention_body,
        [bfloat(audio_rows, HEAD_DIM)] * 4,
        [frames_video, aligns, keep, came],
        scratch=[
            pltpu.VMEM((span, width), jnp.bfloat16),
            pltpu.VMEM((seq_size, audio_rows, HEAD_DIM), jnp.bfloat16),
        ],
        limit=9,
    )
    out_fourth, own_piece = lax.optimization_barrier((out_fourth, own_piece))
    fourth_rest = swap(out_fourth, "grp", 1)
    far_piece = swap(far_piece, "seq", 2)
    farther_piece = swap(farther_piece, "seq", 3)
    near_piece = swap(near_piece, "seq", 1)

    columns = out_weight.shape[1]
    weights = [out_weight, out_partner, partner_rest]
    weights += [out_third, third_rest, out_fourth, fourth_rest]
    send, keep = kernel_call(
        out_body,
        [
            jax.ShapeDtypeStruct((2, audio_rows, columns), jnp.bfloat16),
            jax.ShapeDtypeStruct((2, audio_rows, columns), jnp.float32),
        ],
        [own_piece, near_piece, far_piece, farther_piece, *weights],
        scratch=[
            pltpu.VMEM((seq_size, audio_rows, HEAD_DIM), jnp.bfloat16),
            pltpu.VMEM((seq_size, *out_weight.shape), jnp.bfloat16),
            pltpu.SemaphoreType.DMA,
        ],
        loose_in=(4,),
        limit=7,
    )
    came = swap(send, "rep", 1)
    across = swap((keep[1] + came[1].astype(jnp.float32)).astype(jnp.bfloat16), "mem", 1)
    residual = lax.dynamic_slice_in_dim(audio_tokens, place * columns, columns, 1)
    own_part = taylor(video_cache, plan, 2 * half_depth)
    base = residual.astype(jnp.float32) + (keep[0] + came[0].astype(jnp.float32))
    base, across = lax.optimization_barrier((base, across))
    audio_output = (base + across.astype(jnp.float32)).astype(jnp.bfloat16)
    return (own_part, audio_output)


def solution(mesh):
    sizes = dict(mesh.shape)
    square = (sizes["grp"], sizes["seq"], sizes["mem"], sizes["rep"]) == (2, 4, 2, 2)

    def on_device(*arrays):
        heads = arrays[5].shape[1] // HEAD_DIM
        return (by_head if square and heads == sizes["seq"] else general)(*arrays)

    return jax.shard_map(
        on_device,
        mesh=mesh,
        in_specs=(
            P(None, ("grp", "seq"), "mem"),
            P("grp"),
            P(("grp", "seq")),
            P(("grp", "seq"), None),
            P("seq", ("mem", "rep")),
            P("seq", ("mem", "rep")),
            P(("mem", "rep"), "seq"),
        ),
        out_specs=(P(("grp", "seq"), "mem"), P(("grp", "seq"), ("mem", "rep"))),
        check_vma=False,
    )
```

```python
import math

import jax
import jax.numpy as jnp
from jax import lax
from jax.experimental import pallas as pl
from jax.experimental.pallas import tpu as pltpu
from jax.sharding import PartitionSpec as P

HEAD_DIM = 128
FRAMES = 24


SLOPE = 4.0


def taylor_ratio(plan):
    history = plan.shape[0]
    step_ids = jnp.arange(history, dtype=jnp.int32)
    marked = step_ids * plan
    last_fresh = jnp.max(marked)
    prior_fresh = jnp.max(jnp.where(step_ids < last_fresh, marked, 0))
    return (history - last_fresh).astype(jnp.float32) / (last_fresh - prior_fresh).astype(
        jnp.float32
    )


def combine(orders, step_ratio):
    values = orders.astype(jnp.float32)
    return (values[0] + step_ratio * values[1] + 0.5 * step_ratio * step_ratio * values[2]).astype(
        jnp.bfloat16
    )


def general(video_cache, plan, alignment, audio_tokens, kv_weight, query_weight, out_weight):
    step_ratio = taylor_ratio(plan)
    own_part = combine(video_cache, step_ratio)
    features_all = lax.all_gather(own_part, "mem", axis=1, tiled=True)
    video_rows = features_all.shape[0]
    kv_local = jnp.dot(
        features_all,
        lax.all_gather(kv_weight, "seq", axis=0, tiled=True),
        preferred_element_type=jnp.float32,
    )
    head_size = HEAD_DIM
    local_heads = query_weight.shape[1] // head_size
    kv_local = kv_local.astype(jnp.bfloat16).reshape(video_rows, local_heads, 2, head_size)
    key_rows = kv_local[:, :, 0, :]
    value_rows = kv_local[:, :, 1, :]
    query_full, out_full = (
        lax.all_gather(query_weight, "seq", axis=0, tiled=True),
        lax.all_gather(out_weight, "seq", axis=1, tiled=True),
    )
    audio_rows = audio_tokens.shape[0]
    queries = jnp.dot(audio_tokens, query_full, preferred_element_type=jnp.float32).astype(
        jnp.bfloat16
    )
    queries = queries.reshape(audio_rows, local_heads, head_size)
    scale = 1.0 / head_size**0.5
    span = video_rows * lax.axis_size("seq")
    initial = (
        jnp.full((local_heads, audio_rows), -1e30, jnp.float32),
        jnp.zeros((local_heads, audio_rows), jnp.float32),
        jnp.zeros((local_heads, audio_rows, head_size), jnp.float32),
    )
    key_piece = lax.all_gather(key_rows, "seq", axis=0, tiled=True)
    value_piece = lax.all_gather(value_rows, "seq", axis=0, tiled=True)
    row_count = key_piece.shape[0]
    block_len = math.gcd(row_count, 1024)

    def advance(block_index, carried):
        row_max, row_sum, weighted = carried
        key_block = lax.dynamic_slice_in_dim(key_piece, block_index * block_len, block_len, 0)
        value_block = lax.dynamic_slice_in_dim(value_piece, block_index * block_len, block_len, 0)
        positions = block_index * block_len + jnp.arange(block_len, dtype=jnp.int32)
        frames_video = positions * FRAMES // span
        distance_bias = (
            -SLOPE
            * jnp.abs(frames_video[None, :] - alignment[:, None]).astype(jnp.float32)
            / FRAMES
        )
        scores = (
            jnp.einsum("qhd,khd->hqk", queries, key_block, preferred_element_type=jnp.float32)
            * scale
        )
        scores = scores + distance_bias[None]
        new_max = jnp.maximum(row_max, jnp.max(scores, axis=2))
        rescale = jnp.exp(row_max - new_max)
        exp_terms = jnp.exp(scores - new_max[:, :, None])
        row_sum = row_sum * rescale + jnp.sum(exp_terms, axis=2)
        weighted = weighted * rescale[:, :, None] + jnp.einsum(
            "hqk,khd->hqd",
            exp_terms.astype(jnp.bfloat16),
            value_block,
            preferred_element_type=jnp.float32,
        )
        return (new_max, row_sum, weighted)

    row_max, row_sum, weighted = lax.fori_loop(0, row_count // block_len, advance, initial)
    attended = (weighted / row_sum[:, :, None]).astype(jnp.bfloat16)
    attended = jnp.transpose(attended, (1, 0, 2)).reshape(audio_rows, local_heads * head_size)
    partial_update = jnp.dot(attended, out_full, preferred_element_type=jnp.float32)
    update = lax.psum_scatter(
        partial_update.astype(jnp.bfloat16), ("mem", "rep"), scatter_dimension=1, tiled=True
    ).astype(jnp.float32)
    own_columns = update.shape[1]
    residual = lax.dynamic_slice_in_dim(
        audio_tokens, lax.axis_index(("mem", "rep")) * own_columns, own_columns, 1
    )
    audio_output = (residual.astype(jnp.float32) + update).astype(jnp.bfloat16)
    return (own_part, audio_output)


def swap(value, axis, bit):
    size = lax.axis_size(axis)
    return lax.ppermute(value, axis, [(i, i ^ bit) for i in range(size)])


VMEM = pl.BlockSpec(memory_space=pltpu.VMEM)
SMEM = pl.BlockSpec(memory_space=pltpu.SMEM)
ANY = pl.BlockSpec(memory_space=pl.ANY)
HBM = pl.BlockSpec(memory_space=pltpu.HBM)


def kernel_call(body, outs, ins, after=(), scratch=(), smem=(), loose_in=(), loose_out=(), limit=14):
    def whole(*refs):
        body(*refs[: len(ins)], *refs[len(ins) + len(after) :])

    spots = [SMEM if i in smem else HBM if i in loose_in else VMEM for i in range(len(ins))]
    return pl.pallas_call(
        whole,
        out_shape=outs,
        in_specs=spots + [ANY] * len(after),
        out_specs=[HBM if i in loose_out else VMEM for i in range(len(outs))],
        scratch_shapes=scratch,
        compiler_params=pltpu.CompilerParams(vmem_limit_bytes=limit * 2**20),
    )(*ins, *after)


def plan_ratio(plan_ref, columns):
    history = plan_ref.shape[0]
    last_fresh, prior_fresh = jnp.int32(0), jnp.int32(0)
    for step in range(history):
        fresh = plan_ref[step] == 1
        prior_fresh = jnp.where(fresh, last_fresh, prior_fresh)
        last_fresh = jnp.where(fresh, step, last_fresh)
    ahead = jnp.full((1, columns), history - last_fresh, jnp.int32).astype(jnp.float32)
    apart = jnp.full((1, columns), last_fresh - prior_fresh, jnp.int32).astype(jnp.float32)
    return ahead / apart


def taylor_rows(cache_ref, out_ref, step_ratio, first, last):
    half_square = 0.5 * step_ratio * step_ratio
    for at in range(first, last, 16):
        terms = [cache_ref[order, at : at + 16, :].astype(jnp.float32) for order in range(3)]
        out_ref[at : at + 16, :] = (
            terms[0] + step_ratio * terms[1] + half_square * terms[2]
        ).astype(jnp.bfloat16)


def taylor_body(plan_ref, cache_ref, out_ref):
    rows, columns = out_ref.shape
    taylor_rows(cache_ref, out_ref, plan_ratio(plan_ref, columns), 0, rows)


def taylor(video_cache, plan, width):
    orders, rows, columns = video_cache.shape
    return pl.pallas_call(
        taylor_body,
        out_shape=jax.ShapeDtypeStruct((rows, columns), jnp.bfloat16),
        grid=(columns // width,),
        in_specs=[SMEM, pl.BlockSpec((orders, rows, width), lambda i: (0, 0, i))],
        out_specs=pl.BlockSpec((rows, width), lambda i: (0, i)),
        compiler_params=pltpu.CompilerParams(vmem_limit_bytes=6 * 2**20),
    )(plan, video_cache)


def first_body(
    plan_ref,
    cache_ref,
    audio_ref,
    kv_ref,
    query_ref,
    out_w,
    packed_ref,
    other_ref,
    half_ref,
    held_ref,
    made_ref,
    other_vmem,
    half_vmem,
    plan_smem,
    sems,
):
    rep_at, mem_at, grp_at = (lax.axis_index(name) for name in ("rep", "mem", "grp"))
    rows, width = held_ref.shape[1:]
    width = width // 2
    copies = []

    def copy(source, target):
        copies.append(pltpu.make_async_copy(source, target, sems.at[len(copies)]))

    def part(index, size):
        return pl.ds(pl.multiple_of(index * size, size), size)

    plan_copy = pltpu.make_async_copy(plan_ref, plan_smem, sems.at[25])
    plan_copy.start()
    blocks = 4
    step = rows // blocks
    for block in range(blocks):
        at = pl.ds(block * step, step)
        for shard in range(2):
            copy(
                cache_ref.at[:, at, part(2 * shard + rep_at, width)],
                held_ref.at[:, at, pl.ds(shard * width, width)],
            )
    lane = width // 2
    for shard in range(2):
        copy(
            audio_ref.at[:, part(2 * (2 * mem_at + shard) + rep_at, lane)],
            made_ref.at[pl.ds(2 * rows, audio_ref.shape[0]), pl.ds(shard * lane, lane)],
        )
    depth, columns = kv_ref.shape[0] // 2, query_ref.shape[1]
    copy(kv_ref.at[part(1 - rep_at, depth)], other_vmem.at[pl.ds(0, depth)])
    quarter = query_ref.shape[0] // 4
    for side in range(2):
        copy(
            query_ref.at[part(2 * (1 - rep_at) + side, quarter)],
            other_vmem.at[pl.ds(depth, quarter), pl.ds(side * columns, columns)],
        )
    copy(out_w.at[part(grp_at, half_ref.shape[0])], half_vmem)
    for started in copies:
        started.start()
    plan_copy.wait()
    step_ratio = plan_ratio(plan_smem, width)
    for block in range(blocks):
        for shard in range(2):
            copies[2 * block + shard].wait()
            taylor_rows(
                held_ref.at[:, :, pl.ds(shard * width, width)],
                made_ref.at[pl.ds(shard * rows, rows)],
                step_ratio,
                block * step,
                (block + 1) * step,
            )
            at = pl.ds(shard * rows + block * step, step)
            copy(made_ref.at[at], packed_ref.at[at])
            copies[-1].start()
    audio_at = pl.ds(2 * rows, audio_ref.shape[0])
    stages = (
        (2, made_ref.at[audio_at], packed_ref.at[audio_at]),
        (3, other_vmem, other_ref),
        (1, half_vmem, half_ref),
    )
    at = 2 * blocks
    for count, source, target in stages:
        for arriving in copies[at : at + count]:
            arriving.wait()
        at += count
        copy(source, target)
        copies[-1].start()
    for leaving in copies[at:]:
        leaving.wait()


def weight_body(align_ref, kv_ref, query_ref, other_ref, own_ref, *piece_refs):
    seq_at, rep_at, grp_at = (lax.axis_index(name) for name in ("seq", "rep", "grp"))
    kv_half, query_half = kv_ref.shape[0] // 2, query_ref.shape[0] // 2
    kv_rows, query_rows = kv_half // 2, query_half // 2
    fold = query_rows // 2

    def fill(out_ref, bit, group, kv_at, query_at):
        head = seq_at ^ bit
        width = 2 * HEAD_DIM
        lanes = pl.ds(pl.multiple_of(head * width, width), width)
        at = pl.ds(pl.multiple_of(rep_at * kv_half + group * kv_rows, kv_rows), kv_rows)
        out_ref[kv_at : kv_at + kv_rows, :width] = kv_ref[at, lanes]
        at = pl.ds(pl.multiple_of(group * kv_rows, kv_rows), kv_rows)
        out_ref[kv_at : kv_at + kv_rows, width:] = other_ref[at, lanes]
        lanes = pl.ds(pl.multiple_of(head * HEAD_DIM, HEAD_DIM), HEAD_DIM)
        other_lanes = pl.ds(
            pl.multiple_of(group * query_ref.shape[1] + head * HEAD_DIM, HEAD_DIM), HEAD_DIM
        )
        for side in range(2):
            first = rep_at * query_half + group * query_rows + side * fold
            at = pl.ds(pl.multiple_of(first, fold), fold)
            to = slice(query_at, query_at + fold)
            out_ref[to, side * width : side * width + HEAD_DIM] = query_ref[at, lanes]
            out_ref[to, side * width + HEAD_DIM : (side + 1) * width] = other_ref[
                kv_half + side * fold : kv_half + (side + 1) * fold, other_lanes
            ]

    for group in range(2):
        fill(own_ref, 0, group, group * kv_rows, kv_half + group * fold)
    for bit, piece_ref in enumerate(piece_refs, 1):
        fill(piece_ref, bit, grp_at, 0, kv_rows)
        spare = (piece_ref.shape[0] - kv_rows - fold, piece_ref.shape[1])
        align = align_ref[...].astype(jnp.float32).astype(piece_ref.dtype)
        row = jnp.concatenate(
            [align, jnp.zeros((1, spare[1] - align.shape[1]), piece_ref.dtype)], axis=1
        )
        piece_ref[kv_rows + fold :, :] = jnp.broadcast_to(row, spare)


def products_body(*refs):
    packed_refs, weight_refs = refs[:8], refs[8:15]
    own_align, align_ref, send_ref, keep_ref, rows_ref, audio_ref, kv_ref, query_ref = refs[15:]
    seq_at, mem_at, grp_at = (lax.axis_index(name) for name in ("seq", "mem", "grp"))
    rows, audio_rows = rows_ref.shape[0] // 4, audio_ref.shape[0] // 4
    depth, lane = rows_ref.shape[1] // 4, audio_ref.shape[1] // 4
    for at, packed_ref in enumerate(packed_refs):
        slot, mem = divmod(at, 2)
        for part in range(2):
            shard = 2 * (mem_at ^ mem) + part
            lanes = pl.ds(pl.multiple_of(shard * depth, depth), depth)
            rows_ref[slot * rows : (slot + 1) * rows, lanes] = packed_ref[
                part * rows : (part + 1) * rows, :
            ]
            lanes = pl.ds(pl.multiple_of(shard * lane, lane), lane)
            audio_ref[slot * audio_rows : (slot + 1) * audio_rows, lanes] = packed_ref[
                2 * rows :, part * lane : (part + 1) * lane
            ]
    kv_half, fold = depth // 2, lane // 4
    width = query_ref.shape[1]

    def place(piece_ref, shard, group, kv_at, query_at):
        to = pl.ds(pl.multiple_of((2 * shard + group) * kv_half, kv_half), kv_half)
        kv_ref[to, :] = piece_ref[kv_at : kv_at + kv_half, :]
        for side in range(2):
            to = pl.ds(pl.multiple_of((4 * shard + 2 * group + side) * fold, fold), fold)
            query_ref[to, :] = piece_ref[
                query_at : query_at + fold, side * width : (side + 1) * width
            ]

    for group in range(2):
        place(weight_refs[0], seq_at, group, group * kv_half, 2 * kv_half + group * fold)
    for bit in range(1, 4):
        place(weight_refs[2 * bit - 1], seq_at ^ bit, grp_at, 0, kv_half)
        place(weight_refs[2 * bit], seq_at ^ bit, 1 - grp_at, 0, kv_half)
        align_ref[bit] = weight_refs[2 * bit - 1][kv_half + fold :, : align_ref.shape[2]]
    align_ref[0] = jnp.broadcast_to(
        own_align[...].astype(jnp.float32).astype(align_ref.dtype), align_ref.shape[1:]
    )

    count = 4 * rows
    columns = keep_ref.shape[1]
    total = jnp.dot(rows_ref[...], kv_ref[...], preferred_element_type=jnp.float32)
    keep_ref[:count, :] = total[:, :columns]
    send_ref[:count, :] = total[:, columns:]
    total = jnp.dot(audio_ref[...], query_ref[...], preferred_element_type=jnp.float32)
    folded = 2 * audio_rows
    for side in range(2):
        at = slice(side * folded, (side + 1) * folded)
        to = slice(side * HEAD_DIM, (side + 1) * HEAD_DIM)
        keep_ref[count:, to] = total[at, :HEAD_DIM]
        send_ref[count:, to] = total[at, HEAD_DIM:]


def attend(queries, kv_ref, frames_ref, align):
    scores = lax.dot_general(
        queries,
        kv_ref[:, :HEAD_DIM],
        (((1,), (1,)), ((), ())),
        preferred_element_type=jnp.float32,
    ) * (1.0 / HEAD_DIM**0.5)
    scores = scores - SLOPE * jnp.abs(frames_ref[...] - align) / FRAMES
    exp_terms = jnp.exp(scores - jnp.max(scores, axis=1, keepdims=True))
    weighted = jnp.dot(
        exp_terms.astype(jnp.bfloat16), kv_ref[:, HEAD_DIM:], preferred_element_type=jnp.float32
    )
    return (weighted / jnp.sum(exp_terms, axis=1, keepdims=True)).astype(jnp.bfloat16)


def attention_body(frames_ref, align_ref, keep_ref, came_ref, *refs):
    *out_refs, kv_ref, query_ref = refs
    count, audio_rows = kv_ref.shape[0], query_ref.shape[1]

    def summed(rows, columns=slice(None)):
        return (keep_ref[rows, columns] + came_ref[rows, columns]).astype(jnp.bfloat16)

    kv_ref[...] = summed(slice(0, count))
    for slot in range(4):
        side, half = divmod(slot, 2)
        query_ref[slot] = summed(
            slice(count + half * audio_rows, count + (half + 1) * audio_rows),
            slice(side * HEAD_DIM, (side + 1) * HEAD_DIM),
        )
    for bit, out_ref in enumerate(out_refs):
        align = align_ref[bit].astype(jnp.float32)[:8].T[:, :1]
        out_ref[...] = attend(query_ref[bit], kv_ref, frames_ref, align)


def out_body(*refs):
    piece_refs, (audio_ref, own_w, partner_w, *part_refs) = refs[:4], refs[4:11]
    send_ref, keep_ref, heads_ref, weight_ref, residual_ref, sems = refs[11:]
    seq_at, grp_at = lax.axis_index("seq"), lax.axis_index("grp")
    place = lax.axis_index("mem") * 2 + lax.axis_index("rep")
    copy = pltpu.make_async_copy(own_w, weight_ref.at[0], sems.at[0])
    copy.start()
    width = residual_ref.shape[1]
    columns = pl.ds(pl.multiple_of(place * width, width), width)
    residual_copy = pltpu.make_async_copy(audio_ref.at[:, columns], residual_ref, sems.at[1])
    residual_copy.start()
    for bit, piece_ref in enumerate(piece_refs):
        heads_ref[seq_at ^ bit] = piece_ref[...]
    heads = jnp.concatenate([heads_ref[head] for head in range(heads_ref.shape[0])], axis=1)
    depth = part_refs[0].shape[0]
    mine = pl.ds(pl.multiple_of(grp_at * depth, depth), depth)
    rest = pl.ds(pl.multiple_of((1 - grp_at) * depth, depth), depth)
    for bit in range(2):
        weight_ref[1 + bit, mine] = part_refs[2 * bit][...]
        weight_ref[1 + bit, rest] = part_refs[2 * bit + 1][...]
    for bit in (1, 2, 3, 0):
        if bit == 0:
            copy.wait()
        slot = seq_at ^ bit ^ place
        weight = partner_w[...] if bit == 1 else weight_ref[max(bit - 1, 0)]
        value = jnp.dot(heads, weight, preferred_element_type=jnp.float32)

        @pl.when(slot % 2 == 1)
        def _():
            send_ref[slot // 2] = value.astype(send_ref.dtype)

        @pl.when(slot % 2 == 0)
        def _():
            keep_ref[slot // 2] = value

    residual_copy.wait()
    keep_ref[0] += residual_ref[...].astype(jnp.float32)


def by_head(video_cache, plan, alignment, audio_tokens, kv_weight, query_weight, out_weight):
    seq_size = lax.axis_size("seq")
    seq_at = lax.axis_index("seq")
    video_rows = video_cache.shape[1]
    audio_rows = audio_tokens.shape[0]
    half_depth, width = kv_weight.shape[0] // 2, 2 * HEAD_DIM
    query_quarter = query_weight.shape[0] // 4

    def bfloat(*shape):
        return jax.ShapeDtypeStruct(shape, jnp.bfloat16)

    packed, other, out_half = kernel_call(
        first_body,
        [
            bfloat(2 * video_rows + audio_rows, half_depth),
            bfloat(half_depth + query_quarter, kv_weight.shape[1]),
            bfloat(out_weight.shape[0] // 2, out_weight.shape[1]),
        ],
        [plan, video_cache, audio_tokens, kv_weight, query_weight, out_weight],
        scratch=[
            pltpu.VMEM((3, video_rows, 2 * half_depth), jnp.bfloat16),
            pltpu.VMEM((2 * video_rows + audio_rows, half_depth), jnp.bfloat16),
            pltpu.VMEM((half_depth + query_quarter, kv_weight.shape[1]), jnp.bfloat16),
            pltpu.VMEM((out_weight.shape[0] // 2, out_weight.shape[1]), jnp.bfloat16),
            pltpu.SMEM(plan.shape, jnp.int32),
            pltpu.SemaphoreType.DMA((26,)),
        ],
        loose_in=(0, 1, 2, 3, 4, 5),
        loose_out=(0, 1, 2),
        limit=61,
    )

    tokens = [packed, swap(packed, "seq", 1), swap(packed, "seq", 2)]
    across = [swap(packed, "mem", 1)]
    other = swap(other, "rep", 1)
    rows = half_depth // 2 + query_quarter // 2
    weight_own, *pieces = kernel_call(
        weight_body,
        [bfloat(2 * rows, 2 * width)] + [bfloat(rows + 16, 2 * width)] * 3,
        [alignment[None], kv_weight, query_weight, other],
        limit=4,
    )
    pieces[0] = swap(pieces[0], "seq", 1)
    tokens[1], tokens[2], across[0], *pieces = lax.optimization_barrier(
        (tokens[1], tokens[2], across[0], *pieces)
    )

    tokens.append(swap(tokens[2], "seq", 1))
    across += [swap(tokens[1], "mem", 1), swap(tokens[2], "mem", 1)]
    pieces[1:] = [swap(piece, "seq", bit) for bit, piece in enumerate(pieces[1:], 2)]
    rest = [swap(pieces[0], "grp", 1)]
    tokens[3], across[1], across[2], pieces[1], pieces[2], rest[0], out_half = (
        lax.optimization_barrier(
            (tokens[3], across[1], across[2], pieces[1], pieces[2], rest[0], out_half)
        )
    )

    across.append(swap(tokens[3], "mem", 1))
    rest += [swap(piece, "grp", 1) for piece in pieces[1:]]
    out_partner, out_third = swap(out_weight, "seq", 1), swap(out_half, "seq", 2)
    weights = [weight_own]
    for piece, other in zip(pieces, rest):
        weights += [piece, other]
    rows = seq_size * (video_rows + audio_rows // 2)
    sums = jax.ShapeDtypeStruct((rows, width), jnp.float32)
    aligns, send, keep = kernel_call(
        products_body,
        [bfloat(4, 16, audio_rows), sums, sums],
        [value for pair in zip(tokens, across) for value in pair] + weights + [alignment[None]],
        after=(out_partner, out_third),
        scratch=[
            pltpu.VMEM((seq_size * video_rows, 4 * half_depth), jnp.bfloat16),
            pltpu.VMEM((seq_size * audio_rows, 8 * query_quarter), jnp.bfloat16),
            pltpu.VMEM((4 * half_depth, 2 * width), jnp.bfloat16),
            pltpu.VMEM((8 * query_quarter, width), jnp.bfloat16),
        ],
        limit=15,
    )
    out_fourth, third_rest = swap(out_third, "seq", 1), swap(out_third, "grp", 1)
    came = swap(send, "rep", 1)

    span = video_rows * seq_size
    blocks = jnp.stack([seq_at, seq_at ^ 1, seq_at ^ 2, seq_at ^ 3])
    positions = blocks[:, None] * video_rows + jnp.arange(video_rows, dtype=jnp.int32)[None, :]
    frames_video = (positions.reshape(1, span) * FRAMES // span).astype(jnp.float32)
    own_piece, near_piece, far_piece, farther_piece = kernel_call(
        attention_body,
        [bfloat(audio_rows, HEAD_DIM)] * 4,
        [frames_video, aligns, keep, came],
        scratch=[
            pltpu.VMEM((span, width), jnp.bfloat16),
            pltpu.VMEM((seq_size, audio_rows, HEAD_DIM), jnp.bfloat16),
        ],
        limit=9,
    )
    out_fourth, own_piece = lax.optimization_barrier((out_fourth, own_piece))
    fourth_rest = swap(out_fourth, "grp", 1)
    far_piece = swap(far_piece, "seq", 2)
    farther_piece = swap(farther_piece, "seq", 3)
    near_piece = swap(near_piece, "seq", 1)

    columns = out_weight.shape[1]
    weights = [out_weight, out_partner, out_third, third_rest, out_fourth, fourth_rest]
    send, keep = kernel_call(
        out_body,
        [
            jax.ShapeDtypeStruct((2, audio_rows, columns), jnp.bfloat16),
            jax.ShapeDtypeStruct((2, audio_rows, columns), jnp.float32),
        ],
        [own_piece, near_piece, far_piece, farther_piece, audio_tokens, *weights],
        scratch=[
            pltpu.VMEM((seq_size, audio_rows, HEAD_DIM), jnp.bfloat16),
            pltpu.VMEM((3, *out_weight.shape), jnp.bfloat16),
            pltpu.VMEM((audio_rows, columns), jnp.bfloat16),
            pltpu.SemaphoreType.DMA((2,)),
        ],
        loose_in=(4, 5),
        limit=7,
    )
    came = swap(send, "rep", 1)
    across = swap((keep[1] + came[1].astype(jnp.float32)).astype(jnp.bfloat16), "mem", 1)
    own_part = taylor(video_cache, plan, 2 * half_depth)
    audio_output = (
        keep[0] + came[0].astype(jnp.float32) + across.astype(jnp.float32)
    ).astype(jnp.bfloat16)
    return (own_part, audio_output)


def solution(mesh):
    sizes = dict(mesh.shape)
    square = (sizes["grp"], sizes["seq"], sizes["mem"], sizes["rep"]) == (2, 4, 2, 2)

    def on_device(*arrays):
        heads = arrays[5].shape[1] // HEAD_DIM
        return (by_head if square and heads == sizes["seq"] else general)(*arrays)

    return jax.shard_map(
        on_device,
        mesh=mesh,
        in_specs=(
            P(None, ("grp", "seq"), "mem"),
            P("grp"),
            P(("grp", "seq")),
            P(("grp", "seq"), None),
            P("seq", ("mem", "rep")),
            P("seq", ("mem", "rep")),
            P(("mem", "rep"), "seq"),
        ),
        out_specs=(P(("grp", "seq"), "mem"), P(("grp", "seq"), ("mem", "rep"))),
        check_vma=False,
    )
```

```python
import math

import jax
import jax.numpy as jnp
from jax import lax
from jax.experimental import pallas as pl
from jax.experimental.pallas import tpu as pltpu
from jax.sharding import PartitionSpec as P

HEAD_DIM = 128
FRAMES = 24


SLOPE = 4.0


def taylor_ratio(plan):
    history = plan.shape[0]
    step_ids = jnp.arange(history, dtype=jnp.int32)
    marked = step_ids * plan
    last_fresh = jnp.max(marked)
    prior_fresh = jnp.max(jnp.where(step_ids < last_fresh, marked, 0))
    return (history - last_fresh).astype(jnp.float32) / (last_fresh - prior_fresh).astype(
        jnp.float32
    )


def combine(orders, step_ratio):
    values = orders.astype(jnp.float32)
    return (values[0] + step_ratio * values[1] + 0.5 * step_ratio * step_ratio * values[2]).astype(
        jnp.bfloat16
    )


def general(video_cache, plan, alignment, audio_tokens, kv_weight, query_weight, out_weight):
    step_ratio = taylor_ratio(plan)
    own_part = combine(video_cache, step_ratio)
    features_all = lax.all_gather(own_part, "mem", axis=1, tiled=True)
    video_rows = features_all.shape[0]
    kv_local = jnp.dot(
        features_all,
        lax.all_gather(kv_weight, "seq", axis=0, tiled=True),
        preferred_element_type=jnp.float32,
    )
    head_size = HEAD_DIM
    local_heads = query_weight.shape[1] // head_size
    kv_local = kv_local.astype(jnp.bfloat16).reshape(video_rows, local_heads, 2, head_size)
    key_rows = kv_local[:, :, 0, :]
    value_rows = kv_local[:, :, 1, :]
    query_full, out_full = (
        lax.all_gather(query_weight, "seq", axis=0, tiled=True),
        lax.all_gather(out_weight, "seq", axis=1, tiled=True),
    )
    audio_rows = audio_tokens.shape[0]
    queries = jnp.dot(audio_tokens, query_full, preferred_element_type=jnp.float32).astype(
        jnp.bfloat16
    )
    queries = queries.reshape(audio_rows, local_heads, head_size)
    scale = 1.0 / head_size**0.5
    span = video_rows * lax.axis_size("seq")
    initial = (
        jnp.full((local_heads, audio_rows), -1e30, jnp.float32),
        jnp.zeros((local_heads, audio_rows), jnp.float32),
        jnp.zeros((local_heads, audio_rows, head_size), jnp.float32),
    )
    key_piece = lax.all_gather(key_rows, "seq", axis=0, tiled=True)
    value_piece = lax.all_gather(value_rows, "seq", axis=0, tiled=True)
    row_count = key_piece.shape[0]
    block_len = math.gcd(row_count, 1024)

    def advance(block_index, carried):
        row_max, row_sum, weighted = carried
        key_block = lax.dynamic_slice_in_dim(key_piece, block_index * block_len, block_len, 0)
        value_block = lax.dynamic_slice_in_dim(value_piece, block_index * block_len, block_len, 0)
        positions = block_index * block_len + jnp.arange(block_len, dtype=jnp.int32)
        frames_video = positions * FRAMES // span
        distance_bias = (
            -SLOPE
            * jnp.abs(frames_video[None, :] - alignment[:, None]).astype(jnp.float32)
            / FRAMES
        )
        scores = (
            jnp.einsum("qhd,khd->hqk", queries, key_block, preferred_element_type=jnp.float32)
            * scale
        )
        scores = scores + distance_bias[None]
        new_max = jnp.maximum(row_max, jnp.max(scores, axis=2))
        rescale = jnp.exp(row_max - new_max)
        exp_terms = jnp.exp(scores - new_max[:, :, None])
        row_sum = row_sum * rescale + jnp.sum(exp_terms, axis=2)
        weighted = weighted * rescale[:, :, None] + jnp.einsum(
            "hqk,khd->hqd",
            exp_terms.astype(jnp.bfloat16),
            value_block,
            preferred_element_type=jnp.float32,
        )
        return (new_max, row_sum, weighted)

    row_max, row_sum, weighted = lax.fori_loop(0, row_count // block_len, advance, initial)
    attended = (weighted / row_sum[:, :, None]).astype(jnp.bfloat16)
    attended = jnp.transpose(attended, (1, 0, 2)).reshape(audio_rows, local_heads * head_size)
    partial_update = jnp.dot(attended, out_full, preferred_element_type=jnp.float32)
    update = lax.psum_scatter(
        partial_update.astype(jnp.bfloat16), ("mem", "rep"), scatter_dimension=1, tiled=True
    ).astype(jnp.float32)
    own_columns = update.shape[1]
    residual = lax.dynamic_slice_in_dim(
        audio_tokens, lax.axis_index(("mem", "rep")) * own_columns, own_columns, 1
    )
    audio_output = (residual.astype(jnp.float32) + update).astype(jnp.bfloat16)
    return (own_part, audio_output)


def swap(value, axis, bit):
    size = lax.axis_size(axis)
    return lax.ppermute(value, axis, [(i, i ^ bit) for i in range(size)])


VMEM = pl.BlockSpec(memory_space=pltpu.VMEM)
SMEM = pl.BlockSpec(memory_space=pltpu.SMEM)
ANY = pl.BlockSpec(memory_space=pl.ANY)
HBM = pl.BlockSpec(memory_space=pltpu.HBM)


def kernel_call(body, outs, ins, after=(), scratch=(), smem=(), loose_in=(), loose_out=(), limit=14):
    def whole(*refs):
        body(*refs[: len(ins)], *refs[len(ins) + len(after) :])

    spots = [SMEM if i in smem else HBM if i in loose_in else VMEM for i in range(len(ins))]
    return pl.pallas_call(
        whole,
        out_shape=outs,
        in_specs=spots + [ANY] * len(after),
        out_specs=[HBM if i in loose_out else VMEM for i in range(len(outs))],
        scratch_shapes=scratch,
        compiler_params=pltpu.CompilerParams(vmem_limit_bytes=limit * 2**20),
    )(*ins, *after)


def plan_ratio(plan_ref, columns):
    history = plan_ref.shape[0]
    last_fresh, prior_fresh = jnp.int32(0), jnp.int32(0)
    for step in range(history):
        fresh = plan_ref[step] == 1
        prior_fresh = jnp.where(fresh, last_fresh, prior_fresh)
        last_fresh = jnp.where(fresh, step, last_fresh)
    ahead = jnp.full((1, columns), history - last_fresh, jnp.int32).astype(jnp.float32)
    apart = jnp.full((1, columns), last_fresh - prior_fresh, jnp.int32).astype(jnp.float32)
    return ahead / apart


def taylor_rows(cache_ref, out_ref, step_ratio, first, last):
    half_square = 0.5 * step_ratio * step_ratio
    for at in range(first, last, 16):
        terms = [cache_ref[order, at : at + 16, :].astype(jnp.float32) for order in range(3)]
        out_ref[at : at + 16, :] = (
            terms[0] + step_ratio * terms[1] + half_square * terms[2]
        ).astype(jnp.bfloat16)


def taylor_body(plan_ref, cache_ref, out_ref):
    rows, columns = out_ref.shape
    taylor_rows(cache_ref, out_ref, plan_ratio(plan_ref, columns), 0, rows)


def taylor(video_cache, plan, width):
    orders, rows, columns = video_cache.shape
    return pl.pallas_call(
        taylor_body,
        out_shape=jax.ShapeDtypeStruct((rows, columns), jnp.bfloat16),
        grid=(columns // width,),
        in_specs=[SMEM, pl.BlockSpec((orders, rows, width), lambda i: (0, 0, i))],
        out_specs=pl.BlockSpec((rows, width), lambda i: (0, i)),
        compiler_params=pltpu.CompilerParams(vmem_limit_bytes=6 * 2**20),
    )(plan, video_cache)


def first_body(
    plan_ref,
    cache_ref,
    audio_ref,
    kv_ref,
    query_ref,
    out_w,
    packed_ref,
    other_ref,
    half_ref,
    held_ref,
    made_ref,
    other_vmem,
    half_vmem,
    plan_smem,
    sems,
):
    rep_at, mem_at, grp_at = (lax.axis_index(name) for name in ("rep", "mem", "grp"))
    rows, width = held_ref.shape[1:]
    width = width // 2
    copies = []

    def copy(source, target):
        copies.append(pltpu.make_async_copy(source, target, sems.at[len(copies)]))

    def part(index, size):
        return pl.ds(pl.multiple_of(index * size, size), size)

    plan_copy = pltpu.make_async_copy(plan_ref, plan_smem, sems.at[25])
    plan_copy.start()
    blocks = 4
    step = rows // blocks
    for block in range(blocks):
        at = pl.ds(block * step, step)
        for shard in range(2):
            copy(
                cache_ref.at[:, at, part(2 * shard + rep_at, width)],
                held_ref.at[:, at, pl.ds(shard * width, width)],
            )
    lane = width // 2
    for shard in range(2):
        copy(
            audio_ref.at[:, part(2 * (2 * mem_at + shard) + rep_at, lane)],
            made_ref.at[pl.ds(2 * rows, audio_ref.shape[0]), pl.ds(shard * lane, lane)],
        )
    depth, columns = kv_ref.shape[0] // 2, query_ref.shape[1]
    copy(kv_ref.at[part(1 - rep_at, depth)], other_vmem.at[pl.ds(0, depth)])
    quarter = query_ref.shape[0] // 4
    for side in range(2):
        copy(
            query_ref.at[part(2 * (1 - rep_at) + side, quarter)],
            other_vmem.at[pl.ds(depth, quarter), pl.ds(side * columns, columns)],
        )
    copy(out_w.at[part(grp_at, half_ref.shape[0])], half_vmem)
    for started in copies:
        started.start()
    plan_copy.wait()
    step_ratio = plan_ratio(plan_smem, width)
    for block in range(blocks):
        for shard in range(2):
            copies[2 * block + shard].wait()
            taylor_rows(
                held_ref.at[:, :, pl.ds(shard * width, width)],
                made_ref.at[pl.ds(shard * rows, rows)],
                step_ratio,
                block * step,
                (block + 1) * step,
            )
            at = pl.ds(shard * rows + block * step, step)
            copy(made_ref.at[at], packed_ref.at[at])
            copies[-1].start()
    audio_at = pl.ds(2 * rows, audio_ref.shape[0])
    stages = (
        (2, made_ref.at[audio_at], packed_ref.at[audio_at]),
        (3, other_vmem, other_ref),
        (1, half_vmem, half_ref),
    )
    at = 2 * blocks
    for count, source, target in stages:
        for arriving in copies[at : at + count]:
            arriving.wait()
        at += count
        copy(source, target)
        copies[-1].start()
    for leaving in copies[at:]:
        leaving.wait()


def weight_body(align_ref, kv_ref, query_ref, other_ref, own_ref, *piece_refs):
    seq_at, rep_at, grp_at = (lax.axis_index(name) for name in ("seq", "rep", "grp"))
    kv_half, query_half = kv_ref.shape[0] // 2, query_ref.shape[0] // 2
    kv_rows, query_rows = kv_half // 2, query_half // 2
    fold = query_rows // 2

    def fill(out_ref, bit, group, kv_at, query_at):
        head = seq_at ^ bit
        width = 2 * HEAD_DIM
        lanes = pl.ds(pl.multiple_of(head * width, width), width)
        at = pl.ds(pl.multiple_of(rep_at * kv_half + group * kv_rows, kv_rows), kv_rows)
        out_ref[kv_at : kv_at + kv_rows, :width] = kv_ref[at, lanes]
        at = pl.ds(pl.multiple_of(group * kv_rows, kv_rows), kv_rows)
        out_ref[kv_at : kv_at + kv_rows, width:] = other_ref[at, lanes]
        lanes = pl.ds(pl.multiple_of(head * HEAD_DIM, HEAD_DIM), HEAD_DIM)
        other_lanes = pl.ds(
            pl.multiple_of(group * query_ref.shape[1] + head * HEAD_DIM, HEAD_DIM), HEAD_DIM
        )
        for side in range(2):
            first = rep_at * query_half + group * query_rows + side * fold
            at = pl.ds(pl.multiple_of(first, fold), fold)
            to = slice(query_at, query_at + fold)
            out_ref[to, side * width : side * width + HEAD_DIM] = query_ref[at, lanes]
            out_ref[to, side * width + HEAD_DIM : (side + 1) * width] = other_ref[
                kv_half + side * fold : kv_half + (side + 1) * fold, other_lanes
            ]

    for group in range(2):
        fill(own_ref, 0, group, group * kv_rows, kv_half + group * fold)
    for bit, piece_ref in enumerate(piece_refs, 1):
        fill(piece_ref, bit, grp_at, 0, kv_rows)
        spare = (piece_ref.shape[0] - kv_rows - fold, piece_ref.shape[1])
        align = align_ref[...].astype(jnp.float32).astype(piece_ref.dtype)
        row = jnp.concatenate(
            [align, jnp.zeros((1, spare[1] - align.shape[1]), piece_ref.dtype)], axis=1
        )
        piece_ref[kv_rows + fold :, :] = jnp.broadcast_to(row, spare)


def products_body(*refs):
    packed_refs, weight_refs = refs[:8], refs[8:15]
    own_align, near_align, align_ref, send_ref, keep_ref, rows_ref, audio_ref, kv_ref, query_ref = refs[15:]
    seq_at, mem_at, grp_at = (lax.axis_index(name) for name in ("seq", "mem", "grp"))
    rows, audio_rows = rows_ref.shape[0] // 4, audio_ref.shape[0] // 4
    depth, lane = rows_ref.shape[1] // 4, audio_ref.shape[1] // 4
    for at, packed_ref in enumerate(packed_refs):
        slot, mem = divmod(at, 2)
        for part in range(2):
            shard = 2 * (mem_at ^ mem) + part
            lanes = pl.ds(pl.multiple_of(shard * depth, depth), depth)
            rows_ref[slot * rows : (slot + 1) * rows, lanes] = packed_ref[
                part * rows : (part + 1) * rows, :
            ]
            lanes = pl.ds(pl.multiple_of(shard * lane, lane), lane)
            audio_ref[slot * audio_rows : (slot + 1) * audio_rows, lanes] = packed_ref[
                2 * rows :, part * lane : (part + 1) * lane
            ]
    kv_half, fold = depth // 2, lane // 4
    width = query_ref.shape[1]

    def place(piece_ref, shard, group, kv_at, query_at):
        to = pl.ds(pl.multiple_of((2 * shard + group) * kv_half, kv_half), kv_half)
        kv_ref[to, :] = piece_ref[kv_at : kv_at + kv_half, :]
        for side in range(2):
            to = pl.ds(pl.multiple_of((4 * shard + 2 * group + side) * fold, fold), fold)
            query_ref[to, :] = piece_ref[
                query_at : query_at + fold, side * width : (side + 1) * width
            ]

    for group in range(2):
        place(weight_refs[0], seq_at, group, group * kv_half, 2 * kv_half + group * fold)
    for bit in range(1, 4):
        place(weight_refs[2 * bit - 1], seq_at ^ bit, grp_at, 0, kv_half)
        place(weight_refs[2 * bit], seq_at ^ bit, 1 - grp_at, 0, kv_half)
        if bit > 1:
            align_ref[bit] = weight_refs[2 * bit - 1][kv_half + fold :, : align_ref.shape[2]]
    align_ref[1] = near_align[...].astype(align_ref.dtype)
    align_ref[0] = jnp.broadcast_to(
        own_align[...].astype(jnp.float32).astype(align_ref.dtype), align_ref.shape[1:]
    )

    count = 4 * rows
    columns = keep_ref.shape[1]
    total = jnp.dot(rows_ref[...], kv_ref[...], preferred_element_type=jnp.float32)
    keep_ref[:count, :] = total[:, :columns]
    send_ref[:count, :] = total[:, columns:]
    total = jnp.dot(audio_ref[...], query_ref[...], preferred_element_type=jnp.float32)
    folded = 2 * audio_rows
    for side in range(2):
        at = slice(side * folded, (side + 1) * folded)
        to = slice(side * HEAD_DIM, (side + 1) * HEAD_DIM)
        keep_ref[count:, to] = total[at, :HEAD_DIM]
        send_ref[count:, to] = total[at, HEAD_DIM:]


def attend(queries, kv_ref, frames_ref, align):
    scores = lax.dot_general(
        queries,
        kv_ref[:, :HEAD_DIM],
        (((1,), (1,)), ((), ())),
        preferred_element_type=jnp.float32,
    ) * (1.0 / HEAD_DIM**0.5)
    scores = scores - SLOPE * jnp.abs(frames_ref[...] - align) / FRAMES
    exp_terms = jnp.exp(scores - jnp.max(scores, axis=1, keepdims=True))
    weighted = jnp.dot(
        exp_terms.astype(jnp.bfloat16), kv_ref[:, HEAD_DIM:], preferred_element_type=jnp.float32
    )
    return (weighted / jnp.sum(exp_terms, axis=1, keepdims=True)).astype(jnp.bfloat16)


def attention_body(frames_ref, align_ref, keep_ref, came_ref, *refs):
    *out_refs, kv_ref, query_ref = refs
    count, audio_rows = kv_ref.shape[0], query_ref.shape[1]

    def summed(rows, columns=slice(None)):
        return (keep_ref[rows, columns] + came_ref[rows, columns]).astype(jnp.bfloat16)

    kv_ref[...] = summed(slice(0, count))
    for slot in range(4):
        side, half = divmod(slot, 2)
        query_ref[slot] = summed(
            slice(count + half * audio_rows, count + (half + 1) * audio_rows),
            slice(side * HEAD_DIM, (side + 1) * HEAD_DIM),
        )
    for bit, out_ref in enumerate(out_refs):
        align = align_ref[bit].astype(jnp.float32)[:8].T[:, :1]
        out_ref[...] = attend(query_ref[bit], kv_ref, frames_ref, align)


def out_body(*refs):
    piece_refs, (audio_ref, own_w, *part_refs) = refs[:4], refs[4:12]
    send_ref, keep_ref, heads_ref, weight_ref, residual_ref, sems = refs[12:]
    seq_at, grp_at = lax.axis_index("seq"), lax.axis_index("grp")
    place = lax.axis_index("mem") * 2 + lax.axis_index("rep")
    copy = pltpu.make_async_copy(own_w, weight_ref.at[0], sems.at[0])
    copy.start()
    width = residual_ref.shape[1]
    columns = pl.ds(pl.multiple_of(place * width, width), width)
    residual_copy = pltpu.make_async_copy(audio_ref.at[:, columns], residual_ref, sems.at[1])
    residual_copy.start()
    for bit, piece_ref in enumerate(piece_refs):
        heads_ref[seq_at ^ bit] = piece_ref[...]
    heads = jnp.concatenate([heads_ref[head] for head in range(heads_ref.shape[0])], axis=1)
    depth = part_refs[0].shape[0]
    mine = pl.ds(pl.multiple_of(grp_at * depth, depth), depth)
    rest = pl.ds(pl.multiple_of((1 - grp_at) * depth, depth), depth)
    for bit in range(1, 4):
        weight_ref[bit, mine] = part_refs[2 * bit - 2][...]
        weight_ref[bit, rest] = part_refs[2 * bit - 1][...]
    for bit in (1, 2, 3, 0):
        if bit == 0:
            copy.wait()
        slot = seq_at ^ bit ^ place
        value = jnp.dot(heads, weight_ref[bit], preferred_element_type=jnp.float32)

        @pl.when(slot % 2 == 1)
        def _():
            send_ref[slot // 2] = value.astype(send_ref.dtype)

        @pl.when(slot % 2 == 0)
        def _():
            keep_ref[slot // 2] = value

    residual_copy.wait()
    keep_ref[0] += residual_ref[...].astype(jnp.float32)


def by_head(video_cache, plan, alignment, audio_tokens, kv_weight, query_weight, out_weight):
    seq_size = lax.axis_size("seq")
    seq_at = lax.axis_index("seq")
    video_rows = video_cache.shape[1]
    audio_rows = audio_tokens.shape[0]
    half_depth, width = kv_weight.shape[0] // 2, 2 * HEAD_DIM
    query_quarter = query_weight.shape[0] // 4

    def bfloat(*shape):
        return jax.ShapeDtypeStruct(shape, jnp.bfloat16)

    packed, other, out_half = kernel_call(
        first_body,
        [
            bfloat(2 * video_rows + audio_rows, half_depth),
            bfloat(half_depth + query_quarter, kv_weight.shape[1]),
            bfloat(out_weight.shape[0] // 2, out_weight.shape[1]),
        ],
        [plan, video_cache, audio_tokens, kv_weight, query_weight, out_weight],
        scratch=[
            pltpu.VMEM((3, video_rows, 2 * half_depth), jnp.bfloat16),
            pltpu.VMEM((2 * video_rows + audio_rows, half_depth), jnp.bfloat16),
            pltpu.VMEM((half_depth + query_quarter, kv_weight.shape[1]), jnp.bfloat16),
            pltpu.VMEM((out_weight.shape[0] // 2, out_weight.shape[1]), jnp.bfloat16),
            pltpu.SMEM(plan.shape, jnp.int32),
            pltpu.SemaphoreType.DMA((26,)),
        ],
        loose_in=(0, 1, 2, 3, 4, 5),
        loose_out=(0, 1, 2),
        limit=61,
    )

    tokens = [packed, swap(packed, "seq", 1), swap(packed, "seq", 2)]
    across = [swap(packed, "mem", 1)]
    other = swap(other, "rep", 1)
    rows = half_depth // 2 + query_quarter // 2
    weight_own, *pieces = kernel_call(
        weight_body,
        [bfloat(2 * rows, 2 * width)] + [bfloat(rows + 16, 2 * width)] * 3,
        [alignment[None], kv_weight, query_weight, other],
        limit=4,
    )
    pieces = [swap(piece, "seq", bit) for bit, piece in enumerate(pieces, 1)]

    across += [swap(tokens[1], "mem", 1), swap(tokens[2], "mem", 1)]
    near_align = pieces[0][rows:, :audio_rows].astype(jnp.float32)
    tokens[2], near_align = lax.optimization_barrier((tokens[2], near_align))
    tokens.append(swap(tokens[2], "seq", 1))
    pieces[0], across[0], across[1] = lax.optimization_barrier(
        (pieces[0], across[0], across[1])
    )
    rest = [swap(pieces[0], "grp", 1)]
    tokens[3], across[2], rest[0], pieces[1] = lax.optimization_barrier(
        (tokens[3], across[2], rest[0], pieces[1])
    )
    across.append(swap(tokens[3], "mem", 1))
    rest.append(swap(pieces[1], "grp", 1))
    pieces[2], rest[1] = lax.optimization_barrier((pieces[2], rest[1]))
    rest.append(swap(pieces[2], "grp", 1))

    out_half, tokens[3] = lax.optimization_barrier((out_half, tokens[3]))
    out_third, out_partner = swap(out_half, "seq", 2), swap(out_half, "seq", 1)
    weights = [weight_own]
    for piece, other in zip(pieces, rest):
        weights += [piece, other]
    rows = seq_size * (video_rows + audio_rows // 2)
    sums = jax.ShapeDtypeStruct((rows, width), jnp.float32)
    aligns, send, keep = kernel_call(
        products_body,
        [bfloat(4, 16, audio_rows), sums, sums],
        [value for pair in zip(tokens, across) for value in pair] + weights
        + [alignment[None], near_align],
        scratch=[
            pltpu.VMEM((seq_size * video_rows, 4 * half_depth), jnp.bfloat16),
            pltpu.VMEM((seq_size * audio_rows, 8 * query_quarter), jnp.bfloat16),
            pltpu.VMEM((4 * half_depth, 2 * width), jnp.bfloat16),
            pltpu.VMEM((8 * query_quarter, width), jnp.bfloat16),
        ],
        limit=15,
    )
    send, out_third, out_partner = lax.optimization_barrier((send, out_third, out_partner))
    came = swap(send, "rep", 1)
    out_fourth, third_rest = swap(out_third, "seq", 1), swap(out_third, "grp", 1)
    partner_rest = swap(out_partner, "grp", 1)

    span = video_rows * seq_size
    blocks = jnp.stack([seq_at, seq_at ^ 1, seq_at ^ 2, seq_at ^ 3])
    positions = blocks[:, None] * video_rows + jnp.arange(video_rows, dtype=jnp.int32)[None, :]
    frames_video = (positions.reshape(1, span) * FRAMES // span).astype(jnp.float32)
    own_piece, near_piece, far_piece, farther_piece = kernel_call(
        attention_body,
        [bfloat(audio_rows, HEAD_DIM)] * 4,
        [frames_video, aligns, keep, came],
        scratch=[
            pltpu.VMEM((span, width), jnp.bfloat16),
            pltpu.VMEM((seq_size, audio_rows, HEAD_DIM), jnp.bfloat16),
        ],
        limit=9,
    )
    out_fourth, own_piece = lax.optimization_barrier((out_fourth, own_piece))
    fourth_rest = swap(out_fourth, "grp", 1)
    far_piece = swap(far_piece, "seq", 2)
    farther_piece = swap(farther_piece, "seq", 3)
    near_piece = swap(near_piece, "seq", 1)

    columns = out_weight.shape[1]
    weights = [out_weight, out_partner, partner_rest]
    weights += [out_third, third_rest, out_fourth, fourth_rest]
    send, keep = kernel_call(
        out_body,
        [
            jax.ShapeDtypeStruct((2, audio_rows, columns), jnp.bfloat16),
            jax.ShapeDtypeStruct((2, audio_rows, columns), jnp.float32),
        ],
        [own_piece, near_piece, far_piece, farther_piece, audio_tokens, *weights],
        scratch=[
            pltpu.VMEM((seq_size, audio_rows, HEAD_DIM), jnp.bfloat16),
            pltpu.VMEM((seq_size, *out_weight.shape), jnp.bfloat16),
            pltpu.VMEM((audio_rows, columns), jnp.bfloat16),
            pltpu.SemaphoreType.DMA((2,)),
        ],
        loose_in=(4, 5),
        limit=7,
    )
    came = swap(send, "rep", 1)
    across = swap((keep[1] + came[1].astype(jnp.float32)).astype(jnp.bfloat16), "mem", 1)
    own_part = taylor(video_cache, plan, 2 * half_depth)
    audio_output = (
        keep[0] + came[0].astype(jnp.float32) + across.astype(jnp.float32)
    ).astype(jnp.bfloat16)
    return (own_part, audio_output)


def solution(mesh):
    sizes = dict(mesh.shape)
    square = (sizes["grp"], sizes["seq"], sizes["mem"], sizes["rep"]) == (2, 4, 2, 2)

    def on_device(*arrays):
        heads = arrays[5].shape[1] // HEAD_DIM
        return (by_head if square and heads == sizes["seq"] else general)(*arrays)

    return jax.shard_map(
        on_device,
        mesh=mesh,
        in_specs=(
            P(None, ("grp", "seq"), "mem"),
            P("grp"),
            P(("grp", "seq")),
            P(("grp", "seq"), None),
            P("seq", ("mem", "rep")),
            P("seq", ("mem", "rep")),
            P(("mem", "rep"), "seq"),
        ),
        out_specs=(P(("grp", "seq"), "mem"), P(("grp", "seq"), ("mem", "rep"))),
        check_vma=False,
    )
```

```python
import math

import jax
import jax.numpy as jnp
from jax import lax
from jax.experimental import pallas as pl
from jax.experimental.pallas import tpu as pltpu
from jax.sharding import PartitionSpec as P

HEAD_DIM = 128
FRAMES = 24


SLOPE = 4.0


def taylor_ratio(plan):
    history = plan.shape[0]
    step_ids = jnp.arange(history, dtype=jnp.int32)
    marked = step_ids * plan
    last_fresh = jnp.max(marked)
    prior_fresh = jnp.max(jnp.where(step_ids < last_fresh, marked, 0))
    return (history - last_fresh).astype(jnp.float32) / (last_fresh - prior_fresh).astype(
        jnp.float32
    )


def combine(orders, step_ratio):
    values = orders.astype(jnp.float32)
    return (values[0] + step_ratio * values[1] + 0.5 * step_ratio * step_ratio * values[2]).astype(
        jnp.bfloat16
    )


def general(video_cache, plan, alignment, audio_tokens, kv_weight, query_weight, out_weight):
    step_ratio = taylor_ratio(plan)
    own_part = combine(video_cache, step_ratio)
    features_all = lax.all_gather(own_part, "mem", axis=1, tiled=True)
    video_rows = features_all.shape[0]
    kv_local = jnp.dot(
        features_all,
        lax.all_gather(kv_weight, "seq", axis=0, tiled=True),
        preferred_element_type=jnp.float32,
    )
    head_size = HEAD_DIM
    local_heads = query_weight.shape[1] // head_size
    kv_local = kv_local.astype(jnp.bfloat16).reshape(video_rows, local_heads, 2, head_size)
    key_rows = kv_local[:, :, 0, :]
    value_rows = kv_local[:, :, 1, :]
    query_full, out_full = (
        lax.all_gather(query_weight, "seq", axis=0, tiled=True),
        lax.all_gather(out_weight, "seq", axis=1, tiled=True),
    )
    audio_rows = audio_tokens.shape[0]
    queries = jnp.dot(audio_tokens, query_full, preferred_element_type=jnp.float32).astype(
        jnp.bfloat16
    )
    queries = queries.reshape(audio_rows, local_heads, head_size)
    scale = 1.0 / head_size**0.5
    span = video_rows * lax.axis_size("seq")
    initial = (
        jnp.full((local_heads, audio_rows), -1e30, jnp.float32),
        jnp.zeros((local_heads, audio_rows), jnp.float32),
        jnp.zeros((local_heads, audio_rows, head_size), jnp.float32),
    )
    key_piece = lax.all_gather(key_rows, "seq", axis=0, tiled=True)
    value_piece = lax.all_gather(value_rows, "seq", axis=0, tiled=True)
    row_count = key_piece.shape[0]
    block_len = math.gcd(row_count, 1024)

    def advance(block_index, carried):
        row_max, row_sum, weighted = carried
        key_block = lax.dynamic_slice_in_dim(key_piece, block_index * block_len, block_len, 0)
        value_block = lax.dynamic_slice_in_dim(value_piece, block_index * block_len, block_len, 0)
        positions = block_index * block_len + jnp.arange(block_len, dtype=jnp.int32)
        frames_video = positions * FRAMES // span
        distance_bias = (
            -SLOPE
            * jnp.abs(frames_video[None, :] - alignment[:, None]).astype(jnp.float32)
            / FRAMES
        )
        scores = (
            jnp.einsum("qhd,khd->hqk", queries, key_block, preferred_element_type=jnp.float32)
            * scale
        )
        scores = scores + distance_bias[None]
        new_max = jnp.maximum(row_max, jnp.max(scores, axis=2))
        rescale = jnp.exp(row_max - new_max)
        exp_terms = jnp.exp(scores - new_max[:, :, None])
        row_sum = row_sum * rescale + jnp.sum(exp_terms, axis=2)
        weighted = weighted * rescale[:, :, None] + jnp.einsum(
            "hqk,khd->hqd",
            exp_terms.astype(jnp.bfloat16),
            value_block,
            preferred_element_type=jnp.float32,
        )
        return (new_max, row_sum, weighted)

    row_max, row_sum, weighted = lax.fori_loop(0, row_count // block_len, advance, initial)
    attended = (weighted / row_sum[:, :, None]).astype(jnp.bfloat16)
    attended = jnp.transpose(attended, (1, 0, 2)).reshape(audio_rows, local_heads * head_size)
    partial_update = jnp.dot(attended, out_full, preferred_element_type=jnp.float32)
    update = lax.psum_scatter(
        partial_update.astype(jnp.bfloat16), ("mem", "rep"), scatter_dimension=1, tiled=True
    ).astype(jnp.float32)
    own_columns = update.shape[1]
    residual = lax.dynamic_slice_in_dim(
        audio_tokens, lax.axis_index(("mem", "rep")) * own_columns, own_columns, 1
    )
    audio_output = (residual.astype(jnp.float32) + update).astype(jnp.bfloat16)
    return (own_part, audio_output)


def swap(value, axis, bit):
    size = lax.axis_size(axis)
    return lax.ppermute(value, axis, [(i, i ^ bit) for i in range(size)])


VMEM = pl.BlockSpec(memory_space=pltpu.VMEM)
SMEM = pl.BlockSpec(memory_space=pltpu.SMEM)
ANY = pl.BlockSpec(memory_space=pl.ANY)
HBM = pl.BlockSpec(memory_space=pltpu.HBM)


def kernel_call(body, outs, ins, after=(), scratch=(), smem=(), loose_in=(), loose_out=(), limit=14):
    def whole(*refs):
        body(*refs[: len(ins)], *refs[len(ins) + len(after) :])

    spots = [SMEM if i in smem else HBM if i in loose_in else VMEM for i in range(len(ins))]
    return pl.pallas_call(
        whole,
        out_shape=outs,
        in_specs=spots + [ANY] * len(after),
        out_specs=[HBM if i in loose_out else VMEM for i in range(len(outs))],
        scratch_shapes=scratch,
        compiler_params=pltpu.CompilerParams(vmem_limit_bytes=limit * 2**20),
    )(*ins, *after)


def plan_ratio(plan_ref, columns):
    history = plan_ref.shape[0]
    last_fresh, prior_fresh = jnp.int32(0), jnp.int32(0)
    for step in range(history):
        fresh = plan_ref[step] == 1
        prior_fresh = jnp.where(fresh, last_fresh, prior_fresh)
        last_fresh = jnp.where(fresh, step, last_fresh)
    ahead = jnp.full((1, columns), history - last_fresh, jnp.int32).astype(jnp.float32)
    apart = jnp.full((1, columns), last_fresh - prior_fresh, jnp.int32).astype(jnp.float32)
    return ahead / apart


def taylor_rows(cache_ref, out_ref, step_ratio, first, last):
    half_square = 0.5 * step_ratio * step_ratio
    for at in range(first, last, 16):
        terms = [cache_ref[order, at : at + 16, :].astype(jnp.float32) for order in range(3)]
        out_ref[at : at + 16, :] = (
            terms[0] + step_ratio * terms[1] + half_square * terms[2]
        ).astype(jnp.bfloat16)


def taylor_body(plan_ref, cache_ref, out_ref):
    rows, columns = out_ref.shape
    taylor_rows(cache_ref, out_ref, plan_ratio(plan_ref, columns), 0, rows)


def taylor(video_cache, plan, width):
    orders, rows, columns = video_cache.shape
    return pl.pallas_call(
        taylor_body,
        out_shape=jax.ShapeDtypeStruct((rows, columns), jnp.bfloat16),
        grid=(columns // width,),
        in_specs=[SMEM, pl.BlockSpec((orders, rows, width), lambda i: (0, 0, i))],
        out_specs=pl.BlockSpec((rows, width), lambda i: (0, i)),
        compiler_params=pltpu.CompilerParams(vmem_limit_bytes=6 * 2**20),
    )(plan, video_cache)


def first_body(
    plan_ref,
    cache_ref,
    audio_ref,
    kv_ref,
    query_ref,
    out_w,
    packed_ref,
    other_ref,
    half_ref,
    held_ref,
    made_ref,
    other_vmem,
    half_vmem,
    plan_smem,
    sems,
):
    rep_at, mem_at, grp_at = (lax.axis_index(name) for name in ("rep", "mem", "grp"))
    rows, width = held_ref.shape[1:]
    width = width // 2
    copies = []

    def copy(source, target):
        copies.append(pltpu.make_async_copy(source, target, sems.at[len(copies)]))

    def part(index, size):
        return pl.ds(pl.multiple_of(index * size, size), size)

    plan_copy = pltpu.make_async_copy(plan_ref, plan_smem, sems.at[25])
    plan_copy.start()
    blocks = 4
    step = rows // blocks
    for block in range(blocks):
        at = pl.ds(block * step, step)
        for shard in range(2):
            copy(
                cache_ref.at[:, at, part(2 * shard + rep_at, width)],
                held_ref.at[:, at, pl.ds(shard * width, width)],
            )
    lane = width // 2
    for shard in range(2):
        copy(
            audio_ref.at[:, part(2 * (2 * mem_at + shard) + rep_at, lane)],
            made_ref.at[pl.ds(2 * rows, audio_ref.shape[0]), pl.ds(shard * lane, lane)],
        )
    depth, columns = kv_ref.shape[0] // 2, query_ref.shape[1]
    copy(kv_ref.at[part(1 - rep_at, depth)], other_vmem.at[pl.ds(0, depth)])
    quarter = query_ref.shape[0] // 4
    for side in range(2):
        copy(
            query_ref.at[part(2 * (1 - rep_at) + side, quarter)],
            other_vmem.at[pl.ds(depth, quarter), pl.ds(side * columns, columns)],
        )
    copy(out_w.at[part(grp_at, half_ref.shape[0])], half_vmem)
    for started in copies:
        started.start()
    plan_copy.wait()
    step_ratio = plan_ratio(plan_smem, width)
    for block in range(blocks):
        for shard in range(2):
            copies[2 * block + shard].wait()
            taylor_rows(
                held_ref.at[:, :, pl.ds(shard * width, width)],
                made_ref.at[pl.ds(shard * rows, rows)],
                step_ratio,
                block * step,
                (block + 1) * step,
            )
            at = pl.ds(shard * rows + block * step, step)
            copy(made_ref.at[at], packed_ref.at[at])
            copies[-1].start()
    audio_at = pl.ds(2 * rows, audio_ref.shape[0])
    stages = (
        (2, made_ref.at[audio_at], packed_ref.at[audio_at]),
        (3, other_vmem, other_ref),
        (1, half_vmem, half_ref),
    )
    at = 2 * blocks
    for count, source, target in stages:
        for arriving in copies[at : at + count]:
            arriving.wait()
        at += count
        copy(source, target)
        copies[-1].start()
    for leaving in copies[at:]:
        leaving.wait()


def weight_body(align_ref, kv_ref, query_ref, other_ref, own_ref, *piece_refs):
    seq_at, rep_at, grp_at = (lax.axis_index(name) for name in ("seq", "rep", "grp"))
    kv_half, query_half = kv_ref.shape[0] // 2, query_ref.shape[0] // 2
    kv_rows, query_rows = kv_half // 2, query_half // 2
    fold = query_rows // 2

    def fill(out_ref, bit, group, kv_at, query_at):
        head = seq_at ^ bit
        width = 2 * HEAD_DIM
        lanes = pl.ds(pl.multiple_of(head * width, width), width)
        at = pl.ds(pl.multiple_of(rep_at * kv_half + group * kv_rows, kv_rows), kv_rows)
        out_ref[kv_at : kv_at + kv_rows, :width] = kv_ref[at, lanes]
        at = pl.ds(pl.multiple_of(group * kv_rows, kv_rows), kv_rows)
        out_ref[kv_at : kv_at + kv_rows, width:] = other_ref[at, lanes]
        lanes = pl.ds(pl.multiple_of(head * HEAD_DIM, HEAD_DIM), HEAD_DIM)
        other_lanes = pl.ds(
            pl.multiple_of(group * query_ref.shape[1] + head * HEAD_DIM, HEAD_DIM), HEAD_DIM
        )
        for side in range(2):
            first = rep_at * query_half + group * query_rows + side * fold
            at = pl.ds(pl.multiple_of(first, fold), fold)
            to = slice(query_at, query_at + fold)
            out_ref[to, side * width : side * width + HEAD_DIM] = query_ref[at, lanes]
            out_ref[to, side * width + HEAD_DIM : (side + 1) * width] = other_ref[
                kv_half + side * fold : kv_half + (side + 1) * fold, other_lanes
            ]

    for group in range(2):
        fill(own_ref, 0, group, group * kv_rows, kv_half + group * fold)
    for bit, piece_ref in enumerate(piece_refs, 1):
        fill(piece_ref, bit, grp_at, 0, kv_rows)
        spare = (piece_ref.shape[0] - kv_rows - fold, piece_ref.shape[1])
        align = align_ref[...].astype(jnp.float32).astype(piece_ref.dtype)
        row = jnp.concatenate(
            [align, jnp.zeros((1, spare[1] - align.shape[1]), piece_ref.dtype)], axis=1
        )
        piece_ref[kv_rows + fold :, :] = jnp.broadcast_to(row, spare)


def products_body(*refs):
    packed_refs, weight_refs = refs[:8], refs[8:15]
    own_align, near_align, align_ref, send_ref, keep_ref, rows_ref, audio_ref, kv_ref, query_ref = refs[15:]
    seq_at, mem_at, grp_at = (lax.axis_index(name) for name in ("seq", "mem", "grp"))
    rows, audio_rows = rows_ref.shape[0] // 4, audio_ref.shape[0] // 4
    depth, lane = rows_ref.shape[1] // 4, audio_ref.shape[1] // 4
    for at, packed_ref in enumerate(packed_refs):
        slot, mem = divmod(at, 2)
        for part in range(2):
            shard = 2 * (mem_at ^ mem) + part
            lanes = pl.ds(pl.multiple_of(shard * depth, depth), depth)
            rows_ref[slot * rows : (slot + 1) * rows, lanes] = packed_ref[
                part * rows : (part + 1) * rows, :
            ]
            lanes = pl.ds(pl.multiple_of(shard * lane, lane), lane)
            audio_ref[slot * audio_rows : (slot + 1) * audio_rows, lanes] = packed_ref[
                2 * rows :, part * lane : (part + 1) * lane
            ]
    kv_half, fold = depth // 2, lane // 4
    width = query_ref.shape[1]

    def place(piece_ref, shard, group, kv_at, query_at):
        to = pl.ds(pl.multiple_of((2 * shard + group) * kv_half, kv_half), kv_half)
        kv_ref[to, :] = piece_ref[kv_at : kv_at + kv_half, :]
        for side in range(2):
            to = pl.ds(pl.multiple_of((4 * shard + 2 * group + side) * fold, fold), fold)
            query_ref[to, :] = piece_ref[
                query_at : query_at + fold, side * width : (side + 1) * width
            ]

    for group in range(2):
        place(weight_refs[0], seq_at, group, group * kv_half, 2 * kv_half + group * fold)
    for bit in range(1, 4):
        place(weight_refs[2 * bit - 1], seq_at ^ bit, grp_at, 0, kv_half)
        place(weight_refs[2 * bit], seq_at ^ bit, 1 - grp_at, 0, kv_half)
        if bit > 1:
            align_ref[bit] = weight_refs[2 * bit - 1][kv_half + fold :, : align_ref.shape[2]]
    align_ref[1] = near_align[...].astype(align_ref.dtype)
    align_ref[0] = jnp.broadcast_to(
        own_align[...].astype(jnp.float32).astype(align_ref.dtype), align_ref.shape[1:]
    )

    count = 4 * rows
    columns = keep_ref.shape[1]
    total = jnp.dot(rows_ref[...], kv_ref[...], preferred_element_type=jnp.float32)
    keep_ref[:count, :] = total[:, :columns]
    send_ref[:count, :] = total[:, columns:]
    total = jnp.dot(audio_ref[...], query_ref[...], preferred_element_type=jnp.float32)
    folded = 2 * audio_rows
    for side in range(2):
        at = slice(side * folded, (side + 1) * folded)
        to = slice(side * HEAD_DIM, (side + 1) * HEAD_DIM)
        keep_ref[count:, to] = total[at, :HEAD_DIM]
        send_ref[count:, to] = total[at, HEAD_DIM:]


def attend(queries, kv_ref, frames_ref, align):
    scores = lax.dot_general(
        queries,
        kv_ref[:, :HEAD_DIM],
        (((1,), (1,)), ((), ())),
        preferred_element_type=jnp.float32,
    ) * (1.0 / HEAD_DIM**0.5)
    scores = scores - SLOPE * jnp.abs(frames_ref[...] - align) / FRAMES
    exp_terms = jnp.exp(scores - jnp.max(scores, axis=1, keepdims=True))
    weighted = jnp.dot(
        exp_terms.astype(jnp.bfloat16), kv_ref[:, HEAD_DIM:], preferred_element_type=jnp.float32
    )
    return (weighted / jnp.sum(exp_terms, axis=1, keepdims=True)).astype(jnp.bfloat16)


def attention_body(frames_ref, align_ref, keep_ref, came_ref, *refs):
    *out_refs, kv_ref, query_ref = refs
    count, audio_rows = kv_ref.shape[0], query_ref.shape[1]

    def summed(rows, columns=slice(None)):
        return (keep_ref[rows, columns] + came_ref[rows, columns]).astype(jnp.bfloat16)

    kv_ref[...] = summed(slice(0, count))
    for slot in range(4):
        side, half = divmod(slot, 2)
        query_ref[slot] = summed(
            slice(count + half * audio_rows, count + (half + 1) * audio_rows),
            slice(side * HEAD_DIM, (side + 1) * HEAD_DIM),
        )
    for bit, out_ref in enumerate(out_refs):
        align = align_ref[bit].astype(jnp.float32)[:8].T[:, :1]
        out_ref[...] = attend(query_ref[bit], kv_ref, frames_ref, align)


def out_body(*refs):
    piece_refs, (audio_ref, own_w, *part_refs) = refs[:4], refs[4:12]
    send_ref, keep_ref, heads_ref, weight_ref, residual_ref, sems = refs[12:]
    seq_at, grp_at = lax.axis_index("seq"), lax.axis_index("grp")
    place = lax.axis_index("mem") * 2 + lax.axis_index("rep")
    copy = pltpu.make_async_copy(own_w, weight_ref.at[0], sems.at[0])
    copy.start()
    width = residual_ref.shape[1]
    columns = pl.ds(pl.multiple_of(place * width, width), width)
    residual_copy = pltpu.make_async_copy(audio_ref.at[:, columns], residual_ref, sems.at[1])
    residual_copy.start()
    for bit, piece_ref in enumerate(piece_refs):
        heads_ref[seq_at ^ bit] = piece_ref[...]
    heads = jnp.concatenate([heads_ref[head] for head in range(heads_ref.shape[0])], axis=1)
    depth = part_refs[0].shape[0]
    mine = pl.ds(pl.multiple_of(grp_at * depth, depth), depth)
    rest = pl.ds(pl.multiple_of((1 - grp_at) * depth, depth), depth)
    for bit in range(1, 4):
        weight_ref[bit, mine] = part_refs[2 * bit - 2][...]
        weight_ref[bit, rest] = part_refs[2 * bit - 1][...]
    for bit in (1, 2, 3, 0):
        if bit == 0:
            copy.wait()
        slot = seq_at ^ bit ^ place
        value = jnp.dot(heads, weight_ref[bit], preferred_element_type=jnp.float32)

        @pl.when(slot % 2 == 1)
        def _():
            send_ref[slot // 2] = value.astype(send_ref.dtype)

        @pl.when(slot % 2 == 0)
        def _():
            keep_ref[slot // 2] = value

    residual_copy.wait()
    keep_ref[0] += residual_ref[...].astype(jnp.float32)


def by_head(video_cache, plan, alignment, audio_tokens, kv_weight, query_weight, out_weight):
    seq_size = lax.axis_size("seq")
    seq_at = lax.axis_index("seq")
    video_rows = video_cache.shape[1]
    audio_rows = audio_tokens.shape[0]
    half_depth, width = kv_weight.shape[0] // 2, 2 * HEAD_DIM
    query_quarter = query_weight.shape[0] // 4

    def bfloat(*shape):
        return jax.ShapeDtypeStruct(shape, jnp.bfloat16)

    packed, other, out_half = kernel_call(
        first_body,
        [
            bfloat(2 * video_rows + audio_rows, half_depth),
            bfloat(half_depth + query_quarter, kv_weight.shape[1]),
            bfloat(out_weight.shape[0] // 2, out_weight.shape[1]),
        ],
        [plan, video_cache, audio_tokens, kv_weight, query_weight, out_weight],
        scratch=[
            pltpu.VMEM((3, video_rows, 2 * half_depth), jnp.bfloat16),
            pltpu.VMEM((2 * video_rows + audio_rows, half_depth), jnp.bfloat16),
            pltpu.VMEM((half_depth + query_quarter, kv_weight.shape[1]), jnp.bfloat16),
            pltpu.VMEM((out_weight.shape[0] // 2, out_weight.shape[1]), jnp.bfloat16),
            pltpu.SMEM(plan.shape, jnp.int32),
            pltpu.SemaphoreType.DMA((26,)),
        ],
        loose_in=(0, 1, 2, 3, 4, 5),
        loose_out=(0, 1, 2),
        limit=61,
    )

    tokens = [packed, swap(packed, "seq", 1), swap(packed, "seq", 2)]
    across = [swap(packed, "mem", 1)]
    other = swap(other, "rep", 1)
    rows = half_depth // 2 + query_quarter // 2
    weight_own, *pieces = kernel_call(
        weight_body,
        [bfloat(2 * rows, 2 * width)] + [bfloat(rows + 16, 2 * width)] * 3,
        [alignment[None], kv_weight, query_weight, other],
        limit=4,
    )
    pieces = [swap(piece, "seq", bit) for bit, piece in enumerate(pieces, 1)]

    across += [swap(tokens[1], "mem", 1), swap(tokens[2], "mem", 1)]
    near_align = pieces[0][rows:, :audio_rows].astype(jnp.float32)
    tokens[2], near_align = lax.optimization_barrier((tokens[2], near_align))
    tokens.append(swap(tokens[2], "seq", 1))
    rest = [swap(pieces[0], "grp", 1)]
    pieces[1], across[0], across[1], rest[0] = lax.optimization_barrier(
        (pieces[1], across[0], across[1], rest[0])
    )
    rest.append(swap(pieces[1], "grp", 1))
    tokens[3], across[2], rest[1] = lax.optimization_barrier((tokens[3], across[2], rest[1]))
    across.append(swap(tokens[3], "mem", 1))
    rest.append(swap(pieces[2], "grp", 1))

    out_half, tokens[3] = lax.optimization_barrier((out_half, tokens[3]))
    out_third, out_partner = swap(out_half, "seq", 2), swap(out_half, "seq", 1)
    weights = [weight_own]
    for piece, other in zip(pieces, rest):
        weights += [piece, other]
    rows = seq_size * (video_rows + audio_rows // 2)
    sums = jax.ShapeDtypeStruct((rows, width), jnp.float32)
    aligns, send, keep = kernel_call(
        products_body,
        [bfloat(4, 16, audio_rows), sums, sums],
        [value for pair in zip(tokens, across) for value in pair] + weights
        + [alignment[None], near_align],
        scratch=[
            pltpu.VMEM((seq_size * video_rows, 4 * half_depth), jnp.bfloat16),
            pltpu.VMEM((seq_size * audio_rows, 8 * query_quarter), jnp.bfloat16),
            pltpu.VMEM((4 * half_depth, 2 * width), jnp.bfloat16),
            pltpu.VMEM((8 * query_quarter, width), jnp.bfloat16),
        ],
        limit=15,
    )
    send, out_third, out_partner = lax.optimization_barrier((send, out_third, out_partner))
    came = swap(send, "rep", 1)
    out_fourth, third_rest = swap(out_third, "seq", 1), swap(out_third, "grp", 1)
    partner_rest = swap(out_partner, "grp", 1)

    span = video_rows * seq_size
    blocks = jnp.stack([seq_at, seq_at ^ 1, seq_at ^ 2, seq_at ^ 3])
    positions = blocks[:, None] * video_rows + jnp.arange(video_rows, dtype=jnp.int32)[None, :]
    frames_video = (positions.reshape(1, span) * FRAMES // span).astype(jnp.float32)
    own_piece, near_piece, far_piece, farther_piece = kernel_call(
        attention_body,
        [bfloat(audio_rows, HEAD_DIM)] * 4,
        [frames_video, aligns, keep, came],
        scratch=[
            pltpu.VMEM((span, width), jnp.bfloat16),
            pltpu.VMEM((seq_size, audio_rows, HEAD_DIM), jnp.bfloat16),
        ],
        limit=9,
    )
    out_fourth, own_piece = lax.optimization_barrier((out_fourth, own_piece))
    fourth_rest = swap(out_fourth, "grp", 1)
    far_piece = swap(far_piece, "seq", 2)
    farther_piece = swap(farther_piece, "seq", 3)
    near_piece = swap(near_piece, "seq", 1)

    columns = out_weight.shape[1]
    weights = [out_weight, out_partner, partner_rest]
    weights += [out_third, third_rest, out_fourth, fourth_rest]
    send, keep = kernel_call(
        out_body,
        [
            jax.ShapeDtypeStruct((2, audio_rows, columns), jnp.bfloat16),
            jax.ShapeDtypeStruct((2, audio_rows, columns), jnp.float32),
        ],
        [own_piece, near_piece, far_piece, farther_piece, audio_tokens, *weights],
        scratch=[
            pltpu.VMEM((seq_size, audio_rows, HEAD_DIM), jnp.bfloat16),
            pltpu.VMEM((seq_size, *out_weight.shape), jnp.bfloat16),
            pltpu.VMEM((audio_rows, columns), jnp.bfloat16),
            pltpu.SemaphoreType.DMA((2,)),
        ],
        loose_in=(4, 5),
        limit=7,
    )
    came = swap(send, "rep", 1)
    across = swap((keep[1] + came[1].astype(jnp.float32)).astype(jnp.bfloat16), "mem", 1)
    own_part = taylor(video_cache, plan, 2 * half_depth)
    audio_output = (
        keep[0] + came[0].astype(jnp.float32) + across.astype(jnp.float32)
    ).astype(jnp.bfloat16)
    return (own_part, audio_output)


def solution(mesh):
    sizes = dict(mesh.shape)
    square = (sizes["grp"], sizes["seq"], sizes["mem"], sizes["rep"]) == (2, 4, 2, 2)

    def on_device(*arrays):
        heads = arrays[5].shape[1] // HEAD_DIM
        return (by_head if square and heads == sizes["seq"] else general)(*arrays)

    return jax.shard_map(
        on_device,
        mesh=mesh,
        in_specs=(
            P(None, ("grp", "seq"), "mem"),
            P("grp"),
            P(("grp", "seq")),
            P(("grp", "seq"), None),
            P("seq", ("mem", "rep")),
            P("seq", ("mem", "rep")),
            P(("mem", "rep"), "seq"),
        ),
        out_specs=(P(("grp", "seq"), "mem"), P(("grp", "seq"), ("mem", "rep"))),
        check_vma=False,
    )
```

```python
import math

import jax
import jax.numpy as jnp
from jax import lax
from jax.experimental import pallas as pl
from jax.experimental.pallas import tpu as pltpu
from jax.sharding import PartitionSpec as P

HEAD_DIM = 128
FRAMES = 24


SLOPE = 4.0


def taylor_ratio(plan):
    history = plan.shape[0]
    step_ids = jnp.arange(history, dtype=jnp.int32)
    marked = step_ids * plan
    last_fresh = jnp.max(marked)
    prior_fresh = jnp.max(jnp.where(step_ids < last_fresh, marked, 0))
    return (history - last_fresh).astype(jnp.float32) / (last_fresh - prior_fresh).astype(
        jnp.float32
    )


def combine(orders, step_ratio):
    values = orders.astype(jnp.float32)
    return (values[0] + step_ratio * values[1] + 0.5 * step_ratio * step_ratio * values[2]).astype(
        jnp.bfloat16
    )


def general(video_cache, plan, alignment, audio_tokens, kv_weight, query_weight, out_weight):
    step_ratio = taylor_ratio(plan)
    own_part = combine(video_cache, step_ratio)
    features_all = lax.all_gather(own_part, "mem", axis=1, tiled=True)
    video_rows = features_all.shape[0]
    kv_local = jnp.dot(
        features_all,
        lax.all_gather(kv_weight, "seq", axis=0, tiled=True),
        preferred_element_type=jnp.float32,
    )
    head_size = HEAD_DIM
    local_heads = query_weight.shape[1] // head_size
    kv_local = kv_local.astype(jnp.bfloat16).reshape(video_rows, local_heads, 2, head_size)
    key_rows = kv_local[:, :, 0, :]
    value_rows = kv_local[:, :, 1, :]
    query_full, out_full = (
        lax.all_gather(query_weight, "seq", axis=0, tiled=True),
        lax.all_gather(out_weight, "seq", axis=1, tiled=True),
    )
    audio_rows = audio_tokens.shape[0]
    queries = jnp.dot(audio_tokens, query_full, preferred_element_type=jnp.float32).astype(
        jnp.bfloat16
    )
    queries = queries.reshape(audio_rows, local_heads, head_size)
    scale = 1.0 / head_size**0.5
    span = video_rows * lax.axis_size("seq")
    initial = (
        jnp.full((local_heads, audio_rows), -1e30, jnp.float32),
        jnp.zeros((local_heads, audio_rows), jnp.float32),
        jnp.zeros((local_heads, audio_rows, head_size), jnp.float32),
    )
    key_piece = lax.all_gather(key_rows, "seq", axis=0, tiled=True)
    value_piece = lax.all_gather(value_rows, "seq", axis=0, tiled=True)
    row_count = key_piece.shape[0]
    block_len = math.gcd(row_count, 1024)

    def advance(block_index, carried):
        row_max, row_sum, weighted = carried
        key_block = lax.dynamic_slice_in_dim(key_piece, block_index * block_len, block_len, 0)
        value_block = lax.dynamic_slice_in_dim(value_piece, block_index * block_len, block_len, 0)
        positions = block_index * block_len + jnp.arange(block_len, dtype=jnp.int32)
        frames_video = positions * FRAMES // span
        distance_bias = (
            -SLOPE
            * jnp.abs(frames_video[None, :] - alignment[:, None]).astype(jnp.float32)
            / FRAMES
        )
        scores = (
            jnp.einsum("qhd,khd->hqk", queries, key_block, preferred_element_type=jnp.float32)
            * scale
        )
        scores = scores + distance_bias[None]
        new_max = jnp.maximum(row_max, jnp.max(scores, axis=2))
        rescale = jnp.exp(row_max - new_max)
        exp_terms = jnp.exp(scores - new_max[:, :, None])
        row_sum = row_sum * rescale + jnp.sum(exp_terms, axis=2)
        weighted = weighted * rescale[:, :, None] + jnp.einsum(
            "hqk,khd->hqd",
            exp_terms.astype(jnp.bfloat16),
            value_block,
            preferred_element_type=jnp.float32,
        )
        return (new_max, row_sum, weighted)

    row_max, row_sum, weighted = lax.fori_loop(0, row_count // block_len, advance, initial)
    attended = (weighted / row_sum[:, :, None]).astype(jnp.bfloat16)
    attended = jnp.transpose(attended, (1, 0, 2)).reshape(audio_rows, local_heads * head_size)
    partial_update = jnp.dot(attended, out_full, preferred_element_type=jnp.float32)
    update = lax.psum_scatter(
        partial_update.astype(jnp.bfloat16), ("mem", "rep"), scatter_dimension=1, tiled=True
    ).astype(jnp.float32)
    own_columns = update.shape[1]
    residual = lax.dynamic_slice_in_dim(
        audio_tokens, lax.axis_index(("mem", "rep")) * own_columns, own_columns, 1
    )
    audio_output = (residual.astype(jnp.float32) + update).astype(jnp.bfloat16)
    return (own_part, audio_output)


def swap(value, axis, bit):
    size = lax.axis_size(axis)
    return lax.ppermute(value, axis, [(i, i ^ bit) for i in range(size)])


VMEM = pl.BlockSpec(memory_space=pltpu.VMEM)
SMEM = pl.BlockSpec(memory_space=pltpu.SMEM)
ANY = pl.BlockSpec(memory_space=pl.ANY)
HBM = pl.BlockSpec(memory_space=pltpu.HBM)


def kernel_call(body, outs, ins, after=(), scratch=(), smem=(), loose_in=(), loose_out=(), limit=14):
    def whole(*refs):
        body(*refs[: len(ins)], *refs[len(ins) + len(after) :])

    spots = [SMEM if i in smem else HBM if i in loose_in else VMEM for i in range(len(ins))]
    return pl.pallas_call(
        whole,
        out_shape=outs,
        in_specs=spots + [ANY] * len(after),
        out_specs=[HBM if i in loose_out else VMEM for i in range(len(outs))],
        scratch_shapes=scratch,
        compiler_params=pltpu.CompilerParams(vmem_limit_bytes=limit * 2**20),
    )(*ins, *after)


def plan_ratio(plan_ref, columns):
    history = plan_ref.shape[0]
    last_fresh, prior_fresh = jnp.int32(0), jnp.int32(0)
    for step in range(history):
        fresh = plan_ref[step] == 1
        prior_fresh = jnp.where(fresh, last_fresh, prior_fresh)
        last_fresh = jnp.where(fresh, step, last_fresh)
    ahead = jnp.full((1, columns), history - last_fresh, jnp.int32).astype(jnp.float32)
    apart = jnp.full((1, columns), last_fresh - prior_fresh, jnp.int32).astype(jnp.float32)
    return ahead / apart


def taylor_rows(cache_ref, out_ref, step_ratio, first, last):
    half_square = 0.5 * step_ratio * step_ratio
    for at in range(first, last, 16):
        terms = [cache_ref[order, at : at + 16, :].astype(jnp.float32) for order in range(3)]
        out_ref[at : at + 16, :] = (
            terms[0] + step_ratio * terms[1] + half_square * terms[2]
        ).astype(jnp.bfloat16)


def taylor_body(plan_ref, cache_ref, out_ref):
    rows, columns = out_ref.shape
    taylor_rows(cache_ref, out_ref, plan_ratio(plan_ref, columns), 0, rows)


def taylor(video_cache, plan, width):
    orders, rows, columns = video_cache.shape
    return pl.pallas_call(
        taylor_body,
        out_shape=jax.ShapeDtypeStruct((rows, columns), jnp.bfloat16),
        grid=(columns // width,),
        in_specs=[SMEM, pl.BlockSpec((orders, rows, width), lambda i: (0, 0, i))],
        out_specs=pl.BlockSpec((rows, width), lambda i: (0, i)),
        compiler_params=pltpu.CompilerParams(vmem_limit_bytes=6 * 2**20),
    )(plan, video_cache)


def first_body(
    plan_ref,
    cache_ref,
    audio_ref,
    kv_ref,
    query_ref,
    out_w,
    packed_ref,
    other_ref,
    half_ref,
    held_ref,
    made_ref,
    other_vmem,
    half_vmem,
    plan_smem,
    sems,
):
    rep_at, mem_at, grp_at = (lax.axis_index(name) for name in ("rep", "mem", "grp"))
    rows, width = held_ref.shape[1:]
    width = width // 2
    copies = []

    def copy(source, target):
        copies.append(pltpu.make_async_copy(source, target, sems.at[len(copies)]))

    def part(index, size):
        return pl.ds(pl.multiple_of(index * size, size), size)

    plan_copy = pltpu.make_async_copy(plan_ref, plan_smem, sems.at[25])
    plan_copy.start()
    blocks = 4
    step = rows // blocks
    for block in range(blocks):
        at = pl.ds(block * step, step)
        for shard in range(2):
            copy(
                cache_ref.at[:, at, part(2 * shard + rep_at, width)],
                held_ref.at[:, at, pl.ds(shard * width, width)],
            )
    lane = width // 2
    for shard in range(2):
        copy(
            audio_ref.at[:, part(2 * (2 * mem_at + shard) + rep_at, lane)],
            made_ref.at[pl.ds(2 * rows, audio_ref.shape[0]), pl.ds(shard * lane, lane)],
        )
    depth, columns = kv_ref.shape[0] // 2, query_ref.shape[1]
    copy(kv_ref.at[part(1 - rep_at, depth)], other_vmem.at[pl.ds(0, depth)])
    quarter = query_ref.shape[0] // 4
    for side in range(2):
        copy(
            query_ref.at[part(2 * (1 - rep_at) + side, quarter)],
            other_vmem.at[pl.ds(depth, quarter), pl.ds(side * columns, columns)],
        )
    copy(out_w.at[part(grp_at, half_ref.shape[0])], half_vmem)
    for started in copies:
        started.start()
    plan_copy.wait()
    step_ratio = plan_ratio(plan_smem, width)
    for block in range(blocks):
        for shard in range(2):
            copies[2 * block + shard].wait()
            taylor_rows(
                held_ref.at[:, :, pl.ds(shard * width, width)],
                made_ref.at[pl.ds(shard * rows, rows)],
                step_ratio,
                block * step,
                (block + 1) * step,
            )
            at = pl.ds(shard * rows + block * step, step)
            copy(made_ref.at[at], packed_ref.at[at])
            copies[-1].start()
    audio_at = pl.ds(2 * rows, audio_ref.shape[0])
    stages = (
        (2, made_ref.at[audio_at], packed_ref.at[audio_at]),
        (3, other_vmem, other_ref),
        (1, half_vmem, half_ref),
    )
    at = 2 * blocks
    for count, source, target in stages:
        for arriving in copies[at : at + count]:
            arriving.wait()
        at += count
        copy(source, target)
        copies[-1].start()
    for leaving in copies[at:]:
        leaving.wait()


def weight_body(align_ref, kv_ref, query_ref, other_ref, own_ref, *piece_refs):
    seq_at, rep_at, grp_at = (lax.axis_index(name) for name in ("seq", "rep", "grp"))
    kv_half, query_half = kv_ref.shape[0] // 2, query_ref.shape[0] // 2
    kv_rows, query_rows = kv_half // 2, query_half // 2
    fold = query_rows // 2

    def fill(out_ref, bit, group, kv_at, query_at):
        head = seq_at ^ bit
        width = 2 * HEAD_DIM
        lanes = pl.ds(pl.multiple_of(head * width, width), width)
        at = pl.ds(pl.multiple_of(rep_at * kv_half + group * kv_rows, kv_rows), kv_rows)
        out_ref[kv_at : kv_at + kv_rows, :width] = kv_ref[at, lanes]
        at = pl.ds(pl.multiple_of(group * kv_rows, kv_rows), kv_rows)
        out_ref[kv_at : kv_at + kv_rows, width:] = other_ref[at, lanes]
        lanes = pl.ds(pl.multiple_of(head * HEAD_DIM, HEAD_DIM), HEAD_DIM)
        other_lanes = pl.ds(
            pl.multiple_of(group * query_ref.shape[1] + head * HEAD_DIM, HEAD_DIM), HEAD_DIM
        )
        for side in range(2):
            first = rep_at * query_half + group * query_rows + side * fold
            at = pl.ds(pl.multiple_of(first, fold), fold)
            to = slice(query_at, query_at + fold)
            out_ref[to, side * width : side * width + HEAD_DIM] = query_ref[at, lanes]
            out_ref[to, side * width + HEAD_DIM : (side + 1) * width] = other_ref[
                kv_half + side * fold : kv_half + (side + 1) * fold, other_lanes
            ]

    for group in range(2):
        fill(own_ref, 0, group, group * kv_rows, kv_half + group * fold)
    for bit, piece_ref in enumerate(piece_refs, 1):
        fill(piece_ref, bit, grp_at, 0, kv_rows)
        spare = (piece_ref.shape[0] - kv_rows - fold, piece_ref.shape[1])
        align = align_ref[...].astype(jnp.float32).astype(piece_ref.dtype)
        row = jnp.concatenate(
            [align, jnp.zeros((1, spare[1] - align.shape[1]), piece_ref.dtype)], axis=1
        )
        piece_ref[kv_rows + fold :, :] = jnp.broadcast_to(row, spare)


def products_body(*refs):
    packed_refs, weight_refs = refs[:8], refs[8:15]
    own_align, near_align, align_ref, send_ref, keep_ref, rows_ref, audio_ref, kv_ref, query_ref = refs[15:]
    seq_at, mem_at, grp_at = (lax.axis_index(name) for name in ("seq", "mem", "grp"))
    rows, audio_rows = rows_ref.shape[0] // 4, audio_ref.shape[0] // 4
    depth, lane = rows_ref.shape[1] // 4, audio_ref.shape[1] // 4
    for at, packed_ref in enumerate(packed_refs):
        slot, mem = divmod(at, 2)
        for part in range(2):
            shard = 2 * (mem_at ^ mem) + part
            lanes = pl.ds(pl.multiple_of(shard * depth, depth), depth)
            rows_ref[slot * rows : (slot + 1) * rows, lanes] = packed_ref[
                part * rows : (part + 1) * rows, :
            ]
            lanes = pl.ds(pl.multiple_of(shard * lane, lane), lane)
            audio_ref[slot * audio_rows : (slot + 1) * audio_rows, lanes] = packed_ref[
                2 * rows :, part * lane : (part + 1) * lane
            ]
    kv_half, fold = depth // 2, lane // 4
    width = query_ref.shape[1]

    def place(piece_ref, shard, group, kv_at, query_at):
        to = pl.ds(pl.multiple_of((2 * shard + group) * kv_half, kv_half), kv_half)
        kv_ref[to, :] = piece_ref[kv_at : kv_at + kv_half, :]
        for side in range(2):
            to = pl.ds(pl.multiple_of((4 * shard + 2 * group + side) * fold, fold), fold)
            query_ref[to, :] = piece_ref[
                query_at : query_at + fold, side * width : (side + 1) * width
            ]

    for group in range(2):
        place(weight_refs[0], seq_at, group, group * kv_half, 2 * kv_half + group * fold)
    for bit in range(1, 4):
        place(weight_refs[2 * bit - 1], seq_at ^ bit, grp_at, 0, kv_half)
        place(weight_refs[2 * bit], seq_at ^ bit, 1 - grp_at, 0, kv_half)
        if bit > 1:
            align_ref[bit] = weight_refs[2 * bit - 1][kv_half + fold :, : align_ref.shape[2]]
    align_ref[1] = near_align[...].astype(align_ref.dtype)
    align_ref[0] = jnp.broadcast_to(
        own_align[...].astype(jnp.float32).astype(align_ref.dtype), align_ref.shape[1:]
    )

    count = 4 * rows
    columns = keep_ref.shape[1]
    total = jnp.dot(rows_ref[...], kv_ref[...], preferred_element_type=jnp.float32)
    keep_ref[:count, :] = total[:, :columns]
    send_ref[:count, :] = total[:, columns:]
    total = jnp.dot(audio_ref[...], query_ref[...], preferred_element_type=jnp.float32)
    folded = 2 * audio_rows
    for side in range(2):
        at = slice(side * folded, (side + 1) * folded)
        to = slice(side * HEAD_DIM, (side + 1) * HEAD_DIM)
        keep_ref[count:, to] = total[at, :HEAD_DIM]
        send_ref[count:, to] = total[at, HEAD_DIM:]


def attend(queries, kv_ref, frames_ref, align):
    scores = lax.dot_general(
        queries,
        kv_ref[:, :HEAD_DIM],
        (((1,), (1,)), ((), ())),
        preferred_element_type=jnp.float32,
    ) * (1.0 / HEAD_DIM**0.5)
    scores = scores - SLOPE * jnp.abs(frames_ref[...] - align) / FRAMES
    exp_terms = jnp.exp(scores - jnp.max(scores, axis=1, keepdims=True))
    weighted = jnp.dot(
        exp_terms.astype(jnp.bfloat16), kv_ref[:, HEAD_DIM:], preferred_element_type=jnp.float32
    )
    return (weighted / jnp.sum(exp_terms, axis=1, keepdims=True)).astype(jnp.bfloat16)


def attention_body(frames_ref, align_ref, keep_ref, came_ref, *refs):
    *out_refs, kv_ref, query_ref = refs
    count, audio_rows = kv_ref.shape[0], query_ref.shape[1]

    def summed(rows, columns=slice(None)):
        return (keep_ref[rows, columns] + came_ref[rows, columns]).astype(jnp.bfloat16)

    kv_ref[...] = summed(slice(0, count))
    for slot in range(4):
        side, half = divmod(slot, 2)
        query_ref[slot] = summed(
            slice(count + half * audio_rows, count + (half + 1) * audio_rows),
            slice(side * HEAD_DIM, (side + 1) * HEAD_DIM),
        )
    for bit, out_ref in enumerate(out_refs):
        align = align_ref[bit].astype(jnp.float32)[:8].T[:, :1]
        out_ref[...] = attend(query_ref[bit], kv_ref, frames_ref, align)


def out_body(*refs):
    piece_refs, (audio_ref, own_w, *part_refs) = refs[:4], refs[4:12]
    send_ref, keep_ref, heads_ref, weight_ref, residual_ref, sems = refs[12:]
    seq_at, grp_at = lax.axis_index("seq"), lax.axis_index("grp")
    place = lax.axis_index("mem") * 2 + lax.axis_index("rep")
    copy = pltpu.make_async_copy(own_w, weight_ref.at[0], sems.at[0])
    copy.start()
    width = residual_ref.shape[1]
    columns = pl.ds(pl.multiple_of(place * width, width), width)
    residual_copy = pltpu.make_async_copy(audio_ref.at[:, columns], residual_ref, sems.at[1])
    residual_copy.start()
    for bit, piece_ref in enumerate(piece_refs):
        heads_ref[seq_at ^ bit] = piece_ref[...]
    heads = jnp.concatenate([heads_ref[head] for head in range(heads_ref.shape[0])], axis=1)
    depth = part_refs[0].shape[0]
    mine = pl.ds(pl.multiple_of(grp_at * depth, depth), depth)
    rest = pl.ds(pl.multiple_of((1 - grp_at) * depth, depth), depth)
    for bit in range(1, 4):
        weight_ref[bit, mine] = part_refs[2 * bit - 2][...]
        weight_ref[bit, rest] = part_refs[2 * bit - 1][...]
    for bit in (1, 2, 3, 0):
        if bit == 0:
            copy.wait()
        slot = seq_at ^ bit ^ place
        value = jnp.dot(heads, weight_ref[bit], preferred_element_type=jnp.float32)

        @pl.when(slot % 2 == 1)
        def _():
            send_ref[slot // 2] = value.astype(send_ref.dtype)

        @pl.when(slot % 2 == 0)
        def _():
            keep_ref[slot // 2] = value

    residual_copy.wait()
    keep_ref[0] += residual_ref[...].astype(jnp.float32)


def by_head(video_cache, plan, alignment, audio_tokens, kv_weight, query_weight, out_weight):
    seq_size = lax.axis_size("seq")
    seq_at = lax.axis_index("seq")
    video_rows = video_cache.shape[1]
    audio_rows = audio_tokens.shape[0]
    half_depth, width = kv_weight.shape[0] // 2, 2 * HEAD_DIM
    query_quarter = query_weight.shape[0] // 4

    def bfloat(*shape):
        return jax.ShapeDtypeStruct(shape, jnp.bfloat16)

    packed, other, out_half = kernel_call(
        first_body,
        [
            bfloat(2 * video_rows + audio_rows, half_depth),
            bfloat(half_depth + query_quarter, kv_weight.shape[1]),
            bfloat(out_weight.shape[0] // 2, out_weight.shape[1]),
        ],
        [plan, video_cache, audio_tokens, kv_weight, query_weight, out_weight],
        scratch=[
            pltpu.VMEM((3, video_rows, 2 * half_depth), jnp.bfloat16),
            pltpu.VMEM((2 * video_rows + audio_rows, half_depth), jnp.bfloat16),
            pltpu.VMEM((half_depth + query_quarter, kv_weight.shape[1]), jnp.bfloat16),
            pltpu.VMEM((out_weight.shape[0] // 2, out_weight.shape[1]), jnp.bfloat16),
            pltpu.SMEM(plan.shape, jnp.int32),
            pltpu.SemaphoreType.DMA((26,)),
        ],
        loose_in=(0, 1, 2, 3, 4, 5),
        loose_out=(0, 1, 2),
        limit=61,
    )

    tokens = [packed, swap(packed, "seq", 1), swap(packed, "seq", 2)]
    across = [swap(packed, "mem", 1)]
    other = swap(other, "rep", 1)
    rows = half_depth // 2 + query_quarter // 2
    weight_own, *pieces = kernel_call(
        weight_body,
        [bfloat(2 * rows, 2 * width)] + [bfloat(rows + 16, 2 * width)] * 3,
        [alignment[None], kv_weight, query_weight, other],
        limit=4,
    )
    pieces = [swap(piece, "seq", bit) for bit, piece in enumerate(pieces, 1)]

    across += [swap(tokens[1], "mem", 1), swap(tokens[2], "mem", 1)]
    near_align = pieces[0][rows:, :audio_rows].astype(jnp.float32)
    tokens[2], near_align = lax.optimization_barrier((tokens[2], near_align))
    tokens.append(swap(tokens[2], "seq", 1))
    pieces[0], across[0], across[1] = lax.optimization_barrier(
        (pieces[0], across[0], across[1])
    )
    rest = [swap(pieces[0], "grp", 1)]
    tokens[3], across[2], rest[0], pieces[1] = lax.optimization_barrier(
        (tokens[3], across[2], rest[0], pieces[1])
    )
    across.append(swap(tokens[3], "mem", 1))
    rest.append(swap(pieces[1], "grp", 1))
    pieces[2], rest[1] = lax.optimization_barrier((pieces[2], rest[1]))
    rest.append(swap(pieces[2], "grp", 1))

    out_half, tokens[3] = lax.optimization_barrier((out_half, tokens[3]))
    out_third, out_partner = swap(out_half, "seq", 2), swap(out_half, "seq", 1)
    weights = [weight_own]
    for piece, other in zip(pieces, rest):
        weights += [piece, other]
    rows = seq_size * (video_rows + audio_rows // 2)
    sums = jax.ShapeDtypeStruct((rows, width), jnp.float32)
    aligns, send, keep = kernel_call(
        products_body,
        [bfloat(4, 16, audio_rows), sums, sums],
        [value for pair in zip(tokens, across) for value in pair] + weights
        + [alignment[None], near_align],
        scratch=[
            pltpu.VMEM((seq_size * video_rows, 4 * half_depth), jnp.bfloat16),
            pltpu.VMEM((seq_size * audio_rows, 8 * query_quarter), jnp.bfloat16),
            pltpu.VMEM((4 * half_depth, 2 * width), jnp.bfloat16),
            pltpu.VMEM((8 * query_quarter, width), jnp.bfloat16),
        ],
        limit=15,
    )
    send, out_third, out_partner = lax.optimization_barrier((send, out_third, out_partner))
    came = swap(send, "rep", 1)
    third_rest, out_fourth = swap(out_third, "grp", 1), swap(out_third, "seq", 1)

    span = video_rows * seq_size
    blocks = jnp.stack([seq_at, seq_at ^ 1, seq_at ^ 2, seq_at ^ 3])
    positions = blocks[:, None] * video_rows + jnp.arange(video_rows, dtype=jnp.int32)[None, :]
    frames_video = (positions.reshape(1, span) * FRAMES // span).astype(jnp.float32)
    own_piece, near_piece, far_piece, farther_piece = kernel_call(
        attention_body,
        [bfloat(audio_rows, HEAD_DIM)] * 4,
        [frames_video, aligns, keep, came],
        scratch=[
            pltpu.VMEM((span, width), jnp.bfloat16),
            pltpu.VMEM((seq_size, audio_rows, HEAD_DIM), jnp.bfloat16),
        ],
        limit=9,
    )
    third_rest, out_partner, own_piece = lax.optimization_barrier(
        (third_rest, out_partner, own_piece)
    )
    fourth_rest, partner_rest = swap(third_rest, "seq", 1), swap(out_partner, "grp", 1)
    far_piece = swap(far_piece, "seq", 2)
    farther_piece = swap(farther_piece, "seq", 3)
    near_piece = swap(near_piece, "seq", 1)

    columns = out_weight.shape[1]
    weights = [out_weight, out_partner, partner_rest]
    weights += [out_third, third_rest, out_fourth, fourth_rest]
    send, keep = kernel_call(
        out_body,
        [
            jax.ShapeDtypeStruct((2, audio_rows, columns), jnp.bfloat16),
            jax.ShapeDtypeStruct((2, audio_rows, columns), jnp.float32),
        ],
        [own_piece, near_piece, far_piece, farther_piece, audio_tokens, *weights],
        scratch=[
            pltpu.VMEM((seq_size, audio_rows, HEAD_DIM), jnp.bfloat16),
            pltpu.VMEM((seq_size, *out_weight.shape), jnp.bfloat16),
            pltpu.VMEM((audio_rows, columns), jnp.bfloat16),
            pltpu.SemaphoreType.DMA((2,)),
        ],
        loose_in=(4, 5),
        limit=7,
    )
    came = swap(send, "rep", 1)
    across = swap((keep[1] + came[1].astype(jnp.float32)).astype(jnp.bfloat16), "mem", 1)
    own_part = taylor(video_cache, plan, 2 * half_depth)
    audio_output = (
        keep[0] + came[0].astype(jnp.float32) + across.astype(jnp.float32)
    ).astype(jnp.bfloat16)
    return (own_part, audio_output)


def solution(mesh):
    sizes = dict(mesh.shape)
    square = (sizes["grp"], sizes["seq"], sizes["mem"], sizes["rep"]) == (2, 4, 2, 2)

    def on_device(*arrays):
        heads = arrays[5].shape[1] // HEAD_DIM
        return (by_head if square and heads == sizes["seq"] else general)(*arrays)

    return jax.shard_map(
        on_device,
        mesh=mesh,
        in_specs=(
            P(None, ("grp", "seq"), "mem"),
            P("grp"),
            P(("grp", "seq")),
            P(("grp", "seq"), None),
            P("seq", ("mem", "rep")),
            P("seq", ("mem", "rep")),
            P(("mem", "rep"), "seq"),
        ),
        out_specs=(P(("grp", "seq"), "mem"), P(("grp", "seq"), ("mem", "rep"))),
        check_vma=False,
    )
```

```python
import math

import jax
import jax.numpy as jnp
from jax import lax
from jax.experimental import pallas as pl
from jax.experimental.pallas import tpu as pltpu
from jax.sharding import PartitionSpec as P

HEAD_DIM = 128
FRAMES = 24


SLOPE = 4.0


def taylor_ratio(plan):
    history = plan.shape[0]
    step_ids = jnp.arange(history, dtype=jnp.int32)
    marked = step_ids * plan
    last_fresh = jnp.max(marked)
    prior_fresh = jnp.max(jnp.where(step_ids < last_fresh, marked, 0))
    return (history - last_fresh).astype(jnp.float32) / (last_fresh - prior_fresh).astype(
        jnp.float32
    )


def combine(orders, step_ratio):
    values = orders.astype(jnp.float32)
    return (values[0] + step_ratio * values[1] + 0.5 * step_ratio * step_ratio * values[2]).astype(
        jnp.bfloat16
    )


def general(video_cache, plan, alignment, audio_tokens, kv_weight, query_weight, out_weight):
    step_ratio = taylor_ratio(plan)
    own_part = combine(video_cache, step_ratio)
    features_all = lax.all_gather(own_part, "mem", axis=1, tiled=True)
    video_rows = features_all.shape[0]
    kv_local = jnp.dot(
        features_all,
        lax.all_gather(kv_weight, "seq", axis=0, tiled=True),
        preferred_element_type=jnp.float32,
    )
    head_size = HEAD_DIM
    local_heads = query_weight.shape[1] // head_size
    kv_local = kv_local.astype(jnp.bfloat16).reshape(video_rows, local_heads, 2, head_size)
    key_rows = kv_local[:, :, 0, :]
    value_rows = kv_local[:, :, 1, :]
    query_full, out_full = (
        lax.all_gather(query_weight, "seq", axis=0, tiled=True),
        lax.all_gather(out_weight, "seq", axis=1, tiled=True),
    )
    audio_rows = audio_tokens.shape[0]
    queries = jnp.dot(audio_tokens, query_full, preferred_element_type=jnp.float32).astype(
        jnp.bfloat16
    )
    queries = queries.reshape(audio_rows, local_heads, head_size)
    scale = 1.0 / head_size**0.5
    span = video_rows * lax.axis_size("seq")
    initial = (
        jnp.full((local_heads, audio_rows), -1e30, jnp.float32),
        jnp.zeros((local_heads, audio_rows), jnp.float32),
        jnp.zeros((local_heads, audio_rows, head_size), jnp.float32),
    )
    key_piece = lax.all_gather(key_rows, "seq", axis=0, tiled=True)
    value_piece = lax.all_gather(value_rows, "seq", axis=0, tiled=True)
    row_count = key_piece.shape[0]
    block_len = math.gcd(row_count, 1024)

    def advance(block_index, carried):
        row_max, row_sum, weighted = carried
        key_block = lax.dynamic_slice_in_dim(key_piece, block_index * block_len, block_len, 0)
        value_block = lax.dynamic_slice_in_dim(value_piece, block_index * block_len, block_len, 0)
        positions = block_index * block_len + jnp.arange(block_len, dtype=jnp.int32)
        frames_video = positions * FRAMES // span
        distance_bias = (
            -SLOPE
            * jnp.abs(frames_video[None, :] - alignment[:, None]).astype(jnp.float32)
            / FRAMES
        )
        scores = (
            jnp.einsum("qhd,khd->hqk", queries, key_block, preferred_element_type=jnp.float32)
            * scale
        )
        scores = scores + distance_bias[None]
        new_max = jnp.maximum(row_max, jnp.max(scores, axis=2))
        rescale = jnp.exp(row_max - new_max)
        exp_terms = jnp.exp(scores - new_max[:, :, None])
        row_sum = row_sum * rescale + jnp.sum(exp_terms, axis=2)
        weighted = weighted * rescale[:, :, None] + jnp.einsum(
            "hqk,khd->hqd",
            exp_terms.astype(jnp.bfloat16),
            value_block,
            preferred_element_type=jnp.float32,
        )
        return (new_max, row_sum, weighted)

    row_max, row_sum, weighted = lax.fori_loop(0, row_count // block_len, advance, initial)
    attended = (weighted / row_sum[:, :, None]).astype(jnp.bfloat16)
    attended = jnp.transpose(attended, (1, 0, 2)).reshape(audio_rows, local_heads * head_size)
    partial_update = jnp.dot(attended, out_full, preferred_element_type=jnp.float32)
    update = lax.psum_scatter(
        partial_update.astype(jnp.bfloat16), ("mem", "rep"), scatter_dimension=1, tiled=True
    ).astype(jnp.float32)
    own_columns = update.shape[1]
    residual = lax.dynamic_slice_in_dim(
        audio_tokens, lax.axis_index(("mem", "rep")) * own_columns, own_columns, 1
    )
    audio_output = (residual.astype(jnp.float32) + update).astype(jnp.bfloat16)
    return (own_part, audio_output)


def swap(value, axis, bit):
    size = lax.axis_size(axis)
    return lax.ppermute(value, axis, [(i, i ^ bit) for i in range(size)])


VMEM = pl.BlockSpec(memory_space=pltpu.VMEM)
SMEM = pl.BlockSpec(memory_space=pltpu.SMEM)
ANY = pl.BlockSpec(memory_space=pl.ANY)
HBM = pl.BlockSpec(memory_space=pltpu.HBM)


def kernel_call(body, outs, ins, after=(), scratch=(), smem=(), loose_in=(), loose_out=(), limit=14, cost=None):
    def whole(*refs):
        body(*refs[: len(ins)], *refs[len(ins) + len(after) :])

    spots = [SMEM if i in smem else HBM if i in loose_in else VMEM for i in range(len(ins))]
    return pl.pallas_call(
        whole,
        out_shape=outs,
        in_specs=spots + [ANY] * len(after),
        out_specs=[HBM if i in loose_out else VMEM for i in range(len(outs))],
        scratch_shapes=scratch,
        cost_estimate=cost,
        compiler_params=pltpu.CompilerParams(vmem_limit_bytes=limit * 2**20),
    )(*ins, *after)


def plan_ratio(plan_ref, columns):
    history = plan_ref.shape[0]
    last_fresh, prior_fresh = jnp.int32(0), jnp.int32(0)
    for step in range(history):
        fresh = plan_ref[step] == 1
        prior_fresh = jnp.where(fresh, last_fresh, prior_fresh)
        last_fresh = jnp.where(fresh, step, last_fresh)
    ahead = jnp.full((1, columns), history - last_fresh, jnp.int32).astype(jnp.float32)
    apart = jnp.full((1, columns), last_fresh - prior_fresh, jnp.int32).astype(jnp.float32)
    return ahead / apart


def taylor_rows(cache_ref, out_ref, step_ratio, first, last):
    half_square = 0.5 * step_ratio * step_ratio
    for at in range(first, last, 16):
        terms = [cache_ref[order, at : at + 16, :].astype(jnp.float32) for order in range(3)]
        out_ref[at : at + 16, :] = (
            terms[0] + step_ratio * terms[1] + half_square * terms[2]
        ).astype(jnp.bfloat16)


def taylor_body(plan_ref, cache_ref, out_ref):
    rows, columns = out_ref.shape
    taylor_rows(cache_ref, out_ref, plan_ratio(plan_ref, columns), 0, rows)


def taylor(video_cache, plan, width):
    orders, rows, columns = video_cache.shape
    return pl.pallas_call(
        taylor_body,
        out_shape=jax.ShapeDtypeStruct((rows, columns), jnp.bfloat16),
        grid=(columns // width,),
        in_specs=[SMEM, pl.BlockSpec((orders, rows, width), lambda i: (0, 0, i))],
        out_specs=pl.BlockSpec((rows, width), lambda i: (0, i)),
        compiler_params=pltpu.CompilerParams(vmem_limit_bytes=6 * 2**20),
    )(plan, video_cache)


def first_body(
    plan_ref,
    cache_ref,
    audio_ref,
    kv_ref,
    query_ref,
    out_w,
    packed_ref,
    other_ref,
    half_ref,
    held_ref,
    made_ref,
    other_vmem,
    half_vmem,
    plan_smem,
    sems,
):
    rep_at, mem_at, grp_at = (lax.axis_index(name) for name in ("rep", "mem", "grp"))
    rows, width = held_ref.shape[1:]
    width = width // 2
    copies = []

    def copy(source, target):
        copies.append(pltpu.make_async_copy(source, target, sems.at[len(copies)]))

    def part(index, size):
        return pl.ds(pl.multiple_of(index * size, size), size)

    plan_copy = pltpu.make_async_copy(plan_ref, plan_smem, sems.at[25])
    plan_copy.start()
    blocks = 4
    step = rows // blocks
    for block in range(blocks):
        at = pl.ds(block * step, step)
        for shard in range(2):
            copy(
                cache_ref.at[:, at, part(2 * shard + rep_at, width)],
                held_ref.at[:, at, pl.ds(shard * width, width)],
            )
    lane = width // 2
    for shard in range(2):
        copy(
            audio_ref.at[:, part(2 * (2 * mem_at + shard) + rep_at, lane)],
            made_ref.at[pl.ds(2 * rows, audio_ref.shape[0]), pl.ds(shard * lane, lane)],
        )
    depth, columns = kv_ref.shape[0] // 2, query_ref.shape[1]
    copy(kv_ref.at[part(1 - rep_at, depth)], other_vmem.at[pl.ds(0, depth)])
    quarter = query_ref.shape[0] // 4
    for side in range(2):
        copy(
            query_ref.at[part(2 * (1 - rep_at) + side, quarter)],
            other_vmem.at[pl.ds(depth, quarter), pl.ds(side * columns, columns)],
        )
    copy(out_w.at[part(grp_at, half_ref.shape[0])], half_vmem)
    for started in copies:
        started.start()
    plan_copy.wait()
    step_ratio = plan_ratio(plan_smem, width)
    for block in range(blocks):
        for shard in range(2):
            copies[2 * block + shard].wait()
            taylor_rows(
                held_ref.at[:, :, pl.ds(shard * width, width)],
                made_ref.at[pl.ds(shard * rows, rows)],
                step_ratio,
                block * step,
                (block + 1) * step,
            )
            at = pl.ds(shard * rows + block * step, step)
            copy(made_ref.at[at], packed_ref.at[at])
            copies[-1].start()
    audio_at = pl.ds(2 * rows, audio_ref.shape[0])
    stages = (
        (2, made_ref.at[audio_at], packed_ref.at[audio_at]),
        (3, other_vmem, other_ref),
        (1, half_vmem, half_ref),
    )
    at = 2 * blocks
    for count, source, target in stages:
        for arriving in copies[at : at + count]:
            arriving.wait()
        at += count
        copy(source, target)
        copies[-1].start()
    for leaving in copies[at:]:
        leaving.wait()


def weight_body(align_ref, kv_ref, query_ref, other_ref, own_ref, *piece_refs):
    seq_at, rep_at, grp_at = (lax.axis_index(name) for name in ("seq", "rep", "grp"))
    kv_half, query_half = kv_ref.shape[0] // 2, query_ref.shape[0] // 2
    kv_rows, query_rows = kv_half // 2, query_half // 2
    fold = query_rows // 2

    def fill(out_ref, bit, group, kv_at, query_at):
        head = seq_at ^ bit
        width = 2 * HEAD_DIM
        lanes = pl.ds(pl.multiple_of(head * width, width), width)
        at = pl.ds(pl.multiple_of(rep_at * kv_half + group * kv_rows, kv_rows), kv_rows)
        out_ref[kv_at : kv_at + kv_rows, :width] = kv_ref[at, lanes]
        at = pl.ds(pl.multiple_of(group * kv_rows, kv_rows), kv_rows)
        out_ref[kv_at : kv_at + kv_rows, width:] = other_ref[at, lanes]
        lanes = pl.ds(pl.multiple_of(head * HEAD_DIM, HEAD_DIM), HEAD_DIM)
        other_lanes = pl.ds(
            pl.multiple_of(group * query_ref.shape[1] + head * HEAD_DIM, HEAD_DIM), HEAD_DIM
        )
        for side in range(2):
            first = rep_at * query_half + group * query_rows + side * fold
            at = pl.ds(pl.multiple_of(first, fold), fold)
            to = slice(query_at, query_at + fold)
            out_ref[to, side * width : side * width + HEAD_DIM] = query_ref[at, lanes]
            out_ref[to, side * width + HEAD_DIM : (side + 1) * width] = other_ref[
                kv_half + side * fold : kv_half + (side + 1) * fold, other_lanes
            ]

    for group in range(2):
        fill(own_ref, 0, group, group * kv_rows, kv_half + group * fold)
    for bit, piece_ref in enumerate(piece_refs, 1):
        fill(piece_ref, bit, grp_at, 0, kv_rows)
        spare = (piece_ref.shape[0] - kv_rows - fold, piece_ref.shape[1])
        align = align_ref[...].astype(jnp.float32).astype(piece_ref.dtype)
        row = jnp.concatenate(
            [align, jnp.zeros((1, spare[1] - align.shape[1]), piece_ref.dtype)], axis=1
        )
        piece_ref[kv_rows + fold :, :] = jnp.broadcast_to(row, spare)


def products_body(*refs):
    packed_refs, weight_refs = refs[:8], refs[8:15]
    own_align, near_align, align_ref, send_ref, keep_ref, rows_ref, audio_ref, kv_ref, query_ref = refs[15:]
    seq_at, mem_at, grp_at = (lax.axis_index(name) for name in ("seq", "mem", "grp"))
    rows, audio_rows = rows_ref.shape[0] // 4, audio_ref.shape[0] // 4
    depth, lane = rows_ref.shape[1] // 4, audio_ref.shape[1] // 4
    for at, packed_ref in enumerate(packed_refs):
        slot, mem = divmod(at, 2)
        for part in range(2):
            shard = 2 * (mem_at ^ mem) + part
            lanes = pl.ds(pl.multiple_of(shard * depth, depth), depth)
            rows_ref[slot * rows : (slot + 1) * rows, lanes] = packed_ref[
                part * rows : (part + 1) * rows, :
            ]
            lanes = pl.ds(pl.multiple_of(shard * lane, lane), lane)
            audio_ref[slot * audio_rows : (slot + 1) * audio_rows, lanes] = packed_ref[
                2 * rows :, part * lane : (part + 1) * lane
            ]
    kv_half, fold = depth // 2, lane // 4
    width = query_ref.shape[1]

    def place(piece_ref, shard, group, kv_at, query_at):
        to = pl.ds(pl.multiple_of((2 * shard + group) * kv_half, kv_half), kv_half)
        kv_ref[to, :] = piece_ref[kv_at : kv_at + kv_half, :]
        for side in range(2):
            to = pl.ds(pl.multiple_of((4 * shard + 2 * group + side) * fold, fold), fold)
            query_ref[to, :] = piece_ref[
                query_at : query_at + fold, side * width : (side + 1) * width
            ]

    for group in range(2):
        place(weight_refs[0], seq_at, group, group * kv_half, 2 * kv_half + group * fold)
    for bit in range(1, 4):
        place(weight_refs[2 * bit - 1], seq_at ^ bit, grp_at, 0, kv_half)
        place(weight_refs[2 * bit], seq_at ^ bit, 1 - grp_at, 0, kv_half)
        if bit > 1:
            align_ref[bit] = weight_refs[2 * bit - 1][kv_half + fold :, : align_ref.shape[2]]
    align_ref[1] = near_align[...].astype(align_ref.dtype)
    align_ref[0] = jnp.broadcast_to(
        own_align[...].astype(jnp.float32).astype(align_ref.dtype), align_ref.shape[1:]
    )

    count = 4 * rows
    columns = keep_ref.shape[1]
    total = jnp.dot(rows_ref[...], kv_ref[...], preferred_element_type=jnp.float32)
    keep_ref[:count, :] = total[:, :columns]
    send_ref[:count, :] = total[:, columns:]
    total = jnp.dot(audio_ref[...], query_ref[...], preferred_element_type=jnp.float32)
    folded = 2 * audio_rows
    for side in range(2):
        at = slice(side * folded, (side + 1) * folded)
        to = slice(side * HEAD_DIM, (side + 1) * HEAD_DIM)
        keep_ref[count:, to] = total[at, :HEAD_DIM]
        send_ref[count:, to] = total[at, HEAD_DIM:]


def attend(queries, kv_ref, frames_ref, align):
    scores = lax.dot_general(
        queries,
        kv_ref[:, :HEAD_DIM],
        (((1,), (1,)), ((), ())),
        preferred_element_type=jnp.float32,
    ) * (1.0 / HEAD_DIM**0.5)
    scores = scores - SLOPE * jnp.abs(frames_ref[...] - align) / FRAMES
    exp_terms = jnp.exp(scores - jnp.max(scores, axis=1, keepdims=True))
    weighted = jnp.dot(
        exp_terms.astype(jnp.bfloat16), kv_ref[:, HEAD_DIM:], preferred_element_type=jnp.float32
    )
    return (weighted / jnp.sum(exp_terms, axis=1, keepdims=True)).astype(jnp.bfloat16)


def attention_body(frames_ref, align_ref, keep_ref, came_ref, *refs):
    *out_refs, kv_ref, query_ref = refs
    count, audio_rows = kv_ref.shape[0], query_ref.shape[1]

    def summed(rows, columns=slice(None)):
        return (keep_ref[rows, columns] + came_ref[rows, columns]).astype(jnp.bfloat16)

    kv_ref[...] = summed(slice(0, count))
    for slot in range(4):
        side, half = divmod(slot, 2)
        query_ref[slot] = summed(
            slice(count + half * audio_rows, count + (half + 1) * audio_rows),
            slice(side * HEAD_DIM, (side + 1) * HEAD_DIM),
        )
    for bit, out_ref in enumerate(out_refs):
        align = align_ref[bit].astype(jnp.float32)[:8].T[:, :1]
        out_ref[...] = attend(query_ref[bit], kv_ref, frames_ref, align)


def out_body(*refs):
    piece_refs, (audio_ref, own_w, *part_refs) = refs[:4], refs[4:10]
    total_ref, late_ref, heads_ref, weight_ref, residual_ref, sems = refs[10:]
    seq_at, grp_at = lax.axis_index("seq"), lax.axis_index("grp")
    place = lax.axis_index("mem") * 2 + lax.axis_index("rep")
    copy = pltpu.make_async_copy(own_w, weight_ref.at[0], sems.at[0])
    copy.start()
    width = residual_ref.shape[1]
    columns = pl.ds(pl.multiple_of(place * width, width), width)
    residual_copy = pltpu.make_async_copy(audio_ref.at[:, columns], residual_ref, sems.at[1])
    residual_copy.start()
    for bit, piece_ref in enumerate(piece_refs):
        heads_ref[seq_at ^ bit] = piece_ref[...]
    heads = jnp.concatenate([heads_ref[head] for head in range(heads_ref.shape[0])], axis=1)

    def half(group):
        return jnp.concatenate([heads_ref[2 * group], heads_ref[2 * group + 1]], axis=1)

    mine = half(grp_at)
    late_ref[...] = half(1 - grp_at)
    partner_w, third_w, third_rest_w, fourth_w = part_refs
    depth = partner_w.shape[0]
    weight_ref[1, pl.ds(pl.multiple_of(grp_at * depth, depth), depth)] = third_w[...]
    weight_ref[1, pl.ds(pl.multiple_of((1 - grp_at) * depth, depth), depth)] = third_rest_w[...]

    def product(rows, weight):
        return jnp.dot(rows, weight, preferred_element_type=jnp.float32)

    total_ref[1] = product(mine, partner_w[...])
    total_ref[3] = product(mine, fourth_w[...])
    total_ref[2] = product(heads, weight_ref[1])
    copy.wait()
    total_ref[0] = product(heads, weight_ref[0])
    residual_copy.wait()
    total_ref[seq_at ^ place] += residual_ref[...].astype(jnp.float32)


def late_out_body(total_ref, late_ref, partner_w, fourth_w, send_ref, keep_ref):
    place = lax.axis_index("mem") * 2 + lax.axis_index("rep")
    for bit in range(4):
        slot = lax.axis_index("seq") ^ bit ^ place
        value = total_ref[bit]
        if bit % 2:
            weight = (partner_w if bit == 1 else fourth_w)[...]
            value += jnp.dot(late_ref[...], weight, preferred_element_type=jnp.float32)

        @pl.when(slot % 2 == 1)
        def _():
            send_ref[slot // 2] = value.astype(send_ref.dtype)

        @pl.when(slot % 2 == 0)
        def _():
            keep_ref[slot // 2] = value


def by_head(video_cache, plan, alignment, audio_tokens, kv_weight, query_weight, out_weight):
    seq_size = lax.axis_size("seq")
    seq_at = lax.axis_index("seq")
    video_rows = video_cache.shape[1]
    audio_rows = audio_tokens.shape[0]
    half_depth, width = kv_weight.shape[0] // 2, 2 * HEAD_DIM
    query_quarter = query_weight.shape[0] // 4

    def bfloat(*shape):
        return jax.ShapeDtypeStruct(shape, jnp.bfloat16)

    packed, other, out_half = kernel_call(
        first_body,
        [
            bfloat(2 * video_rows + audio_rows, half_depth),
            bfloat(half_depth + query_quarter, kv_weight.shape[1]),
            bfloat(out_weight.shape[0] // 2, out_weight.shape[1]),
        ],
        [plan, video_cache, audio_tokens, kv_weight, query_weight, out_weight],
        scratch=[
            pltpu.VMEM((3, video_rows, 2 * half_depth), jnp.bfloat16),
            pltpu.VMEM((2 * video_rows + audio_rows, half_depth), jnp.bfloat16),
            pltpu.VMEM((half_depth + query_quarter, kv_weight.shape[1]), jnp.bfloat16),
            pltpu.VMEM((out_weight.shape[0] // 2, out_weight.shape[1]), jnp.bfloat16),
            pltpu.SMEM(plan.shape, jnp.int32),
            pltpu.SemaphoreType.DMA((26,)),
        ],
        loose_in=(0, 1, 2, 3, 4, 5),
        loose_out=(0, 1, 2),
        limit=61,
    )

    tokens = [packed, swap(packed, "seq", 1), swap(packed, "seq", 2)]
    across = [swap(packed, "mem", 1)]
    other = swap(other, "rep", 1)
    rows = half_depth // 2 + query_quarter // 2
    weight_own, *pieces = kernel_call(
        weight_body,
        [bfloat(2 * rows, 2 * width)] + [bfloat(rows + 16, 2 * width)] * 3,
        [alignment[None], kv_weight, query_weight, other],
        limit=4,
    )
    pieces = [swap(piece, "seq", bit) for bit, piece in enumerate(pieces, 1)]

    across += [swap(tokens[1], "mem", 1), swap(tokens[2], "mem", 1)]
    near_align = pieces[0][rows:, :audio_rows].astype(jnp.float32)
    tokens[2], near_align = lax.optimization_barrier((tokens[2], near_align))
    tokens.append(swap(tokens[2], "seq", 1))
    pieces[0], across[0], across[1] = lax.optimization_barrier(
        (pieces[0], across[0], across[1])
    )
    rest = [swap(pieces[0], "grp", 1)]
    tokens[3], across[2], rest[0], pieces[1] = lax.optimization_barrier(
        (tokens[3], across[2], rest[0], pieces[1])
    )
    across.append(swap(tokens[3], "mem", 1))
    rest.append(swap(pieces[1], "grp", 1))
    pieces[2], rest[1] = lax.optimization_barrier((pieces[2], rest[1]))
    rest.append(swap(pieces[2], "grp", 1))

    out_half, tokens[3] = lax.optimization_barrier((out_half, tokens[3]))
    out_third, out_partner = swap(out_half, "seq", 2), swap(out_half, "seq", 1)
    weights = [weight_own]
    for piece, other in zip(pieces, rest):
        weights += [piece, other]
    rows = seq_size * (video_rows + audio_rows // 2)
    sums = jax.ShapeDtypeStruct((rows, width), jnp.float32)
    aligns, send, keep = kernel_call(
        products_body,
        [bfloat(4, 16, audio_rows), sums, sums],
        [value for pair in zip(tokens, across) for value in pair] + weights
        + [alignment[None], near_align],
        scratch=[
            pltpu.VMEM((seq_size * video_rows, 4 * half_depth), jnp.bfloat16),
            pltpu.VMEM((seq_size * audio_rows, 8 * query_quarter), jnp.bfloat16),
            pltpu.VMEM((4 * half_depth, 2 * width), jnp.bfloat16),
            pltpu.VMEM((8 * query_quarter, width), jnp.bfloat16),
        ],
        limit=15,
    )
    send, out_third, out_partner = lax.optimization_barrier((send, out_third, out_partner))
    came = swap(send, "rep", 1)
    third_rest, out_fourth = swap(out_third, "grp", 1), swap(out_third, "seq", 1)

    span = video_rows * seq_size
    blocks = jnp.stack([seq_at, seq_at ^ 1, seq_at ^ 2, seq_at ^ 3])
    positions = blocks[:, None] * video_rows + jnp.arange(video_rows, dtype=jnp.int32)[None, :]
    frames_video = (positions.reshape(1, span) * FRAMES // span).astype(jnp.float32)
    own_piece, near_piece, far_piece, farther_piece = kernel_call(
        attention_body,
        [bfloat(audio_rows, HEAD_DIM)] * 4,
        [frames_video, aligns, keep, came],
        scratch=[
            pltpu.VMEM((span, width), jnp.bfloat16),
            pltpu.VMEM((seq_size, audio_rows, HEAD_DIM), jnp.bfloat16),
        ],
        limit=9,
    )
    third_rest, out_partner, own_piece = lax.optimization_barrier(
        (third_rest, out_partner, own_piece)
    )
    fourth_rest, partner_rest = swap(third_rest, "seq", 1), swap(out_partner, "grp", 1)
    far_piece = swap(far_piece, "seq", 2)
    farther_piece = swap(farther_piece, "seq", 3)
    near_piece = swap(near_piece, "seq", 1)

    columns = out_weight.shape[1]
    total, late_heads = kernel_call(
        out_body,
        [
            jax.ShapeDtypeStruct((seq_size, audio_rows, columns), jnp.float32),
            bfloat(audio_rows, 2 * HEAD_DIM),
        ],
        [
            own_piece,
            near_piece,
            far_piece,
            farther_piece,
            audio_tokens,
            out_weight,
            out_partner,
            out_third,
            third_rest,
            out_fourth,
        ],
        scratch=[
            pltpu.VMEM((seq_size, audio_rows, HEAD_DIM), jnp.bfloat16),
            pltpu.VMEM((2, *out_weight.shape), jnp.bfloat16),
            pltpu.VMEM((audio_rows, columns), jnp.bfloat16),
            pltpu.SemaphoreType.DMA((2,)),
        ],
        loose_in=(4, 5),
        limit=7,
        cost=pl.CostEstimate(flops=10000000000, bytes_accessed=10000000, transcendentals=0),
    )
    send, keep = kernel_call(
        late_out_body,
        [
            bfloat(2, audio_rows, columns),
            jax.ShapeDtypeStruct((2, audio_rows, columns), jnp.float32),
        ],
        [total, late_heads, partner_rest, fourth_rest],
        limit=5,
    )
    came = swap(send, "rep", 1)
    across = swap((keep[1] + came[1].astype(jnp.float32)).astype(jnp.bfloat16), "mem", 1)
    own_part = taylor(video_cache, plan, 2 * half_depth)
    audio_output = (
        keep[0] + came[0].astype(jnp.float32) + across.astype(jnp.float32)
    ).astype(jnp.bfloat16)
    return (own_part, audio_output)


def solution(mesh):
    sizes = dict(mesh.shape)
    square = (sizes["grp"], sizes["seq"], sizes["mem"], sizes["rep"]) == (2, 4, 2, 2)

    def on_device(*arrays):
        heads = arrays[5].shape[1] // HEAD_DIM
        return (by_head if square and heads == sizes["seq"] else general)(*arrays)

    return jax.shard_map(
        on_device,
        mesh=mesh,
        in_specs=(
            P(None, ("grp", "seq"), "mem"),
            P("grp"),
            P(("grp", "seq")),
            P(("grp", "seq"), None),
            P("seq", ("mem", "rep")),
            P("seq", ("mem", "rep")),
            P(("mem", "rep"), "seq"),
        ),
        out_specs=(P(("grp", "seq"), "mem"), P(("grp", "seq"), ("mem", "rep"))),
        check_vma=False,
    )
```

```python
import math

import jax
import jax.numpy as jnp
from jax import lax
from jax.experimental import pallas as pl
from jax.experimental.pallas import tpu as pltpu
from jax.sharding import PartitionSpec as P

HEAD_DIM = 128
FRAMES = 24


SLOPE = 4.0


def taylor_ratio(plan):
    history = plan.shape[0]
    step_ids = jnp.arange(history, dtype=jnp.int32)
    marked = step_ids * plan
    last_fresh = jnp.max(marked)
    prior_fresh = jnp.max(jnp.where(step_ids < last_fresh, marked, 0))
    return (history - last_fresh).astype(jnp.float32) / (last_fresh - prior_fresh).astype(
        jnp.float32
    )


def combine(orders, step_ratio):
    values = orders.astype(jnp.float32)
    return (values[0] + step_ratio * values[1] + 0.5 * step_ratio * step_ratio * values[2]).astype(
        jnp.bfloat16
    )


def general(video_cache, plan, alignment, audio_tokens, kv_weight, query_weight, out_weight):
    step_ratio = taylor_ratio(plan)
    own_part = combine(video_cache, step_ratio)
    features_all = lax.all_gather(own_part, "mem", axis=1, tiled=True)
    video_rows = features_all.shape[0]
    kv_local = jnp.dot(
        features_all,
        lax.all_gather(kv_weight, "seq", axis=0, tiled=True),
        preferred_element_type=jnp.float32,
    )
    head_size = HEAD_DIM
    local_heads = query_weight.shape[1] // head_size
    kv_local = kv_local.astype(jnp.bfloat16).reshape(video_rows, local_heads, 2, head_size)
    key_rows = kv_local[:, :, 0, :]
    value_rows = kv_local[:, :, 1, :]
    query_full, out_full = (
        lax.all_gather(query_weight, "seq", axis=0, tiled=True),
        lax.all_gather(out_weight, "seq", axis=1, tiled=True),
    )
    audio_rows = audio_tokens.shape[0]
    queries = jnp.dot(audio_tokens, query_full, preferred_element_type=jnp.float32).astype(
        jnp.bfloat16
    )
    queries = queries.reshape(audio_rows, local_heads, head_size)
    scale = 1.0 / head_size**0.5
    span = video_rows * lax.axis_size("seq")
    initial = (
        jnp.full((local_heads, audio_rows), -1e30, jnp.float32),
        jnp.zeros((local_heads, audio_rows), jnp.float32),
        jnp.zeros((local_heads, audio_rows, head_size), jnp.float32),
    )
    key_piece = lax.all_gather(key_rows, "seq", axis=0, tiled=True)
    value_piece = lax.all_gather(value_rows, "seq", axis=0, tiled=True)
    row_count = key_piece.shape[0]
    block_len = math.gcd(row_count, 1024)

    def advance(block_index, carried):
        row_max, row_sum, weighted = carried
        key_block = lax.dynamic_slice_in_dim(key_piece, block_index * block_len, block_len, 0)
        value_block = lax.dynamic_slice_in_dim(value_piece, block_index * block_len, block_len, 0)
        positions = block_index * block_len + jnp.arange(block_len, dtype=jnp.int32)
        frames_video = positions * FRAMES // span
        distance_bias = (
            -SLOPE
            * jnp.abs(frames_video[None, :] - alignment[:, None]).astype(jnp.float32)
            / FRAMES
        )
        scores = (
            jnp.einsum("qhd,khd->hqk", queries, key_block, preferred_element_type=jnp.float32)
            * scale
        )
        scores = scores + distance_bias[None]
        new_max = jnp.maximum(row_max, jnp.max(scores, axis=2))
        rescale = jnp.exp(row_max - new_max)
        exp_terms = jnp.exp(scores - new_max[:, :, None])
        row_sum = row_sum * rescale + jnp.sum(exp_terms, axis=2)
        weighted = weighted * rescale[:, :, None] + jnp.einsum(
            "hqk,khd->hqd",
            exp_terms.astype(jnp.bfloat16),
            value_block,
            preferred_element_type=jnp.float32,
        )
        return (new_max, row_sum, weighted)

    row_max, row_sum, weighted = lax.fori_loop(0, row_count // block_len, advance, initial)
    attended = (weighted / row_sum[:, :, None]).astype(jnp.bfloat16)
    attended = jnp.transpose(attended, (1, 0, 2)).reshape(audio_rows, local_heads * head_size)
    partial_update = jnp.dot(attended, out_full, preferred_element_type=jnp.float32)
    update = lax.psum_scatter(
        partial_update.astype(jnp.bfloat16), ("mem", "rep"), scatter_dimension=1, tiled=True
    ).astype(jnp.float32)
    own_columns = update.shape[1]
    residual = lax.dynamic_slice_in_dim(
        audio_tokens, lax.axis_index(("mem", "rep")) * own_columns, own_columns, 1
    )
    audio_output = (residual.astype(jnp.float32) + update).astype(jnp.bfloat16)
    return (own_part, audio_output)


def swap(value, axis, bit):
    size = lax.axis_size(axis)
    return lax.ppermute(value, axis, [(i, i ^ bit) for i in range(size)])


VMEM = pl.BlockSpec(memory_space=pltpu.VMEM)
SMEM = pl.BlockSpec(memory_space=pltpu.SMEM)
ANY = pl.BlockSpec(memory_space=pl.ANY)
HBM = pl.BlockSpec(memory_space=pltpu.HBM)


def kernel_call(body, outs, ins, after=(), scratch=(), smem=(), loose_in=(), loose_out=(), limit=14, cost=None):
    def whole(*refs):
        body(*refs[: len(ins)], *refs[len(ins) + len(after) :])

    spots = [SMEM if i in smem else HBM if i in loose_in else VMEM for i in range(len(ins))]
    return pl.pallas_call(
        whole,
        out_shape=outs,
        in_specs=spots + [ANY] * len(after),
        out_specs=[HBM if i in loose_out else VMEM for i in range(len(outs))],
        scratch_shapes=scratch,
        cost_estimate=cost,
        compiler_params=pltpu.CompilerParams(vmem_limit_bytes=limit * 2**20),
    )(*ins, *after)


def plan_ratio(plan_ref, columns):
    history = plan_ref.shape[0]
    last_fresh, prior_fresh = jnp.int32(0), jnp.int32(0)
    for step in range(history):
        fresh = plan_ref[step] == 1
        prior_fresh = jnp.where(fresh, last_fresh, prior_fresh)
        last_fresh = jnp.where(fresh, step, last_fresh)
    ahead = jnp.full((1, columns), history - last_fresh, jnp.int32).astype(jnp.float32)
    apart = jnp.full((1, columns), last_fresh - prior_fresh, jnp.int32).astype(jnp.float32)
    return ahead / apart


def taylor_rows(cache_ref, out_ref, step_ratio, first, last):
    half_square = 0.5 * step_ratio * step_ratio
    for at in range(first, last, 16):
        terms = [cache_ref[order, at : at + 16, :].astype(jnp.float32) for order in range(3)]
        out_ref[at : at + 16, :] = (
            terms[0] + step_ratio * terms[1] + half_square * terms[2]
        ).astype(jnp.bfloat16)


def taylor_body(plan_ref, cache_ref, out_ref):
    rows, columns = out_ref.shape
    taylor_rows(cache_ref, out_ref, plan_ratio(plan_ref, columns), 0, rows)


def taylor(video_cache, plan, width):
    orders, rows, columns = video_cache.shape
    return pl.pallas_call(
        taylor_body,
        out_shape=jax.ShapeDtypeStruct((rows, columns), jnp.bfloat16),
        grid=(columns // width,),
        in_specs=[SMEM, pl.BlockSpec((orders, rows, width), lambda i: (0, 0, i))],
        out_specs=pl.BlockSpec((rows, width), lambda i: (0, i)),
        compiler_params=pltpu.CompilerParams(vmem_limit_bytes=6 * 2**20),
    )(plan, video_cache)


def first_body(
    plan_ref,
    cache_ref,
    audio_ref,
    kv_ref,
    query_ref,
    out_w,
    packed_ref,
    other_ref,
    half_ref,
    held_ref,
    made_ref,
    other_vmem,
    half_vmem,
    plan_smem,
    sems,
):
    rep_at, mem_at, grp_at = (lax.axis_index(name) for name in ("rep", "mem", "grp"))
    rows, width = held_ref.shape[1:]
    width = width // 2
    copies = []

    def copy(source, target):
        copies.append(pltpu.make_async_copy(source, target, sems.at[len(copies)]))

    def part(index, size):
        return pl.ds(pl.multiple_of(index * size, size), size)

    plan_copy = pltpu.make_async_copy(plan_ref, plan_smem, sems.at[25])
    plan_copy.start()
    blocks = 4
    step = rows // blocks
    for block in range(blocks):
        at = pl.ds(block * step, step)
        for shard in range(2):
            copy(
                cache_ref.at[:, at, part(2 * shard + rep_at, width)],
                held_ref.at[:, at, pl.ds(shard * width, width)],
            )
    lane = width // 2
    for shard in range(2):
        copy(
            audio_ref.at[:, part(2 * (2 * mem_at + shard) + rep_at, lane)],
            made_ref.at[pl.ds(2 * rows, audio_ref.shape[0]), pl.ds(shard * lane, lane)],
        )
    depth, columns = kv_ref.shape[0] // 2, query_ref.shape[1]
    copy(kv_ref.at[part(1 - rep_at, depth)], other_vmem.at[pl.ds(0, depth)])
    quarter = query_ref.shape[0] // 4
    for side in range(2):
        copy(
            query_ref.at[part(2 * (1 - rep_at) + side, quarter)],
            other_vmem.at[pl.ds(depth, quarter), pl.ds(side * columns, columns)],
        )
    copy(out_w.at[part(grp_at, half_ref.shape[0])], half_vmem)
    for started in copies:
        started.start()
    plan_copy.wait()
    step_ratio = plan_ratio(plan_smem, width)
    for block in range(blocks):
        for shard in range(2):
            copies[2 * block + shard].wait()
            taylor_rows(
                held_ref.at[:, :, pl.ds(shard * width, width)],
                made_ref.at[pl.ds(shard * rows, rows)],
                step_ratio,
                block * step,
                (block + 1) * step,
            )
            at = pl.ds(shard * rows + block * step, step)
            copy(made_ref.at[at], packed_ref.at[at])
            copies[-1].start()
    audio_at = pl.ds(2 * rows, audio_ref.shape[0])
    stages = (
        (2, made_ref.at[audio_at], packed_ref.at[audio_at]),
        (3, other_vmem, other_ref),
        (1, half_vmem, half_ref),
    )
    at = 2 * blocks
    for count, source, target in stages:
        for arriving in copies[at : at + count]:
            arriving.wait()
        at += count
        copy(source, target)
        copies[-1].start()
    for leaving in copies[at:]:
        leaving.wait()


def weight_body(align_ref, kv_ref, query_ref, other_ref, own_ref, *piece_refs):
    seq_at, rep_at, grp_at = (lax.axis_index(name) for name in ("seq", "rep", "grp"))
    kv_half, query_half = kv_ref.shape[0] // 2, query_ref.shape[0] // 2
    kv_rows, query_rows = kv_half // 2, query_half // 2
    fold = query_rows // 2

    def fill(out_ref, bit, group, kv_at, query_at):
        head = seq_at ^ bit
        width = 2 * HEAD_DIM
        lanes = pl.ds(pl.multiple_of(head * width, width), width)
        at = pl.ds(pl.multiple_of(rep_at * kv_half + group * kv_rows, kv_rows), kv_rows)
        out_ref[kv_at : kv_at + kv_rows, :width] = kv_ref[at, lanes]
        at = pl.ds(pl.multiple_of(group * kv_rows, kv_rows), kv_rows)
        out_ref[kv_at : kv_at + kv_rows, width:] = other_ref[at, lanes]
        lanes = pl.ds(pl.multiple_of(head * HEAD_DIM, HEAD_DIM), HEAD_DIM)
        other_lanes = pl.ds(
            pl.multiple_of(group * query_ref.shape[1] + head * HEAD_DIM, HEAD_DIM), HEAD_DIM
        )
        for side in range(2):
            first = rep_at * query_half + group * query_rows + side * fold
            at = pl.ds(pl.multiple_of(first, fold), fold)
            to = slice(query_at, query_at + fold)
            out_ref[to, side * width : side * width + HEAD_DIM] = query_ref[at, lanes]
            out_ref[to, side * width + HEAD_DIM : (side + 1) * width] = other_ref[
                kv_half + side * fold : kv_half + (side + 1) * fold, other_lanes
            ]

    for group in range(2):
        fill(own_ref, 0, group, group * kv_rows, kv_half + group * fold)
    for bit, piece_ref in enumerate(piece_refs, 1):
        fill(piece_ref, bit, grp_at, 0, kv_rows)
        spare = (piece_ref.shape[0] - kv_rows - fold, piece_ref.shape[1])
        align = align_ref[...].astype(jnp.float32).astype(piece_ref.dtype)
        row = jnp.concatenate(
            [align, jnp.zeros((1, spare[1] - align.shape[1]), piece_ref.dtype)], axis=1
        )
        piece_ref[kv_rows + fold :, :] = jnp.broadcast_to(row, spare)


def lay_tokens(slot, rows, use_own, own_ref, across_ref, rows_ref, audio_ref):
    depth, lane = rows_ref.shape[1] // 2, audio_ref.shape[1] // 2
    audio_rows = own_ref.shape[0] - 2 * rows
    for used, packed_ref in ((use_own, own_ref), (jnp.logical_not(use_own), across_ref)):

        @pl.when(used)
        def _():
            for part in range(2):
                rows_ref[
                    slot * rows : (slot + 1) * rows, part * depth : (part + 1) * depth
                ] = packed_ref[part * rows : (part + 1) * rows, :]
                audio_ref[
                    slot * audio_rows : (slot + 1) * audio_rows, part * lane : (part + 1) * lane
                ] = packed_ref[2 * rows :, part * lane : (part + 1) * lane]


def lay_weights(piece_ref, part, group, at, kv_ref, query_ref):
    kv_half, fold, width = kv_ref.shape[0] // 4, query_ref.shape[0] // 8, query_ref.shape[1]
    to = pl.ds(pl.multiple_of((2 * part + group) * kv_half, kv_half), kv_half)
    kv_ref[to, :] = piece_ref[at[0] : at[0] + kv_half, :]
    for side in range(2):
        to = pl.ds(pl.multiple_of((4 * part + 2 * group + side) * fold, fold), fold)
        query_ref[to, :] = piece_ref[at[1] : at[1] + fold, side * width : (side + 1) * width]


def half_places():
    seq_at = lax.axis_index("seq")
    return seq_at % 2, lax.axis_index("mem") == seq_at // 2, lax.axis_index("grp")


def near_body(*refs):
    packed_refs, (own_w, near_w, near_rest) = refs[:6], refs[6:9]
    kv_sum, query_sum, kv_ref, query_ref, rows_ref, audio_ref = refs[9:]
    part, use_own, grp_at = half_places()
    rows = rows_ref.shape[0] // 3
    for slot in range(3):
        lay_tokens(slot, rows, use_own, *packed_refs[2 * slot : 2 * slot + 2], rows_ref, audio_ref)
    kv_half, fold = kv_ref.shape[0] // 4, query_ref.shape[0] // 8
    for group in range(2):
        at = (group * kv_half, 2 * kv_half + group * fold)
        lay_weights(own_w, part, group, at, kv_ref, query_ref)
    for group, piece_ref in ((grp_at, near_w), (1 - grp_at, near_rest)):
        lay_weights(piece_ref, 1 - part, group, (0, kv_half), kv_ref, query_ref)
    kv_sum[...] = jnp.dot(rows_ref[...], kv_ref[...], preferred_element_type=jnp.float32)
    query_sum[...] = jnp.dot(audio_ref[...], query_ref[...], preferred_element_type=jnp.float32)


def products_body(*refs):
    packed_refs, piece_refs = refs[:8], refs[8:12]
    kv_sum, query_sum, near_kv, near_query, own_align, near_align = refs[12:18]
    align_ref, send_ref, keep_ref = refs[18:21]
    rows_ref, audio_ref, last_rows, last_audio, kv_ref, query_ref = refs[21:]
    part, use_own, grp_at = half_places()
    rows, audio_rows = last_rows.shape[0], last_audio.shape[0]
    kv_half, fold = kv_ref.shape[0] // 4, query_ref.shape[0] // 8
    lay_tokens(0, rows, use_own, *packed_refs[6:], last_rows, last_audio)
    for slot in range(4):
        across = jnp.logical_not(use_own)
        lay_tokens(slot, rows, across, *packed_refs[2 * slot : 2 * slot + 2], rows_ref, audio_ref)
    for at, shard in enumerate((part, 1 - part)):
        for group, piece_ref in ((grp_at, piece_refs[2 * at]), (1 - grp_at, piece_refs[2 * at + 1])):
            lay_weights(piece_ref, shard, group, (0, kv_half), kv_ref, query_ref)
    align_ref[0] = jnp.broadcast_to(
        own_align[...].astype(jnp.float32).astype(align_ref.dtype), align_ref.shape[1:]
    )
    align_ref[1] = near_align[...].astype(align_ref.dtype)
    for bit, piece_ref in ((2, piece_refs[0]), (3, piece_refs[2])):
        align_ref[bit] = piece_ref[kv_half + fold :, : align_ref.shape[2]]

    def product(left, right):
        return jnp.dot(left[...], right[...], preferred_element_type=jnp.float32)

    columns = keep_ref.shape[1]
    first, count = 3 * rows, 4 * rows
    total = product(rows_ref, kv_ref)
    for at, more in (
        (slice(0, first), kv_sum[...]),
        (slice(first, count), product(last_rows, near_kv)),
    ):
        keep_ref[at, :] = total[at, :columns] + more[:, :columns]
        send_ref[at, :] = total[at, columns:] + more[:, columns:]
    total = product(audio_ref, query_ref)
    last = product(last_audio, near_query)
    for slot in range(4):
        side, half = divmod(slot, 2)
        more = last if slot == 3 else query_sum[slot * audio_rows : (slot + 1) * audio_rows, :]
        part_sum = total[slot * audio_rows : (slot + 1) * audio_rows] + more
        at = slice(count + half * audio_rows, count + (half + 1) * audio_rows)
        to = slice(side * HEAD_DIM, (side + 1) * HEAD_DIM)
        keep_ref[at, to] = part_sum[:, :HEAD_DIM]
        send_ref[at, to] = part_sum[:, HEAD_DIM:]


def attend(queries, kv_ref, frames_ref, align):
    scores = lax.dot_general(
        queries,
        kv_ref[:, :HEAD_DIM],
        (((1,), (1,)), ((), ())),
        preferred_element_type=jnp.float32,
    ) * (1.0 / HEAD_DIM**0.5)
    scores = scores - SLOPE * jnp.abs(frames_ref[...] - align) / FRAMES
    exp_terms = jnp.exp(scores - jnp.max(scores, axis=1, keepdims=True))
    weighted = jnp.dot(
        exp_terms.astype(jnp.bfloat16), kv_ref[:, HEAD_DIM:], preferred_element_type=jnp.float32
    )
    return (weighted / jnp.sum(exp_terms, axis=1, keepdims=True)).astype(jnp.bfloat16)


def attention_body(frames_ref, align_ref, keep_ref, came_ref, *refs):
    *out_refs, kv_ref, query_ref = refs
    count, audio_rows = kv_ref.shape[0], query_ref.shape[1]

    def summed(rows, columns=slice(None)):
        return (keep_ref[rows, columns] + came_ref[rows, columns]).astype(jnp.bfloat16)

    kv_ref[...] = summed(slice(0, count))
    for slot in range(4):
        side, half = divmod(slot, 2)
        query_ref[slot] = summed(
            slice(count + half * audio_rows, count + (half + 1) * audio_rows),
            slice(side * HEAD_DIM, (side + 1) * HEAD_DIM),
        )
    for bit, out_ref in enumerate(out_refs):
        align = align_ref[bit].astype(jnp.float32)[:8].T[:, :1]
        out_ref[...] = attend(query_ref[bit], kv_ref, frames_ref, align)


def out_body(*refs):
    piece_refs, (audio_ref, own_w, *part_refs) = refs[:4], refs[4:10]
    total_ref, late_ref, heads_ref, weight_ref, residual_ref, sems = refs[10:]
    seq_at, grp_at = lax.axis_index("seq"), lax.axis_index("grp")
    place = lax.axis_index("mem") * 2 + lax.axis_index("rep")
    copy = pltpu.make_async_copy(own_w, weight_ref.at[0], sems.at[0])
    copy.start()
    width = residual_ref.shape[1]
    columns = pl.ds(pl.multiple_of(place * width, width), width)
    residual_copy = pltpu.make_async_copy(audio_ref.at[:, columns], residual_ref, sems.at[1])
    residual_copy.start()
    for bit, piece_ref in enumerate(piece_refs):
        heads_ref[seq_at ^ bit] = piece_ref[...]
    heads = jnp.concatenate([heads_ref[head] for head in range(heads_ref.shape[0])], axis=1)

    def half(group):
        return jnp.concatenate([heads_ref[2 * group], heads_ref[2 * group + 1]], axis=1)

    mine = half(grp_at)
    late_ref[...] = half(1 - grp_at)
    partner_w, third_w, third_rest_w, fourth_w = part_refs
    depth = partner_w.shape[0]
    weight_ref[1, pl.ds(pl.multiple_of(grp_at * depth, depth), depth)] = third_w[...]
    weight_ref[1, pl.ds(pl.multiple_of((1 - grp_at) * depth, depth), depth)] = third_rest_w[...]

    def product(rows, weight):
        return jnp.dot(rows, weight, preferred_element_type=jnp.float32)

    total_ref[1] = product(mine, partner_w[...])
    total_ref[3] = product(mine, fourth_w[...])
    total_ref[2] = product(heads, weight_ref[1])
    copy.wait()
    total_ref[0] = product(heads, weight_ref[0])
    residual_copy.wait()
    total_ref[seq_at ^ place] += residual_ref[...].astype(jnp.float32)


def late_out_body(total_ref, late_ref, partner_w, fourth_w, send_ref, keep_ref):
    place = lax.axis_index("mem") * 2 + lax.axis_index("rep")
    for bit in range(4):
        slot = lax.axis_index("seq") ^ bit ^ place
        value = total_ref[bit]
        if bit % 2:
            weight = (partner_w if bit == 1 else fourth_w)[...]
            value += jnp.dot(late_ref[...], weight, preferred_element_type=jnp.float32)

        @pl.when(slot % 2 == 1)
        def _():
            send_ref[slot // 2] = value.astype(send_ref.dtype)

        @pl.when(slot % 2 == 0)
        def _():
            keep_ref[slot // 2] = value


def by_head(video_cache, plan, alignment, audio_tokens, kv_weight, query_weight, out_weight):
    seq_size = lax.axis_size("seq")
    seq_at = lax.axis_index("seq")
    video_rows = video_cache.shape[1]
    audio_rows = audio_tokens.shape[0]
    half_depth, width = kv_weight.shape[0] // 2, 2 * HEAD_DIM
    query_quarter = query_weight.shape[0] // 4

    def bfloat(*shape):
        return jax.ShapeDtypeStruct(shape, jnp.bfloat16)

    packed, other, out_half = kernel_call(
        first_body,
        [
            bfloat(2 * video_rows + audio_rows, half_depth),
            bfloat(half_depth + query_quarter, kv_weight.shape[1]),
            bfloat(out_weight.shape[0] // 2, out_weight.shape[1]),
        ],
        [plan, video_cache, audio_tokens, kv_weight, query_weight, out_weight],
        scratch=[
            pltpu.VMEM((3, video_rows, 2 * half_depth), jnp.bfloat16),
            pltpu.VMEM((2 * video_rows + audio_rows, half_depth), jnp.bfloat16),
            pltpu.VMEM((half_depth + query_quarter, kv_weight.shape[1]), jnp.bfloat16),
            pltpu.VMEM((out_weight.shape[0] // 2, out_weight.shape[1]), jnp.bfloat16),
            pltpu.SMEM(plan.shape, jnp.int32),
            pltpu.SemaphoreType.DMA((26,)),
        ],
        loose_in=(0, 1, 2, 3, 4, 5),
        loose_out=(0, 1, 2),
        limit=61,
    )

    tokens = [packed, swap(packed, "seq", 1), swap(packed, "seq", 2)]
    across = [swap(packed, "mem", 1)]
    other = swap(other, "rep", 1)
    rows = (half_depth + query_quarter) // 2
    weight_own, *pieces = kernel_call(
        weight_body,
        [bfloat(2 * rows, 2 * width)] + [bfloat(rows + 16, 2 * width)] * 3,
        [alignment[None], kv_weight, query_weight, other],
        limit=4,
    )
    pieces = [swap(piece, "seq", bit) for bit, piece in enumerate(pieces, 1)]

    across += [swap(tokens[1], "mem", 1), swap(tokens[2], "mem", 1)]
    near_align = pieces[0][rows:, :audio_rows].astype(jnp.float32)
    tokens[2], near_align = lax.optimization_barrier((tokens[2], near_align))
    tokens.append(swap(tokens[2], "seq", 1))
    pieces[0], across[0], across[1] = lax.optimization_barrier(
        (pieces[0], across[0], across[1])
    )
    rest = [swap(pieces[0], "grp", 1)]
    tokens[3], across[2], rest[0], pieces[1] = lax.optimization_barrier(
        (tokens[3], across[2], rest[0], pieces[1])
    )
    packed_shape = (seq_size * video_rows, 2 * half_depth), (seq_size * audio_rows, half_depth)
    weight_shape = (2 * half_depth, 2 * width), (half_depth, width)
    near_sums = kernel_call(
        near_body,
        [
            jax.ShapeDtypeStruct((3 * video_rows, 2 * width), jnp.float32),
            jax.ShapeDtypeStruct((3 * audio_rows, width), jnp.float32),
            *(bfloat(*shape) for shape in weight_shape),
        ],
        [value for pair in zip(tokens[:3], across) for value in pair]
        + [weight_own, pieces[0], rest[0]],
        scratch=[
            pltpu.VMEM((3 * video_rows, 2 * half_depth), jnp.bfloat16),
            pltpu.VMEM((3 * audio_rows, half_depth), jnp.bfloat16),
        ],
        limit=12,
        cost=pl.CostEstimate(flops=1000000000, bytes_accessed=1000000, transcendentals=0),
    )
    across.append(swap(tokens[3], "mem", 1))
    rest.append(swap(pieces[1], "grp", 1))
    pieces[2], rest[1], *near_sums = lax.optimization_barrier((pieces[2], rest[1], *near_sums))
    rest.append(swap(pieces[2], "grp", 1))

    out_half, tokens[3] = lax.optimization_barrier((out_half, tokens[3]))
    out_third, out_partner = swap(out_half, "seq", 2), swap(out_half, "seq", 1)
    rows = seq_size * (video_rows + audio_rows // 2)
    sums = jax.ShapeDtypeStruct((rows, width), jnp.float32)
    aligns, send, keep = kernel_call(
        products_body,
        [bfloat(seq_size, 16, audio_rows), sums, sums],
        [value for pair in zip(tokens, across) for value in pair]
        + [pieces[1], rest[1], pieces[2], rest[2], *near_sums, alignment[None], near_align],
        scratch=[
            *(pltpu.VMEM(shape, jnp.bfloat16) for shape in packed_shape),
            pltpu.VMEM((video_rows, 2 * half_depth), jnp.bfloat16),
            pltpu.VMEM((audio_rows, half_depth), jnp.bfloat16),
            *(pltpu.VMEM(shape, jnp.bfloat16) for shape in weight_shape),
        ],
        limit=14,
    )
    send, out_third, out_partner = lax.optimization_barrier((send, out_third, out_partner))
    came = swap(send, "rep", 1)
    third_rest, out_fourth = swap(out_third, "grp", 1), swap(out_third, "seq", 1)

    span = video_rows * seq_size
    blocks = jnp.stack([seq_at, seq_at ^ 1, seq_at ^ 2, seq_at ^ 3])
    positions = blocks[:, None] * video_rows + jnp.arange(video_rows, dtype=jnp.int32)[None, :]
    frames_video = (positions.reshape(1, span) * FRAMES // span).astype(jnp.float32)
    own_piece, near_piece, far_piece, farther_piece = kernel_call(
        attention_body,
        [bfloat(audio_rows, HEAD_DIM)] * 4,
        [frames_video, aligns, keep, came],
        scratch=[
            pltpu.VMEM((span, width), jnp.bfloat16),
            pltpu.VMEM((seq_size, audio_rows, HEAD_DIM), jnp.bfloat16),
        ],
        limit=9,
    )
    third_rest, out_partner, own_piece = lax.optimization_barrier(
        (third_rest, out_partner, own_piece)
    )
    fourth_rest, partner_rest = swap(third_rest, "seq", 1), swap(out_partner, "grp", 1)
    far_piece = swap(far_piece, "seq", 2)
    farther_piece = swap(farther_piece, "seq", 3)
    near_piece = swap(near_piece, "seq", 1)

    columns = out_weight.shape[1]
    total, late_heads = kernel_call(
        out_body,
        [
            jax.ShapeDtypeStruct((seq_size, audio_rows, columns), jnp.float32),
            bfloat(audio_rows, 2 * HEAD_DIM),
        ],
        [
            own_piece,
            near_piece,
            far_piece,
            farther_piece,
            audio_tokens,
            out_weight,
            out_partner,
            out_third,
            third_rest,
            out_fourth,
        ],
        scratch=[
            pltpu.VMEM((seq_size, audio_rows, HEAD_DIM), jnp.bfloat16),
            pltpu.VMEM((2, *out_weight.shape), jnp.bfloat16),
            pltpu.VMEM((audio_rows, columns), jnp.bfloat16),
            pltpu.SemaphoreType.DMA((2,)),
        ],
        loose_in=(4, 5),
        limit=7,
        cost=pl.CostEstimate(flops=10000000000, bytes_accessed=10000000, transcendentals=0),
    )
    send, keep = kernel_call(
        late_out_body,
        [
            bfloat(2, audio_rows, columns),
            jax.ShapeDtypeStruct((2, audio_rows, columns), jnp.float32),
        ],
        [total, late_heads, partner_rest, fourth_rest],
        limit=5,
    )
    came = swap(send, "rep", 1)
    across = swap((keep[1] + came[1].astype(jnp.float32)).astype(jnp.bfloat16), "mem", 1)
    own_part = taylor(video_cache, plan, 2 * half_depth)
    audio_output = (
        keep[0] + came[0].astype(jnp.float32) + across.astype(jnp.float32)
    ).astype(jnp.bfloat16)
    return (own_part, audio_output)


def solution(mesh):
    sizes = dict(mesh.shape)
    square = (sizes["grp"], sizes["seq"], sizes["mem"], sizes["rep"]) == (2, 4, 2, 2)

    def on_device(*arrays):
        heads = arrays[5].shape[1] // HEAD_DIM
        return (by_head if square and heads == sizes["seq"] else general)(*arrays)

    return jax.shard_map(
        on_device,
        mesh=mesh,
        in_specs=(
            P(None, ("grp", "seq"), "mem"),
            P("grp"),
            P(("grp", "seq")),
            P(("grp", "seq"), None),
            P("seq", ("mem", "rep")),
            P("seq", ("mem", "rep")),
            P(("mem", "rep"), "seq"),
        ),
        out_specs=(P(("grp", "seq"), "mem"), P(("grp", "seq"), ("mem", "rep"))),
        check_vma=False,
    )
```

```python
import math

import jax
import jax.numpy as jnp
from jax import lax
from jax.experimental import pallas as pl
from jax.experimental.pallas import tpu as pltpu
from jax.sharding import PartitionSpec as P

HEAD_DIM = 128
FRAMES = 24


SLOPE = 4.0


def taylor_ratio(plan):
    history = plan.shape[0]
    step_ids = jnp.arange(history, dtype=jnp.int32)
    marked = step_ids * plan
    last_fresh = jnp.max(marked)
    prior_fresh = jnp.max(jnp.where(step_ids < last_fresh, marked, 0))
    return (history - last_fresh).astype(jnp.float32) / (last_fresh - prior_fresh).astype(
        jnp.float32
    )


def combine(orders, step_ratio):
    values = orders.astype(jnp.float32)
    return (values[0] + step_ratio * values[1] + 0.5 * step_ratio * step_ratio * values[2]).astype(
        jnp.bfloat16
    )


def general(video_cache, plan, alignment, audio_tokens, kv_weight, query_weight, out_weight):
    step_ratio = taylor_ratio(plan)
    own_part = combine(video_cache, step_ratio)
    features_all = lax.all_gather(own_part, "mem", axis=1, tiled=True)
    video_rows = features_all.shape[0]
    kv_local = jnp.dot(
        features_all,
        lax.all_gather(kv_weight, "seq", axis=0, tiled=True),
        preferred_element_type=jnp.float32,
    )
    head_size = HEAD_DIM
    local_heads = query_weight.shape[1] // head_size
    kv_local = kv_local.astype(jnp.bfloat16).reshape(video_rows, local_heads, 2, head_size)
    key_rows = kv_local[:, :, 0, :]
    value_rows = kv_local[:, :, 1, :]
    query_full, out_full = (
        lax.all_gather(query_weight, "seq", axis=0, tiled=True),
        lax.all_gather(out_weight, "seq", axis=1, tiled=True),
    )
    audio_rows = audio_tokens.shape[0]
    queries = jnp.dot(audio_tokens, query_full, preferred_element_type=jnp.float32).astype(
        jnp.bfloat16
    )
    queries = queries.reshape(audio_rows, local_heads, head_size)
    scale = 1.0 / head_size**0.5
    span = video_rows * lax.axis_size("seq")
    initial = (
        jnp.full((local_heads, audio_rows), -1e30, jnp.float32),
        jnp.zeros((local_heads, audio_rows), jnp.float32),
        jnp.zeros((local_heads, audio_rows, head_size), jnp.float32),
    )
    key_piece = lax.all_gather(key_rows, "seq", axis=0, tiled=True)
    value_piece = lax.all_gather(value_rows, "seq", axis=0, tiled=True)
    row_count = key_piece.shape[0]
    block_len = math.gcd(row_count, 1024)

    def advance(block_index, carried):
        row_max, row_sum, weighted = carried
        key_block = lax.dynamic_slice_in_dim(key_piece, block_index * block_len, block_len, 0)
        value_block = lax.dynamic_slice_in_dim(value_piece, block_index * block_len, block_len, 0)
        positions = block_index * block_len + jnp.arange(block_len, dtype=jnp.int32)
        frames_video = positions * FRAMES // span
        distance_bias = (
            -SLOPE
            * jnp.abs(frames_video[None, :] - alignment[:, None]).astype(jnp.float32)
            / FRAMES
        )
        scores = (
            jnp.einsum("qhd,khd->hqk", queries, key_block, preferred_element_type=jnp.float32)
            * scale
        )
        scores = scores + distance_bias[None]
        new_max = jnp.maximum(row_max, jnp.max(scores, axis=2))
        rescale = jnp.exp(row_max - new_max)
        exp_terms = jnp.exp(scores - new_max[:, :, None])
        row_sum = row_sum * rescale + jnp.sum(exp_terms, axis=2)
        weighted = weighted * rescale[:, :, None] + jnp.einsum(
            "hqk,khd->hqd",
            exp_terms.astype(jnp.bfloat16),
            value_block,
            preferred_element_type=jnp.float32,
        )
        return (new_max, row_sum, weighted)

    row_max, row_sum, weighted = lax.fori_loop(0, row_count // block_len, advance, initial)
    attended = (weighted / row_sum[:, :, None]).astype(jnp.bfloat16)
    attended = jnp.transpose(attended, (1, 0, 2)).reshape(audio_rows, local_heads * head_size)
    partial_update = jnp.dot(attended, out_full, preferred_element_type=jnp.float32)
    update = lax.psum_scatter(
        partial_update.astype(jnp.bfloat16), ("mem", "rep"), scatter_dimension=1, tiled=True
    ).astype(jnp.float32)
    own_columns = update.shape[1]
    residual = lax.dynamic_slice_in_dim(
        audio_tokens, lax.axis_index(("mem", "rep")) * own_columns, own_columns, 1
    )
    audio_output = (residual.astype(jnp.float32) + update).astype(jnp.bfloat16)
    return (own_part, audio_output)


def swap(value, axis, bit):
    size = lax.axis_size(axis)
    return lax.ppermute(value, axis, [(i, i ^ bit) for i in range(size)])


VMEM = pl.BlockSpec(memory_space=pltpu.VMEM)
SMEM = pl.BlockSpec(memory_space=pltpu.SMEM)
ANY = pl.BlockSpec(memory_space=pl.ANY)
HBM = pl.BlockSpec(memory_space=pltpu.HBM)


def kernel_call(body, outs, ins, after=(), scratch=(), smem=(), loose_in=(), loose_out=(), limit=14, cost=None):
    def whole(*refs):
        body(*refs[: len(ins)], *refs[len(ins) + len(after) :])

    spots = [SMEM if i in smem else HBM if i in loose_in else VMEM for i in range(len(ins))]
    return pl.pallas_call(
        whole,
        out_shape=outs,
        in_specs=spots + [ANY] * len(after),
        out_specs=[HBM if i in loose_out else VMEM for i in range(len(outs))],
        scratch_shapes=scratch,
        cost_estimate=cost,
        compiler_params=pltpu.CompilerParams(vmem_limit_bytes=limit * 2**20),
    )(*ins, *after)


def plan_ratio(plan_ref, columns):
    history = plan_ref.shape[0]
    last_fresh, prior_fresh = jnp.int32(0), jnp.int32(0)
    for step in range(history):
        fresh = plan_ref[step] == 1
        prior_fresh = jnp.where(fresh, last_fresh, prior_fresh)
        last_fresh = jnp.where(fresh, step, last_fresh)
    ahead = jnp.full((1, columns), history - last_fresh, jnp.int32).astype(jnp.float32)
    apart = jnp.full((1, columns), last_fresh - prior_fresh, jnp.int32).astype(jnp.float32)
    return ahead / apart


def taylor_rows(cache_ref, out_ref, step_ratio, first, last):
    half_square = 0.5 * step_ratio * step_ratio
    for at in range(first, last, 16):
        terms = [cache_ref[order, at : at + 16, :].astype(jnp.float32) for order in range(3)]
        out_ref[at : at + 16, :] = (
            terms[0] + step_ratio * terms[1] + half_square * terms[2]
        ).astype(jnp.bfloat16)


def taylor_body(plan_ref, cache_ref, out_ref):
    rows, columns = out_ref.shape
    taylor_rows(cache_ref, out_ref, plan_ratio(plan_ref, columns), 0, rows)


def taylor(video_cache, plan, width):
    orders, rows, columns = video_cache.shape
    return pl.pallas_call(
        taylor_body,
        out_shape=jax.ShapeDtypeStruct((rows, columns), jnp.bfloat16),
        grid=(columns // width,),
        in_specs=[SMEM, pl.BlockSpec((orders, rows, width), lambda i: (0, 0, i))],
        out_specs=pl.BlockSpec((rows, width), lambda i: (0, i)),
        compiler_params=pltpu.CompilerParams(vmem_limit_bytes=6 * 2**20),
    )(plan, video_cache)


def first_body(
    plan_ref,
    cache_ref,
    audio_ref,
    kv_ref,
    query_ref,
    out_w,
    packed_ref,
    other_ref,
    half_ref,
    held_ref,
    made_ref,
    other_vmem,
    half_vmem,
    plan_smem,
    sems,
):
    rep_at, mem_at, grp_at = (lax.axis_index(name) for name in ("rep", "mem", "grp"))
    rows, width = held_ref.shape[1:]
    width = width // 2
    copies = []

    def copy(source, target):
        copies.append(pltpu.make_async_copy(source, target, sems.at[len(copies)]))

    def part(index, size):
        return pl.ds(pl.multiple_of(index * size, size), size)

    plan_copy = pltpu.make_async_copy(plan_ref, plan_smem, sems.at[25])
    plan_copy.start()
    blocks = 4
    step = rows // blocks
    for block in range(blocks):
        at = pl.ds(block * step, step)
        for shard in range(2):
            copy(
                cache_ref.at[:, at, part(2 * shard + rep_at, width)],
                held_ref.at[:, at, pl.ds(shard * width, width)],
            )
    lane = width // 2
    for shard in range(2):
        copy(
            audio_ref.at[:, part(2 * (2 * mem_at + shard) + rep_at, lane)],
            made_ref.at[pl.ds(2 * rows, audio_ref.shape[0]), pl.ds(shard * lane, lane)],
        )
    depth, columns = kv_ref.shape[0] // 2, query_ref.shape[1]
    copy(kv_ref.at[part(1 - rep_at, depth)], other_vmem.at[pl.ds(0, depth)])
    quarter = query_ref.shape[0] // 4
    for side in range(2):
        copy(
            query_ref.at[part(2 * (1 - rep_at) + side, quarter)],
            other_vmem.at[pl.ds(depth, quarter), pl.ds(side * columns, columns)],
        )
    copy(out_w.at[part(grp_at, half_ref.shape[0])], half_vmem)
    for started in copies:
        started.start()
    plan_copy.wait()
    step_ratio = plan_ratio(plan_smem, width)
    for block in range(blocks):
        for shard in range(2):
            copies[2 * block + shard].wait()
            taylor_rows(
                held_ref.at[:, :, pl.ds(shard * width, width)],
                made_ref.at[pl.ds(shard * rows, rows)],
                step_ratio,
                block * step,
                (block + 1) * step,
            )
            at = pl.ds(shard * rows + block * step, step)
            copy(made_ref.at[at], packed_ref.at[at])
            copies[-1].start()
    audio_at = pl.ds(2 * rows, audio_ref.shape[0])
    stages = (
        (2, made_ref.at[audio_at], packed_ref.at[audio_at]),
        (3, other_vmem, other_ref),
        (1, half_vmem, half_ref),
    )
    at = 2 * blocks
    for count, source, target in stages:
        for arriving in copies[at : at + count]:
            arriving.wait()
        at += count
        copy(source, target)
        copies[-1].start()
    for leaving in copies[at:]:
        leaving.wait()


def weight_body(align_ref, kv_ref, query_ref, other_ref, own_ref, *piece_refs):
    seq_at, rep_at, grp_at = (lax.axis_index(name) for name in ("seq", "rep", "grp"))
    kv_half, query_half = kv_ref.shape[0] // 2, query_ref.shape[0] // 2
    kv_rows, query_rows = kv_half // 2, query_half // 2
    fold = query_rows // 2

    def fill(out_ref, bit, group, kv_at, query_at):
        head = seq_at ^ bit
        width = 2 * HEAD_DIM
        lanes = pl.ds(pl.multiple_of(head * width, width), width)
        at = pl.ds(pl.multiple_of(rep_at * kv_half + group * kv_rows, kv_rows), kv_rows)
        out_ref[kv_at : kv_at + kv_rows, :width] = kv_ref[at, lanes]
        at = pl.ds(pl.multiple_of(group * kv_rows, kv_rows), kv_rows)
        out_ref[kv_at : kv_at + kv_rows, width:] = other_ref[at, lanes]
        lanes = pl.ds(pl.multiple_of(head * HEAD_DIM, HEAD_DIM), HEAD_DIM)
        other_lanes = pl.ds(
            pl.multiple_of(group * query_ref.shape[1] + head * HEAD_DIM, HEAD_DIM), HEAD_DIM
        )
        for side in range(2):
            first = rep_at * query_half + group * query_rows + side * fold
            at = pl.ds(pl.multiple_of(first, fold), fold)
            to = slice(query_at, query_at + fold)
            out_ref[to, side * width : side * width + HEAD_DIM] = query_ref[at, lanes]
            out_ref[to, side * width + HEAD_DIM : (side + 1) * width] = other_ref[
                kv_half + side * fold : kv_half + (side + 1) * fold, other_lanes
            ]

    for group in range(2):
        fill(own_ref, 0, group, group * kv_rows, kv_half + group * fold)
    for bit, piece_ref in enumerate(piece_refs, 1):
        fill(piece_ref, bit, grp_at, 0, kv_rows)
        spare = (piece_ref.shape[0] - kv_rows - fold, piece_ref.shape[1])
        align = align_ref[...].astype(jnp.float32).astype(piece_ref.dtype)
        row = jnp.concatenate(
            [align, jnp.zeros((1, spare[1] - align.shape[1]), piece_ref.dtype)], axis=1
        )
        piece_ref[kv_rows + fold :, :] = jnp.broadcast_to(row, spare)


def lay_tokens(slot, rows, use_own, own_ref, across_ref, rows_ref, audio_ref):
    depth, lane = rows_ref.shape[1] // 2, audio_ref.shape[1] // 2
    audio_rows = own_ref.shape[0] - 2 * rows
    for used, packed_ref in ((use_own, own_ref), (jnp.logical_not(use_own), across_ref)):

        @pl.when(used)
        def _():
            for part in range(2):
                rows_ref[
                    slot * rows : (slot + 1) * rows, part * depth : (part + 1) * depth
                ] = packed_ref[part * rows : (part + 1) * rows, :]
                audio_ref[
                    slot * audio_rows : (slot + 1) * audio_rows, part * lane : (part + 1) * lane
                ] = packed_ref[2 * rows :, part * lane : (part + 1) * lane]


def lay_weights(piece_ref, part, group, at, kv_ref, query_ref):
    kv_half, fold, width = kv_ref.shape[0] // 4, query_ref.shape[0] // 8, query_ref.shape[1]
    to = pl.ds(pl.multiple_of((2 * part + group) * kv_half, kv_half), kv_half)
    kv_ref[to, :] = piece_ref[at[0] : at[0] + kv_half, :]
    for side in range(2):
        to = pl.ds(pl.multiple_of((4 * part + 2 * group + side) * fold, fold), fold)
        query_ref[to, :] = piece_ref[at[1] : at[1] + fold, side * width : (side + 1) * width]


def half_places():
    seq_at = lax.axis_index("seq")
    return seq_at % 2, lax.axis_index("mem") == seq_at // 2, lax.axis_index("grp")


def near_body(*refs):
    packed_refs, (own_w, near_w, near_rest) = refs[:6], refs[6:9]
    kv_sum, query_sum, kv_ref, query_ref, rows_ref, audio_ref = refs[9:]
    part, use_own, grp_at = half_places()
    rows = rows_ref.shape[0] // 3
    for slot in range(3):
        lay_tokens(slot, rows, use_own, *packed_refs[2 * slot : 2 * slot + 2], rows_ref, audio_ref)
    kv_half, fold = kv_ref.shape[0] // 4, query_ref.shape[0] // 8
    for group in range(2):
        at = (group * kv_half, 2 * kv_half + group * fold)
        lay_weights(own_w, part, group, at, kv_ref, query_ref)
    for group, piece_ref in ((grp_at, near_w), (1 - grp_at, near_rest)):
        lay_weights(piece_ref, 1 - part, group, (0, kv_half), kv_ref, query_ref)
    kv_sum[...] = jnp.dot(rows_ref[...], kv_ref[...], preferred_element_type=jnp.float32)
    query_sum[...] = jnp.dot(audio_ref[...], query_ref[...], preferred_element_type=jnp.float32)


def products_body(*refs):
    packed_refs, piece_refs = refs[:8], refs[8:12]
    kv_sum, query_sum, near_kv, near_query, own_align, near_align = refs[12:18]
    align_ref, send_ref, keep_ref = refs[18:21]
    rows_ref, audio_ref, last_rows, last_audio, kv_ref, query_ref = refs[21:]
    part, use_own, grp_at = half_places()
    rows, audio_rows = last_rows.shape[0], last_audio.shape[0]
    kv_half, fold = kv_ref.shape[0] // 4, query_ref.shape[0] // 8
    lay_tokens(0, rows, use_own, *packed_refs[6:], last_rows, last_audio)
    for slot in range(4):
        across = jnp.logical_not(use_own)
        lay_tokens(slot, rows, across, *packed_refs[2 * slot : 2 * slot + 2], rows_ref, audio_ref)
    for at, shard in enumerate((part, 1 - part)):
        for group, piece_ref in ((grp_at, piece_refs[2 * at]), (1 - grp_at, piece_refs[2 * at + 1])):
            lay_weights(piece_ref, shard, group, (0, kv_half), kv_ref, query_ref)
    align_ref[0] = jnp.broadcast_to(
        own_align[...].astype(jnp.float32).astype(align_ref.dtype), align_ref.shape[1:]
    )
    align_ref[1] = near_align[...].astype(align_ref.dtype)
    for bit, piece_ref in ((2, piece_refs[0]), (3, piece_refs[2])):
        align_ref[bit] = piece_ref[kv_half + fold :, : align_ref.shape[2]]

    def product(left, right):
        return jnp.dot(left[...], right[...], preferred_element_type=jnp.float32)

    columns = keep_ref.shape[1]
    first, count = 3 * rows, 4 * rows
    total = product(rows_ref, kv_ref)
    for at, more in (
        (slice(0, first), kv_sum[...]),
        (slice(first, count), product(last_rows, near_kv)),
    ):
        keep_ref[at, :] = total[at, :columns] + more[:, :columns]
        send_ref[at, :] = total[at, columns:] + more[:, columns:]
    total = product(audio_ref, query_ref)
    last = product(last_audio, near_query)
    for slot in range(4):
        side, half = divmod(slot, 2)
        more = last if slot == 3 else query_sum[slot * audio_rows : (slot + 1) * audio_rows, :]
        part_sum = total[slot * audio_rows : (slot + 1) * audio_rows] + more
        at = slice(count + half * audio_rows, count + (half + 1) * audio_rows)
        to = slice(side * HEAD_DIM, (side + 1) * HEAD_DIM)
        keep_ref[at, to] = part_sum[:, :HEAD_DIM]
        send_ref[at, to] = part_sum[:, HEAD_DIM:]


def attend(queries, kv_ref, frames_ref, align):
    scores = lax.dot_general(
        queries,
        kv_ref[:, :HEAD_DIM],
        (((1,), (1,)), ((), ())),
        preferred_element_type=jnp.float32,
    ) * (1.0 / HEAD_DIM**0.5)
    scores = scores - SLOPE * jnp.abs(frames_ref[...] - align) / FRAMES
    exp_terms = jnp.exp(scores - jnp.max(scores, axis=1, keepdims=True))
    weighted = jnp.dot(
        exp_terms.astype(jnp.bfloat16), kv_ref[:, HEAD_DIM:], preferred_element_type=jnp.float32
    )
    return (weighted / jnp.sum(exp_terms, axis=1, keepdims=True)).astype(jnp.bfloat16)


def attention_body(frames_ref, align_ref, keep_ref, came_ref, *refs):
    *out_refs, kv_ref, query_ref = refs
    count, audio_rows = kv_ref.shape[0], query_ref.shape[1]

    def summed(rows, columns=slice(None)):
        return (keep_ref[rows, columns] + came_ref[rows, columns]).astype(jnp.bfloat16)

    kv_ref[...] = summed(slice(0, count))
    for slot in range(4):
        side, half = divmod(slot, 2)
        query_ref[slot] = summed(
            slice(count + half * audio_rows, count + (half + 1) * audio_rows),
            slice(side * HEAD_DIM, (side + 1) * HEAD_DIM),
        )
    for bit, out_ref in enumerate(out_refs):
        align = align_ref[bit].astype(jnp.float32)[:8].T[:, :1]
        out_ref[...] = attend(query_ref[bit], kv_ref, frames_ref, align)


def out_body(*refs):
    piece_refs, (audio_ref, own_w, *part_refs) = refs[:4], refs[4:10]
    total_ref, late_ref, heads_ref, weight_ref, residual_ref, sems = refs[10:]
    seq_at, grp_at = lax.axis_index("seq"), lax.axis_index("grp")
    place = lax.axis_index("mem") * 2 + lax.axis_index("rep")
    copy = pltpu.make_async_copy(own_w, weight_ref.at[0], sems.at[0])
    copy.start()
    width = residual_ref.shape[1]
    columns = pl.ds(pl.multiple_of(place * width, width), width)
    residual_copy = pltpu.make_async_copy(audio_ref.at[:, columns], residual_ref, sems.at[1])
    residual_copy.start()
    for bit, piece_ref in enumerate(piece_refs):
        heads_ref[seq_at ^ bit] = piece_ref[...]
    heads = jnp.concatenate([heads_ref[head] for head in range(heads_ref.shape[0])], axis=1)

    def half(group):
        return jnp.concatenate([heads_ref[2 * group], heads_ref[2 * group + 1]], axis=1)

    mine = half(grp_at)
    late_ref[...] = half(1 - grp_at)
    partner_w, third_w, third_rest_w, fourth_w = part_refs
    depth = partner_w.shape[0]
    weight_ref[1, pl.ds(pl.multiple_of(grp_at * depth, depth), depth)] = third_w[...]
    weight_ref[1, pl.ds(pl.multiple_of((1 - grp_at) * depth, depth), depth)] = third_rest_w[...]

    def product(rows, weight):
        return jnp.dot(rows, weight, preferred_element_type=jnp.float32)

    total_ref[1] = product(mine, partner_w[...])
    total_ref[3] = product(mine, fourth_w[...])
    total_ref[2] = product(heads, weight_ref[1])
    copy.wait()
    total_ref[0] = product(heads, weight_ref[0])
    residual_copy.wait()
    total_ref[seq_at ^ place] += residual_ref[...].astype(jnp.float32)


def late_out_body(total_ref, late_ref, fourth_w, partner_w, send_ref, keep_ref):
    place = lax.axis_index("mem") * 2 + lax.axis_index("rep")
    for bit in range(4):
        slot = lax.axis_index("seq") ^ bit ^ place
        value = total_ref[bit]
        if bit % 2:
            weight = (partner_w if bit == 1 else fourth_w)[...]
            value += jnp.dot(late_ref[...], weight, preferred_element_type=jnp.float32)

        @pl.when(slot % 2 == 1)
        def _():
            send_ref[slot // 2] = value.astype(send_ref.dtype)

        @pl.when(slot % 2 == 0)
        def _():
            keep_ref[slot // 2] = value


def by_head(video_cache, plan, alignment, audio_tokens, kv_weight, query_weight, out_weight):
    seq_size = lax.axis_size("seq")
    seq_at = lax.axis_index("seq")
    video_rows = video_cache.shape[1]
    audio_rows = audio_tokens.shape[0]
    half_depth, width = kv_weight.shape[0] // 2, 2 * HEAD_DIM
    query_quarter = query_weight.shape[0] // 4

    def bfloat(*shape):
        return jax.ShapeDtypeStruct(shape, jnp.bfloat16)

    packed, other, out_half = kernel_call(
        first_body,
        [
            bfloat(2 * video_rows + audio_rows, half_depth),
            bfloat(half_depth + query_quarter, kv_weight.shape[1]),
            bfloat(out_weight.shape[0] // 2, out_weight.shape[1]),
        ],
        [plan, video_cache, audio_tokens, kv_weight, query_weight, out_weight],
        scratch=[
            pltpu.VMEM((3, video_rows, 2 * half_depth), jnp.bfloat16),
            pltpu.VMEM((2 * video_rows + audio_rows, half_depth), jnp.bfloat16),
            pltpu.VMEM((half_depth + query_quarter, kv_weight.shape[1]), jnp.bfloat16),
            pltpu.VMEM((out_weight.shape[0] // 2, out_weight.shape[1]), jnp.bfloat16),
            pltpu.SMEM(plan.shape, jnp.int32),
            pltpu.SemaphoreType.DMA((26,)),
        ],
        loose_in=(0, 1, 2, 3, 4, 5),
        loose_out=(0, 1, 2),
        limit=61,
    )

    tokens = [packed, swap(packed, "seq", 1), swap(packed, "seq", 2)]
    across = [swap(packed, "mem", 1)]
    other = swap(other, "rep", 1)
    rows = (half_depth + query_quarter) // 2
    weight_own, *pieces = kernel_call(
        weight_body,
        [bfloat(2 * rows, 2 * width)] + [bfloat(rows + 16, 2 * width)] * 3,
        [alignment[None], kv_weight, query_weight, other],
        limit=4,
    )
    pieces = [swap(piece, "seq", bit) for bit, piece in enumerate(pieces, 1)]

    across += [swap(tokens[1], "mem", 1), swap(tokens[2], "mem", 1)]
    near_align = pieces[0][rows:, :audio_rows].astype(jnp.float32)
    tokens[2], near_align = lax.optimization_barrier((tokens[2], near_align))
    tokens.append(swap(tokens[2], "seq", 1))
    rest = [swap(pieces[0], "grp", 1)]
    tokens[3], rest[0], pieces[1], across[0], across[1], across[2] = lax.optimization_barrier(
        (tokens[3], rest[0], pieces[1], across[0], across[1], across[2])
    )
    packed_shape = (seq_size * video_rows, 2 * half_depth), (seq_size * audio_rows, half_depth)
    weight_shape = (2 * half_depth, 2 * width), (half_depth, width)
    near_sums = kernel_call(
        near_body,
        [
            jax.ShapeDtypeStruct((3 * video_rows, 2 * width), jnp.float32),
            jax.ShapeDtypeStruct((3 * audio_rows, width), jnp.float32),
            *(bfloat(*shape) for shape in weight_shape),
        ],
        [value for pair in zip(tokens[:3], across) for value in pair]
        + [weight_own, pieces[0], rest[0]],
        scratch=[
            pltpu.VMEM((3 * video_rows, 2 * half_depth), jnp.bfloat16),
            pltpu.VMEM((3 * audio_rows, half_depth), jnp.bfloat16),
        ],
        limit=12,
        cost=pl.CostEstimate(flops=1000000000, bytes_accessed=1000000, transcendentals=0),
    )
    across.append(swap(tokens[3], "mem", 1))
    rest.append(swap(pieces[1], "grp", 1))
    pieces[2], rest[1], *near_sums = lax.optimization_barrier((pieces[2], rest[1], *near_sums))
    rest.append(swap(pieces[2], "grp", 1))

    out_half, tokens[3] = lax.optimization_barrier((out_half, tokens[3]))
    out_third, out_partner = swap(out_half, "seq", 2), swap(out_half, "seq", 1)
    rows = seq_size * (video_rows + audio_rows // 2)
    sums = jax.ShapeDtypeStruct((rows, width), jnp.float32)
    aligns, send, keep = kernel_call(
        products_body,
        [bfloat(seq_size, 16, audio_rows), sums, sums],
        [value for pair in zip(tokens, across) for value in pair]
        + [pieces[1], rest[1], pieces[2], rest[2], *near_sums, alignment[None], near_align],
        scratch=[
            *(pltpu.VMEM(shape, jnp.bfloat16) for shape in packed_shape),
            pltpu.VMEM((video_rows, 2 * half_depth), jnp.bfloat16),
            pltpu.VMEM((audio_rows, half_depth), jnp.bfloat16),
            *(pltpu.VMEM(shape, jnp.bfloat16) for shape in weight_shape),
        ],
        limit=14,
    )
    send, out_third, out_partner = lax.optimization_barrier((send, out_third, out_partner))
    came = swap(send, "rep", 1)
    third_rest, out_fourth = swap(out_third, "grp", 1), swap(out_third, "seq", 1)

    span = video_rows * seq_size
    blocks = jnp.stack([seq_at, seq_at ^ 1, seq_at ^ 2, seq_at ^ 3])
    positions = blocks[:, None] * video_rows + jnp.arange(video_rows, dtype=jnp.int32)[None, :]
    frames_video = (positions.reshape(1, span) * FRAMES // span).astype(jnp.float32)
    own_piece, near_piece, far_piece, farther_piece = kernel_call(
        attention_body,
        [bfloat(audio_rows, HEAD_DIM)] * 4,
        [frames_video, aligns, keep, came],
        scratch=[
            pltpu.VMEM((span, width), jnp.bfloat16),
            pltpu.VMEM((seq_size, audio_rows, HEAD_DIM), jnp.bfloat16),
        ],
        limit=9,
    )
    third_rest, out_partner, own_piece = lax.optimization_barrier(
        (third_rest, out_partner, own_piece)
    )
    fourth_rest, partner_rest = swap(third_rest, "seq", 1), swap(out_partner, "grp", 1)
    far_piece = swap(far_piece, "seq", 2)
    farther_piece = swap(farther_piece, "seq", 3)
    near_piece = swap(near_piece, "seq", 1)

    columns = out_weight.shape[1]
    total, late_heads = kernel_call(
        out_body,
        [
            jax.ShapeDtypeStruct((seq_size, audio_rows, columns), jnp.float32),
            bfloat(audio_rows, 2 * HEAD_DIM),
        ],
        [
            own_piece,
            near_piece,
            far_piece,
            farther_piece,
            audio_tokens,
            out_weight,
            out_partner,
            out_third,
            third_rest,
            out_fourth,
        ],
        scratch=[
            pltpu.VMEM((seq_size, audio_rows, HEAD_DIM), jnp.bfloat16),
            pltpu.VMEM((2, *out_weight.shape), jnp.bfloat16),
            pltpu.VMEM((audio_rows, columns), jnp.bfloat16),
            pltpu.SemaphoreType.DMA((2,)),
        ],
        loose_in=(4, 5),
        limit=7,
        cost=pl.CostEstimate(flops=10000000000, bytes_accessed=10000000, transcendentals=0),
    )
    send, keep = kernel_call(
        late_out_body,
        [
            bfloat(2, audio_rows, columns),
            jax.ShapeDtypeStruct((2, audio_rows, columns), jnp.float32),
        ],
        [total, late_heads, fourth_rest, partner_rest],
        limit=5,
    )
    came = swap(send, "rep", 1)
    across = swap((keep[1] + came[1].astype(jnp.float32)).astype(jnp.bfloat16), "mem", 1)
    own_part = taylor(video_cache, plan, 2 * half_depth)
    audio_output = (
        keep[0] + came[0].astype(jnp.float32) + across.astype(jnp.float32)
    ).astype(jnp.bfloat16)
    return (own_part, audio_output)


def solution(mesh):
    sizes = dict(mesh.shape)
    square = (sizes["grp"], sizes["seq"], sizes["mem"], sizes["rep"]) == (2, 4, 2, 2)

    def on_device(*arrays):
        heads = arrays[5].shape[1] // HEAD_DIM
        return (by_head if square and heads == sizes["seq"] else general)(*arrays)

    return jax.shard_map(
        on_device,
        mesh=mesh,
        in_specs=(
            P(None, ("grp", "seq"), "mem"),
            P("grp"),
            P(("grp", "seq")),
            P(("grp", "seq"), None),
            P("seq", ("mem", "rep")),
            P("seq", ("mem", "rep")),
            P(("mem", "rep"), "seq"),
        ),
        out_specs=(P(("grp", "seq"), "mem"), P(("grp", "seq"), ("mem", "rep"))),
        check_vma=False,
    )
```

```python
import math

import jax
import jax.numpy as jnp
from jax import lax
from jax.experimental import pallas as pl
from jax.experimental.pallas import tpu as pltpu
from jax.sharding import PartitionSpec as P

HEAD_DIM = 128
FRAMES = 24


SLOPE = 4.0


def taylor_ratio(plan):
    history = plan.shape[0]
    step_ids = jnp.arange(history, dtype=jnp.int32)
    marked = step_ids * plan
    last_fresh = jnp.max(marked)
    prior_fresh = jnp.max(jnp.where(step_ids < last_fresh, marked, 0))
    return (history - last_fresh).astype(jnp.float32) / (last_fresh - prior_fresh).astype(
        jnp.float32
    )


def combine(orders, step_ratio):
    values = orders.astype(jnp.float32)
    return (values[0] + step_ratio * values[1] + 0.5 * step_ratio * step_ratio * values[2]).astype(
        jnp.bfloat16
    )


def general(video_cache, plan, alignment, audio_tokens, kv_weight, query_weight, out_weight):
    step_ratio = taylor_ratio(plan)
    own_part = combine(video_cache, step_ratio)
    features_all = lax.all_gather(own_part, "mem", axis=1, tiled=True)
    video_rows = features_all.shape[0]
    kv_local = jnp.dot(
        features_all,
        lax.all_gather(kv_weight, "seq", axis=0, tiled=True),
        preferred_element_type=jnp.float32,
    )
    head_size = HEAD_DIM
    local_heads = query_weight.shape[1] // head_size
    kv_local = kv_local.astype(jnp.bfloat16).reshape(video_rows, local_heads, 2, head_size)
    key_rows = kv_local[:, :, 0, :]
    value_rows = kv_local[:, :, 1, :]
    query_full, out_full = (
        lax.all_gather(query_weight, "seq", axis=0, tiled=True),
        lax.all_gather(out_weight, "seq", axis=1, tiled=True),
    )
    audio_rows = audio_tokens.shape[0]
    queries = jnp.dot(audio_tokens, query_full, preferred_element_type=jnp.float32).astype(
        jnp.bfloat16
    )
    queries = queries.reshape(audio_rows, local_heads, head_size)
    scale = 1.0 / head_size**0.5
    span = video_rows * lax.axis_size("seq")
    initial = (
        jnp.full((local_heads, audio_rows), -1e30, jnp.float32),
        jnp.zeros((local_heads, audio_rows), jnp.float32),
        jnp.zeros((local_heads, audio_rows, head_size), jnp.float32),
    )
    key_piece = lax.all_gather(key_rows, "seq", axis=0, tiled=True)
    value_piece = lax.all_gather(value_rows, "seq", axis=0, tiled=True)
    row_count = key_piece.shape[0]
    block_len = math.gcd(row_count, 1024)

    def advance(block_index, carried):
        row_max, row_sum, weighted = carried
        key_block = lax.dynamic_slice_in_dim(key_piece, block_index * block_len, block_len, 0)
        value_block = lax.dynamic_slice_in_dim(value_piece, block_index * block_len, block_len, 0)
        positions = block_index * block_len + jnp.arange(block_len, dtype=jnp.int32)
        frames_video = positions * FRAMES // span
        distance_bias = (
            -SLOPE
            * jnp.abs(frames_video[None, :] - alignment[:, None]).astype(jnp.float32)
            / FRAMES
        )
        scores = (
            jnp.einsum("qhd,khd->hqk", queries, key_block, preferred_element_type=jnp.float32)
            * scale
        )
        scores = scores + distance_bias[None]
        new_max = jnp.maximum(row_max, jnp.max(scores, axis=2))
        rescale = jnp.exp(row_max - new_max)
        exp_terms = jnp.exp(scores - new_max[:, :, None])
        row_sum = row_sum * rescale + jnp.sum(exp_terms, axis=2)
        weighted = weighted * rescale[:, :, None] + jnp.einsum(
            "hqk,khd->hqd",
            exp_terms.astype(jnp.bfloat16),
            value_block,
            preferred_element_type=jnp.float32,
        )
        return (new_max, row_sum, weighted)

    row_max, row_sum, weighted = lax.fori_loop(0, row_count // block_len, advance, initial)
    attended = (weighted / row_sum[:, :, None]).astype(jnp.bfloat16)
    attended = jnp.transpose(attended, (1, 0, 2)).reshape(audio_rows, local_heads * head_size)
    partial_update = jnp.dot(attended, out_full, preferred_element_type=jnp.float32)
    update = lax.psum_scatter(
        partial_update.astype(jnp.bfloat16), ("mem", "rep"), scatter_dimension=1, tiled=True
    ).astype(jnp.float32)
    own_columns = update.shape[1]
    residual = lax.dynamic_slice_in_dim(
        audio_tokens, lax.axis_index(("mem", "rep")) * own_columns, own_columns, 1
    )
    audio_output = (residual.astype(jnp.float32) + update).astype(jnp.bfloat16)
    return (own_part, audio_output)


def swap(value, axis, bit):
    size = lax.axis_size(axis)
    return lax.ppermute(value, axis, [(i, i ^ bit) for i in range(size)])


VMEM = pl.BlockSpec(memory_space=pltpu.VMEM)
SMEM = pl.BlockSpec(memory_space=pltpu.SMEM)
ANY = pl.BlockSpec(memory_space=pl.ANY)
HBM = pl.BlockSpec(memory_space=pltpu.HBM)


def kernel_call(body, outs, ins, after=(), scratch=(), smem=(), loose_in=(), loose_out=(), limit=14, cost=None):
    def whole(*refs):
        body(*refs[: len(ins)], *refs[len(ins) + len(after) :])

    spots = [SMEM if i in smem else HBM if i in loose_in else VMEM for i in range(len(ins))]
    return pl.pallas_call(
        whole,
        out_shape=outs,
        in_specs=spots + [ANY] * len(after),
        out_specs=[HBM if i in loose_out else VMEM for i in range(len(outs))],
        scratch_shapes=scratch,
        cost_estimate=cost,
        compiler_params=pltpu.CompilerParams(vmem_limit_bytes=limit * 2**20),
    )(*ins, *after)


def plan_ratio(plan_ref, columns):
    history = plan_ref.shape[0]
    last_fresh, prior_fresh = jnp.int32(0), jnp.int32(0)
    for step in range(history):
        fresh = plan_ref[step] == 1
        prior_fresh = jnp.where(fresh, last_fresh, prior_fresh)
        last_fresh = jnp.where(fresh, step, last_fresh)
    ahead = jnp.full((1, columns), history - last_fresh, jnp.int32).astype(jnp.float32)
    apart = jnp.full((1, columns), last_fresh - prior_fresh, jnp.int32).astype(jnp.float32)
    return ahead / apart


def taylor_rows(cache_ref, out_ref, step_ratio, first, last):
    half_square = 0.5 * step_ratio * step_ratio
    for at in range(first, last, 16):
        terms = [cache_ref[order, at : at + 16, :].astype(jnp.float32) for order in range(3)]
        out_ref[at : at + 16, :] = (
            terms[0] + step_ratio * terms[1] + half_square * terms[2]
        ).astype(jnp.bfloat16)


def taylor_body(plan_ref, cache_ref, out_ref):
    rows, columns = out_ref.shape
    taylor_rows(cache_ref, out_ref, plan_ratio(plan_ref, columns), 0, rows)


def taylor(video_cache, plan, width):
    orders, rows, columns = video_cache.shape
    return pl.pallas_call(
        taylor_body,
        out_shape=jax.ShapeDtypeStruct((rows, columns), jnp.bfloat16),
        grid=(columns // width,),
        in_specs=[SMEM, pl.BlockSpec((orders, rows, width), lambda i: (0, 0, i))],
        out_specs=pl.BlockSpec((rows, width), lambda i: (0, i)),
        compiler_params=pltpu.CompilerParams(vmem_limit_bytes=6 * 2**20),
    )(plan, video_cache)


def first_body(
    plan_ref,
    cache_ref,
    audio_ref,
    kv_ref,
    query_ref,
    out_w,
    packed_ref,
    other_ref,
    half_ref,
    held_ref,
    made_ref,
    other_vmem,
    half_vmem,
    plan_smem,
    sems,
):
    rep_at, mem_at, grp_at = (lax.axis_index(name) for name in ("rep", "mem", "grp"))
    rows, width = held_ref.shape[1:]
    width = width // 2
    copies = []

    def copy(source, target):
        copies.append(pltpu.make_async_copy(source, target, sems.at[len(copies)]))

    def part(index, size):
        return pl.ds(pl.multiple_of(index * size, size), size)

    plan_copy = pltpu.make_async_copy(plan_ref, plan_smem, sems.at[25])
    plan_copy.start()
    blocks = 4
    step = rows // blocks
    for block in range(blocks):
        at = pl.ds(block * step, step)
        for shard in range(2):
            copy(
                cache_ref.at[:, at, part(2 * shard + rep_at, width)],
                held_ref.at[:, at, pl.ds(shard * width, width)],
            )
    lane = width // 2
    for shard in range(2):
        copy(
            audio_ref.at[:, part(2 * (2 * mem_at + shard) + rep_at, lane)],
            made_ref.at[pl.ds(2 * rows, audio_ref.shape[0]), pl.ds(shard * lane, lane)],
        )
    depth, columns = kv_ref.shape[0] // 2, query_ref.shape[1]
    copy(kv_ref.at[part(1 - rep_at, depth)], other_vmem.at[pl.ds(0, depth)])
    quarter = query_ref.shape[0] // 4
    for side in range(2):
        copy(
            query_ref.at[part(2 * (1 - rep_at) + side, quarter)],
            other_vmem.at[pl.ds(depth, quarter), pl.ds(side * columns, columns)],
        )
    copy(out_w.at[part(grp_at, half_ref.shape[0])], half_vmem)
    for started in copies:
        started.start()
    plan_copy.wait()
    step_ratio = plan_ratio(plan_smem, width)
    for block in range(blocks):
        for shard in range(2):
            copies[2 * block + shard].wait()
            taylor_rows(
                held_ref.at[:, :, pl.ds(shard * width, width)],
                made_ref.at[pl.ds(shard * rows, rows)],
                step_ratio,
                block * step,
                (block + 1) * step,
            )
            at = pl.ds(shard * rows + block * step, step)
            copy(made_ref.at[at], packed_ref.at[at])
            copies[-1].start()
    audio_at = pl.ds(2 * rows, audio_ref.shape[0])
    stages = (
        (2, made_ref.at[audio_at], packed_ref.at[audio_at]),
        (3, other_vmem, other_ref),
        (1, half_vmem, half_ref),
    )
    at = 2 * blocks
    for count, source, target in stages:
        for arriving in copies[at : at + count]:
            arriving.wait()
        at += count
        copy(source, target)
        copies[-1].start()
    for leaving in copies[at:]:
        leaving.wait()


def weight_body(align_ref, kv_ref, query_ref, other_ref, own_ref, *piece_refs):
    seq_at, rep_at, grp_at = (lax.axis_index(name) for name in ("seq", "rep", "grp"))
    kv_half, query_half = kv_ref.shape[0] // 2, query_ref.shape[0] // 2
    kv_rows, query_rows = kv_half // 2, query_half // 2
    fold = query_rows // 2

    def fill(out_ref, bit, group, kv_at, query_at):
        head = seq_at ^ bit
        width = 2 * HEAD_DIM
        lanes = pl.ds(pl.multiple_of(head * width, width), width)
        at = pl.ds(pl.multiple_of(rep_at * kv_half + group * kv_rows, kv_rows), kv_rows)
        out_ref[kv_at : kv_at + kv_rows, :width] = kv_ref[at, lanes]
        at = pl.ds(pl.multiple_of(group * kv_rows, kv_rows), kv_rows)
        out_ref[kv_at : kv_at + kv_rows, width:] = other_ref[at, lanes]
        lanes = pl.ds(pl.multiple_of(head * HEAD_DIM, HEAD_DIM), HEAD_DIM)
        other_lanes = pl.ds(
            pl.multiple_of(group * query_ref.shape[1] + head * HEAD_DIM, HEAD_DIM), HEAD_DIM
        )
        for side in range(2):
            first = rep_at * query_half + group * query_rows + side * fold
            at = pl.ds(pl.multiple_of(first, fold), fold)
            to = slice(query_at, query_at + fold)
            out_ref[to, side * width : side * width + HEAD_DIM] = query_ref[at, lanes]
            out_ref[to, side * width + HEAD_DIM : (side + 1) * width] = other_ref[
                kv_half + side * fold : kv_half + (side + 1) * fold, other_lanes
            ]

    for group in range(2):
        fill(own_ref, 0, group, group * kv_rows, kv_half + group * fold)
    for bit, piece_ref in enumerate(piece_refs, 1):
        fill(piece_ref, bit, grp_at, 0, kv_rows)
        spare = (piece_ref.shape[0] - kv_rows - fold, piece_ref.shape[1])
        align = align_ref[...].astype(jnp.float32).astype(piece_ref.dtype)
        row = jnp.concatenate(
            [align, jnp.zeros((1, spare[1] - align.shape[1]), piece_ref.dtype)], axis=1
        )
        piece_ref[kv_rows + fold :, :] = jnp.broadcast_to(row, spare)


def lay_tokens(slot, rows, use_own, own_ref, across_ref, rows_ref, audio_ref):
    depth, lane = rows_ref.shape[1] // 2, audio_ref.shape[1] // 2
    audio_rows = own_ref.shape[0] - 2 * rows
    for used, packed_ref in ((use_own, own_ref), (jnp.logical_not(use_own), across_ref)):

        @pl.when(used)
        def _():
            for part in range(2):
                rows_ref[
                    slot * rows : (slot + 1) * rows, part * depth : (part + 1) * depth
                ] = packed_ref[part * rows : (part + 1) * rows, :]
                audio_ref[
                    slot * audio_rows : (slot + 1) * audio_rows, part * lane : (part + 1) * lane
                ] = packed_ref[2 * rows :, part * lane : (part + 1) * lane]


def lay_weights(piece_ref, part, group, at, kv_ref, query_ref):
    kv_half, fold, width = kv_ref.shape[0] // 4, query_ref.shape[0] // 8, query_ref.shape[1]
    to = pl.ds(pl.multiple_of((2 * part + group) * kv_half, kv_half), kv_half)
    kv_ref[to, :] = piece_ref[at[0] : at[0] + kv_half, :]
    for side in range(2):
        to = pl.ds(pl.multiple_of((4 * part + 2 * group + side) * fold, fold), fold)
        query_ref[to, :] = piece_ref[at[1] : at[1] + fold, side * width : (side + 1) * width]


def half_places():
    seq_at = lax.axis_index("seq")
    return seq_at % 2, lax.axis_index("mem") == seq_at // 2, lax.axis_index("grp")


def near_body(*refs):
    packed_refs, (own_w, near_w, near_rest) = refs[:6], refs[6:9]
    kv_sum, query_sum, kv_ref, query_ref, rows_ref, audio_ref = refs[9:]
    part, use_own, grp_at = half_places()
    rows = rows_ref.shape[0] // 3
    for slot in range(3):
        lay_tokens(slot, rows, use_own, *packed_refs[2 * slot : 2 * slot + 2], rows_ref, audio_ref)
    kv_half, fold = kv_ref.shape[0] // 4, query_ref.shape[0] // 8
    for group in range(2):
        at = (group * kv_half, 2 * kv_half + group * fold)
        lay_weights(own_w, part, group, at, kv_ref, query_ref)
    for group, piece_ref in ((grp_at, near_w), (1 - grp_at, near_rest)):
        lay_weights(piece_ref, 1 - part, group, (0, kv_half), kv_ref, query_ref)
    kv_sum[...] = jnp.dot(rows_ref[...], kv_ref[...], preferred_element_type=jnp.float32)
    query_sum[...] = jnp.dot(audio_ref[...], query_ref[...], preferred_element_type=jnp.float32)


def products_body(*refs):
    packed_refs, piece_refs = refs[:8], refs[8:12]
    kv_sum, query_sum, near_kv, near_query, own_align, near_align = refs[12:18]
    align_ref, send_ref, keep_ref = refs[18:21]
    rows_ref, audio_ref, last_rows, last_audio, kv_ref, query_ref = refs[21:]
    part, use_own, grp_at = half_places()
    rows, audio_rows = last_rows.shape[0], last_audio.shape[0]
    kv_half, fold = kv_ref.shape[0] // 4, query_ref.shape[0] // 8
    lay_tokens(0, rows, use_own, *packed_refs[6:], last_rows, last_audio)
    for slot in range(4):
        across = jnp.logical_not(use_own)
        lay_tokens(slot, rows, across, *packed_refs[2 * slot : 2 * slot + 2], rows_ref, audio_ref)
    for at, shard in enumerate((part, 1 - part)):
        for group, piece_ref in ((grp_at, piece_refs[2 * at]), (1 - grp_at, piece_refs[2 * at + 1])):
            lay_weights(piece_ref, shard, group, (0, kv_half), kv_ref, query_ref)
    align_ref[0] = jnp.broadcast_to(
        own_align[...].astype(jnp.float32).astype(align_ref.dtype), align_ref.shape[1:]
    )
    align_ref[1] = near_align[...].astype(align_ref.dtype)
    for bit, piece_ref in ((2, piece_refs[0]), (3, piece_refs[2])):
        align_ref[bit] = piece_ref[kv_half + fold :, : align_ref.shape[2]]

    def product(left, right):
        return jnp.dot(left[...], right[...], preferred_element_type=jnp.float32)

    columns = keep_ref.shape[1]
    first, count = 3 * rows, 4 * rows
    total = product(rows_ref, kv_ref)
    for at, more in (
        (slice(0, first), kv_sum[...]),
        (slice(first, count), product(last_rows, near_kv)),
    ):
        keep_ref[at, :] = total[at, :columns] + more[:, :columns]
        send_ref[at, :] = total[at, columns:] + more[:, columns:]
    total = product(audio_ref, query_ref)
    last = product(last_audio, near_query)
    for slot in range(4):
        side, half = divmod(slot, 2)
        more = last if slot == 3 else query_sum[slot * audio_rows : (slot + 1) * audio_rows, :]
        part_sum = total[slot * audio_rows : (slot + 1) * audio_rows] + more
        at = slice(count + half * audio_rows, count + (half + 1) * audio_rows)
        to = slice(side * HEAD_DIM, (side + 1) * HEAD_DIM)
        keep_ref[at, to] = part_sum[:, :HEAD_DIM]
        send_ref[at, to] = part_sum[:, HEAD_DIM:]


def attend(queries, kv_ref, frames_ref, align):
    scores = lax.dot_general(
        queries,
        kv_ref[:, :HEAD_DIM],
        (((1,), (1,)), ((), ())),
        preferred_element_type=jnp.float32,
    ) * (1.0 / HEAD_DIM**0.5)
    scores = scores - SLOPE * jnp.abs(frames_ref[...] - align) / FRAMES
    exp_terms = jnp.exp(scores - jnp.max(scores, axis=1, keepdims=True))
    weighted = jnp.dot(
        exp_terms.astype(jnp.bfloat16), kv_ref[:, HEAD_DIM:], preferred_element_type=jnp.float32
    )
    return (weighted / jnp.sum(exp_terms, axis=1, keepdims=True)).astype(jnp.bfloat16)


def attention_body(frames_ref, align_ref, keep_ref, came_ref, *refs):
    *out_refs, kv_ref, query_ref = refs
    count, audio_rows = kv_ref.shape[0], query_ref.shape[1]

    def summed(rows, columns=slice(None)):
        return (keep_ref[rows, columns] + came_ref[rows, columns]).astype(jnp.bfloat16)

    kv_ref[...] = summed(slice(0, count))
    for slot in range(4):
        side, half = divmod(slot, 2)
        query_ref[slot] = summed(
            slice(count + half * audio_rows, count + (half + 1) * audio_rows),
            slice(side * HEAD_DIM, (side + 1) * HEAD_DIM),
        )
    for bit, out_ref in enumerate(out_refs):
        align = align_ref[bit].astype(jnp.float32)[:8].T[:, :1]
        out_ref[...] = attend(query_ref[bit], kv_ref, frames_ref, align)


def out_body(*refs):
    piece_refs, (audio_ref, own_w, *part_refs) = refs[:4], refs[4:10]
    total_ref, late_ref, heads_ref, weight_ref, residual_ref, sems = refs[10:]
    seq_at, grp_at = lax.axis_index("seq"), lax.axis_index("grp")
    place = lax.axis_index("mem") * 2 + lax.axis_index("rep")
    copy = pltpu.make_async_copy(own_w, weight_ref.at[0], sems.at[0])
    copy.start()
    width = residual_ref.shape[1]
    columns = pl.ds(pl.multiple_of(place * width, width), width)
    residual_copy = pltpu.make_async_copy(audio_ref.at[:, columns], residual_ref, sems.at[1])
    residual_copy.start()
    for bit, piece_ref in enumerate(piece_refs):
        heads_ref[seq_at ^ bit] = piece_ref[...]
    heads = jnp.concatenate([heads_ref[head] for head in range(heads_ref.shape[0])], axis=1)

    def half(group):
        return jnp.concatenate([heads_ref[2 * group], heads_ref[2 * group + 1]], axis=1)

    mine = half(grp_at)
    late_ref[...] = half(1 - grp_at)
    partner_w, third_w, third_rest_w, fourth_w = part_refs
    depth = partner_w.shape[0]
    weight_ref[1, pl.ds(pl.multiple_of(grp_at * depth, depth), depth)] = third_w[...]
    weight_ref[1, pl.ds(pl.multiple_of((1 - grp_at) * depth, depth), depth)] = third_rest_w[...]

    def product(rows, weight):
        return jnp.dot(rows, weight, preferred_element_type=jnp.float32)

    total_ref[1] = product(mine, partner_w[...])
    total_ref[3] = product(mine, fourth_w[...])
    total_ref[2] = product(heads, weight_ref[1])
    copy.wait()
    total_ref[0] = product(heads, weight_ref[0])
    residual_copy.wait()
    total_ref[seq_at ^ place] += residual_ref[...].astype(jnp.float32)


def late_out_body(total_ref, late_ref, fourth_w, partner_w, send_ref, keep_ref):
    place = lax.axis_index("mem") * 2 + lax.axis_index("rep")
    for bit in range(4):
        slot = lax.axis_index("seq") ^ bit ^ place
        value = total_ref[bit]
        if bit % 2:
            weight = (partner_w if bit == 1 else fourth_w)[...]
            value += jnp.dot(late_ref[...], weight, preferred_element_type=jnp.float32)

        @pl.when(slot % 2 == 1)
        def _():
            send_ref[slot // 2] = value.astype(send_ref.dtype)

        @pl.when(slot % 2 == 0)
        def _():
            keep_ref[slot // 2] = value


def by_head(video_cache, plan, alignment, audio_tokens, kv_weight, query_weight, out_weight):
    seq_size = lax.axis_size("seq")
    seq_at = lax.axis_index("seq")
    video_rows = video_cache.shape[1]
    audio_rows = audio_tokens.shape[0]
    half_depth, width = kv_weight.shape[0] // 2, 2 * HEAD_DIM
    query_quarter = query_weight.shape[0] // 4

    def bfloat(*shape):
        return jax.ShapeDtypeStruct(shape, jnp.bfloat16)

    packed, other, out_half = kernel_call(
        first_body,
        [
            bfloat(2 * video_rows + audio_rows, half_depth),
            bfloat(half_depth + query_quarter, kv_weight.shape[1]),
            bfloat(out_weight.shape[0] // 2, out_weight.shape[1]),
        ],
        [plan, video_cache, audio_tokens, kv_weight, query_weight, out_weight],
        scratch=[
            pltpu.VMEM((3, video_rows, 2 * half_depth), jnp.bfloat16),
            pltpu.VMEM((2 * video_rows + audio_rows, half_depth), jnp.bfloat16),
            pltpu.VMEM((half_depth + query_quarter, kv_weight.shape[1]), jnp.bfloat16),
            pltpu.VMEM((out_weight.shape[0] // 2, out_weight.shape[1]), jnp.bfloat16),
            pltpu.SMEM(plan.shape, jnp.int32),
            pltpu.SemaphoreType.DMA((26,)),
        ],
        loose_in=(0, 1, 2, 3, 4, 5),
        loose_out=(0, 1, 2),
        limit=61,
    )

    tokens = [packed, swap(packed, "seq", 1), swap(packed, "seq", 2)]
    across = [swap(packed, "mem", 1)]
    other = swap(other, "rep", 1)
    rows = (half_depth + query_quarter) // 2
    weight_own, *pieces = kernel_call(
        weight_body,
        [bfloat(2 * rows, 2 * width)] + [bfloat(rows + 16, 2 * width)] * 3,
        [alignment[None], kv_weight, query_weight, other],
        limit=4,
    )
    pieces = [swap(piece, "seq", bit) for bit, piece in enumerate(pieces, 1)]

    across += [swap(tokens[1], "mem", 1), swap(tokens[2], "mem", 1)]
    near_align = pieces[0][rows:, :audio_rows].astype(jnp.float32)
    tokens[2], near_align = lax.optimization_barrier((tokens[2], near_align))
    tokens.append(swap(tokens[2], "seq", 1))
    pieces[0], across[0], across[1] = lax.optimization_barrier(
        (pieces[0], across[0], across[1])
    )
    rest = [swap(pieces[0], "grp", 1)]
    tokens[3], across[2], rest[0], pieces[1] = lax.optimization_barrier(
        (tokens[3], across[2], rest[0], pieces[1])
    )
    packed_shape = (seq_size * video_rows, 2 * half_depth), (seq_size * audio_rows, half_depth)
    weight_shape = (2 * half_depth, 2 * width), (half_depth, width)
    near_sums = kernel_call(
        near_body,
        [
            jax.ShapeDtypeStruct((3 * video_rows, 2 * width), jnp.float32),
            jax.ShapeDtypeStruct((3 * audio_rows, width), jnp.float32),
            *(bfloat(*shape) for shape in weight_shape),
        ],
        [value for pair in zip(tokens[:3], across) for value in pair]
        + [weight_own, pieces[0], rest[0]],
        scratch=[
            pltpu.VMEM((3 * video_rows, 2 * half_depth), jnp.bfloat16),
            pltpu.VMEM((3 * audio_rows, half_depth), jnp.bfloat16),
        ],
        limit=12,
        cost=pl.CostEstimate(flops=1000000000, bytes_accessed=1000000, transcendentals=0),
    )
    across.append(swap(tokens[3], "mem", 1))
    rest.append(swap(pieces[1], "grp", 1))
    pieces[2], rest[1], *near_sums = lax.optimization_barrier((pieces[2], rest[1], *near_sums))
    rest.append(swap(pieces[2], "grp", 1))

    out_half, tokens[3] = lax.optimization_barrier((out_half, tokens[3]))
    out_third, out_partner = swap(out_half, "seq", 2), swap(out_half, "seq", 1)
    rows = seq_size * (video_rows + audio_rows // 2)
    sums = jax.ShapeDtypeStruct((rows, width), jnp.float32)
    aligns, send, keep = kernel_call(
        products_body,
        [bfloat(seq_size, 16, audio_rows), sums, sums],
        [value for pair in zip(tokens, across) for value in pair]
        + [pieces[1], rest[1], pieces[2], rest[2], *near_sums, alignment[None], near_align],
        scratch=[
            *(pltpu.VMEM(shape, jnp.bfloat16) for shape in packed_shape),
            pltpu.VMEM((video_rows, 2 * half_depth), jnp.bfloat16),
            pltpu.VMEM((audio_rows, half_depth), jnp.bfloat16),
            *(pltpu.VMEM(shape, jnp.bfloat16) for shape in weight_shape),
        ],
        limit=14,
    )
    send, out_third, out_partner = lax.optimization_barrier((send, out_third, out_partner))
    came = swap(send, "rep", 1)
    third_rest, out_fourth = swap(out_third, "grp", 1), swap(out_third, "seq", 1)

    span = video_rows * seq_size
    blocks = jnp.stack([seq_at, seq_at ^ 1, seq_at ^ 2, seq_at ^ 3])
    positions = blocks[:, None] * video_rows + jnp.arange(video_rows, dtype=jnp.int32)[None, :]
    frames_video = (positions.reshape(1, span) * FRAMES // span).astype(jnp.float32)
    own_piece, near_piece, far_piece, farther_piece = kernel_call(
        attention_body,
        [bfloat(audio_rows, HEAD_DIM)] * 4,
        [frames_video, aligns, keep, came],
        scratch=[
            pltpu.VMEM((span, width), jnp.bfloat16),
            pltpu.VMEM((seq_size, audio_rows, HEAD_DIM), jnp.bfloat16),
        ],
        limit=9,
    )
    third_rest, out_partner, own_piece = lax.optimization_barrier(
        (third_rest, out_partner, own_piece)
    )
    fourth_rest, partner_rest = swap(third_rest, "seq", 1), swap(out_partner, "grp", 1)
    far_piece = swap(far_piece, "seq", 2)
    farther_piece = swap(farther_piece, "seq", 3)
    near_piece = swap(near_piece, "seq", 1)

    columns = out_weight.shape[1]
    total, late_heads = kernel_call(
        out_body,
        [
            jax.ShapeDtypeStruct((seq_size, audio_rows, columns), jnp.float32),
            bfloat(audio_rows, 2 * HEAD_DIM),
        ],
        [
            own_piece,
            near_piece,
            far_piece,
            farther_piece,
            audio_tokens,
            out_weight,
            out_partner,
            out_third,
            third_rest,
            out_fourth,
        ],
        scratch=[
            pltpu.VMEM((seq_size, audio_rows, HEAD_DIM), jnp.bfloat16),
            pltpu.VMEM((2, *out_weight.shape), jnp.bfloat16),
            pltpu.VMEM((audio_rows, columns), jnp.bfloat16),
            pltpu.SemaphoreType.DMA((2,)),
        ],
        loose_in=(4, 5),
        limit=7,
        cost=pl.CostEstimate(flops=10000000000, bytes_accessed=10000000, transcendentals=0),
    )
    send, keep = kernel_call(
        late_out_body,
        [
            bfloat(2, audio_rows, columns),
            jax.ShapeDtypeStruct((2, audio_rows, columns), jnp.float32),
        ],
        [total, late_heads, fourth_rest, partner_rest],
        limit=5,
    )
    came = swap(send, "rep", 1)
    across = swap((keep[1] + came[1].astype(jnp.float32)).astype(jnp.bfloat16), "mem", 1)
    own_part = taylor(video_cache, plan, 2 * half_depth)
    audio_output = (
        keep[0] + came[0].astype(jnp.float32) + across.astype(jnp.float32)
    ).astype(jnp.bfloat16)
    return (own_part, audio_output)


def solution(mesh):
    sizes = dict(mesh.shape)
    square = (sizes["grp"], sizes["seq"], sizes["mem"], sizes["rep"]) == (2, 4, 2, 2)

    def on_device(*arrays):
        heads = arrays[5].shape[1] // HEAD_DIM
        return (by_head if square and heads == sizes["seq"] else general)(*arrays)

    return jax.shard_map(
        on_device,
        mesh=mesh,
        in_specs=(
            P(None, ("grp", "seq"), "mem"),
            P("grp"),
            P(("grp", "seq")),
            P(("grp", "seq"), None),
            P("seq", ("mem", "rep")),
            P("seq", ("mem", "rep")),
            P(("mem", "rep"), "seq"),
        ),
        out_specs=(P(("grp", "seq"), "mem"), P(("grp", "seq"), ("mem", "rep"))),
        check_vma=False,
    )
```

```python
import math

import jax
import jax.numpy as jnp
from jax import lax
from jax.experimental import pallas as pl
from jax.experimental.pallas import tpu as pltpu
from jax.sharding import PartitionSpec as P

HEAD_DIM = 128
FRAMES = 24


SLOPE = 4.0


def taylor_ratio(plan):
    history = plan.shape[0]
    step_ids = jnp.arange(history, dtype=jnp.int32)
    marked = step_ids * plan
    last_fresh = jnp.max(marked)
    prior_fresh = jnp.max(jnp.where(step_ids < last_fresh, marked, 0))
    return (history - last_fresh).astype(jnp.float32) / (last_fresh - prior_fresh).astype(
        jnp.float32
    )


def combine(orders, step_ratio):
    values = orders.astype(jnp.float32)
    return (values[0] + step_ratio * values[1] + 0.5 * step_ratio * step_ratio * values[2]).astype(
        jnp.bfloat16
    )


def general(video_cache, plan, alignment, audio_tokens, kv_weight, query_weight, out_weight):
    step_ratio = taylor_ratio(plan)
    own_part = combine(video_cache, step_ratio)
    features_all = lax.all_gather(own_part, "mem", axis=1, tiled=True)
    video_rows = features_all.shape[0]
    kv_local = jnp.dot(
        features_all,
        lax.all_gather(kv_weight, "seq", axis=0, tiled=True),
        preferred_element_type=jnp.float32,
    )
    head_size = HEAD_DIM
    local_heads = query_weight.shape[1] // head_size
    kv_local = kv_local.astype(jnp.bfloat16).reshape(video_rows, local_heads, 2, head_size)
    key_rows = kv_local[:, :, 0, :]
    value_rows = kv_local[:, :, 1, :]
    query_full, out_full = (
        lax.all_gather(query_weight, "seq", axis=0, tiled=True),
        lax.all_gather(out_weight, "seq", axis=1, tiled=True),
    )
    audio_rows = audio_tokens.shape[0]
    queries = jnp.dot(audio_tokens, query_full, preferred_element_type=jnp.float32).astype(
        jnp.bfloat16
    )
    queries = queries.reshape(audio_rows, local_heads, head_size)
    scale = 1.0 / head_size**0.5
    span = video_rows * lax.axis_size("seq")
    initial = (
        jnp.full((local_heads, audio_rows), -1e30, jnp.float32),
        jnp.zeros((local_heads, audio_rows), jnp.float32),
        jnp.zeros((local_heads, audio_rows, head_size), jnp.float32),
    )
    key_piece = lax.all_gather(key_rows, "seq", axis=0, tiled=True)
    value_piece = lax.all_gather(value_rows, "seq", axis=0, tiled=True)
    row_count = key_piece.shape[0]
    block_len = math.gcd(row_count, 1024)

    def advance(block_index, carried):
        row_max, row_sum, weighted = carried
        key_block = lax.dynamic_slice_in_dim(key_piece, block_index * block_len, block_len, 0)
        value_block = lax.dynamic_slice_in_dim(value_piece, block_index * block_len, block_len, 0)
        positions = block_index * block_len + jnp.arange(block_len, dtype=jnp.int32)
        frames_video = positions * FRAMES // span
        distance_bias = (
            -SLOPE
            * jnp.abs(frames_video[None, :] - alignment[:, None]).astype(jnp.float32)
            / FRAMES
        )
        scores = (
            jnp.einsum("qhd,khd->hqk", queries, key_block, preferred_element_type=jnp.float32)
            * scale
        )
        scores = scores + distance_bias[None]
        new_max = jnp.maximum(row_max, jnp.max(scores, axis=2))
        rescale = jnp.exp(row_max - new_max)
        exp_terms = jnp.exp(scores - new_max[:, :, None])
        row_sum = row_sum * rescale + jnp.sum(exp_terms, axis=2)
        weighted = weighted * rescale[:, :, None] + jnp.einsum(
            "hqk,khd->hqd",
            exp_terms.astype(jnp.bfloat16),
            value_block,
            preferred_element_type=jnp.float32,
        )
        return (new_max, row_sum, weighted)

    row_max, row_sum, weighted = lax.fori_loop(0, row_count // block_len, advance, initial)
    attended = (weighted / row_sum[:, :, None]).astype(jnp.bfloat16)
    attended = jnp.transpose(attended, (1, 0, 2)).reshape(audio_rows, local_heads * head_size)
    partial_update = jnp.dot(attended, out_full, preferred_element_type=jnp.float32)
    update = lax.psum_scatter(
        partial_update.astype(jnp.bfloat16), ("mem", "rep"), scatter_dimension=1, tiled=True
    ).astype(jnp.float32)
    own_columns = update.shape[1]
    residual = lax.dynamic_slice_in_dim(
        audio_tokens, lax.axis_index(("mem", "rep")) * own_columns, own_columns, 1
    )
    audio_output = (residual.astype(jnp.float32) + update).astype(jnp.bfloat16)
    return (own_part, audio_output)


def swap(value, axis, bit):
    size = lax.axis_size(axis)
    return lax.ppermute(value, axis, [(i, i ^ bit) for i in range(size)])


VMEM = pl.BlockSpec(memory_space=pltpu.VMEM)
SMEM = pl.BlockSpec(memory_space=pltpu.SMEM)
ANY = pl.BlockSpec(memory_space=pl.ANY)
HBM = pl.BlockSpec(memory_space=pltpu.HBM)


def kernel_call(body, outs, ins, after=(), scratch=(), smem=(), loose_in=(), loose_out=(), limit=14, cost=None):
    def whole(*refs):
        body(*refs[: len(ins)], *refs[len(ins) + len(after) :])

    spots = [SMEM if i in smem else HBM if i in loose_in else VMEM for i in range(len(ins))]
    return pl.pallas_call(
        whole,
        out_shape=outs,
        in_specs=spots + [ANY] * len(after),
        out_specs=[HBM if i in loose_out else VMEM for i in range(len(outs))],
        scratch_shapes=scratch,
        cost_estimate=cost,
        compiler_params=pltpu.CompilerParams(vmem_limit_bytes=limit * 2**20),
    )(*ins, *after)


def plan_ratio(plan_ref, columns):
    history = plan_ref.shape[0]
    last_fresh, prior_fresh = jnp.int32(0), jnp.int32(0)
    for step in range(history):
        fresh = plan_ref[step] == 1
        prior_fresh = jnp.where(fresh, last_fresh, prior_fresh)
        last_fresh = jnp.where(fresh, step, last_fresh)
    ahead = jnp.full((1, columns), history - last_fresh, jnp.int32).astype(jnp.float32)
    apart = jnp.full((1, columns), last_fresh - prior_fresh, jnp.int32).astype(jnp.float32)
    return ahead / apart


def taylor_rows(cache_ref, out_ref, step_ratio, first, last):
    half_square = 0.5 * step_ratio * step_ratio
    for at in range(first, last, 16):
        terms = [cache_ref[order, at : at + 16, :].astype(jnp.float32) for order in range(3)]
        out_ref[at : at + 16, :] = (
            terms[0] + step_ratio * terms[1] + half_square * terms[2]
        ).astype(jnp.bfloat16)


def taylor_body(plan_ref, cache_ref, out_ref):
    rows, columns = out_ref.shape
    taylor_rows(cache_ref, out_ref, plan_ratio(plan_ref, columns), 0, rows)


def taylor(video_cache, plan, width):
    orders, rows, columns = video_cache.shape
    return pl.pallas_call(
        taylor_body,
        out_shape=jax.ShapeDtypeStruct((rows, columns), jnp.bfloat16),
        grid=(columns // width,),
        in_specs=[SMEM, pl.BlockSpec((orders, rows, width), lambda i: (0, 0, i))],
        out_specs=pl.BlockSpec((rows, width), lambda i: (0, i)),
        compiler_params=pltpu.CompilerParams(vmem_limit_bytes=6 * 2**20),
    )(plan, video_cache)


def first_body(
    plan_ref,
    cache_ref,
    audio_ref,
    kv_ref,
    query_ref,
    out_w,
    packed_ref,
    other_ref,
    half_ref,
    held_ref,
    made_ref,
    other_vmem,
    half_vmem,
    plan_smem,
    sems,
):
    rep_at, mem_at, grp_at = (lax.axis_index(name) for name in ("rep", "mem", "grp"))
    rows, width = held_ref.shape[1:]
    width = width // 2
    copies = []

    def copy(source, target):
        copies.append(pltpu.make_async_copy(source, target, sems.at[len(copies)]))

    def part(index, size):
        return pl.ds(pl.multiple_of(index * size, size), size)

    plan_copy = pltpu.make_async_copy(plan_ref, plan_smem, sems.at[25])
    plan_copy.start()
    blocks = 4
    step = rows // blocks
    for block in range(blocks):
        at = pl.ds(block * step, step)
        for shard in range(2):
            copy(
                cache_ref.at[:, at, part(2 * shard + rep_at, width)],
                held_ref.at[:, at, pl.ds(shard * width, width)],
            )
    lane = width // 2
    for shard in range(2):
        copy(
            audio_ref.at[:, part(2 * (2 * mem_at + shard) + rep_at, lane)],
            made_ref.at[pl.ds(2 * rows, audio_ref.shape[0]), pl.ds(shard * lane, lane)],
        )
    depth, columns = kv_ref.shape[0] // 2, query_ref.shape[1]
    copy(kv_ref.at[part(1 - rep_at, depth)], other_vmem.at[pl.ds(0, depth)])
    quarter = query_ref.shape[0] // 4
    for side in range(2):
        copy(
            query_ref.at[part(2 * (1 - rep_at) + side, quarter)],
            other_vmem.at[pl.ds(depth, quarter), pl.ds(side * columns, columns)],
        )
    copy(out_w.at[part(grp_at, half_ref.shape[0])], half_vmem)
    for started in copies:
        started.start()
    plan_copy.wait()
    step_ratio = plan_ratio(plan_smem, width)
    for block in range(blocks):
        for shard in range(2):
            copies[2 * block + shard].wait()
            taylor_rows(
                held_ref.at[:, :, pl.ds(shard * width, width)],
                made_ref.at[pl.ds(shard * rows, rows)],
                step_ratio,
                block * step,
                (block + 1) * step,
            )
            at = pl.ds(shard * rows + block * step, step)
            copy(made_ref.at[at], packed_ref.at[at])
            copies[-1].start()
    audio_at = pl.ds(2 * rows, audio_ref.shape[0])
    stages = (
        (2, made_ref.at[audio_at], packed_ref.at[audio_at]),
        (3, other_vmem, other_ref),
        (1, half_vmem, half_ref),
    )
    at = 2 * blocks
    for count, source, target in stages:
        for arriving in copies[at : at + count]:
            arriving.wait()
        at += count
        copy(source, target)
        copies[-1].start()
    for leaving in copies[at:]:
        leaving.wait()


def weight_body(align_ref, kv_ref, query_ref, other_ref, own_ref, *piece_refs):
    seq_at, rep_at, grp_at = (lax.axis_index(name) for name in ("seq", "rep", "grp"))
    kv_half, query_half = kv_ref.shape[0] // 2, query_ref.shape[0] // 2
    kv_rows, query_rows = kv_half // 2, query_half // 2
    fold = query_rows // 2

    def fill(out_ref, bit, group, kv_at, query_at):
        head = seq_at ^ bit
        width = 2 * HEAD_DIM
        lanes = pl.ds(pl.multiple_of(head * width, width), width)
        at = pl.ds(pl.multiple_of(rep_at * kv_half + group * kv_rows, kv_rows), kv_rows)
        out_ref[kv_at : kv_at + kv_rows, :width] = kv_ref[at, lanes]
        at = pl.ds(pl.multiple_of(group * kv_rows, kv_rows), kv_rows)
        out_ref[kv_at : kv_at + kv_rows, width:] = other_ref[at, lanes]
        lanes = pl.ds(pl.multiple_of(head * HEAD_DIM, HEAD_DIM), HEAD_DIM)
        other_lanes = pl.ds(
            pl.multiple_of(group * query_ref.shape[1] + head * HEAD_DIM, HEAD_DIM), HEAD_DIM
        )
        for side in range(2):
            first = rep_at * query_half + group * query_rows + side * fold
            at = pl.ds(pl.multiple_of(first, fold), fold)
            to = slice(query_at, query_at + fold)
            out_ref[to, side * width : side * width + HEAD_DIM] = query_ref[at, lanes]
            out_ref[to, side * width + HEAD_DIM : (side + 1) * width] = other_ref[
                kv_half + side * fold : kv_half + (side + 1) * fold, other_lanes
            ]

    for group in range(2):
        fill(own_ref, 0, group, group * kv_rows, kv_half + group * fold)
    for bit, piece_ref in enumerate(piece_refs, 1):
        fill(piece_ref, bit, grp_at, 0, kv_rows)
        spare = (piece_ref.shape[0] - kv_rows - fold, piece_ref.shape[1])
        align = align_ref[...].astype(jnp.float32).astype(piece_ref.dtype)
        row = jnp.concatenate(
            [align, jnp.zeros((1, spare[1] - align.shape[1]), piece_ref.dtype)], axis=1
        )
        piece_ref[kv_rows + fold :, :] = jnp.broadcast_to(row, spare)


def products_body(*refs):
    packed_refs, weight_refs = refs[:8], refs[8:15]
    own_align, near_align, align_ref, send_ref, keep_ref, rows_ref, audio_ref, kv_ref, query_ref = refs[15:]
    seq_at, mem_at, grp_at = (lax.axis_index(name) for name in ("seq", "mem", "grp"))
    rows, audio_rows = rows_ref.shape[0] // 4, audio_ref.shape[0] // 4
    depth, lane = rows_ref.shape[1] // 4, audio_ref.shape[1] // 4
    for at, packed_ref in enumerate(packed_refs):
        slot, mem = divmod(at, 2)
        for part in range(2):
            shard = 2 * (mem_at ^ mem) + part
            lanes = pl.ds(pl.multiple_of(shard * depth, depth), depth)
            rows_ref[slot * rows : (slot + 1) * rows, lanes] = packed_ref[
                part * rows : (part + 1) * rows, :
            ]
            lanes = pl.ds(pl.multiple_of(shard * lane, lane), lane)
            audio_ref[slot * audio_rows : (slot + 1) * audio_rows, lanes] = packed_ref[
                2 * rows :, part * lane : (part + 1) * lane
            ]
    kv_half, fold = depth // 2, lane // 4
    width = query_ref.shape[1]

    def place(piece_ref, shard, group, kv_at, query_at):
        to = pl.ds(pl.multiple_of((2 * shard + group) * kv_half, kv_half), kv_half)
        kv_ref[to, :] = piece_ref[kv_at : kv_at + kv_half, :]
        for side in range(2):
            to = pl.ds(pl.multiple_of((4 * shard + 2 * group + side) * fold, fold), fold)
            query_ref[to, :] = piece_ref[
                query_at : query_at + fold, side * width : (side + 1) * width
            ]

    for group in range(2):
        place(weight_refs[0], seq_at, group, group * kv_half, 2 * kv_half + group * fold)
    for bit in range(1, 4):
        place(weight_refs[2 * bit - 1], seq_at ^ bit, grp_at, 0, kv_half)
        place(weight_refs[2 * bit], seq_at ^ bit, 1 - grp_at, 0, kv_half)
        if bit > 1:
            align_ref[bit] = weight_refs[2 * bit - 1][kv_half + fold :, : align_ref.shape[2]]
    align_ref[1] = near_align[...].astype(align_ref.dtype)
    align_ref[0] = jnp.broadcast_to(
        own_align[...].astype(jnp.float32).astype(align_ref.dtype), align_ref.shape[1:]
    )

    count = 4 * rows
    columns = keep_ref.shape[1]
    total = jnp.dot(rows_ref[...], kv_ref[...], preferred_element_type=jnp.float32)
    keep_ref[:count, :] = total[:, :columns]
    send_ref[:count, :] = total[:, columns:]
    total = jnp.dot(audio_ref[...], query_ref[...], preferred_element_type=jnp.float32)
    folded = 2 * audio_rows
    for side in range(2):
        at = slice(side * folded, (side + 1) * folded)
        to = slice(side * HEAD_DIM, (side + 1) * HEAD_DIM)
        keep_ref[count:, to] = total[at, :HEAD_DIM]
        send_ref[count:, to] = total[at, HEAD_DIM:]


def attend(queries, kv_ref, frames_ref, align):
    scores = lax.dot_general(
        queries,
        kv_ref[:, :HEAD_DIM],
        (((1,), (1,)), ((), ())),
        preferred_element_type=jnp.float32,
    ) * (1.0 / HEAD_DIM**0.5)
    scores = scores - SLOPE * jnp.abs(frames_ref[...] - align) / FRAMES
    exp_terms = jnp.exp(scores - jnp.max(scores, axis=1, keepdims=True))
    weighted = jnp.dot(
        exp_terms.astype(jnp.bfloat16), kv_ref[:, HEAD_DIM:], preferred_element_type=jnp.float32
    )
    return (weighted / jnp.sum(exp_terms, axis=1, keepdims=True)).astype(jnp.bfloat16)


def attention_body(frames_ref, align_ref, keep_ref, came_ref, *refs):
    *out_refs, kv_ref, query_ref = refs
    count, audio_rows = kv_ref.shape[0], query_ref.shape[1]

    def summed(rows, columns=slice(None)):
        return (keep_ref[rows, columns] + came_ref[rows, columns]).astype(jnp.bfloat16)

    kv_ref[...] = summed(slice(0, count))
    for slot in range(4):
        side, half = divmod(slot, 2)
        query_ref[slot] = summed(
            slice(count + half * audio_rows, count + (half + 1) * audio_rows),
            slice(side * HEAD_DIM, (side + 1) * HEAD_DIM),
        )
    for bit, out_ref in enumerate(out_refs):
        align = align_ref[bit].astype(jnp.float32)[:8].T[:, :1]
        out_ref[...] = attend(query_ref[bit], kv_ref, frames_ref, align)


def out_body(*refs):
    piece_refs, (audio_ref, own_w, *part_refs) = refs[:4], refs[4:10]
    total_ref, late_ref, heads_ref, weight_ref, residual_ref, sems = refs[10:]
    seq_at, grp_at = lax.axis_index("seq"), lax.axis_index("grp")
    place = lax.axis_index("mem") * 2 + lax.axis_index("rep")
    copy = pltpu.make_async_copy(own_w, weight_ref.at[0], sems.at[0])
    copy.start()
    width = residual_ref.shape[1]
    columns = pl.ds(pl.multiple_of(place * width, width), width)
    residual_copy = pltpu.make_async_copy(audio_ref.at[:, columns], residual_ref, sems.at[1])
    residual_copy.start()
    for bit, piece_ref in enumerate(piece_refs):
        heads_ref[seq_at ^ bit] = piece_ref[...]
    heads = jnp.concatenate([heads_ref[head] for head in range(heads_ref.shape[0])], axis=1)

    def half(group):
        return jnp.concatenate([heads_ref[2 * group], heads_ref[2 * group + 1]], axis=1)

    mine = half(grp_at)
    late_ref[...] = half(1 - grp_at)
    partner_w, third_w, third_rest_w, fourth_w = part_refs
    depth = partner_w.shape[0]
    weight_ref[1, pl.ds(pl.multiple_of(grp_at * depth, depth), depth)] = third_w[...]
    weight_ref[1, pl.ds(pl.multiple_of((1 - grp_at) * depth, depth), depth)] = third_rest_w[...]

    def product(rows, weight):
        return jnp.dot(rows, weight, preferred_element_type=jnp.float32)

    total_ref[1] = product(mine, partner_w[...])
    total_ref[3] = product(mine, fourth_w[...])
    total_ref[2] = product(heads, weight_ref[1])
    copy.wait()
    total_ref[0] = product(heads, weight_ref[0])
    residual_copy.wait()
    total_ref[seq_at ^ place] += residual_ref[...].astype(jnp.float32)


def late_out_body(total_ref, late_ref, fourth_w, partner_w, send_ref, keep_ref):
    place = lax.axis_index("mem") * 2 + lax.axis_index("rep")
    for bit in range(4):
        slot = lax.axis_index("seq") ^ bit ^ place
        value = total_ref[bit]
        if bit % 2:
            weight = (partner_w if bit == 1 else fourth_w)[...]
            value += jnp.dot(late_ref[...], weight, preferred_element_type=jnp.float32)

        @pl.when(slot % 2 == 1)
        def _():
            send_ref[slot // 2] = value.astype(send_ref.dtype)

        @pl.when(slot % 2 == 0)
        def _():
            keep_ref[slot // 2] = value


def by_head(video_cache, plan, alignment, audio_tokens, kv_weight, query_weight, out_weight):
    seq_size = lax.axis_size("seq")
    seq_at = lax.axis_index("seq")
    video_rows = video_cache.shape[1]
    audio_rows = audio_tokens.shape[0]
    half_depth, width = kv_weight.shape[0] // 2, 2 * HEAD_DIM
    query_quarter = query_weight.shape[0] // 4

    def bfloat(*shape):
        return jax.ShapeDtypeStruct(shape, jnp.bfloat16)

    packed, other, out_half = kernel_call(
        first_body,
        [
            bfloat(2 * video_rows + audio_rows, half_depth),
            bfloat(half_depth + query_quarter, kv_weight.shape[1]),
            bfloat(out_weight.shape[0] // 2, out_weight.shape[1]),
        ],
        [plan, video_cache, audio_tokens, kv_weight, query_weight, out_weight],
        scratch=[
            pltpu.VMEM((3, video_rows, 2 * half_depth), jnp.bfloat16),
            pltpu.VMEM((2 * video_rows + audio_rows, half_depth), jnp.bfloat16),
            pltpu.VMEM((half_depth + query_quarter, kv_weight.shape[1]), jnp.bfloat16),
            pltpu.VMEM((out_weight.shape[0] // 2, out_weight.shape[1]), jnp.bfloat16),
            pltpu.SMEM(plan.shape, jnp.int32),
            pltpu.SemaphoreType.DMA((26,)),
        ],
        loose_in=(0, 1, 2, 3, 4, 5),
        loose_out=(0, 1, 2),
        limit=61,
    )

    tokens = [packed, swap(packed, "seq", 1), swap(packed, "seq", 2)]
    across = [swap(packed, "mem", 1)]
    other = swap(other, "rep", 1)
    rows = half_depth // 2 + query_quarter // 2
    weight_own, *pieces = kernel_call(
        weight_body,
        [bfloat(2 * rows, 2 * width)] + [bfloat(rows + 16, 2 * width)] * 3,
        [alignment[None], kv_weight, query_weight, other],
        limit=4,
    )
    pieces = [swap(piece, "seq", bit) for bit, piece in enumerate(pieces, 1)]

    across += [swap(tokens[1], "mem", 1), swap(tokens[2], "mem", 1)]
    near_align = pieces[0][rows:, :audio_rows].astype(jnp.float32)
    tokens[2], near_align = lax.optimization_barrier((tokens[2], near_align))
    tokens.append(swap(tokens[2], "seq", 1))
    pieces[0], across[0], across[1] = lax.optimization_barrier(
        (pieces[0], across[0], across[1])
    )
    rest = [swap(pieces[0], "grp", 1)]
    tokens[3], across[2], rest[0], pieces[1] = lax.optimization_barrier(
        (tokens[3], across[2], rest[0], pieces[1])
    )
    across.append(swap(tokens[3], "mem", 1))
    rest.append(swap(pieces[1], "grp", 1))
    pieces[2], rest[1] = lax.optimization_barrier((pieces[2], rest[1]))
    rest.append(swap(pieces[2], "grp", 1))

    out_half, tokens[3] = lax.optimization_barrier((out_half, tokens[3]))
    out_third, out_partner = swap(out_half, "seq", 2), swap(out_half, "seq", 1)
    weights = [weight_own]
    for piece, other in zip(pieces, rest):
        weights += [piece, other]
    rows = seq_size * (video_rows + audio_rows // 2)
    sums = jax.ShapeDtypeStruct((rows, width), jnp.float32)
    aligns, send, keep = kernel_call(
        products_body,
        [bfloat(4, 16, audio_rows), sums, sums],
        [value for pair in zip(tokens, across) for value in pair] + weights
        + [alignment[None], near_align],
        scratch=[
            pltpu.VMEM((seq_size * video_rows, 4 * half_depth), jnp.bfloat16),
            pltpu.VMEM((seq_size * audio_rows, 8 * query_quarter), jnp.bfloat16),
            pltpu.VMEM((4 * half_depth, 2 * width), jnp.bfloat16),
            pltpu.VMEM((8 * query_quarter, width), jnp.bfloat16),
        ],
        limit=15,
    )
    send, out_third = lax.optimization_barrier((send, out_third))
    came = swap(send, "rep", 1)
    third_rest, out_fourth = swap(out_third, "grp", 1), swap(out_third, "seq", 1)

    span = video_rows * seq_size
    blocks = jnp.stack([seq_at, seq_at ^ 1, seq_at ^ 2, seq_at ^ 3])
    positions = blocks[:, None] * video_rows + jnp.arange(video_rows, dtype=jnp.int32)[None, :]
    frames_video = (positions.reshape(1, span) * FRAMES // span).astype(jnp.float32)
    own_piece, near_piece, far_piece, farther_piece = kernel_call(
        attention_body,
        [bfloat(audio_rows, HEAD_DIM)] * 4,
        [frames_video, aligns, keep, came],
        scratch=[
            pltpu.VMEM((span, width), jnp.bfloat16),
            pltpu.VMEM((seq_size, audio_rows, HEAD_DIM), jnp.bfloat16),
        ],
        limit=9,
    )
    third_rest, out_partner, own_piece = lax.optimization_barrier(
        (third_rest, out_partner, own_piece)
    )
    fourth_rest, partner_rest = swap(third_rest, "seq", 1), swap(out_partner, "grp", 1)
    far_piece = swap(far_piece, "seq", 2)
    farther_piece = swap(farther_piece, "seq", 3)
    near_piece = swap(near_piece, "seq", 1)

    columns = out_weight.shape[1]
    total, late_heads = kernel_call(
        out_body,
        [
            jax.ShapeDtypeStruct((seq_size, audio_rows, columns), jnp.float32),
            bfloat(audio_rows, 2 * HEAD_DIM),
        ],
        [
            own_piece,
            near_piece,
            far_piece,
            farther_piece,
            audio_tokens,
            out_weight,
            out_partner,
            out_third,
            third_rest,
            out_fourth,
        ],
        scratch=[
            pltpu.VMEM((seq_size, audio_rows, HEAD_DIM), jnp.bfloat16),
            pltpu.VMEM((2, *out_weight.shape), jnp.bfloat16),
            pltpu.VMEM((audio_rows, columns), jnp.bfloat16),
            pltpu.SemaphoreType.DMA((2,)),
        ],
        loose_in=(4, 5),
        limit=7,
        cost=pl.CostEstimate(flops=10000000000, bytes_accessed=10000000, transcendentals=0),
    )
    send, keep = kernel_call(
        late_out_body,
        [
            bfloat(2, audio_rows, columns),
            jax.ShapeDtypeStruct((2, audio_rows, columns), jnp.float32),
        ],
        [total, late_heads, fourth_rest, partner_rest],
        limit=5,
    )
    came = swap(send, "rep", 1)
    across = swap((keep[1] + came[1].astype(jnp.float32)).astype(jnp.bfloat16), "mem", 1)
    own_part = taylor(video_cache, plan, 2 * half_depth)
    audio_output = (
        keep[0] + came[0].astype(jnp.float32) + across.astype(jnp.float32)
    ).astype(jnp.bfloat16)
    return (own_part, audio_output)


def solution(mesh):
    sizes = dict(mesh.shape)
    square = (sizes["grp"], sizes["seq"], sizes["mem"], sizes["rep"]) == (2, 4, 2, 2)

    def on_device(*arrays):
        heads = arrays[5].shape[1] // HEAD_DIM
        return (by_head if square and heads == sizes["seq"] else general)(*arrays)

    return jax.shard_map(
        on_device,
        mesh=mesh,
        in_specs=(
            P(None, ("grp", "seq"), "mem"),
            P("grp"),
            P(("grp", "seq")),
            P(("grp", "seq"), None),
            P("seq", ("mem", "rep")),
            P("seq", ("mem", "rep")),
            P(("mem", "rep"), "seq"),
        ),
        out_specs=(P(("grp", "seq"), "mem"), P(("grp", "seq"), ("mem", "rep"))),
        check_vma=False,
    )
```

```python
import math

import jax
import jax.numpy as jnp
from jax import lax
from jax.experimental import pallas as pl
from jax.experimental.pallas import tpu as pltpu
from jax.sharding import PartitionSpec as P

HEAD_DIM = 128
FRAMES = 24


SLOPE = 4.0


def taylor_ratio(plan):
    history = plan.shape[0]
    step_ids = jnp.arange(history, dtype=jnp.int32)
    marked = step_ids * plan
    last_fresh = jnp.max(marked)
    prior_fresh = jnp.max(jnp.where(step_ids < last_fresh, marked, 0))
    return (history - last_fresh).astype(jnp.float32) / (last_fresh - prior_fresh).astype(
        jnp.float32
    )


def combine(orders, step_ratio):
    values = orders.astype(jnp.float32)
    return (values[0] + step_ratio * values[1] + 0.5 * step_ratio * step_ratio * values[2]).astype(
        jnp.bfloat16
    )


def general(video_cache, plan, alignment, audio_tokens, kv_weight, query_weight, out_weight):
    step_ratio = taylor_ratio(plan)
    own_part = combine(video_cache, step_ratio)
    features_all = lax.all_gather(own_part, "mem", axis=1, tiled=True)
    video_rows = features_all.shape[0]
    kv_local = jnp.dot(
        features_all,
        lax.all_gather(kv_weight, "seq", axis=0, tiled=True),
        preferred_element_type=jnp.float32,
    )
    head_size = HEAD_DIM
    local_heads = query_weight.shape[1] // head_size
    kv_local = kv_local.astype(jnp.bfloat16).reshape(video_rows, local_heads, 2, head_size)
    key_rows = kv_local[:, :, 0, :]
    value_rows = kv_local[:, :, 1, :]
    query_full, out_full = (
        lax.all_gather(query_weight, "seq", axis=0, tiled=True),
        lax.all_gather(out_weight, "seq", axis=1, tiled=True),
    )
    audio_rows = audio_tokens.shape[0]
    queries = jnp.dot(audio_tokens, query_full, preferred_element_type=jnp.float32).astype(
        jnp.bfloat16
    )
    queries = queries.reshape(audio_rows, local_heads, head_size)
    scale = 1.0 / head_size**0.5
    span = video_rows * lax.axis_size("seq")
    initial = (
        jnp.full((local_heads, audio_rows), -1e30, jnp.float32),
        jnp.zeros((local_heads, audio_rows), jnp.float32),
        jnp.zeros((local_heads, audio_rows, head_size), jnp.float32),
    )
    key_piece = lax.all_gather(key_rows, "seq", axis=0, tiled=True)
    value_piece = lax.all_gather(value_rows, "seq", axis=0, tiled=True)
    row_count = key_piece.shape[0]
    block_len = math.gcd(row_count, 1024)

    def advance(block_index, carried):
        row_max, row_sum, weighted = carried
        key_block = lax.dynamic_slice_in_dim(key_piece, block_index * block_len, block_len, 0)
        value_block = lax.dynamic_slice_in_dim(value_piece, block_index * block_len, block_len, 0)
        positions = block_index * block_len + jnp.arange(block_len, dtype=jnp.int32)
        frames_video = positions * FRAMES // span
        distance_bias = (
            -SLOPE
            * jnp.abs(frames_video[None, :] - alignment[:, None]).astype(jnp.float32)
            / FRAMES
        )
        scores = (
            jnp.einsum("qhd,khd->hqk", queries, key_block, preferred_element_type=jnp.float32)
            * scale
        )
        scores = scores + distance_bias[None]
        new_max = jnp.maximum(row_max, jnp.max(scores, axis=2))
        rescale = jnp.exp(row_max - new_max)
        exp_terms = jnp.exp(scores - new_max[:, :, None])
        row_sum = row_sum * rescale + jnp.sum(exp_terms, axis=2)
        weighted = weighted * rescale[:, :, None] + jnp.einsum(
            "hqk,khd->hqd",
            exp_terms.astype(jnp.bfloat16),
            value_block,
            preferred_element_type=jnp.float32,
        )
        return (new_max, row_sum, weighted)

    row_max, row_sum, weighted = lax.fori_loop(0, row_count // block_len, advance, initial)
    attended = (weighted / row_sum[:, :, None]).astype(jnp.bfloat16)
    attended = jnp.transpose(attended, (1, 0, 2)).reshape(audio_rows, local_heads * head_size)
    partial_update = jnp.dot(attended, out_full, preferred_element_type=jnp.float32)
    update = lax.psum_scatter(
        partial_update.astype(jnp.bfloat16), ("mem", "rep"), scatter_dimension=1, tiled=True
    ).astype(jnp.float32)
    own_columns = update.shape[1]
    residual = lax.dynamic_slice_in_dim(
        audio_tokens, lax.axis_index(("mem", "rep")) * own_columns, own_columns, 1
    )
    audio_output = (residual.astype(jnp.float32) + update).astype(jnp.bfloat16)
    return (own_part, audio_output)


def swap(value, axis, bit):
    size = lax.axis_size(axis)
    return lax.ppermute(value, axis, [(i, i ^ bit) for i in range(size)])


VMEM = pl.BlockSpec(memory_space=pltpu.VMEM)
SMEM = pl.BlockSpec(memory_space=pltpu.SMEM)
ANY = pl.BlockSpec(memory_space=pl.ANY)
HBM = pl.BlockSpec(memory_space=pltpu.HBM)


def kernel_call(body, outs, ins, after=(), scratch=(), smem=(), loose_in=(), loose_out=(), limit=14, cost=None):
    def whole(*refs):
        body(*refs[: len(ins)], *refs[len(ins) + len(after) :])

    spots = [SMEM if i in smem else HBM if i in loose_in else VMEM for i in range(len(ins))]
    return pl.pallas_call(
        whole,
        out_shape=outs,
        in_specs=spots + [ANY] * len(after),
        out_specs=[HBM if i in loose_out else VMEM for i in range(len(outs))],
        scratch_shapes=scratch,
        cost_estimate=cost,
        compiler_params=pltpu.CompilerParams(vmem_limit_bytes=limit * 2**20),
    )(*ins, *after)


def plan_ratio(plan_ref, columns):
    history = plan_ref.shape[0]
    last_fresh, prior_fresh = jnp.int32(0), jnp.int32(0)
    for step in range(history):
        fresh = plan_ref[step] == 1
        prior_fresh = jnp.where(fresh, last_fresh, prior_fresh)
        last_fresh = jnp.where(fresh, step, last_fresh)
    ahead = jnp.full((1, columns), history - last_fresh, jnp.int32).astype(jnp.float32)
    apart = jnp.full((1, columns), last_fresh - prior_fresh, jnp.int32).astype(jnp.float32)
    return ahead / apart


def taylor_rows(cache_ref, out_ref, step_ratio, first, last):
    half_square = 0.5 * step_ratio * step_ratio
    for at in range(first, last, 16):
        terms = [cache_ref[order, at : at + 16, :].astype(jnp.float32) for order in range(3)]
        out_ref[at : at + 16, :] = (
            terms[0] + step_ratio * terms[1] + half_square * terms[2]
        ).astype(jnp.bfloat16)


def taylor_body(plan_ref, cache_ref, out_ref):
    rows, columns = out_ref.shape
    taylor_rows(cache_ref, out_ref, plan_ratio(plan_ref, columns), 0, rows)


def taylor(video_cache, plan, width):
    orders, rows, columns = video_cache.shape
    return pl.pallas_call(
        taylor_body,
        out_shape=jax.ShapeDtypeStruct((rows, columns), jnp.bfloat16),
        grid=(columns // width,),
        in_specs=[SMEM, pl.BlockSpec((orders, rows, width), lambda i: (0, 0, i))],
        out_specs=pl.BlockSpec((rows, width), lambda i: (0, i)),
        compiler_params=pltpu.CompilerParams(vmem_limit_bytes=6 * 2**20),
    )(plan, video_cache)


def first_body(
    plan_ref,
    cache_ref,
    audio_ref,
    kv_ref,
    query_ref,
    packed_ref,
    other_ref,
    held_ref,
    made_ref,
    other_vmem,
    plan_smem,
    sems,
):
    rep_at, mem_at = lax.axis_index("rep"), lax.axis_index("mem")
    rows, width = held_ref.shape[1:]
    width = width // 2
    copies = []

    def copy(source, target):
        copies.append(pltpu.make_async_copy(source, target, sems.at[len(copies)]))

    def part(index, size):
        return pl.ds(pl.multiple_of(index * size, size), size)

    plan_copy = pltpu.make_async_copy(plan_ref, plan_smem, sems.at[25])
    plan_copy.start()
    blocks = 2
    step = rows // blocks
    for block in range(blocks):
        at = pl.ds(block * step, step)
        for shard in range(2):
            copy(
                cache_ref.at[:, at, part(2 * shard + rep_at, width)],
                held_ref.at[:, at, pl.ds(shard * width, width)],
            )
    lane = width // 2
    for shard in range(2):
        copy(
            audio_ref.at[:, part(2 * (2 * mem_at + shard) + rep_at, lane)],
            made_ref.at[pl.ds(2 * rows, audio_ref.shape[0]), pl.ds(shard * lane, lane)],
        )
    depth, columns = kv_ref.shape[0] // 2, query_ref.shape[1]
    copy(kv_ref.at[part(1 - rep_at, depth)], other_vmem.at[pl.ds(0, depth)])
    quarter = query_ref.shape[0] // 4
    for side in range(2):
        copy(
            query_ref.at[part(2 * (1 - rep_at) + side, quarter)],
            other_vmem.at[pl.ds(depth, quarter), pl.ds(side * columns, columns)],
        )
    for started in copies:
        started.start()
    plan_copy.wait()
    step_ratio = plan_ratio(plan_smem, width)
    for block in range(blocks):
        for shard in range(2):
            copies[2 * block + shard].wait()
            taylor_rows(
                held_ref.at[:, :, pl.ds(shard * width, width)],
                made_ref.at[pl.ds(shard * rows, rows)],
                step_ratio,
                block * step,
                (block + 1) * step,
            )
            at = pl.ds(shard * rows + block * step, step)
            copy(made_ref.at[at], packed_ref.at[at])
            copies[-1].start()
    audio_at = pl.ds(2 * rows, audio_ref.shape[0])
    stages = (
        (2, made_ref.at[audio_at], packed_ref.at[audio_at]),
        (3, other_vmem, other_ref),
    )
    at = 2 * blocks
    for count, source, target in stages:
        for arriving in copies[at : at + count]:
            arriving.wait()
        at += count
        copy(source, target)
        copies[-1].start()
    for leaving in copies[at:]:
        leaving.wait()


def weight_body(align_ref, kv_ref, query_ref, other_ref, out_w, half_ref, own_ref, *piece_refs):
    seq_at, rep_at, grp_at = (lax.axis_index(name) for name in ("seq", "rep", "grp"))
    kv_half, query_half = kv_ref.shape[0] // 2, query_ref.shape[0] // 2
    kv_rows, query_rows = kv_half // 2, query_half // 2
    fold = query_rows // 2

    def fill(out_ref, bit, group, kv_at, query_at):
        head = seq_at ^ bit
        width = 2 * HEAD_DIM
        lanes = pl.ds(pl.multiple_of(head * width, width), width)
        at = pl.ds(pl.multiple_of(rep_at * kv_half + group * kv_rows, kv_rows), kv_rows)
        out_ref[kv_at : kv_at + kv_rows, :width] = kv_ref[at, lanes]
        at = pl.ds(pl.multiple_of(group * kv_rows, kv_rows), kv_rows)
        out_ref[kv_at : kv_at + kv_rows, width:] = other_ref[at, lanes]
        lanes = pl.ds(pl.multiple_of(head * HEAD_DIM, HEAD_DIM), HEAD_DIM)
        other_lanes = pl.ds(
            pl.multiple_of(group * query_ref.shape[1] + head * HEAD_DIM, HEAD_DIM), HEAD_DIM
        )
        for side in range(2):
            first = rep_at * query_half + group * query_rows + side * fold
            at = pl.ds(pl.multiple_of(first, fold), fold)
            to = slice(query_at, query_at + fold)
            out_ref[to, side * width : side * width + HEAD_DIM] = query_ref[at, lanes]
            out_ref[to, side * width + HEAD_DIM : (side + 1) * width] = other_ref[
                kv_half + side * fold : kv_half + (side + 1) * fold, other_lanes
            ]

    depth = half_ref.shape[0]
    half_ref[...] = out_w[pl.ds(pl.multiple_of(grp_at * depth, depth), depth), :]
    for group in range(2):
        fill(own_ref, 0, group, group * kv_rows, kv_half + group * fold)
    for bit, piece_ref in enumerate(piece_refs, 1):
        fill(piece_ref, bit, grp_at, 0, kv_rows)
        spare = (piece_ref.shape[0] - kv_rows - fold, piece_ref.shape[1])
        align = align_ref[...].astype(jnp.float32).astype(piece_ref.dtype)
        row = jnp.concatenate(
            [align, jnp.zeros((1, spare[1] - align.shape[1]), piece_ref.dtype)], axis=1
        )
        piece_ref[kv_rows + fold :, :] = jnp.broadcast_to(row, spare)


def products_body(*refs):
    packed_refs, weight_refs = refs[:8], refs[8:15]
    own_align, near_align, align_ref, send_ref, keep_ref, rows_ref, audio_ref, kv_ref, query_ref = refs[15:]
    seq_at, mem_at, grp_at = (lax.axis_index(name) for name in ("seq", "mem", "grp"))
    rows, audio_rows = rows_ref.shape[0] // 4, audio_ref.shape[0] // 4
    depth, lane = rows_ref.shape[1] // 4, audio_ref.shape[1] // 4
    for at, packed_ref in enumerate(packed_refs):
        slot, mem = divmod(at, 2)
        for part in range(2):
            shard = 2 * (mem_at ^ mem) + part
            lanes = pl.ds(pl.multiple_of(shard * depth, depth), depth)
            rows_ref[slot * rows : (slot + 1) * rows, lanes] = packed_ref[
                part * rows : (part + 1) * rows, :
            ]
            lanes = pl.ds(pl.multiple_of(shard * lane, lane), lane)
            audio_ref[slot * audio_rows : (slot + 1) * audio_rows, lanes] = packed_ref[
                2 * rows :, part * lane : (part + 1) * lane
            ]
    kv_half, fold = depth // 2, lane // 4
    width = query_ref.shape[1]

    def place(piece_ref, shard, group, kv_at, query_at):
        to = pl.ds(pl.multiple_of((2 * shard + group) * kv_half, kv_half), kv_half)
        kv_ref[to, :] = piece_ref[kv_at : kv_at + kv_half, :]
        for side in range(2):
            to = pl.ds(pl.multiple_of((4 * shard + 2 * group + side) * fold, fold), fold)
            query_ref[to, :] = piece_ref[
                query_at : query_at + fold, side * width : (side + 1) * width
            ]

    for group in range(2):
        place(weight_refs[0], seq_at, group, group * kv_half, 2 * kv_half + group * fold)
    for bit in range(1, 4):
        place(weight_refs[2 * bit - 1], seq_at ^ bit, grp_at, 0, kv_half)
        place(weight_refs[2 * bit], seq_at ^ bit, 1 - grp_at, 0, kv_half)
        if bit > 1:
            align_ref[bit] = weight_refs[2 * bit - 1][kv_half + fold :, : align_ref.shape[2]]
    align_ref[1] = near_align[...].astype(align_ref.dtype)
    align_ref[0] = jnp.broadcast_to(
        own_align[...].astype(jnp.float32).astype(align_ref.dtype), align_ref.shape[1:]
    )

    count = 4 * rows
    columns = keep_ref.shape[1]
    total = jnp.dot(rows_ref[...], kv_ref[...], preferred_element_type=jnp.float32)
    keep_ref[:count, :] = total[:, :columns]
    send_ref[:count, :] = total[:, columns:]
    total = jnp.dot(audio_ref[...], query_ref[...], preferred_element_type=jnp.float32)
    folded = 2 * audio_rows
    for side in range(2):
        at = slice(side * folded, (side + 1) * folded)
        to = slice(side * HEAD_DIM, (side + 1) * HEAD_DIM)
        keep_ref[count:, to] = total[at, :HEAD_DIM]
        send_ref[count:, to] = total[at, HEAD_DIM:]


def attend(queries, kv_ref, frames_ref, align):
    scores = lax.dot_general(
        queries,
        kv_ref[:, :HEAD_DIM],
        (((1,), (1,)), ((), ())),
        preferred_element_type=jnp.float32,
    ) * (1.0 / HEAD_DIM**0.5)
    scores = scores - SLOPE * jnp.abs(frames_ref[...] - align) / FRAMES
    exp_terms = jnp.exp(scores - jnp.max(scores, axis=1, keepdims=True))
    weighted = jnp.dot(
        exp_terms.astype(jnp.bfloat16), kv_ref[:, HEAD_DIM:], preferred_element_type=jnp.float32
    )
    return (weighted / jnp.sum(exp_terms, axis=1, keepdims=True)).astype(jnp.bfloat16)


def attention_body(frames_ref, align_ref, keep_ref, came_ref, *refs):
    *out_refs, kv_ref, query_ref = refs
    count, audio_rows = kv_ref.shape[0], query_ref.shape[1]

    def summed(rows, columns=slice(None)):
        return (keep_ref[rows, columns] + came_ref[rows, columns]).astype(jnp.bfloat16)

    kv_ref[...] = summed(slice(0, count))
    for slot in range(4):
        side, half = divmod(slot, 2)
        query_ref[slot] = summed(
            slice(count + half * audio_rows, count + (half + 1) * audio_rows),
            slice(side * HEAD_DIM, (side + 1) * HEAD_DIM),
        )
    for bit, out_ref in enumerate(out_refs):
        align = align_ref[bit].astype(jnp.float32)[:8].T[:, :1]
        out_ref[...] = attend(query_ref[bit], kv_ref, frames_ref, align)


def out_body(*refs):
    piece_refs, (audio_ref, own_w, *part_refs) = refs[:4], refs[4:10]
    total_ref, late_ref, heads_ref, weight_ref, residual_ref, sems = refs[10:]
    seq_at, grp_at = lax.axis_index("seq"), lax.axis_index("grp")
    place = lax.axis_index("mem") * 2 + lax.axis_index("rep")
    copy = pltpu.make_async_copy(own_w, weight_ref.at[0], sems.at[0])
    copy.start()
    width = residual_ref.shape[1]
    columns = pl.ds(pl.multiple_of(place * width, width), width)
    residual_copy = pltpu.make_async_copy(audio_ref.at[:, columns], residual_ref, sems.at[1])
    residual_copy.start()
    for bit, piece_ref in enumerate(piece_refs):
        heads_ref[seq_at ^ bit] = piece_ref[...]
    heads = jnp.concatenate([heads_ref[head] for head in range(heads_ref.shape[0])], axis=1)

    def half(group):
        return jnp.concatenate([heads_ref[2 * group], heads_ref[2 * group + 1]], axis=1)

    mine = half(grp_at)
    late_ref[...] = half(1 - grp_at)
    partner_w, third_w, third_rest_w, fourth_w = part_refs
    depth = partner_w.shape[0]
    weight_ref[1, pl.ds(pl.multiple_of(grp_at * depth, depth), depth)] = third_w[...]
    weight_ref[1, pl.ds(pl.multiple_of((1 - grp_at) * depth, depth), depth)] = third_rest_w[...]

    def product(rows, weight):
        return jnp.dot(rows, weight, preferred_element_type=jnp.float32)

    total_ref[1] = product(mine, partner_w[...])
    total_ref[3] = product(mine, fourth_w[...])
    total_ref[2] = product(heads, weight_ref[1])
    copy.wait()
    total_ref[0] = product(heads, weight_ref[0])
    residual_copy.wait()
    total_ref[seq_at ^ place] += residual_ref[...].astype(jnp.float32)


def late_out_body(total_ref, late_ref, partner_w, fourth_w, send_ref, keep_ref):
    place = lax.axis_index("mem") * 2 + lax.axis_index("rep")
    for bit in range(4):
        slot = lax.axis_index("seq") ^ bit ^ place
        value = total_ref[bit]
        if bit % 2:
            weight = (partner_w if bit == 1 else fourth_w)[...]
            value += jnp.dot(late_ref[...], weight, preferred_element_type=jnp.float32)

        @pl.when(slot % 2 == 1)
        def _():
            send_ref[slot // 2] = value.astype(send_ref.dtype)

        @pl.when(slot % 2 == 0)
        def _():
            keep_ref[slot // 2] = value


def by_head(video_cache, plan, alignment, audio_tokens, kv_weight, query_weight, out_weight):
    seq_size = lax.axis_size("seq")
    seq_at = lax.axis_index("seq")
    video_rows = video_cache.shape[1]
    audio_rows = audio_tokens.shape[0]
    half_depth, width = kv_weight.shape[0] // 2, 2 * HEAD_DIM
    query_quarter = query_weight.shape[0] // 4

    def bfloat(*shape):
        return jax.ShapeDtypeStruct(shape, jnp.bfloat16)

    packed, other = kernel_call(
        first_body,
        [
            bfloat(2 * video_rows + audio_rows, half_depth),
            bfloat(half_depth + query_quarter, kv_weight.shape[1]),
        ],
        [plan, video_cache, audio_tokens, kv_weight, query_weight],
        scratch=[
            pltpu.VMEM((3, video_rows, 2 * half_depth), jnp.bfloat16),
            pltpu.VMEM((2 * video_rows + audio_rows, half_depth), jnp.bfloat16),
            pltpu.VMEM((half_depth + query_quarter, kv_weight.shape[1]), jnp.bfloat16),
            pltpu.SMEM(plan.shape, jnp.int32),
            pltpu.SemaphoreType.DMA((26,)),
        ],
        loose_in=(0, 1, 2, 3, 4),
        loose_out=(0, 1),
        limit=61,
    )

    tokens = [packed, swap(packed, "seq", 1), swap(packed, "seq", 2)]
    across = [swap(packed, "mem", 1)]
    other = swap(other, "rep", 1)
    rows = half_depth // 2 + query_quarter // 2
    out_half, weight_own, *pieces = kernel_call(
        weight_body,
        [bfloat(out_weight.shape[0] // 2, out_weight.shape[1]), bfloat(2 * rows, 2 * width)] + [bfloat(rows + 16, 2 * width)] * 3,
        [alignment[None], kv_weight, query_weight, other, out_weight],
        limit=4,
    )
    pieces = [swap(piece, "seq", bit) for bit, piece in enumerate(pieces, 1)]

    across += [swap(tokens[1], "mem", 1), swap(tokens[2], "mem", 1)]
    near_align = pieces[0][rows:, :audio_rows].astype(jnp.float32)
    tokens[2], near_align = lax.optimization_barrier((tokens[2], near_align))
    tokens.append(swap(tokens[2], "seq", 1))
    pieces[0], across[0], across[1] = lax.optimization_barrier(
        (pieces[0], across[0], across[1])
    )
    rest = [swap(pieces[0], "grp", 1)]
    tokens[3], across[2], rest[0], pieces[1] = lax.optimization_barrier(
        (tokens[3], across[2], rest[0], pieces[1])
    )
    across.append(swap(tokens[3], "mem", 1))
    rest.append(swap(pieces[1], "grp", 1))
    pieces[2], rest[1] = lax.optimization_barrier((pieces[2], rest[1]))
    rest.append(swap(pieces[2], "grp", 1))

    out_half, tokens[3] = lax.optimization_barrier((out_half, tokens[3]))
    out_third, out_partner = swap(out_half, "seq", 2), swap(out_half, "seq", 1)
    weights = [weight_own]
    for piece, other in zip(pieces, rest):
        weights += [piece, other]
    rows = seq_size * (video_rows + audio_rows // 2)
    sums = jax.ShapeDtypeStruct((rows, width), jnp.float32)
    aligns, send, keep = kernel_call(
        products_body,
        [bfloat(4, 16, audio_rows), sums, sums],
        [value for pair in zip(tokens, across) for value in pair] + weights
        + [alignment[None], near_align],
        scratch=[
            pltpu.VMEM((seq_size * video_rows, 4 * half_depth), jnp.bfloat16),
            pltpu.VMEM((seq_size * audio_rows, 8 * query_quarter), jnp.bfloat16),
            pltpu.VMEM((4 * half_depth, 2 * width), jnp.bfloat16),
            pltpu.VMEM((8 * query_quarter, width), jnp.bfloat16),
        ],
        limit=15,
    )
    send, out_third, out_partner = lax.optimization_barrier((send, out_third, out_partner))
    came = swap(send, "rep", 1)
    third_rest, out_fourth = swap(out_third, "grp", 1), swap(out_third, "seq", 1)

    span = video_rows * seq_size
    blocks = jnp.stack([seq_at, seq_at ^ 1, seq_at ^ 2, seq_at ^ 3])
    positions = blocks[:, None] * video_rows + jnp.arange(video_rows, dtype=jnp.int32)[None, :]
    frames_video = (positions.reshape(1, span) * FRAMES // span).astype(jnp.float32)
    own_piece, near_piece, far_piece, farther_piece = kernel_call(
        attention_body,
        [bfloat(audio_rows, HEAD_DIM)] * 4,
        [frames_video, aligns, keep, came],
        scratch=[
            pltpu.VMEM((span, width), jnp.bfloat16),
            pltpu.VMEM((seq_size, audio_rows, HEAD_DIM), jnp.bfloat16),
        ],
        limit=9,
    )
    third_rest, out_partner, own_piece = lax.optimization_barrier(
        (third_rest, out_partner, own_piece)
    )
    fourth_rest, partner_rest = swap(third_rest, "seq", 1), swap(out_partner, "grp", 1)
    far_piece = swap(far_piece, "seq", 2)
    farther_piece = swap(farther_piece, "seq", 3)
    near_piece = swap(near_piece, "seq", 1)

    columns = out_weight.shape[1]
    total, late_heads = kernel_call(
        out_body,
        [
            jax.ShapeDtypeStruct((seq_size, audio_rows, columns), jnp.float32),
            bfloat(audio_rows, 2 * HEAD_DIM),
        ],
        [
            own_piece,
            near_piece,
            far_piece,
            farther_piece,
            audio_tokens,
            out_weight,
            out_partner,
            out_third,
            third_rest,
            out_fourth,
        ],
        scratch=[
            pltpu.VMEM((seq_size, audio_rows, HEAD_DIM), jnp.bfloat16),
            pltpu.VMEM((2, *out_weight.shape), jnp.bfloat16),
            pltpu.VMEM((audio_rows, columns), jnp.bfloat16),
            pltpu.SemaphoreType.DMA((2,)),
        ],
        loose_in=(4, 5),
        limit=7,
        cost=pl.CostEstimate(flops=10000000000, bytes_accessed=10000000, transcendentals=0),
    )
    send, keep = kernel_call(
        late_out_body,
        [
            bfloat(2, audio_rows, columns),
            jax.ShapeDtypeStruct((2, audio_rows, columns), jnp.float32),
        ],
        [total, late_heads, partner_rest, fourth_rest],
        limit=5,
    )
    came = swap(send, "rep", 1)
    across = swap((keep[1] + came[1].astype(jnp.float32)).astype(jnp.bfloat16), "mem", 1)
    own_part = taylor(video_cache, plan, 2 * half_depth)
    audio_output = (
        keep[0] + came[0].astype(jnp.float32) + across.astype(jnp.float32)
    ).astype(jnp.bfloat16)
    return (own_part, audio_output)


def solution(mesh):
    sizes = dict(mesh.shape)
    square = (sizes["grp"], sizes["seq"], sizes["mem"], sizes["rep"]) == (2, 4, 2, 2)

    def on_device(*arrays):
        heads = arrays[5].shape[1] // HEAD_DIM
        return (by_head if square and heads == sizes["seq"] else general)(*arrays)

    return jax.shard_map(
        on_device,
        mesh=mesh,
        in_specs=(
            P(None, ("grp", "seq"), "mem"),
            P("grp"),
            P(("grp", "seq")),
            P(("grp", "seq"), None),
            P("seq", ("mem", "rep")),
            P("seq", ("mem", "rep")),
            P(("mem", "rep"), "seq"),
        ),
        out_specs=(P(("grp", "seq"), "mem"), P(("grp", "seq"), ("mem", "rep"))),
        check_vma=False,
    )
```

```python
import math

import jax
import jax.numpy as jnp
from jax import lax
from jax.experimental import pallas as pl
from jax.experimental.pallas import tpu as pltpu
from jax.sharding import PartitionSpec as P

HEAD_DIM = 128
FRAMES = 24


SLOPE = 4.0


def taylor_ratio(plan):
    history = plan.shape[0]
    step_ids = jnp.arange(history, dtype=jnp.int32)
    marked = step_ids * plan
    last_fresh = jnp.max(marked)
    prior_fresh = jnp.max(jnp.where(step_ids < last_fresh, marked, 0))
    return (history - last_fresh).astype(jnp.float32) / (last_fresh - prior_fresh).astype(
        jnp.float32
    )


def combine(orders, step_ratio):
    values = orders.astype(jnp.float32)
    return (values[0] + step_ratio * values[1] + 0.5 * step_ratio * step_ratio * values[2]).astype(
        jnp.bfloat16
    )


def general(video_cache, plan, alignment, audio_tokens, kv_weight, query_weight, out_weight):
    step_ratio = taylor_ratio(plan)
    own_part = combine(video_cache, step_ratio)
    features_all = lax.all_gather(own_part, "mem", axis=1, tiled=True)
    video_rows = features_all.shape[0]
    kv_local = jnp.dot(
        features_all,
        lax.all_gather(kv_weight, "seq", axis=0, tiled=True),
        preferred_element_type=jnp.float32,
    )
    head_size = HEAD_DIM
    local_heads = query_weight.shape[1] // head_size
    kv_local = kv_local.astype(jnp.bfloat16).reshape(video_rows, local_heads, 2, head_size)
    key_rows = kv_local[:, :, 0, :]
    value_rows = kv_local[:, :, 1, :]
    query_full, out_full = (
        lax.all_gather(query_weight, "seq", axis=0, tiled=True),
        lax.all_gather(out_weight, "seq", axis=1, tiled=True),
    )
    audio_rows = audio_tokens.shape[0]
    queries = jnp.dot(audio_tokens, query_full, preferred_element_type=jnp.float32).astype(
        jnp.bfloat16
    )
    queries = queries.reshape(audio_rows, local_heads, head_size)
    scale = 1.0 / head_size**0.5
    span = video_rows * lax.axis_size("seq")
    initial = (
        jnp.full((local_heads, audio_rows), -1e30, jnp.float32),
        jnp.zeros((local_heads, audio_rows), jnp.float32),
        jnp.zeros((local_heads, audio_rows, head_size), jnp.float32),
    )
    key_piece = lax.all_gather(key_rows, "seq", axis=0, tiled=True)
    value_piece = lax.all_gather(value_rows, "seq", axis=0, tiled=True)
    row_count = key_piece.shape[0]
    block_len = math.gcd(row_count, 1024)

    def advance(block_index, carried):
        row_max, row_sum, weighted = carried
        key_block = lax.dynamic_slice_in_dim(key_piece, block_index * block_len, block_len, 0)
        value_block = lax.dynamic_slice_in_dim(value_piece, block_index * block_len, block_len, 0)
        positions = block_index * block_len + jnp.arange(block_len, dtype=jnp.int32)
        frames_video = positions * FRAMES // span
        distance_bias = (
            -SLOPE
            * jnp.abs(frames_video[None, :] - alignment[:, None]).astype(jnp.float32)
            / FRAMES
        )
        scores = (
            jnp.einsum("qhd,khd->hqk", queries, key_block, preferred_element_type=jnp.float32)
            * scale
        )
        scores = scores + distance_bias[None]
        new_max = jnp.maximum(row_max, jnp.max(scores, axis=2))
        rescale = jnp.exp(row_max - new_max)
        exp_terms = jnp.exp(scores - new_max[:, :, None])
        row_sum = row_sum * rescale + jnp.sum(exp_terms, axis=2)
        weighted = weighted * rescale[:, :, None] + jnp.einsum(
            "hqk,khd->hqd",
            exp_terms.astype(jnp.bfloat16),
            value_block,
            preferred_element_type=jnp.float32,
        )
        return (new_max, row_sum, weighted)

    row_max, row_sum, weighted = lax.fori_loop(0, row_count // block_len, advance, initial)
    attended = (weighted / row_sum[:, :, None]).astype(jnp.bfloat16)
    attended = jnp.transpose(attended, (1, 0, 2)).reshape(audio_rows, local_heads * head_size)
    partial_update = jnp.dot(attended, out_full, preferred_element_type=jnp.float32)
    update = lax.psum_scatter(
        partial_update.astype(jnp.bfloat16), ("mem", "rep"), scatter_dimension=1, tiled=True
    ).astype(jnp.float32)
    own_columns = update.shape[1]
    residual = lax.dynamic_slice_in_dim(
        audio_tokens, lax.axis_index(("mem", "rep")) * own_columns, own_columns, 1
    )
    audio_output = (residual.astype(jnp.float32) + update).astype(jnp.bfloat16)
    return (own_part, audio_output)


def swap(value, axis, bit):
    size = lax.axis_size(axis)
    return lax.ppermute(value, axis, [(i, i ^ bit) for i in range(size)])


VMEM = pl.BlockSpec(memory_space=pltpu.VMEM)
SMEM = pl.BlockSpec(memory_space=pltpu.SMEM)
ANY = pl.BlockSpec(memory_space=pl.ANY)
HBM = pl.BlockSpec(memory_space=pltpu.HBM)


def kernel_call(body, outs, ins, after=(), scratch=(), smem=(), loose_in=(), loose_out=(), limit=14, cost=None):
    def whole(*refs):
        body(*refs[: len(ins)], *refs[len(ins) + len(after) :])

    spots = [SMEM if i in smem else HBM if i in loose_in else VMEM for i in range(len(ins))]
    return pl.pallas_call(
        whole,
        out_shape=outs,
        in_specs=spots + [ANY] * len(after),
        out_specs=[HBM if i in loose_out else VMEM for i in range(len(outs))],
        scratch_shapes=scratch,
        cost_estimate=cost,
        compiler_params=pltpu.CompilerParams(vmem_limit_bytes=limit * 2**20),
    )(*ins, *after)


def plan_ratio(plan_ref, columns):
    history = plan_ref.shape[0]
    last_fresh, prior_fresh = jnp.int32(0), jnp.int32(0)
    for step in range(history):
        fresh = plan_ref[step] == 1
        prior_fresh = jnp.where(fresh, last_fresh, prior_fresh)
        last_fresh = jnp.where(fresh, step, last_fresh)
    ahead = jnp.full((1, columns), history - last_fresh, jnp.int32).astype(jnp.float32)
    apart = jnp.full((1, columns), last_fresh - prior_fresh, jnp.int32).astype(jnp.float32)
    return ahead / apart


def taylor_rows(cache_ref, out_ref, step_ratio, first, last):
    half_square = 0.5 * step_ratio * step_ratio
    for at in range(first, last, 16):
        terms = [cache_ref[order, at : at + 16, :].astype(jnp.float32) for order in range(3)]
        out_ref[at : at + 16, :] = (
            terms[0] + step_ratio * terms[1] + half_square * terms[2]
        ).astype(jnp.bfloat16)


def taylor_body(plan_ref, cache_ref, out_ref):
    rows, columns = out_ref.shape
    taylor_rows(cache_ref, out_ref, plan_ratio(plan_ref, columns), 0, rows)


def taylor(video_cache, plan, width):
    orders, rows, columns = video_cache.shape
    return pl.pallas_call(
        taylor_body,
        out_shape=jax.ShapeDtypeStruct((rows, columns), jnp.bfloat16),
        grid=(columns // width,),
        in_specs=[SMEM, pl.BlockSpec((orders, rows, width), lambda i: (0, 0, i))],
        out_specs=pl.BlockSpec((rows, width), lambda i: (0, i)),
        compiler_params=pltpu.CompilerParams(vmem_limit_bytes=6 * 2**20),
    )(plan, video_cache)


def first_body(
    plan_ref,
    cache_ref,
    audio_ref,
    kv_ref,
    query_ref,
    packed_ref,
    other_ref,
    held_ref,
    made_ref,
    other_vmem,
    plan_smem,
    sems,
):
    rep_at, mem_at = lax.axis_index("rep"), lax.axis_index("mem")
    rows, width = held_ref.shape[1:]
    width = width // 2
    copies = []

    def copy(source, target):
        copies.append(pltpu.make_async_copy(source, target, sems.at[len(copies)]))

    def part(index, size):
        return pl.ds(pl.multiple_of(index * size, size), size)

    plan_copy = pltpu.make_async_copy(plan_ref, plan_smem, sems.at[25])
    plan_copy.start()
    blocks = 2
    step = rows // blocks
    for block in range(blocks):
        at = pl.ds(block * step, step)
        for shard in range(2):
            copy(
                cache_ref.at[:, at, part(2 * shard + rep_at, width)],
                held_ref.at[:, at, pl.ds(shard * width, width)],
            )
    lane = width // 2
    for shard in range(2):
        copy(
            audio_ref.at[:, part(2 * (2 * mem_at + shard) + rep_at, lane)],
            made_ref.at[pl.ds(2 * rows, audio_ref.shape[0]), pl.ds(shard * lane, lane)],
        )
    depth, columns = kv_ref.shape[0] // 2, query_ref.shape[1]
    copy(kv_ref.at[part(1 - rep_at, depth)], other_vmem.at[pl.ds(0, depth)])
    quarter = query_ref.shape[0] // 4
    for side in range(2):
        copy(
            query_ref.at[part(2 * (1 - rep_at) + side, quarter)],
            other_vmem.at[pl.ds(depth, quarter), pl.ds(side * columns, columns)],
        )
    for started in copies:
        started.start()
    plan_copy.wait()
    step_ratio = plan_ratio(plan_smem, width)
    for block in range(blocks):
        for shard in range(2):
            copies[2 * block + shard].wait()
            taylor_rows(
                held_ref.at[:, :, pl.ds(shard * width, width)],
                made_ref.at[pl.ds(shard * rows, rows)],
                step_ratio,
                block * step,
                (block + 1) * step,
            )
            at = pl.ds(shard * rows + block * step, step)
            copy(made_ref.at[at], packed_ref.at[at])
            copies[-1].start()
    audio_at = pl.ds(2 * rows, audio_ref.shape[0])
    stages = (
        (2, made_ref.at[audio_at], packed_ref.at[audio_at]),
        (3, other_vmem, other_ref),
    )
    at = 2 * blocks
    for count, source, target in stages:
        for arriving in copies[at : at + count]:
            arriving.wait()
        at += count
        copy(source, target)
        copies[-1].start()
    for leaving in copies[at:]:
        leaving.wait()


def weight_body(align_ref, kv_ref, query_ref, other_ref, out_w, half_ref, own_ref, *piece_refs):
    seq_at, rep_at, grp_at = (lax.axis_index(name) for name in ("seq", "rep", "grp"))
    kv_half, query_half = kv_ref.shape[0] // 2, query_ref.shape[0] // 2
    kv_rows, query_rows = kv_half // 2, query_half // 2
    fold = query_rows // 2

    def fill(out_ref, bit, group, kv_at, query_at):
        head = seq_at ^ bit
        width = 2 * HEAD_DIM
        lanes = pl.ds(pl.multiple_of(head * width, width), width)
        at = pl.ds(pl.multiple_of(rep_at * kv_half + group * kv_rows, kv_rows), kv_rows)
        out_ref[kv_at : kv_at + kv_rows, :width] = kv_ref[at, lanes]
        at = pl.ds(pl.multiple_of(group * kv_rows, kv_rows), kv_rows)
        out_ref[kv_at : kv_at + kv_rows, width:] = other_ref[at, lanes]
        lanes = pl.ds(pl.multiple_of(head * HEAD_DIM, HEAD_DIM), HEAD_DIM)
        other_lanes = pl.ds(
            pl.multiple_of(group * query_ref.shape[1] + head * HEAD_DIM, HEAD_DIM), HEAD_DIM
        )
        for side in range(2):
            first = rep_at * query_half + group * query_rows + side * fold
            at = pl.ds(pl.multiple_of(first, fold), fold)
            to = slice(query_at, query_at + fold)
            out_ref[to, side * width : side * width + HEAD_DIM] = query_ref[at, lanes]
            out_ref[to, side * width + HEAD_DIM : (side + 1) * width] = other_ref[
                kv_half + side * fold : kv_half + (side + 1) * fold, other_lanes
            ]

    depth = half_ref.shape[0]
    half_ref[...] = out_w[pl.ds(pl.multiple_of(grp_at * depth, depth), depth), :]
    for group in range(2):
        fill(own_ref, 0, group, group * kv_rows, kv_half + group * fold)
    for bit, piece_ref in enumerate(piece_refs, 1):
        fill(piece_ref, bit, grp_at, 0, kv_rows)
        spare = (piece_ref.shape[0] - kv_rows - fold, piece_ref.shape[1])
        align = align_ref[...].astype(jnp.float32).astype(piece_ref.dtype)
        row = jnp.concatenate(
            [align, jnp.zeros((1, spare[1] - align.shape[1]), piece_ref.dtype)], axis=1
        )
        piece_ref[kv_rows + fold :, :] = jnp.broadcast_to(row, spare)


def products_body(*refs):
    packed_refs, weight_refs = refs[:8], refs[8:15]
    own_align, near_align, align_ref, send_ref, keep_ref, rows_ref, audio_ref, kv_ref, query_ref = refs[15:]
    seq_at, mem_at, grp_at = (lax.axis_index(name) for name in ("seq", "mem", "grp"))
    rows, audio_rows = rows_ref.shape[0] // 4, audio_ref.shape[0] // 4
    depth, lane = rows_ref.shape[1] // 4, audio_ref.shape[1] // 4
    for at, packed_ref in enumerate(packed_refs):
        slot, mem = divmod(at, 2)
        for part in range(2):
            shard = 2 * (mem_at ^ mem) + part
            lanes = pl.ds(pl.multiple_of(shard * depth, depth), depth)
            rows_ref[slot * rows : (slot + 1) * rows, lanes] = packed_ref[
                part * rows : (part + 1) * rows, :
            ]
            lanes = pl.ds(pl.multiple_of(shard * lane, lane), lane)
            audio_ref[slot * audio_rows : (slot + 1) * audio_rows, lanes] = packed_ref[
                2 * rows :, part * lane : (part + 1) * lane
            ]
    kv_half, fold = depth // 2, lane // 4
    width = query_ref.shape[1]

    def place(piece_ref, shard, group, kv_at, query_at):
        to = pl.ds(pl.multiple_of((2 * shard + group) * kv_half, kv_half), kv_half)
        kv_ref[to, :] = piece_ref[kv_at : kv_at + kv_half, :]
        for side in range(2):
            to = pl.ds(pl.multiple_of((4 * shard + 2 * group + side) * fold, fold), fold)
            query_ref[to, :] = piece_ref[
                query_at : query_at + fold, side * width : (side + 1) * width
            ]

    for group in range(2):
        place(weight_refs[0], seq_at, group, group * kv_half, 2 * kv_half + group * fold)
    for bit in range(1, 4):
        place(weight_refs[2 * bit - 1], seq_at ^ bit, grp_at, 0, kv_half)
        place(weight_refs[2 * bit], seq_at ^ bit, 1 - grp_at, 0, kv_half)
        if bit > 1:
            align_ref[bit] = weight_refs[2 * bit - 1][kv_half + fold :, : align_ref.shape[2]]
    align_ref[1] = near_align[...].astype(align_ref.dtype)
    align_ref[0] = jnp.broadcast_to(
        own_align[...].astype(jnp.float32).astype(align_ref.dtype), align_ref.shape[1:]
    )

    count = 4 * rows
    columns = keep_ref.shape[1]
    total = jnp.dot(rows_ref[...], kv_ref[...], preferred_element_type=jnp.float32)
    keep_ref[:count, :] = total[:, :columns]
    send_ref[:count, :] = total[:, columns:]
    total = jnp.dot(audio_ref[...], query_ref[...], preferred_element_type=jnp.float32)
    folded = 2 * audio_rows
    for side in range(2):
        at = slice(side * folded, (side + 1) * folded)
        to = slice(side * HEAD_DIM, (side + 1) * HEAD_DIM)
        keep_ref[count:, to] = total[at, :HEAD_DIM]
        send_ref[count:, to] = total[at, HEAD_DIM:]


def attend(queries, kv_ref, frames_ref, align):
    scores = lax.dot_general(
        queries,
        kv_ref[:, :HEAD_DIM],
        (((1,), (1,)), ((), ())),
        preferred_element_type=jnp.float32,
    ) * (1.0 / HEAD_DIM**0.5)
    scores = scores - jnp.abs(frames_ref[...] - align)
    exp_terms = jnp.exp(scores - jnp.max(scores, axis=1, keepdims=True))
    weighted = jnp.dot(
        exp_terms.astype(jnp.bfloat16), kv_ref[:, HEAD_DIM:], preferred_element_type=jnp.float32
    )
    return (weighted / jnp.sum(exp_terms, axis=1, keepdims=True)).astype(jnp.bfloat16)


def attention_body(frames_ref, align_ref, keep_ref, came_ref, *refs):
    *out_refs, kv_ref, query_ref = refs
    count, audio_rows = kv_ref.shape[0], query_ref.shape[1]

    def summed(rows, columns=slice(None)):
        return (keep_ref[rows, columns] + came_ref[rows, columns]).astype(jnp.bfloat16)

    kv_ref[...] = summed(slice(0, count))
    for slot in range(4):
        side, half = divmod(slot, 2)
        query_ref[slot] = summed(
            slice(count + half * audio_rows, count + (half + 1) * audio_rows),
            slice(side * HEAD_DIM, (side + 1) * HEAD_DIM),
        )
    for bit, out_ref in enumerate(out_refs):
        align = (align_ref[bit].astype(jnp.float32)[:8] * (SLOPE / FRAMES)).T[:, :1]
        out_ref[...] = attend(query_ref[bit], kv_ref, frames_ref, align)


def out_body(*refs):
    piece_refs, (audio_ref, own_w, *part_refs) = refs[:4], refs[4:10]
    total_ref, late_ref, heads_ref, weight_ref, residual_ref, sems = refs[10:]
    seq_at, grp_at = lax.axis_index("seq"), lax.axis_index("grp")
    place = lax.axis_index("mem") * 2 + lax.axis_index("rep")
    copy = pltpu.make_async_copy(own_w, weight_ref.at[0], sems.at[0])
    copy.start()
    width = residual_ref.shape[1]
    columns = pl.ds(pl.multiple_of(place * width, width), width)
    residual_copy = pltpu.make_async_copy(audio_ref.at[:, columns], residual_ref, sems.at[1])
    residual_copy.start()
    for bit, piece_ref in enumerate(piece_refs):
        heads_ref[seq_at ^ bit] = piece_ref[...]
    heads = jnp.concatenate([heads_ref[head] for head in range(heads_ref.shape[0])], axis=1)

    def half(group):
        return jnp.concatenate([heads_ref[2 * group], heads_ref[2 * group + 1]], axis=1)

    mine = half(grp_at)
    late_ref[...] = half(1 - grp_at)
    partner_w, third_w, third_rest_w, fourth_w = part_refs
    depth = partner_w.shape[0]
    weight_ref[1, pl.ds(pl.multiple_of(grp_at * depth, depth), depth)] = third_w[...]
    weight_ref[1, pl.ds(pl.multiple_of((1 - grp_at) * depth, depth), depth)] = third_rest_w[...]

    def product(rows, weight):
        return jnp.dot(rows, weight, preferred_element_type=jnp.float32)

    total_ref[1] = product(mine, partner_w[...])
    total_ref[3] = product(mine, fourth_w[...])
    total_ref[2] = product(heads, weight_ref[1])
    copy.wait()
    total_ref[0] = product(heads, weight_ref[0])
    residual_copy.wait()
    total_ref[seq_at ^ place] += residual_ref[...].astype(jnp.float32)


def late_out_body(total_ref, late_ref, partner_w, fourth_w, send_ref, keep_ref):
    place = lax.axis_index("mem") * 2 + lax.axis_index("rep")
    for bit in range(4):
        slot = lax.axis_index("seq") ^ bit ^ place
        value = total_ref[bit]
        if bit % 2:
            weight = (partner_w if bit == 1 else fourth_w)[...]
            value += jnp.dot(late_ref[...], weight, preferred_element_type=jnp.float32)

        @pl.when(slot % 2 == 1)
        def _():
            send_ref[slot // 2] = value.astype(send_ref.dtype)

        @pl.when(slot % 2 == 0)
        def _():
            keep_ref[slot // 2] = value


def by_head(video_cache, plan, alignment, audio_tokens, kv_weight, query_weight, out_weight):
    seq_size = lax.axis_size("seq")
    seq_at = lax.axis_index("seq")
    video_rows = video_cache.shape[1]
    audio_rows = audio_tokens.shape[0]
    half_depth, width = kv_weight.shape[0] // 2, 2 * HEAD_DIM
    query_quarter = query_weight.shape[0] // 4

    def bfloat(*shape):
        return jax.ShapeDtypeStruct(shape, jnp.bfloat16)

    packed, other = kernel_call(
        first_body,
        [
            bfloat(2 * video_rows + audio_rows, half_depth),
            bfloat(half_depth + query_quarter, kv_weight.shape[1]),
        ],
        [plan, video_cache, audio_tokens, kv_weight, query_weight],
        scratch=[
            pltpu.VMEM((3, video_rows, 2 * half_depth), jnp.bfloat16),
            pltpu.VMEM((2 * video_rows + audio_rows, half_depth), jnp.bfloat16),
            pltpu.VMEM((half_depth + query_quarter, kv_weight.shape[1]), jnp.bfloat16),
            pltpu.SMEM(plan.shape, jnp.int32),
            pltpu.SemaphoreType.DMA((26,)),
        ],
        loose_in=(0, 1, 2, 3, 4),
        loose_out=(0, 1),
        limit=61,
    )

    tokens = [packed, swap(packed, "seq", 1), swap(packed, "seq", 2)]
    across = [swap(packed, "mem", 1)]
    other = swap(other, "rep", 1)
    rows = half_depth // 2 + query_quarter // 2
    out_half, weight_own, *pieces = kernel_call(
        weight_body,
        [bfloat(out_weight.shape[0] // 2, out_weight.shape[1]), bfloat(2 * rows, 2 * width)] + [bfloat(rows + 16, 2 * width)] * 3,
        [alignment[None], kv_weight, query_weight, other, out_weight],
        limit=4,
    )
    pieces = [swap(piece, "seq", bit) for bit, piece in enumerate(pieces, 1)]

    across += [swap(tokens[1], "mem", 1), swap(tokens[2], "mem", 1)]
    near_align = pieces[0][rows:, :audio_rows].astype(jnp.float32)
    tokens[2], near_align = lax.optimization_barrier((tokens[2], near_align))
    tokens.append(swap(tokens[2], "seq", 1))
    pieces[0], across[0], across[1] = lax.optimization_barrier(
        (pieces[0], across[0], across[1])
    )
    rest = [swap(pieces[0], "grp", 1)]
    tokens[3], across[2], rest[0], pieces[1] = lax.optimization_barrier(
        (tokens[3], across[2], rest[0], pieces[1])
    )
    across.append(swap(tokens[3], "mem", 1))
    rest.append(swap(pieces[1], "grp", 1))
    pieces[2], rest[1] = lax.optimization_barrier((pieces[2], rest[1]))
    rest.append(swap(pieces[2], "grp", 1))

    out_half, tokens[3] = lax.optimization_barrier((out_half, tokens[3]))
    out_third, out_partner = swap(out_half, "seq", 2), swap(out_half, "seq", 1)
    weights = [weight_own]
    for piece, other in zip(pieces, rest):
        weights += [piece, other]
    rows = seq_size * (video_rows + audio_rows // 2)
    sums = jax.ShapeDtypeStruct((rows, width), jnp.float32)
    aligns, send, keep = kernel_call(
        products_body,
        [bfloat(4, 16, audio_rows), sums, sums],
        [value for pair in zip(tokens, across) for value in pair] + weights
        + [alignment[None], near_align],
        scratch=[
            pltpu.VMEM((seq_size * video_rows, 4 * half_depth), jnp.bfloat16),
            pltpu.VMEM((seq_size * audio_rows, 8 * query_quarter), jnp.bfloat16),
            pltpu.VMEM((4 * half_depth, 2 * width), jnp.bfloat16),
            pltpu.VMEM((8 * query_quarter, width), jnp.bfloat16),
        ],
        limit=15,
    )
    send, out_third, out_partner = lax.optimization_barrier((send, out_third, out_partner))
    came = swap(send, "rep", 1)
    third_rest, out_fourth = swap(out_third, "grp", 1), swap(out_third, "seq", 1)

    span = video_rows * seq_size
    blocks = jnp.stack([seq_at, seq_at ^ 1, seq_at ^ 2, seq_at ^ 3])
    positions = blocks[:, None] * video_rows + jnp.arange(video_rows, dtype=jnp.int32)[None, :]
    frames_video = (positions.reshape(1, span) * FRAMES // span).astype(jnp.float32)
    frames_video = frames_video * (SLOPE / FRAMES)
    own_piece, near_piece, far_piece, farther_piece = kernel_call(
        attention_body,
        [bfloat(audio_rows, HEAD_DIM)] * 4,
        [frames_video, aligns, keep, came],
        scratch=[
            pltpu.VMEM((span, width), jnp.bfloat16),
            pltpu.VMEM((seq_size, audio_rows, HEAD_DIM), jnp.bfloat16),
        ],
        limit=9,
    )
    third_rest, out_partner, own_piece = lax.optimization_barrier(
        (third_rest, out_partner, own_piece)
    )
    fourth_rest, partner_rest = swap(third_rest, "seq", 1), swap(out_partner, "grp", 1)
    far_piece = swap(far_piece, "seq", 2)
    farther_piece = swap(farther_piece, "seq", 3)
    near_piece = swap(near_piece, "seq", 1)

    columns = out_weight.shape[1]
    total, late_heads = kernel_call(
        out_body,
        [
            jax.ShapeDtypeStruct((seq_size, audio_rows, columns), jnp.float32),
            bfloat(audio_rows, 2 * HEAD_DIM),
        ],
        [
            own_piece,
            near_piece,
            far_piece,
            farther_piece,
            audio_tokens,
            out_weight,
            out_partner,
            out_third,
            third_rest,
            out_fourth,
        ],
        scratch=[
            pltpu.VMEM((seq_size, audio_rows, HEAD_DIM), jnp.bfloat16),
            pltpu.VMEM((2, *out_weight.shape), jnp.bfloat16),
            pltpu.VMEM((audio_rows, columns), jnp.bfloat16),
            pltpu.SemaphoreType.DMA((2,)),
        ],
        loose_in=(4, 5),
        limit=7,
        cost=pl.CostEstimate(flops=10000000000, bytes_accessed=10000000, transcendentals=0),
    )
    send, keep = kernel_call(
        late_out_body,
        [
            bfloat(2, audio_rows, columns),
            jax.ShapeDtypeStruct((2, audio_rows, columns), jnp.float32),
        ],
        [total, late_heads, partner_rest, fourth_rest],
        limit=5,
    )
    came = swap(send, "rep", 1)
    across = swap((keep[1] + came[1].astype(jnp.float32)).astype(jnp.bfloat16), "mem", 1)
    own_part = taylor(video_cache, plan, 2 * half_depth)
    audio_output = (
        keep[0] + came[0].astype(jnp.float32) + across.astype(jnp.float32)
    ).astype(jnp.bfloat16)
    return (own_part, audio_output)


def solution(mesh):
    sizes = dict(mesh.shape)
    square = (sizes["grp"], sizes["seq"], sizes["mem"], sizes["rep"]) == (2, 4, 2, 2)

    def on_device(*arrays):
        heads = arrays[5].shape[1] // HEAD_DIM
        return (by_head if square and heads == sizes["seq"] else general)(*arrays)

    return jax.shard_map(
        on_device,
        mesh=mesh,
        in_specs=(
            P(None, ("grp", "seq"), "mem"),
            P("grp"),
            P(("grp", "seq")),
            P(("grp", "seq"), None),
            P("seq", ("mem", "rep")),
            P("seq", ("mem", "rep")),
            P(("mem", "rep"), "seq"),
        ),
        out_specs=(P(("grp", "seq"), "mem"), P(("grp", "seq"), ("mem", "rep"))),
        check_vma=False,
    )
```

```python
import math

import jax
import jax.numpy as jnp
from jax import lax
from jax.experimental import pallas as pl
from jax.experimental.pallas import tpu as pltpu
from jax.sharding import PartitionSpec as P

HEAD_DIM = 128
FRAMES = 24


SLOPE = 4.0


def taylor_ratio(plan):
    history = plan.shape[0]
    step_ids = jnp.arange(history, dtype=jnp.int32)
    marked = step_ids * plan
    last_fresh = jnp.max(marked)
    prior_fresh = jnp.max(jnp.where(step_ids < last_fresh, marked, 0))
    return (history - last_fresh).astype(jnp.float32) / (last_fresh - prior_fresh).astype(
        jnp.float32
    )


def combine(orders, step_ratio):
    values = orders.astype(jnp.float32)
    return (values[0] + step_ratio * values[1] + 0.5 * step_ratio * step_ratio * values[2]).astype(
        jnp.bfloat16
    )


def general(video_cache, plan, alignment, audio_tokens, kv_weight, query_weight, out_weight):
    step_ratio = taylor_ratio(plan)
    own_part = combine(video_cache, step_ratio)
    features_all = lax.all_gather(own_part, "mem", axis=1, tiled=True)
    video_rows = features_all.shape[0]
    kv_local = jnp.dot(
        features_all,
        lax.all_gather(kv_weight, "seq", axis=0, tiled=True),
        preferred_element_type=jnp.float32,
    )
    head_size = HEAD_DIM
    local_heads = query_weight.shape[1] // head_size
    kv_local = kv_local.astype(jnp.bfloat16).reshape(video_rows, local_heads, 2, head_size)
    key_rows = kv_local[:, :, 0, :]
    value_rows = kv_local[:, :, 1, :]
    query_full, out_full = (
        lax.all_gather(query_weight, "seq", axis=0, tiled=True),
        lax.all_gather(out_weight, "seq", axis=1, tiled=True),
    )
    audio_rows = audio_tokens.shape[0]
    queries = jnp.dot(audio_tokens, query_full, preferred_element_type=jnp.float32).astype(
        jnp.bfloat16
    )
    queries = queries.reshape(audio_rows, local_heads, head_size)
    scale = 1.0 / head_size**0.5
    span = video_rows * lax.axis_size("seq")
    initial = (
        jnp.full((local_heads, audio_rows), -1e30, jnp.float32),
        jnp.zeros((local_heads, audio_rows), jnp.float32),
        jnp.zeros((local_heads, audio_rows, head_size), jnp.float32),
    )
    key_piece = lax.all_gather(key_rows, "seq", axis=0, tiled=True)
    value_piece = lax.all_gather(value_rows, "seq", axis=0, tiled=True)
    row_count = key_piece.shape[0]
    block_len = math.gcd(row_count, 1024)

    def advance(block_index, carried):
        row_max, row_sum, weighted = carried
        key_block = lax.dynamic_slice_in_dim(key_piece, block_index * block_len, block_len, 0)
        value_block = lax.dynamic_slice_in_dim(value_piece, block_index * block_len, block_len, 0)
        positions = block_index * block_len + jnp.arange(block_len, dtype=jnp.int32)
        frames_video = positions * FRAMES // span
        distance_bias = (
            -SLOPE
            * jnp.abs(frames_video[None, :] - alignment[:, None]).astype(jnp.float32)
            / FRAMES
        )
        scores = (
            jnp.einsum("qhd,khd->hqk", queries, key_block, preferred_element_type=jnp.float32)
            * scale
        )
        scores = scores + distance_bias[None]
        new_max = jnp.maximum(row_max, jnp.max(scores, axis=2))
        rescale = jnp.exp(row_max - new_max)
        exp_terms = jnp.exp(scores - new_max[:, :, None])
        row_sum = row_sum * rescale + jnp.sum(exp_terms, axis=2)
        weighted = weighted * rescale[:, :, None] + jnp.einsum(
            "hqk,khd->hqd",
            exp_terms.astype(jnp.bfloat16),
            value_block,
            preferred_element_type=jnp.float32,
        )
        return (new_max, row_sum, weighted)

    row_max, row_sum, weighted = lax.fori_loop(0, row_count // block_len, advance, initial)
    attended = (weighted / row_sum[:, :, None]).astype(jnp.bfloat16)
    attended = jnp.transpose(attended, (1, 0, 2)).reshape(audio_rows, local_heads * head_size)
    partial_update = jnp.dot(attended, out_full, preferred_element_type=jnp.float32)
    update = lax.psum_scatter(
        partial_update.astype(jnp.bfloat16), ("mem", "rep"), scatter_dimension=1, tiled=True
    ).astype(jnp.float32)
    own_columns = update.shape[1]
    residual = lax.dynamic_slice_in_dim(
        audio_tokens, lax.axis_index(("mem", "rep")) * own_columns, own_columns, 1
    )
    audio_output = (residual.astype(jnp.float32) + update).astype(jnp.bfloat16)
    return (own_part, audio_output)


def swap(value, axis, bit):
    size = lax.axis_size(axis)
    return lax.ppermute(value, axis, [(i, i ^ bit) for i in range(size)])


VMEM = pl.BlockSpec(memory_space=pltpu.VMEM)
SMEM = pl.BlockSpec(memory_space=pltpu.SMEM)
ANY = pl.BlockSpec(memory_space=pl.ANY)
HBM = pl.BlockSpec(memory_space=pltpu.HBM)


def kernel_call(body, outs, ins, after=(), scratch=(), smem=(), loose_in=(), loose_out=(), limit=14, cost=None):
    def whole(*refs):
        body(*refs[: len(ins)], *refs[len(ins) + len(after) :])

    spots = [SMEM if i in smem else HBM if i in loose_in else VMEM for i in range(len(ins))]
    return pl.pallas_call(
        whole,
        out_shape=outs,
        in_specs=spots + [ANY] * len(after),
        out_specs=[HBM if i in loose_out else VMEM for i in range(len(outs))],
        scratch_shapes=scratch,
        cost_estimate=cost,
        compiler_params=pltpu.CompilerParams(vmem_limit_bytes=limit * 2**20),
    )(*ins, *after)


def plan_ratio(plan_ref, columns):
    history = plan_ref.shape[0]
    last_fresh, prior_fresh = jnp.int32(0), jnp.int32(0)
    for step in range(history):
        fresh = plan_ref[step] == 1
        prior_fresh = jnp.where(fresh, last_fresh, prior_fresh)
        last_fresh = jnp.where(fresh, step, last_fresh)
    ahead = jnp.full((1, columns), history - last_fresh, jnp.int32).astype(jnp.float32)
    apart = jnp.full((1, columns), last_fresh - prior_fresh, jnp.int32).astype(jnp.float32)
    return ahead / apart


def taylor_rows(cache_ref, out_ref, step_ratio, first, last):
    half_square = 0.5 * step_ratio * step_ratio
    for at in range(first, last, 16):
        terms = [cache_ref[order, at : at + 16, :].astype(jnp.float32) for order in range(3)]
        out_ref[at : at + 16, :] = (
            terms[0] + step_ratio * terms[1] + half_square * terms[2]
        ).astype(jnp.bfloat16)


def taylor_body(plan_ref, cache_ref, out_ref):
    rows, columns = out_ref.shape
    taylor_rows(cache_ref, out_ref, plan_ratio(plan_ref, columns), 0, rows)


def taylor(video_cache, plan, width):
    orders, rows, columns = video_cache.shape
    return pl.pallas_call(
        taylor_body,
        out_shape=jax.ShapeDtypeStruct((rows, columns), jnp.bfloat16),
        grid=(columns // width,),
        in_specs=[SMEM, pl.BlockSpec((orders, rows, width), lambda i: (0, 0, i))],
        out_specs=pl.BlockSpec((rows, width), lambda i: (0, i)),
        compiler_params=pltpu.CompilerParams(vmem_limit_bytes=6 * 2**20),
    )(plan, video_cache)


def first_body(
    plan_ref,
    cache_ref,
    audio_ref,
    kv_ref,
    query_ref,
    packed_ref,
    other_ref,
    held_ref,
    made_ref,
    other_vmem,
    plan_smem,
    sems,
):
    rep_at, mem_at = lax.axis_index("rep"), lax.axis_index("mem")
    rows, width = held_ref.shape[1:]
    width = width // 2
    copies = []

    def copy(source, target):
        copies.append(pltpu.make_async_copy(source, target, sems.at[len(copies)]))

    def part(index, size):
        return pl.ds(pl.multiple_of(index * size, size), size)

    plan_copy = pltpu.make_async_copy(plan_ref, plan_smem, sems.at[25])
    plan_copy.start()
    blocks = 2
    step = rows // blocks
    for block in range(blocks):
        at = pl.ds(block * step, step)
        for shard in range(2):
            copy(
                cache_ref.at[:, at, part(2 * shard + rep_at, width)],
                held_ref.at[:, at, pl.ds(shard * width, width)],
            )
    lane = width // 2
    for shard in range(2):
        copy(
            audio_ref.at[:, part(2 * (2 * mem_at + shard) + rep_at, lane)],
            made_ref.at[pl.ds(2 * rows, audio_ref.shape[0]), pl.ds(shard * lane, lane)],
        )
    depth, columns = kv_ref.shape[0] // 2, query_ref.shape[1]
    copy(kv_ref.at[part(1 - rep_at, depth)], other_vmem.at[pl.ds(0, depth)])
    quarter = query_ref.shape[0] // 4
    for side in range(2):
        copy(
            query_ref.at[part(2 * (1 - rep_at) + side, quarter)],
            other_vmem.at[pl.ds(depth, quarter), pl.ds(side * columns, columns)],
        )
    for started in copies:
        started.start()
    plan_copy.wait()
    step_ratio = plan_ratio(plan_smem, width)
    for block in range(blocks):
        for shard in range(2):
            copies[2 * block + shard].wait()
            taylor_rows(
                held_ref.at[:, :, pl.ds(shard * width, width)],
                made_ref.at[pl.ds(shard * rows, rows)],
                step_ratio,
                block * step,
                (block + 1) * step,
            )
            at = pl.ds(shard * rows + block * step, step)
            copy(made_ref.at[at], packed_ref.at[at])
            copies[-1].start()
    audio_at = pl.ds(2 * rows, audio_ref.shape[0])
    stages = (
        (2, made_ref.at[audio_at], packed_ref.at[audio_at]),
        (3, other_vmem, other_ref),
    )
    at = 2 * blocks
    for count, source, target in stages:
        for arriving in copies[at : at + count]:
            arriving.wait()
        at += count
        copy(source, target)
        copies[-1].start()
    for leaving in copies[at:]:
        leaving.wait()


def weight_body(align_ref, kv_ref, query_ref, other_ref, out_w, half_ref, own_ref, *piece_refs):
    seq_at, rep_at, grp_at = (lax.axis_index(name) for name in ("seq", "rep", "grp"))
    kv_half, query_half = kv_ref.shape[0] // 2, query_ref.shape[0] // 2
    kv_rows, query_rows = kv_half // 2, query_half // 2
    fold = query_rows // 2

    def fill(out_ref, bit, group, kv_at, query_at):
        head = seq_at ^ bit
        width = 2 * HEAD_DIM
        lanes = pl.ds(pl.multiple_of(head * width, width), width)
        at = pl.ds(pl.multiple_of(rep_at * kv_half + group * kv_rows, kv_rows), kv_rows)
        out_ref[kv_at : kv_at + kv_rows, :width] = kv_ref[at, lanes]
        at = pl.ds(pl.multiple_of(group * kv_rows, kv_rows), kv_rows)
        out_ref[kv_at : kv_at + kv_rows, width:] = other_ref[at, lanes]
        lanes = pl.ds(pl.multiple_of(head * HEAD_DIM, HEAD_DIM), HEAD_DIM)
        other_lanes = pl.ds(
            pl.multiple_of(group * query_ref.shape[1] + head * HEAD_DIM, HEAD_DIM), HEAD_DIM
        )
        for side in range(2):
            first = rep_at * query_half + group * query_rows + side * fold
            at = pl.ds(pl.multiple_of(first, fold), fold)
            to = slice(query_at, query_at + fold)
            out_ref[to, side * width : side * width + HEAD_DIM] = query_ref[at, lanes]
            out_ref[to, side * width + HEAD_DIM : (side + 1) * width] = other_ref[
                kv_half + side * fold : kv_half + (side + 1) * fold, other_lanes
            ]

    depth = half_ref.shape[0]
    half_ref[...] = out_w[pl.ds(pl.multiple_of(grp_at * depth, depth), depth), :]
    for group in range(2):
        fill(own_ref, 0, group, group * kv_rows, kv_half + group * fold)
    for bit, piece_ref in enumerate(piece_refs, 1):
        fill(piece_ref, bit, grp_at, 0, kv_rows)
        spare = (piece_ref.shape[0] - kv_rows - fold, piece_ref.shape[1])
        align = align_ref[...].astype(jnp.float32).astype(piece_ref.dtype)
        row = jnp.concatenate(
            [align, jnp.zeros((1, spare[1] - align.shape[1]), piece_ref.dtype)], axis=1
        )
        piece_ref[kv_rows + fold :, :] = jnp.broadcast_to(row, spare)


def products_body(*refs):
    packed_refs, weight_refs = refs[:8], refs[8:15]
    own_align, near_align, align_ref, send_ref, keep_ref, rows_ref, audio_ref, kv_ref, query_ref = refs[15:]
    seq_at, mem_at, grp_at = (lax.axis_index(name) for name in ("seq", "mem", "grp"))
    rows, audio_rows = rows_ref.shape[0] // 4, audio_ref.shape[0] // 4
    depth, lane = rows_ref.shape[1] // 4, audio_ref.shape[1] // 4
    for at, packed_ref in enumerate(packed_refs):
        slot, mem = divmod(at, 2)
        for part in range(2):
            shard = 2 * (mem_at ^ mem) + part
            lanes = pl.ds(pl.multiple_of(shard * depth, depth), depth)
            rows_ref[slot * rows : (slot + 1) * rows, lanes] = packed_ref[
                part * rows : (part + 1) * rows, :
            ]
            lanes = pl.ds(pl.multiple_of(shard * lane, lane), lane)
            audio_ref[slot * audio_rows : (slot + 1) * audio_rows, lanes] = packed_ref[
                2 * rows :, part * lane : (part + 1) * lane
            ]
    kv_half, fold = depth // 2, lane // 4
    width = query_ref.shape[1]

    def place(piece_ref, shard, group, kv_at, query_at):
        to = pl.ds(pl.multiple_of((2 * shard + group) * kv_half, kv_half), kv_half)
        kv_ref[to, :] = piece_ref[kv_at : kv_at + kv_half, :]
        for side in range(2):
            to = pl.ds(pl.multiple_of((4 * shard + 2 * group + side) * fold, fold), fold)
            query_ref[to, :] = piece_ref[
                query_at : query_at + fold, side * width : (side + 1) * width
            ]

    for group in range(2):
        place(weight_refs[0], seq_at, group, group * kv_half, 2 * kv_half + group * fold)
    for bit in range(1, 4):
        place(weight_refs[2 * bit - 1], seq_at ^ bit, grp_at, 0, kv_half)
        place(weight_refs[2 * bit], seq_at ^ bit, 1 - grp_at, 0, kv_half)
        if bit > 1:
            align_ref[bit] = weight_refs[2 * bit - 1][kv_half + fold :, : align_ref.shape[2]]
    align_ref[1] = near_align[...].astype(align_ref.dtype)
    align_ref[0] = jnp.broadcast_to(
        own_align[...].astype(jnp.float32).astype(align_ref.dtype), align_ref.shape[1:]
    )

    count = 4 * rows
    columns = keep_ref.shape[1]
    total = jnp.dot(rows_ref[...], kv_ref[...], preferred_element_type=jnp.float32)
    keep_ref[:count, :] = total[:, :columns]
    send_ref[:count, :] = total[:, columns:]
    total = jnp.dot(audio_ref[...], query_ref[...], preferred_element_type=jnp.float32)
    folded = 2 * audio_rows
    for side in range(2):
        at = slice(side * folded, (side + 1) * folded)
        to = slice(side * HEAD_DIM, (side + 1) * HEAD_DIM)
        keep_ref[count:, to] = total[at, :HEAD_DIM]
        send_ref[count:, to] = total[at, HEAD_DIM:]


def attend(queries, kv_ref, frames_ref, align):
    scores = lax.dot_general(
        queries,
        kv_ref[:, :HEAD_DIM],
        (((1,), (1,)), ((), ())),
        preferred_element_type=jnp.float32,
    ) * (1.0 / HEAD_DIM**0.5)
    scores = scores - SLOPE * jnp.abs(frames_ref[...] - align) / FRAMES
    exp_terms = jnp.exp(scores - jnp.max(scores, axis=1, keepdims=True))
    weighted = jnp.dot(
        exp_terms.astype(jnp.bfloat16), kv_ref[:, HEAD_DIM:], preferred_element_type=jnp.float32
    )
    return (weighted / jnp.sum(exp_terms, axis=1, keepdims=True)).astype(jnp.bfloat16)


def attention_body(frames_ref, align_ref, keep_ref, came_ref, *refs):
    *out_refs, kv_ref, query_ref = refs
    count, audio_rows = kv_ref.shape[0], query_ref.shape[1]

    def summed(rows, columns=slice(None)):
        return (keep_ref[rows, columns] + came_ref[rows, columns]).astype(jnp.bfloat16)

    kv_ref[...] = summed(slice(0, count))
    for slot in range(4):
        side, half = divmod(slot, 2)
        query_ref[slot] = summed(
            slice(count + half * audio_rows, count + (half + 1) * audio_rows),
            slice(side * HEAD_DIM, (side + 1) * HEAD_DIM),
        )
    for bit, out_ref in enumerate(out_refs):
        align = align_ref[bit].astype(jnp.float32)[:8].T[:, :1]
        out_ref[...] = attend(query_ref[bit], kv_ref, frames_ref, align)


def out_body(*refs):
    piece_refs, (audio_ref, own_w, *part_refs) = refs[:4], refs[4:10]
    total_ref, late_ref, heads_ref, weight_ref, residual_ref, sems = refs[10:]
    seq_at, grp_at = lax.axis_index("seq"), lax.axis_index("grp")
    place = lax.axis_index("mem") * 2 + lax.axis_index("rep")
    copy = pltpu.make_async_copy(own_w, weight_ref.at[0], sems.at[0])
    copy.start()
    width = residual_ref.shape[1]
    columns = pl.ds(pl.multiple_of(place * width, width), width)
    residual_copy = pltpu.make_async_copy(audio_ref.at[:, columns], residual_ref, sems.at[1])
    residual_copy.start()
    for bit, piece_ref in enumerate(piece_refs):
        heads_ref[seq_at ^ bit] = piece_ref[...]
    heads = jnp.concatenate([heads_ref[head] for head in range(heads_ref.shape[0])], axis=1)

    def half(group):
        return jnp.concatenate([heads_ref[2 * group], heads_ref[2 * group + 1]], axis=1)

    mine = half(grp_at)
    late_ref[...] = half(1 - grp_at)
    partner_w, third_w, third_rest_w, fourth_w = part_refs
    depth = partner_w.shape[0]
    weight_ref[1, pl.ds(pl.multiple_of(grp_at * depth, depth), depth)] = third_w[...]
    weight_ref[1, pl.ds(pl.multiple_of((1 - grp_at) * depth, depth), depth)] = third_rest_w[...]

    def product(rows, weight):
        return jnp.dot(rows, weight, preferred_element_type=jnp.float32)

    total_ref[1] = product(mine, partner_w[...])
    total_ref[3] = product(mine, fourth_w[...])
    total_ref[2] = product(heads, weight_ref[1])
    copy.wait()
    total_ref[0] = product(heads, weight_ref[0])
    residual_copy.wait()
    total_ref[seq_at ^ place] += residual_ref[...].astype(jnp.float32)


def late_out_body(total_ref, late_ref, partner_w, fourth_w, send_ref, keep_ref):
    place = lax.axis_index("mem") * 2 + lax.axis_index("rep")
    for bit in range(4):
        slot = lax.axis_index("seq") ^ bit ^ place
        value = total_ref[bit]
        if bit % 2:
            weight = (partner_w if bit == 1 else fourth_w)[...]
            value += jnp.dot(late_ref[...], weight, preferred_element_type=jnp.float32)

        @pl.when(slot % 2 == 1)
        def _():
            send_ref[slot // 2] = value.astype(send_ref.dtype)

        @pl.when(slot % 2 == 0)
        def _():
            keep_ref[slot // 2] = value


def by_head(video_cache, plan, alignment, audio_tokens, kv_weight, query_weight, out_weight):
    seq_size = lax.axis_size("seq")
    seq_at = lax.axis_index("seq")
    video_rows = video_cache.shape[1]
    audio_rows = audio_tokens.shape[0]
    half_depth, width = kv_weight.shape[0] // 2, 2 * HEAD_DIM
    query_quarter = query_weight.shape[0] // 4

    def bfloat(*shape):
        return jax.ShapeDtypeStruct(shape, jnp.bfloat16)

    packed, other = kernel_call(
        first_body,
        [
            bfloat(2 * video_rows + audio_rows, half_depth),
            bfloat(half_depth + query_quarter, kv_weight.shape[1]),
        ],
        [plan, video_cache, audio_tokens, kv_weight, query_weight],
        scratch=[
            pltpu.VMEM((3, video_rows, 2 * half_depth), jnp.bfloat16),
            pltpu.VMEM((2 * video_rows + audio_rows, half_depth), jnp.bfloat16),
            pltpu.VMEM((half_depth + query_quarter, kv_weight.shape[1]), jnp.bfloat16),
            pltpu.SMEM(plan.shape, jnp.int32),
            pltpu.SemaphoreType.DMA((26,)),
        ],
        loose_in=(0, 1, 2, 3, 4),
        loose_out=(0, 1),
        limit=61,
    )

    tokens = [packed, swap(packed, "seq", 1), swap(packed, "seq", 2)]
    across = [swap(packed, "mem", 1)]
    other = swap(other, "rep", 1)
    rows = half_depth // 2 + query_quarter // 2
    out_half, weight_own, *pieces = kernel_call(
        weight_body,
        [bfloat(out_weight.shape[0] // 2, out_weight.shape[1]), bfloat(2 * rows, 2 * width)] + [bfloat(rows + 16, 2 * width)] * 3,
        [alignment[None], kv_weight, query_weight, other, out_weight],
        limit=4,
    )
    pieces = [swap(piece, "seq", bit) for bit, piece in enumerate(pieces, 1)]

    across += [swap(tokens[1], "mem", 1), swap(tokens[2], "mem", 1)]
    near_align = pieces[0][rows:, :audio_rows].astype(jnp.float32)
    tokens[2], near_align = lax.optimization_barrier((tokens[2], near_align))
    tokens.append(swap(tokens[2], "seq", 1))
    pieces[0], across[0], across[1] = lax.optimization_barrier(
        (pieces[0], across[0], across[1])
    )
    rest = [swap(pieces[0], "grp", 1)]
    tokens[3], across[2], rest[0], pieces[1] = lax.optimization_barrier(
        (tokens[3], across[2], rest[0], pieces[1])
    )
    across.append(swap(tokens[3], "mem", 1))
    rest.append(swap(pieces[1], "grp", 1))
    pieces[2], rest[1] = lax.optimization_barrier((pieces[2], rest[1]))
    rest.append(swap(pieces[2], "grp", 1))

    out_half, tokens[3] = lax.optimization_barrier((out_half, tokens[3]))
    out_third, out_partner = swap(out_half, "seq", 2), swap(out_half, "seq", 1)
    weights = [weight_own]
    for piece, other in zip(pieces, rest):
        weights += [piece, other]
    rows = seq_size * (video_rows + audio_rows // 2)
    sums = jax.ShapeDtypeStruct((rows, width), jnp.float32)
    aligns, send, keep = kernel_call(
        products_body,
        [bfloat(4, 16, audio_rows), sums, sums],
        [value for pair in zip(tokens, across) for value in pair] + weights
        + [alignment[None], near_align],
        scratch=[
            pltpu.VMEM((seq_size * video_rows, 4 * half_depth), jnp.bfloat16),
            pltpu.VMEM((seq_size * audio_rows, 8 * query_quarter), jnp.bfloat16),
            pltpu.VMEM((4 * half_depth, 2 * width), jnp.bfloat16),
            pltpu.VMEM((8 * query_quarter, width), jnp.bfloat16),
        ],
        limit=15,
    )
    send, out_third, out_partner = lax.optimization_barrier((send, out_third, out_partner))
    came = swap(send, "rep", 1)
    third_rest, out_fourth = swap(out_third, "grp", 1), swap(out_third, "seq", 1)

    span = video_rows * seq_size
    blocks = jnp.stack([seq_at, seq_at ^ 1, seq_at ^ 2, seq_at ^ 3])
    positions = blocks[:, None] * video_rows + jnp.arange(video_rows, dtype=jnp.int32)[None, :]
    frames_video = (positions.reshape(1, span) * FRAMES // span).astype(jnp.float32)
    own_piece, near_piece, far_piece, farther_piece = kernel_call(
        attention_body,
        [bfloat(audio_rows, HEAD_DIM)] * 4,
        [frames_video, aligns, keep, came],
        scratch=[
            pltpu.VMEM((span, width), jnp.bfloat16),
            pltpu.VMEM((seq_size, audio_rows, HEAD_DIM), jnp.bfloat16),
        ],
        limit=9,
    )
    partner_rest = swap(out_partner, "grp", 1)
    third_rest, partner_rest, own_piece = lax.optimization_barrier(
        (third_rest, partner_rest, own_piece)
    )
    fourth_rest = swap(third_rest, "seq", 1)
    far_piece = swap(far_piece, "seq", 2)
    farther_piece = swap(farther_piece, "seq", 3)
    near_piece = swap(near_piece, "seq", 1)

    columns = out_weight.shape[1]
    total, late_heads = kernel_call(
        out_body,
        [
            jax.ShapeDtypeStruct((seq_size, audio_rows, columns), jnp.float32),
            bfloat(audio_rows, 2 * HEAD_DIM),
        ],
        [
            own_piece,
            near_piece,
            far_piece,
            farther_piece,
            audio_tokens,
            out_weight,
            out_partner,
            out_third,
            third_rest,
            out_fourth,
        ],
        scratch=[
            pltpu.VMEM((seq_size, audio_rows, HEAD_DIM), jnp.bfloat16),
            pltpu.VMEM((2, *out_weight.shape), jnp.bfloat16),
            pltpu.VMEM((audio_rows, columns), jnp.bfloat16),
            pltpu.SemaphoreType.DMA((2,)),
        ],
        loose_in=(4, 5),
        limit=7,
        cost=pl.CostEstimate(flops=10000000000, bytes_accessed=10000000, transcendentals=0),
    )
    send, keep = kernel_call(
        late_out_body,
        [
            bfloat(2, audio_rows, columns),
            jax.ShapeDtypeStruct((2, audio_rows, columns), jnp.float32),
        ],
        [total, late_heads, partner_rest, fourth_rest],
        limit=5,
    )
    came = swap(send, "rep", 1)
    across = swap((keep[1] + came[1].astype(jnp.float32)).astype(jnp.bfloat16), "mem", 1)
    own_part = taylor(video_cache, plan, 2 * half_depth)
    audio_output = (
        keep[0] + came[0].astype(jnp.float32) + across.astype(jnp.float32)
    ).astype(jnp.bfloat16)
    return (own_part, audio_output)


def solution(mesh):
    sizes = dict(mesh.shape)
    square = (sizes["grp"], sizes["seq"], sizes["mem"], sizes["rep"]) == (2, 4, 2, 2)

    def on_device(*arrays):
        heads = arrays[5].shape[1] // HEAD_DIM
        return (by_head if square and heads == sizes["seq"] else general)(*arrays)

    return jax.shard_map(
        on_device,
        mesh=mesh,
        in_specs=(
            P(None, ("grp", "seq"), "mem"),
            P("grp"),
            P(("grp", "seq")),
            P(("grp", "seq"), None),
            P("seq", ("mem", "rep")),
            P("seq", ("mem", "rep")),
            P(("mem", "rep"), "seq"),
        ),
        out_specs=(P(("grp", "seq"), "mem"), P(("grp", "seq"), ("mem", "rep"))),
        check_vma=False,
    )
```

```python
import math

import jax
import jax.numpy as jnp
from jax import lax
from jax.experimental import pallas as pl
from jax.experimental.pallas import tpu as pltpu
from jax.sharding import PartitionSpec as P

HEAD_DIM = 128
FRAMES = 24


SLOPE = 4.0


def taylor_ratio(plan):
    history = plan.shape[0]
    step_ids = jnp.arange(history, dtype=jnp.int32)
    marked = step_ids * plan
    last_fresh = jnp.max(marked)
    prior_fresh = jnp.max(jnp.where(step_ids < last_fresh, marked, 0))
    return (history - last_fresh).astype(jnp.float32) / (last_fresh - prior_fresh).astype(
        jnp.float32
    )


def combine(orders, step_ratio):
    values = orders.astype(jnp.float32)
    return (values[0] + step_ratio * values[1] + 0.5 * step_ratio * step_ratio * values[2]).astype(
        jnp.bfloat16
    )


def general(video_cache, plan, alignment, audio_tokens, kv_weight, query_weight, out_weight):
    step_ratio = taylor_ratio(plan)
    own_part = combine(video_cache, step_ratio)
    features_all = lax.all_gather(own_part, "mem", axis=1, tiled=True)
    video_rows = features_all.shape[0]
    kv_local = jnp.dot(
        features_all,
        lax.all_gather(kv_weight, "seq", axis=0, tiled=True),
        preferred_element_type=jnp.float32,
    )
    head_size = HEAD_DIM
    local_heads = query_weight.shape[1] // head_size
    kv_local = kv_local.astype(jnp.bfloat16).reshape(video_rows, local_heads, 2, head_size)
    key_rows = kv_local[:, :, 0, :]
    value_rows = kv_local[:, :, 1, :]
    query_full, out_full = (
        lax.all_gather(query_weight, "seq", axis=0, tiled=True),
        lax.all_gather(out_weight, "seq", axis=1, tiled=True),
    )
    audio_rows = audio_tokens.shape[0]
    queries = jnp.dot(audio_tokens, query_full, preferred_element_type=jnp.float32).astype(
        jnp.bfloat16
    )
    queries = queries.reshape(audio_rows, local_heads, head_size)
    scale = 1.0 / head_size**0.5
    span = video_rows * lax.axis_size("seq")
    initial = (
        jnp.full((local_heads, audio_rows), -1e30, jnp.float32),
        jnp.zeros((local_heads, audio_rows), jnp.float32),
        jnp.zeros((local_heads, audio_rows, head_size), jnp.float32),
    )
    key_piece = lax.all_gather(key_rows, "seq", axis=0, tiled=True)
    value_piece = lax.all_gather(value_rows, "seq", axis=0, tiled=True)
    row_count = key_piece.shape[0]
    block_len = math.gcd(row_count, 1024)

    def advance(block_index, carried):
        row_max, row_sum, weighted = carried
        key_block = lax.dynamic_slice_in_dim(key_piece, block_index * block_len, block_len, 0)
        value_block = lax.dynamic_slice_in_dim(value_piece, block_index * block_len, block_len, 0)
        positions = block_index * block_len + jnp.arange(block_len, dtype=jnp.int32)
        frames_video = positions * FRAMES // span
        distance_bias = (
            -SLOPE
            * jnp.abs(frames_video[None, :] - alignment[:, None]).astype(jnp.float32)
            / FRAMES
        )
        scores = (
            jnp.einsum("qhd,khd->hqk", queries, key_block, preferred_element_type=jnp.float32)
            * scale
        )
        scores = scores + distance_bias[None]
        new_max = jnp.maximum(row_max, jnp.max(scores, axis=2))
        rescale = jnp.exp(row_max - new_max)
        exp_terms = jnp.exp(scores - new_max[:, :, None])
        row_sum = row_sum * rescale + jnp.sum(exp_terms, axis=2)
        weighted = weighted * rescale[:, :, None] + jnp.einsum(
            "hqk,khd->hqd",
            exp_terms.astype(jnp.bfloat16),
            value_block,
            preferred_element_type=jnp.float32,
        )
        return (new_max, row_sum, weighted)

    row_max, row_sum, weighted = lax.fori_loop(0, row_count // block_len, advance, initial)
    attended = (weighted / row_sum[:, :, None]).astype(jnp.bfloat16)
    attended = jnp.transpose(attended, (1, 0, 2)).reshape(audio_rows, local_heads * head_size)
    partial_update = jnp.dot(attended, out_full, preferred_element_type=jnp.float32)
    update = lax.psum_scatter(
        partial_update.astype(jnp.bfloat16), ("mem", "rep"), scatter_dimension=1, tiled=True
    ).astype(jnp.float32)
    own_columns = update.shape[1]
    residual = lax.dynamic_slice_in_dim(
        audio_tokens, lax.axis_index(("mem", "rep")) * own_columns, own_columns, 1
    )
    audio_output = (residual.astype(jnp.float32) + update).astype(jnp.bfloat16)
    return (own_part, audio_output)


def swap(value, axis, bit):
    size = lax.axis_size(axis)
    return lax.ppermute(value, axis, [(i, i ^ bit) for i in range(size)])


VMEM = pl.BlockSpec(memory_space=pltpu.VMEM)
SMEM = pl.BlockSpec(memory_space=pltpu.SMEM)
ANY = pl.BlockSpec(memory_space=pl.ANY)
HBM = pl.BlockSpec(memory_space=pltpu.HBM)


def kernel_call(body, outs, ins, after=(), scratch=(), smem=(), loose_in=(), loose_out=(), limit=14, cost=None):
    def whole(*refs):
        body(*refs[: len(ins)], *refs[len(ins) + len(after) :])

    spots = [SMEM if i in smem else HBM if i in loose_in else VMEM for i in range(len(ins))]
    return pl.pallas_call(
        whole,
        out_shape=outs,
        in_specs=spots + [ANY] * len(after),
        out_specs=[HBM if i in loose_out else VMEM for i in range(len(outs))],
        scratch_shapes=scratch,
        cost_estimate=cost,
        compiler_params=pltpu.CompilerParams(vmem_limit_bytes=limit * 2**20),
    )(*ins, *after)


def plan_ratio(plan_ref, columns):
    history = plan_ref.shape[0]
    last_fresh, prior_fresh = jnp.int32(0), jnp.int32(0)
    for step in range(history):
        fresh = plan_ref[step] == 1
        prior_fresh = jnp.where(fresh, last_fresh, prior_fresh)
        last_fresh = jnp.where(fresh, step, last_fresh)
    ahead = jnp.full((1, columns), history - last_fresh, jnp.int32).astype(jnp.float32)
    apart = jnp.full((1, columns), last_fresh - prior_fresh, jnp.int32).astype(jnp.float32)
    return ahead / apart


def taylor_rows(cache_ref, out_ref, step_ratio, first, last):
    half_square = 0.5 * step_ratio * step_ratio
    for at in range(first, last, 16):
        terms = [cache_ref[order, at : at + 16, :].astype(jnp.float32) for order in range(3)]
        out_ref[at : at + 16, :] = (
            terms[0] + step_ratio * terms[1] + half_square * terms[2]
        ).astype(jnp.bfloat16)


def taylor_body(plan_ref, cache_ref, out_ref):
    rows, columns = out_ref.shape
    taylor_rows(cache_ref, out_ref, plan_ratio(plan_ref, columns), 0, rows)


def taylor(video_cache, plan, width):
    orders, rows, columns = video_cache.shape
    return pl.pallas_call(
        taylor_body,
        out_shape=jax.ShapeDtypeStruct((rows, columns), jnp.bfloat16),
        grid=(columns // width,),
        in_specs=[SMEM, pl.BlockSpec((orders, rows, width), lambda i: (0, 0, i))],
        out_specs=pl.BlockSpec((rows, width), lambda i: (0, i)),
        compiler_params=pltpu.CompilerParams(vmem_limit_bytes=6 * 2**20),
    )(plan, video_cache)


def first_body(
    plan_ref,
    cache_ref,
    audio_ref,
    kv_ref,
    query_ref,
    packed_ref,
    other_ref,
    held_ref,
    made_ref,
    other_vmem,
    plan_smem,
    sems,
):
    rep_at, mem_at = lax.axis_index("rep"), lax.axis_index("mem")
    rows, width = held_ref.shape[1:]
    width = width // 2
    copies = []

    def copy(source, target):
        copies.append(pltpu.make_async_copy(source, target, sems.at[len(copies)]))

    def part(index, size):
        return pl.ds(pl.multiple_of(index * size, size), size)

    plan_copy = pltpu.make_async_copy(plan_ref, plan_smem, sems.at[25])
    plan_copy.start()
    blocks = 2
    step = rows // blocks
    for block in range(blocks):
        at = pl.ds(block * step, step)
        for shard in range(2):
            copy(
                cache_ref.at[:, at, part(2 * shard + rep_at, width)],
                held_ref.at[:, at, pl.ds(shard * width, width)],
            )
    lane = width // 2
    for shard in range(2):
        copy(
            audio_ref.at[:, part(2 * (2 * mem_at + shard) + rep_at, lane)],
            made_ref.at[pl.ds(2 * rows, audio_ref.shape[0]), pl.ds(shard * lane, lane)],
        )
    depth, columns = kv_ref.shape[0] // 2, query_ref.shape[1]
    copy(kv_ref.at[part(1 - rep_at, depth)], other_vmem.at[pl.ds(0, depth)])
    quarter = query_ref.shape[0] // 4
    for side in range(2):
        copy(
            query_ref.at[part(2 * (1 - rep_at) + side, quarter)],
            other_vmem.at[pl.ds(depth, quarter), pl.ds(side * columns, columns)],
        )
    for started in copies:
        started.start()
    plan_copy.wait()
    step_ratio = plan_ratio(plan_smem, width)
    for block in range(blocks):
        for shard in range(2):
            copies[2 * block + shard].wait()
            taylor_rows(
                held_ref.at[:, :, pl.ds(shard * width, width)],
                made_ref.at[pl.ds(shard * rows, rows)],
                step_ratio,
                block * step,
                (block + 1) * step,
            )
            at = pl.ds(shard * rows + block * step, step)
            copy(made_ref.at[at], packed_ref.at[at])
            copies[-1].start()
    audio_at = pl.ds(2 * rows, audio_ref.shape[0])
    stages = (
        (2, made_ref.at[audio_at], packed_ref.at[audio_at]),
        (3, other_vmem, other_ref),
    )
    at = 2 * blocks
    for count, source, target in stages:
        for arriving in copies[at : at + count]:
            arriving.wait()
        at += count
        copy(source, target)
        copies[-1].start()
    for leaving in copies[at:]:
        leaving.wait()


def weight_body(align_ref, kv_ref, query_ref, other_ref, out_w, half_ref, own_ref, *piece_refs):
    seq_at, rep_at, grp_at = (lax.axis_index(name) for name in ("seq", "rep", "grp"))
    kv_half, query_half = kv_ref.shape[0] // 2, query_ref.shape[0] // 2
    kv_rows, query_rows = kv_half // 2, query_half // 2
    fold = query_rows // 2

    def fill(out_ref, bit, group, kv_at, query_at):
        head = seq_at ^ bit
        width = 2 * HEAD_DIM
        lanes = pl.ds(pl.multiple_of(head * width, width), width)
        at = pl.ds(pl.multiple_of(rep_at * kv_half + group * kv_rows, kv_rows), kv_rows)
        out_ref[kv_at : kv_at + kv_rows, :width] = kv_ref[at, lanes]
        at = pl.ds(pl.multiple_of(group * kv_rows, kv_rows), kv_rows)
        out_ref[kv_at : kv_at + kv_rows, width:] = other_ref[at, lanes]
        lanes = pl.ds(pl.multiple_of(head * HEAD_DIM, HEAD_DIM), HEAD_DIM)
        other_lanes = pl.ds(
            pl.multiple_of(group * query_ref.shape[1] + head * HEAD_DIM, HEAD_DIM), HEAD_DIM
        )
        for side in range(2):
            first = rep_at * query_half + group * query_rows + side * fold
            at = pl.ds(pl.multiple_of(first, fold), fold)
            to = slice(query_at, query_at + fold)
            out_ref[to, side * width : side * width + HEAD_DIM] = query_ref[at, lanes]
            out_ref[to, side * width + HEAD_DIM : (side + 1) * width] = other_ref[
                kv_half + side * fold : kv_half + (side + 1) * fold, other_lanes
            ]

    depth = half_ref.shape[0]
    half_ref[...] = out_w[pl.ds(pl.multiple_of(grp_at * depth, depth), depth), :]
    for group in range(2):
        fill(own_ref, 0, group, group * kv_rows, kv_half + group * fold)
    for bit, piece_ref in enumerate(piece_refs, 1):
        fill(piece_ref, bit, grp_at, 0, kv_rows)
        spare = (piece_ref.shape[0] - kv_rows - fold, piece_ref.shape[1])
        align = align_ref[...].astype(jnp.float32).astype(piece_ref.dtype)
        row = jnp.concatenate(
            [align, jnp.zeros((1, spare[1] - align.shape[1]), piece_ref.dtype)], axis=1
        )
        piece_ref[kv_rows + fold :, :] = jnp.broadcast_to(row, spare)


def lay_tokens(slot, rows, use_own, own_ref, across_ref, rows_ref, audio_ref):
    depth, lane = rows_ref.shape[1] // 2, audio_ref.shape[1] // 2
    audio_rows = own_ref.shape[0] - 2 * rows
    for used, packed_ref in ((use_own, own_ref), (jnp.logical_not(use_own), across_ref)):

        @pl.when(used)
        def _():
            for part in range(2):
                rows_ref[
                    slot * rows : (slot + 1) * rows, part * depth : (part + 1) * depth
                ] = packed_ref[part * rows : (part + 1) * rows, :]
                audio_ref[
                    slot * audio_rows : (slot + 1) * audio_rows, part * lane : (part + 1) * lane
                ] = packed_ref[2 * rows :, part * lane : (part + 1) * lane]


def lay_weights(piece_ref, part, group, at, kv_ref, query_ref):
    kv_half, fold, width = kv_ref.shape[0] // 4, query_ref.shape[0] // 8, query_ref.shape[1]
    to = pl.ds(pl.multiple_of((2 * part + group) * kv_half, kv_half), kv_half)
    kv_ref[to, :] = piece_ref[at[0] : at[0] + kv_half, :]
    for side in range(2):
        to = pl.ds(pl.multiple_of((4 * part + 2 * group + side) * fold, fold), fold)
        query_ref[to, :] = piece_ref[at[1] : at[1] + fold, side * width : (side + 1) * width]


def half_places():
    seq_at = lax.axis_index("seq")
    return seq_at % 2, lax.axis_index("mem") == seq_at // 2, lax.axis_index("grp")


def near_body(*refs):
    packed_refs, (own_w, near_w, near_rest) = refs[:6], refs[6:9]
    kv_sum, query_sum, kv_ref, query_ref, rows_ref, audio_ref = refs[9:]
    part, use_own, grp_at = half_places()
    rows = rows_ref.shape[0] // 3
    for slot in range(3):
        lay_tokens(slot, rows, use_own, *packed_refs[2 * slot : 2 * slot + 2], rows_ref, audio_ref)
    kv_half, fold = kv_ref.shape[0] // 4, query_ref.shape[0] // 8
    for group in range(2):
        at = (group * kv_half, 2 * kv_half + group * fold)
        lay_weights(own_w, part, group, at, kv_ref, query_ref)
    for group, piece_ref in ((grp_at, near_w), (1 - grp_at, near_rest)):
        lay_weights(piece_ref, 1 - part, group, (0, kv_half), kv_ref, query_ref)
    kv_sum[...] = jnp.dot(rows_ref[...], kv_ref[...], preferred_element_type=jnp.float32)
    query_sum[...] = jnp.dot(audio_ref[...], query_ref[...], preferred_element_type=jnp.float32)


def products_body(*refs):
    packed_refs, piece_refs = refs[:8], refs[8:12]
    kv_sum, query_sum, near_kv, near_query, own_align, near_align = refs[12:18]
    align_ref, send_ref, keep_ref = refs[18:21]
    rows_ref, audio_ref, last_rows, last_audio, kv_ref, query_ref = refs[21:]
    part, use_own, grp_at = half_places()
    rows, audio_rows = last_rows.shape[0], last_audio.shape[0]
    kv_half, fold = kv_ref.shape[0] // 4, query_ref.shape[0] // 8
    lay_tokens(0, rows, use_own, *packed_refs[6:], last_rows, last_audio)
    for slot in range(4):
        across = jnp.logical_not(use_own)
        lay_tokens(slot, rows, across, *packed_refs[2 * slot : 2 * slot + 2], rows_ref, audio_ref)
    for at, shard in enumerate((part, 1 - part)):
        for group, piece_ref in ((grp_at, piece_refs[2 * at]), (1 - grp_at, piece_refs[2 * at + 1])):
            lay_weights(piece_ref, shard, group, (0, kv_half), kv_ref, query_ref)
    align_ref[0] = jnp.broadcast_to(
        own_align[...].astype(jnp.float32).astype(align_ref.dtype), align_ref.shape[1:]
    )
    align_ref[1] = near_align[...].astype(align_ref.dtype)
    for bit, piece_ref in ((2, piece_refs[0]), (3, piece_refs[2])):
        align_ref[bit] = piece_ref[kv_half + fold :, : align_ref.shape[2]]

    def product(left, right):
        return jnp.dot(left[...], right[...], preferred_element_type=jnp.float32)

    columns = keep_ref.shape[1]
    first, count = 3 * rows, 4 * rows
    total = product(rows_ref, kv_ref)
    for at, more in (
        (slice(0, first), kv_sum[...]),
        (slice(first, count), product(last_rows, near_kv)),
    ):
        keep_ref[at, :] = total[at, :columns] + more[:, :columns]
        send_ref[at, :] = total[at, columns:] + more[:, columns:]
    total = product(audio_ref, query_ref)
    last = product(last_audio, near_query)
    for slot in range(4):
        side, half = divmod(slot, 2)
        more = last if slot == 3 else query_sum[slot * audio_rows : (slot + 1) * audio_rows, :]
        part_sum = total[slot * audio_rows : (slot + 1) * audio_rows] + more
        at = slice(count + half * audio_rows, count + (half + 1) * audio_rows)
        to = slice(side * HEAD_DIM, (side + 1) * HEAD_DIM)
        keep_ref[at, to] = part_sum[:, :HEAD_DIM]
        send_ref[at, to] = part_sum[:, HEAD_DIM:]


def attend(queries, kv_ref, frames_ref, align):
    scores = lax.dot_general(
        queries,
        kv_ref[:, :HEAD_DIM],
        (((1,), (1,)), ((), ())),
        preferred_element_type=jnp.float32,
    ) * (1.0 / HEAD_DIM**0.5)
    scores = scores - SLOPE * jnp.abs(frames_ref[...] - align) / FRAMES
    exp_terms = jnp.exp(scores - jnp.max(scores, axis=1, keepdims=True))
    weighted = jnp.dot(
        exp_terms.astype(jnp.bfloat16), kv_ref[:, HEAD_DIM:], preferred_element_type=jnp.float32
    )
    return (weighted / jnp.sum(exp_terms, axis=1, keepdims=True)).astype(jnp.bfloat16)


def attention_body(frames_ref, align_ref, keep_ref, came_ref, *refs):
    *out_refs, kv_ref, query_ref = refs
    count, audio_rows = kv_ref.shape[0], query_ref.shape[1]

    def summed(rows, columns=slice(None)):
        return (keep_ref[rows, columns] + came_ref[rows, columns]).astype(jnp.bfloat16)

    kv_ref[...] = summed(slice(0, count))
    for slot in range(4):
        side, half = divmod(slot, 2)
        query_ref[slot] = summed(
            slice(count + half * audio_rows, count + (half + 1) * audio_rows),
            slice(side * HEAD_DIM, (side + 1) * HEAD_DIM),
        )
    for bit, out_ref in enumerate(out_refs):
        align = align_ref[bit].astype(jnp.float32)[:8].T[:, :1]
        out_ref[...] = attend(query_ref[bit], kv_ref, frames_ref, align)


def out_body(*refs):
    piece_refs, (audio_ref, own_w, *part_refs) = refs[:4], refs[4:10]
    total_ref, late_ref, heads_ref, weight_ref, residual_ref, sems = refs[10:]
    seq_at, grp_at = lax.axis_index("seq"), lax.axis_index("grp")
    place = lax.axis_index("mem") * 2 + lax.axis_index("rep")
    copy = pltpu.make_async_copy(own_w, weight_ref.at[0], sems.at[0])
    copy.start()
    width = residual_ref.shape[1]
    columns = pl.ds(pl.multiple_of(place * width, width), width)
    residual_copy = pltpu.make_async_copy(audio_ref.at[:, columns], residual_ref, sems.at[1])
    residual_copy.start()
    for bit, piece_ref in enumerate(piece_refs):
        heads_ref[seq_at ^ bit] = piece_ref[...]
    heads = jnp.concatenate([heads_ref[head] for head in range(heads_ref.shape[0])], axis=1)

    def half(group):
        return jnp.concatenate([heads_ref[2 * group], heads_ref[2 * group + 1]], axis=1)

    mine = half(grp_at)
    late_ref[...] = half(1 - grp_at)
    partner_w, third_w, third_rest_w, fourth_w = part_refs
    depth = partner_w.shape[0]
    weight_ref[1, pl.ds(pl.multiple_of(grp_at * depth, depth), depth)] = third_w[...]
    weight_ref[1, pl.ds(pl.multiple_of((1 - grp_at) * depth, depth), depth)] = third_rest_w[...]

    def product(rows, weight):
        return jnp.dot(rows, weight, preferred_element_type=jnp.float32)

    total_ref[1] = product(mine, partner_w[...])
    total_ref[3] = product(mine, fourth_w[...])
    total_ref[2] = product(heads, weight_ref[1])
    copy.wait()
    total_ref[0] = product(heads, weight_ref[0])
    residual_copy.wait()
    total_ref[seq_at ^ place] += residual_ref[...].astype(jnp.float32)


def late_out_body(total_ref, late_ref, fourth_w, partner_w, send_ref, keep_ref):
    place = lax.axis_index("mem") * 2 + lax.axis_index("rep")
    for bit in range(4):
        slot = lax.axis_index("seq") ^ bit ^ place
        value = total_ref[bit]
        if bit % 2:
            weight = (partner_w if bit == 1 else fourth_w)[...]
            value += jnp.dot(late_ref[...], weight, preferred_element_type=jnp.float32)

        @pl.when(slot % 2 == 1)
        def _():
            send_ref[slot // 2] = value.astype(send_ref.dtype)

        @pl.when(slot % 2 == 0)
        def _():
            keep_ref[slot // 2] = value


def by_head(video_cache, plan, alignment, audio_tokens, kv_weight, query_weight, out_weight):
    seq_size = lax.axis_size("seq")
    seq_at = lax.axis_index("seq")
    video_rows = video_cache.shape[1]
    audio_rows = audio_tokens.shape[0]
    half_depth, width = kv_weight.shape[0] // 2, 2 * HEAD_DIM
    query_quarter = query_weight.shape[0] // 4

    def bfloat(*shape):
        return jax.ShapeDtypeStruct(shape, jnp.bfloat16)

    packed, other = kernel_call(
        first_body,
        [
            bfloat(2 * video_rows + audio_rows, half_depth),
            bfloat(half_depth + query_quarter, kv_weight.shape[1]),
        ],
        [plan, video_cache, audio_tokens, kv_weight, query_weight],
        scratch=[
            pltpu.VMEM((3, video_rows, 2 * half_depth), jnp.bfloat16),
            pltpu.VMEM((2 * video_rows + audio_rows, half_depth), jnp.bfloat16),
            pltpu.VMEM((half_depth + query_quarter, kv_weight.shape[1]), jnp.bfloat16),
            pltpu.SMEM(plan.shape, jnp.int32),
            pltpu.SemaphoreType.DMA((26,)),
        ],
        loose_in=(0, 1, 2, 3, 4),
        loose_out=(0, 1),
        limit=61,
    )

    tokens = [packed, swap(packed, "seq", 1), swap(packed, "seq", 2)]
    across = [swap(packed, "mem", 1)]
    other = swap(other, "rep", 1)
    rows = (half_depth + query_quarter) // 2
    out_half, weight_own, *pieces = kernel_call(
        weight_body,
        [bfloat(out_weight.shape[0] // 2, out_weight.shape[1]), bfloat(2 * rows, 2 * width)] + [bfloat(rows + 16, 2 * width)] * 3,
        [alignment[None], kv_weight, query_weight, other, out_weight],
        limit=4,
    )
    pieces = [swap(piece, "seq", bit) for bit, piece in enumerate(pieces, 1)]

    across += [swap(tokens[1], "mem", 1), swap(tokens[2], "mem", 1)]
    near_align = pieces[0][rows:, :audio_rows].astype(jnp.float32)
    tokens[2], near_align = lax.optimization_barrier((tokens[2], near_align))
    tokens.append(swap(tokens[2], "seq", 1))
    pieces[0], across[0], across[1] = lax.optimization_barrier(
        (pieces[0], across[0], across[1])
    )
    rest = [swap(pieces[0], "grp", 1)]
    tokens[3], across[2], rest[0], pieces[1] = lax.optimization_barrier(
        (tokens[3], across[2], rest[0], pieces[1])
    )
    packed_shape = (seq_size * video_rows, 2 * half_depth), (seq_size * audio_rows, half_depth)
    weight_shape = (2 * half_depth, 2 * width), (half_depth, width)
    near_sums = kernel_call(
        near_body,
        [
            jax.ShapeDtypeStruct((3 * video_rows, 2 * width), jnp.float32),
            jax.ShapeDtypeStruct((3 * audio_rows, width), jnp.float32),
            *(bfloat(*shape) for shape in weight_shape),
        ],
        [value for pair in zip(tokens[:3], across) for value in pair]
        + [weight_own, pieces[0], rest[0]],
        scratch=[
            pltpu.VMEM((3 * video_rows, 2 * half_depth), jnp.bfloat16),
            pltpu.VMEM((3 * audio_rows, half_depth), jnp.bfloat16),
        ],
        limit=12,
        cost=pl.CostEstimate(flops=1000000000, bytes_accessed=1000000, transcendentals=0),
    )
    across.append(swap(tokens[3], "mem", 1))
    rest.append(swap(pieces[1], "grp", 1))
    pieces[2], rest[1], *near_sums = lax.optimization_barrier((pieces[2], rest[1], *near_sums))
    rest.append(swap(pieces[2], "grp", 1))

    out_half, tokens[3] = lax.optimization_barrier((out_half, tokens[3]))
    out_third, out_partner = swap(out_half, "seq", 2), swap(out_half, "seq", 1)
    rows = seq_size * (video_rows + audio_rows // 2)
    sums = jax.ShapeDtypeStruct((rows, width), jnp.float32)
    aligns, send, keep = kernel_call(
        products_body,
        [bfloat(seq_size, 16, audio_rows), sums, sums],
        [value for pair in zip(tokens, across) for value in pair]
        + [pieces[1], rest[1], pieces[2], rest[2], *near_sums, alignment[None], near_align],
        scratch=[
            *(pltpu.VMEM(shape, jnp.bfloat16) for shape in packed_shape),
            pltpu.VMEM((video_rows, 2 * half_depth), jnp.bfloat16),
            pltpu.VMEM((audio_rows, half_depth), jnp.bfloat16),
            *(pltpu.VMEM(shape, jnp.bfloat16) for shape in weight_shape),
        ],
        limit=14,
    )
    send, out_third, out_partner = lax.optimization_barrier((send, out_third, out_partner))
    came = swap(send, "rep", 1)
    third_rest, out_fourth = swap(out_third, "grp", 1), swap(out_third, "seq", 1)

    span = video_rows * seq_size
    blocks = jnp.stack([seq_at, seq_at ^ 1, seq_at ^ 2, seq_at ^ 3])
    positions = blocks[:, None] * video_rows + jnp.arange(video_rows, dtype=jnp.int32)[None, :]
    frames_video = (positions.reshape(1, span) * FRAMES // span).astype(jnp.float32)
    own_piece, near_piece, far_piece, farther_piece = kernel_call(
        attention_body,
        [bfloat(audio_rows, HEAD_DIM)] * 4,
        [frames_video, aligns, keep, came],
        scratch=[
            pltpu.VMEM((span, width), jnp.bfloat16),
            pltpu.VMEM((seq_size, audio_rows, HEAD_DIM), jnp.bfloat16),
        ],
        limit=9,
    )
    third_rest, out_partner, own_piece = lax.optimization_barrier(
        (third_rest, out_partner, own_piece)
    )
    fourth_rest, partner_rest = swap(third_rest, "seq", 1), swap(out_partner, "grp", 1)
    far_piece = swap(far_piece, "seq", 2)
    farther_piece = swap(farther_piece, "seq", 3)
    near_piece = swap(near_piece, "seq", 1)

    columns = out_weight.shape[1]
    total, late_heads = kernel_call(
        out_body,
        [
            jax.ShapeDtypeStruct((seq_size, audio_rows, columns), jnp.float32),
            bfloat(audio_rows, 2 * HEAD_DIM),
        ],
        [
            own_piece,
            near_piece,
            far_piece,
            farther_piece,
            audio_tokens,
            out_weight,
            out_partner,
            out_third,
            third_rest,
            out_fourth,
        ],
        scratch=[
            pltpu.VMEM((seq_size, audio_rows, HEAD_DIM), jnp.bfloat16),
            pltpu.VMEM((2, *out_weight.shape), jnp.bfloat16),
            pltpu.VMEM((audio_rows, columns), jnp.bfloat16),
            pltpu.SemaphoreType.DMA((2,)),
        ],
        loose_in=(4, 5),
        limit=7,
        cost=pl.CostEstimate(flops=10000000000, bytes_accessed=10000000, transcendentals=0),
    )
    send, keep = kernel_call(
        late_out_body,
        [
            bfloat(2, audio_rows, columns),
            jax.ShapeDtypeStruct((2, audio_rows, columns), jnp.float32),
        ],
        [total, late_heads, fourth_rest, partner_rest],
        limit=5,
    )
    came = swap(send, "rep", 1)
    across = swap((keep[1] + came[1].astype(jnp.float32)).astype(jnp.bfloat16), "mem", 1)
    own_part = taylor(video_cache, plan, 2 * half_depth)
    audio_output = (
        keep[0] + came[0].astype(jnp.float32) + across.astype(jnp.float32)
    ).astype(jnp.bfloat16)
    return (own_part, audio_output)


def solution(mesh):
    sizes = dict(mesh.shape)
    square = (sizes["grp"], sizes["seq"], sizes["mem"], sizes["rep"]) == (2, 4, 2, 2)

    def on_device(*arrays):
        heads = arrays[5].shape[1] // HEAD_DIM
        return (by_head if square and heads == sizes["seq"] else general)(*arrays)

    return jax.shard_map(
        on_device,
        mesh=mesh,
        in_specs=(
            P(None, ("grp", "seq"), "mem"),
            P("grp"),
            P(("grp", "seq")),
            P(("grp", "seq"), None),
            P("seq", ("mem", "rep")),
            P("seq", ("mem", "rep")),
            P(("mem", "rep"), "seq"),
        ),
        out_specs=(P(("grp", "seq"), "mem"), P(("grp", "seq"), ("mem", "rep"))),
        check_vma=False,
    )
```
